32 devices in a mesh: dev: 32 (over z, y, x, core).
Axes of the slice: x: 2, y: 2, z: 4, core: 2. Of those that a mesh axis runs over, the one named last changes fastest.
Arguments:
- tokens: bfloat16 [16384, 768], P('dev'), may hold values from -6 to 6
- cotangent: bfloat16 [16384, 768], P('dev'), may hold values from -6 to 6
- segment_ids: int32 [16384], P('dev'), may hold values from -1 to 127, as said below
- wide_weight: float32 [768, 6144], P('dev')
- wide_moment: float32 [768, 6144], P('dev'), may hold values from -5 to 5
- wide_average: float32 [768, 6144], P('dev'), may hold values from -0.21875 to 0.21875
- down_weight: float32 [3072, 768], P('dev'), may hold values from -0.109375 to 0.109375
- down_moment: float32 [3072, 768], P('dev'), may hold values from -5 to 5
- down_average: float32 [3072, 768], P('dev'), may hold values from -0.109375 to 0.109375
- vector_weight: float32 [12, 768], replicated
- vector_moment: float32 [12, 768], replicated, may hold values from -5 to 5
- vector_average: float32 [12, 768], replicated, may hold values from -3 to 3
Outputs:
- block_output: bfloat16 [16384, 768], P('dev')
- input_grad: bfloat16 [16384, 768], P('dev')
- grad_norm: float32 [], replicated
- wide_new: float32 [768, 6144], P('dev')
- wide_moment_new: float32 [768, 6144], P('dev')
- wide_average_new: float32 [768, 6144], P('dev')
- down_new: float32 [3072, 768], P('dev')
- down_moment_new: float32 [3072, 768], P('dev')
- down_average_new: float32 [3072, 768], P('dev')
- vector_new: float32 [12, 768], replicated
- vector_moment_new: float32 [12, 768], replicated
- vector_average_new: float32 [12, 768], replicated
The draws below stay inside these ranges and needn't reach their ends.
Inputs may be any that keep to these rules, and one draw needn't show every extreme that they name: `segment_ids`: -1 marks an empty row. Among the rows of one device at most 16 carry ids of one group 4 * r to 4 * r + 3, and in every draw one group gets exactly 16 rows from every device. Each group holds at most 512 rows in all.
All inputs are finite; a program needn't handle non-finite values.
Results may differ from the reference program's by a relative error of at most 0.012.
The reference program's roundings to bfloat16 on the way count: a program that leaves them out, or rounds other values in their place, can miss the bound.
Values may be sent and summed in bfloat16 or wider, within the bound.
No kernel may reach another device: no remote copies, remote signals or barrier semaphores. Data moves between devices by JAX's collectives and lax.ppermute only.
A program may use at most 128 MiB of HBM per device.

```python
import jax
import jax.numpy as jnp
from jax import lax

D = 768
HEADS = 12
HEAD = 64
FF = 3072
ROWS = 512
DOCS_DEV = 4
CAP = 16
TOKENS = 16384
NVEC = 12
N_DEV = 32


def draw_segment_ids(key, part):
    key = jax.random.fold_in(key, 11)
    devices = TOKENS // ROWS
    streams = jax.random.split(key, 5)
    base_count = jax.random.randint(streams[0], (devices, devices), 1, CAP + 1)
    extra_load = jax.random.randint(streams[1], (devices, 1), 0, CAP // 2 + 1)
    full_group = jax.random.randint(streams[2], (), 0, devices)
    counts = jnp.minimum(base_count + extra_load, CAP)
    counts = jnp.where(jnp.arange(devices)[None, :] == full_group, CAP, counts)
    slots = jnp.arange(ROWS)
    group = slots // CAP
    within = slots % CAP
    is_live = within[None, :] < counts[:, group]
    member = jax.random.randint(streams[3], (devices, ROWS), 0, DOCS_DEV)
    member = jnp.where(within[None, :] == 0, 0, member)
    ids = jnp.where(is_live, group[None, :] * DOCS_DEV + member, -1)
    orders = jax.vmap(lambda stream: jax.random.permutation(stream, ROWS))(jax.random.split(streams[4], devices))
    ids = jnp.take_along_axis(ids, orders, axis=1)
    return ids.reshape(TOKENS).astype(jnp.int32)


def draw_wide_weight(key, part):
    key = jax.random.fold_in(key, 21)
    shape = (D, 4 * D + FF)
    noise = jax.random.normal(key, shape, jnp.float32)
    column = jnp.arange(4 * D + FF)
    out_fan = max(1, 8 * D * DOCS_DEV // ROWS)
    scale = jnp.where((column >= 3 * D) & (column < 4 * D), out_fan ** (-0.5), D ** (-0.5))
    return (noise * scale[None, :]).astype(jnp.float32)


def draw_vector_weight(key, part):
    key = jax.random.fold_in(key, 31)
    streams = jax.random.split(key, 3)
    place = jnp.arange(D, dtype=jnp.float32) / (D - 1)
    rise = 0.7 * 2.2 ** place
    rough = jax.random.uniform(streams[0], (2, D), jnp.float32, 0.85, 1.18)
    gains = rise[None, :] * rough
    shifts = 0.2 * jax.random.normal(streams[1], (2, D), jnp.float32)
    biases = 0.3 * jax.random.normal(streams[2], (NVEC - 4, D), jnp.float32)
    return jnp.concatenate([gains[0:1], shifts[0:1], gains[1:2], shifts[1:2], biases], 0).astype(jnp.float32)


def shard_levels(stream_key, extent, pieces, least, high):
    gain = 1.0
    for position, blocks in pieces:
        steps = jax.random.uniform(jax.random.fold_in(jax.random.fold_in(stream_key, 6), position), (blocks,), jnp.float32, least / len(pieces), high / len(pieces))
        gain = gain * jnp.repeat(jnp.exp(steps), extent[position] // blocks).reshape((-1,) + (1,) * (len(extent) - 1 - position))
    return gain


def bell_draw(own_key, dims, scale, most, cuts=(), kind=jnp.bfloat16):
    entries = jax.random.normal(own_key, dims, jnp.float32) * scale
    if len(cuts) > 0:
        entries = shard_levels(own_key, dims, cuts, -0.22, 0.18) * entries
    return jnp.clip(entries, min=-most, max=most).astype(kind)


def setup_inputs(seed: int = 0) -> dict:
    streams_of = jax.random.split(jax.random.key(seed), 13)
    return {
        "tokens": bell_draw(streams_of[0], (TOKENS, D), 1.0, 6.0, ((0, 32),)),
        "cotangent": bell_draw(streams_of[1], (TOKENS, D), 1.0, 6.0, ((0, 32),)),
        "segment_ids": draw_segment_ids(jax.random.fold_in(streams_of[12], 71), 0),
        "wide_weight": draw_wide_weight(jax.random.fold_in(streams_of[12], 71), 0),
        "wide_moment": bell_draw(streams_of[4], (D, 4 * D + FF), (2048.0 / (4 * D * D + 2 * D * FF) ** 0.5), 5.0, ((0, 32),), jnp.float32),
        "wide_average": bell_draw(streams_of[5], (D, 4 * D + FF), D ** -0.5, 0.21875, ((0, 32),), jnp.float32),
        "down_weight": bell_draw(streams_of[6], (FF, D), FF ** -0.5, 0.109375, ((0, 32),), jnp.float32),
        "down_moment": bell_draw(streams_of[7], (FF, D), (2048.0 / (4 * D * D + 2 * D * FF) ** 0.5), 5.0, ((0, 32),), jnp.float32),
        "down_average": bell_draw(streams_of[8], (FF, D), FF ** -0.5, 0.109375, ((0, 32),), jnp.float32),
        "vector_weight": draw_vector_weight(jax.random.fold_in(streams_of[12], 71), 0),
        "vector_moment": bell_draw(streams_of[10], (NVEC, D), (2048.0 / (4 * D * D + 2 * D * FF) ** 0.5), 5.0, (), jnp.float32),
        "vector_average": bell_draw(streams_of[11], (NVEC, D), 0.5, 3.0, (), jnp.float32),
    }


@jax.custom_vjp
def low(v):
    return lax.optimization_barrier(v.astype(jnp.bfloat16)).astype(jnp.float32)

@jax.custom_vjp
def low_back(v):
    return v

def low_keep(v):
    return (low(v), None)

def low_pass(kept, grad):
    return (grad,)

def back_keep(v):
    return (v, None)

def back_low(kept, grad):
    return (low(grad),)
low.defvjp(low_keep, low_pass)
low_back.defvjp(back_keep, back_low)
highest = lax.Precision.HIGHEST
epsilon = 1e-05
masked_value = -1e+30
momentum = 0.9
learn_rate = 0.01
decay_rate = 0.0001
average_rate = 0.8
clip_norm = 2048.0

def norm_rows(values, gain_row, shift_row):
    center = values - lax.optimization_barrier(jnp.mean(values, -1, keepdims=True))
    spread = lax.optimization_barrier(jnp.mean(center * center, -1, keepdims=True))
    return center * lax.rsqrt(spread + epsilon) * gain_row + shift_row

def matmul(matrix, other):
    return jnp.dot(matrix, other, precision=highest, preferred_element_type=jnp.float32)

def block(work, work_id, wide_low, down_low, vector):
    gain_one, shift_one, gain_two, shift_two, bias_query, bias_value, bias_out, bias_down = [vector[row_index] for row_index in range(8)]
    bias_up = vector[8:].reshape(FF)
    low_one = low(norm_rows(work, gain_one, shift_one))
    bias_all = jnp.concatenate([bias_query, jnp.zeros((D,), jnp.float32), bias_value])
    projected = low_back(low(matmul(low_one, wide_low[:, :3 * D]) + bias_all))
    queries = projected[:, :D].reshape(ROWS, HEADS, HEAD)
    key_rows = projected[:, D:2 * D].reshape(ROWS, HEADS, HEAD)
    value_rows = projected[:, 2 * D:].reshape(ROWS, HEADS, HEAD)
    same_seg = work_id[:, None] == work_id[None, :]
    block_rows = min(512, ROWS)

    def attend(offset):
        query_part = lax.dynamic_slice_in_dim(queries, offset, block_rows, 0)
        allowed = lax.dynamic_slice_in_dim(same_seg, offset, block_rows, 0)
        scores = low_back(jnp.einsum('qhd,khd->hqk', query_part, key_rows, precision=highest) * 0.125)
        scores = jnp.where(allowed[None], scores, masked_value)
        row_max = lax.optimization_barrier(jnp.max(scores, -1, keepdims=True))
        powers = jnp.exp(scores - row_max)
        prob_low = low(powers / lax.optimization_barrier(jnp.sum(powers, -1, keepdims=True)))
        return jnp.einsum('hqk,khd->qhd', prob_low, value_rows, precision=highest)
    offsets = jnp.arange(ROWS // block_rows, dtype=jnp.int32) * block_rows
    attended = lax.map(jax.checkpoint(attend), offsets).reshape(ROWS, D)
    attended = low_back(low(attended))
    resid = work + low_back(matmul(attended, wide_low[:, 3 * D:4 * D]) + bias_out)
    low_two = low(norm_rows(resid, gain_two, shift_two))
    up_pre = low_back(matmul(low_two, wide_low[:, 4 * D:]) + bias_up)
    hidden = low(jax.nn.gelu(up_pre, approximate=False))
    return resid + low_back(matmul(hidden, down_low) + bias_down)

def routing(segment_ids):
    is_live = segment_ids >= 0
    target = jnp.where(is_live, segment_ids // DOCS_DEV, N_DEV).reshape(N_DEV, ROWS)
    onehot = (target[:, :, None] == jnp.arange(N_DEV, dtype=jnp.int32)[None, None, :]).astype(jnp.int32)
    earlier = jnp.cumsum(onehot, axis=1) - onehot
    within = lax.optimization_barrier(jnp.sum(earlier * onehot, axis=2))
    source = jnp.arange(N_DEV, dtype=jnp.int32)[:, None]
    slot_of = jnp.where(target < N_DEV, target * ROWS + source * CAP + within, TOKENS).reshape(TOKENS).astype(jnp.int32)
    anchor = jnp.full((TOKENS,), TOKENS, jnp.int32).at[slot_of].set(jnp.arange(TOKENS, dtype=jnp.int32), mode='drop')
    return (is_live, jnp.minimum(slot_of, TOKENS - 1).astype(jnp.int32), anchor)

def advance(weight, moment, average, gradient, factor, decay_term):
    update = factor * gradient + decay_term * weight
    new_moment = momentum * moment + update
    new_weight = weight - learn_rate * (update + momentum * new_moment)
    new_average = average_rate * average + (1.0 - average_rate) * new_weight
    return (new_weight, new_moment, new_average)

def reference(tokens, cotangent, segment_ids, wide_weight, wide_moment, wide_average, down_weight, down_moment, down_average, vector_weight, vector_moment, vector_average):
    is_live, slot_of, anchor = routing(segment_ids)
    padded_ids = jnp.concatenate([segment_ids, jnp.full((1,), -1, jnp.int32)], 0)
    work_ids = padded_ids[anchor].reshape(N_DEV, ROWS)

    def forward(token_float, wide, down, vector):
        wide_low = low(wide)
        down_low = low(down)
        padded = jnp.concatenate([token_float, jnp.zeros((1, D), jnp.float32)], 0)
        work = padded[anchor].reshape(N_DEV, ROWS, D)

        def per_device(pair):
            return jax.checkpoint(block)(pair[0], pair[1], wide_low, down_low, vector)
        result = lax.map(per_device, (work, work_ids))
        flat = result.reshape(TOKENS, D)
        return jnp.where(is_live[:, None], flat[slot_of], 0.0)
    output, pull = jax.vjp(forward, tokens.astype(jnp.float32), wide_weight, down_weight, vector_weight)
    input_grad, wide_grad, down_grad, vector_grad = pull(cotangent.astype(jnp.float32))
    total = jnp.sum(wide_grad * wide_grad) + jnp.sum(down_grad * down_grad) + jnp.sum(vector_grad * vector_grad)
    grad_norm = jnp.sqrt(total)
    factor = clip_norm / jnp.maximum(grad_norm, clip_norm)
    wide_new, wide_moment_new, wide_average_new = advance(wide_weight, wide_moment, wide_average, wide_grad, factor, decay_rate)
    down_new, down_moment_new, down_average_new = advance(down_weight, down_moment, down_average, down_grad, factor, decay_rate)
    vector_new, vector_moment_new, vector_average_new = advance(vector_weight, vector_moment, vector_average, vector_grad, factor, 0.0)
    return (output.astype(jnp.bfloat16), input_grad.astype(jnp.bfloat16), grad_norm, wide_new, wide_moment_new, wide_average_new, down_new, down_moment_new, down_average_new, vector_new, vector_moment_new, vector_average_new)
```

```python
import math

import jax
import jax.numpy as jnp
from jax import lax
from jax.experimental import pallas as pl
from jax.experimental.pallas import tpu as pltpu
from jax.sharding import PartitionSpec as P

HEADS = 12
HEAD = 64
FF = 3072
DOCS_DEV = 4
PLANE = 8
MIB = 1 << 20


epsilon = 1e-05
masked_value = -1e30
momentum = 0.9
learn_rate = 0.01
decay_rate = 0.0001
average_rate = 0.8
clip_norm = 2048.0


def norm_rows(values, gain_row, shift_row):
    center = values - jnp.mean(values, -1, keepdims=True)
    spread = jnp.mean(center * center, -1, keepdims=True)
    return center * lax.rsqrt(spread + epsilon) * gain_row + shift_row


def gelu_exact(values):
    return jax.nn.gelu(values, approximate=False)


def product(matrix, other):
    return jnp.dot(matrix, other, preferred_element_type=jnp.float32)


def against(matrix, other):
    return lax.dot_general(
        matrix, other, (((1,), (1,)), ((), ())), preferred_element_type=jnp.float32
    )


def inner_rows(matrix, other):
    return lax.dot_general(
        matrix, other, (((0,), (0,)), ((), ())), preferred_element_type=jnp.float32
    )


def advance(weight, moment, average, gradient, factor, decay_term):
    update = factor * gradient + decay_term * weight
    new_moment = momentum * moment + update
    new_weight = weight - learn_rate * (update + momentum * new_moment)
    new_average = average_rate * average + (1.0 - average_rate) * new_weight
    return (new_weight, new_moment, new_average)


def routing(segment_ids, devices, capacity):
    row_count = segment_ids.shape[0]
    is_live = segment_ids >= 0
    target = jnp.where(is_live, segment_ids // DOCS_DEV, devices)
    onehot = (target[:, None] == jnp.arange(devices, dtype=jnp.int32)[None, :]).astype(jnp.int32)
    earlier = jnp.cumsum(onehot, axis=0) - onehot
    within = jnp.sum(earlier * onehot, axis=1)
    slot_of = jnp.where(is_live, target * capacity + within, row_count)
    anchor = (
        jnp.full((row_count,), row_count, jnp.int32)
        .at[slot_of]
        .set(jnp.arange(row_count, dtype=jnp.int32), mode="drop")
    )
    return (is_live, jnp.minimum(slot_of, row_count - 1), anchor)


def plain_body(
    tokens,
    cotangent,
    segment_ids,
    wide_weight,
    wide_moment,
    wide_average,
    down_weight,
    down_moment,
    down_average,
    vector_weight,
    vector_moment,
    vector_average,
):
    wide_full, down_full = (
        lax.all_gather(wide_weight.astype(jnp.bfloat16), "dev", axis=0, tiled=True),
        lax.all_gather(down_weight.astype(jnp.bfloat16), "dev", axis=0, tiled=True),
    )
    devices = lax.axis_size("dev")
    row_count, feature = tokens.shape
    capacity = row_count // devices
    is_live, slot_of, anchor = routing(segment_ids, devices, capacity)
    blank_row = jnp.zeros((1, feature), jnp.bfloat16)
    send_rows = jnp.concatenate([tokens, blank_row], 0)[anchor].reshape(devices, capacity, feature)
    send_grads = jnp.concatenate([cotangent, blank_row], 0)[anchor].reshape(
        devices, capacity, feature
    )
    send_ids = jnp.concatenate([segment_ids, jnp.full((1,), -1, jnp.int32)], 0)[anchor].reshape(
        devices, capacity
    )
    work_rows, work_grads, work_ids = (
        lax.all_to_all(send_rows, "dev", split_axis=0, concat_axis=0, tiled=True),
        lax.all_to_all(send_grads, "dev", split_axis=0, concat_axis=0, tiled=True),
        lax.all_to_all(send_ids, "dev", split_axis=0, concat_axis=0, tiled=True),
    )
    work_rows = work_rows.reshape(row_count, feature)
    work_grads = work_grads.reshape(row_count, feature)
    work_ids = work_ids.reshape(row_count)
    gain_one, shift_one, gain_two, shift_two, bias_query, bias_value, bias_out, bias_down = [
        vector_weight[row_index] for row_index in range(8)
    ]
    bias_up = vector_weight[8:].reshape(FF)
    w_qkv = wide_full[:, : 3 * feature]
    w_out = wide_full[:, 3 * feature : 4 * feature]
    w_up = wide_full[:, 4 * feature :]
    work_float = work_rows.astype(jnp.float32)
    low_one = norm_rows(work_float, gain_one, shift_one).astype(jnp.bfloat16)
    bias_all = jnp.concatenate([bias_query, jnp.zeros_like(bias_query), bias_value])
    projected = (product(low_one, w_qkv) + bias_all).astype(jnp.bfloat16)
    queries = projected[:, :feature].reshape(row_count, HEADS, HEAD)
    key_rows = projected[:, feature : 2 * feature].reshape(row_count, HEADS, HEAD)
    value_rows = projected[:, 2 * feature :].reshape(row_count, HEADS, HEAD)
    same_seg = work_ids[:, None] == work_ids[None, :]
    block_rows = min(512, row_count)
    group_size = math.gcd(HEADS, 4)
    group_count = HEADS // group_size

    def scores_of(offset, first_head):
        query_part = queries[offset : offset + block_rows, first_head : first_head + group_size]
        raw_scores = (
            jnp.einsum(
                "qhd,khd->hqk",
                query_part,
                key_rows[:, first_head : first_head + group_size],
                preferred_element_type=jnp.float32,
            )
            * 0.125
        )
        return jnp.where(same_seg[None], raw_scores, masked_value)

    stored = []
    offset = 0
    head_outs = []
    for group in range(group_count):
        first_head = group * group_size
        scores = scores_of(offset, first_head)
        row_max = jnp.max(scores, -1, keepdims=True)
        powers = jnp.exp(scores - row_max)
        row_sums = jnp.sum(powers, -1, keepdims=True)
        prob_low = (powers / row_sums).astype(jnp.bfloat16)
        head_outs.append(
            jnp.einsum(
                "hqk,khd->qhd",
                prob_low,
                value_rows[:, first_head : first_head + group_size],
                preferred_element_type=jnp.float32,
            )
        )
        stored.append((row_max, row_sums))
    out_blocks = jnp.concatenate(head_outs, 1)
    attended = out_blocks.reshape(row_count, feature).astype(jnp.bfloat16)
    resid = work_float + product(attended, w_out) + bias_out
    low_two = norm_rows(resid, gain_two, shift_two).astype(jnp.bfloat16)
    up_float = product(low_two, w_up) + bias_up
    hidden = gelu_exact(up_float).astype(jnp.bfloat16)
    output_low = (resid + product(hidden, down_full) + bias_down).astype(jnp.bfloat16)
    dy_float = work_grads.astype(jnp.float32)
    dhidden = against(work_grads, down_full)
    gelu_pull = jax.vjp(gelu_exact, up_float)[1]
    dup_low = gelu_pull(dhidden)[0].astype(jnp.bfloat16)
    da_two = against(dup_low, w_up)
    norm_two_pull = jax.vjp(norm_rows, resid, gain_two, shift_two)[1]
    dres_norm, dgain_two, dshift_two = norm_two_pull(da_two)
    dresid = dy_float + dres_norm
    dres_low = dresid.astype(jnp.bfloat16)
    dattended = against(dres_low, w_out).astype(jnp.bfloat16).reshape(row_count, HEADS, HEAD)
    dkey_parts = [
        jnp.zeros((row_count, group_size, HEAD), jnp.float32) for group in range(group_count)
    ]
    dvalue_parts = [
        jnp.zeros((row_count, group_size, HEAD), jnp.float32) for group in range(group_count)
    ]
    position = 0
    offset = 0
    pieces = []
    for group in range(group_count):
        first_head = group * group_size
        scores = scores_of(offset, first_head)
        row_max, row_sums = stored[position]
        position += 1
        prob_float = jnp.exp(scores - row_max) / row_sums
        prob_low = prob_float.astype(jnp.bfloat16)
        dout_part = dattended[offset : offset + block_rows, first_head : first_head + group_size]
        value_part = value_rows[:, first_head : first_head + group_size]
        dvalue_parts[group] = jnp.einsum(
            "hqk,qhd->khd", prob_low, dout_part, preferred_element_type=jnp.float32
        )
        dprob = jnp.einsum(
            "qhd,khd->hqk", dout_part, value_part, preferred_element_type=jnp.float32
        )
        dscore = (prob_float * (dprob - jnp.sum(prob_float * dprob, -1, keepdims=True))).astype(
            jnp.bfloat16
        )
        pieces.append(
            jnp.einsum(
                "hqk,khd->qhd",
                dscore,
                key_rows[:, first_head : first_head + group_size],
                preferred_element_type=jnp.float32,
            )
            * 0.125
        )
        query_part = queries[offset : offset + block_rows, first_head : first_head + group_size]
        dkey_parts[group] = (
            jnp.einsum("hqk,qhd->khd", dscore, query_part, preferred_element_type=jnp.float32)
            * 0.125
        )
    dquery_blocks = jnp.concatenate(pieces, 1)
    dquery_low = dquery_blocks.reshape(row_count, feature).astype(jnp.bfloat16)
    dkey_low = jnp.concatenate(dkey_parts, 1).reshape(row_count, feature).astype(jnp.bfloat16)
    dvalue_low = jnp.concatenate(dvalue_parts, 1).reshape(row_count, feature).astype(jnp.bfloat16)
    dqkv_low = jnp.concatenate([dquery_low, dkey_low, dvalue_low], 1)
    da_one = against(dqkv_low, w_qkv)
    norm_one_pull = jax.vjp(norm_rows, work_float, gain_one, shift_one)[1]
    dinput_norm, dgain_one, dshift_one = norm_one_pull(da_one)
    dinput_low = (dresid + dinput_norm).astype(jnp.bfloat16)
    back_out, back_grad = (
        lax.all_to_all(
            output_low.reshape(devices, capacity, feature),
            "dev",
            split_axis=0,
            concat_axis=0,
            tiled=True,
        ),
        lax.all_to_all(
            dinput_low.reshape(devices, capacity, feature),
            "dev",
            split_axis=0,
            concat_axis=0,
            tiled=True,
        ),
    )
    block_output = jnp.where(
        is_live[:, None], back_out.reshape(row_count, feature)[slot_of], jnp.zeros_like(tokens)
    )
    input_grad = jnp.where(
        is_live[:, None], back_grad.reshape(row_count, feature)[slot_of], jnp.zeros_like(tokens)
    )
    vector_rows = jnp.stack(
        [
            dgain_one,
            dshift_one,
            dgain_two,
            dshift_two,
            jnp.sum(dquery_low.astype(jnp.float32), 0),
            jnp.sum(dvalue_low.astype(jnp.float32), 0),
            jnp.sum(dres_low.astype(jnp.float32), 0),
            jnp.sum(dy_float, 0),
        ],
        0,
    )
    bias_up_grad = jnp.sum(dup_low.astype(jnp.float32), 0).reshape(FF // feature, feature)
    vector_partial = jnp.concatenate([vector_rows, bias_up_grad], 0)
    down_grad = lax.psum_scatter(
        inner_rows(hidden, work_grads), "dev", scatter_dimension=0, tiled=True
    )
    wide_grad = lax.psum_scatter(
        jnp.concatenate(
            [
                inner_rows(low_one, dqkv_low),
                jnp.concatenate([inner_rows(attended, dres_low), inner_rows(low_two, dup_low)], 1),
            ],
            1,
        ),
        "dev",
        scatter_dimension=0,
        tiled=True,
    )
    shard_squares = jnp.sum(wide_grad * wide_grad) + jnp.sum(down_grad * down_grad)
    vector_grad = lax.psum(vector_partial, "dev")
    total = lax.psum(shard_squares, "dev") + jnp.sum(vector_grad * vector_grad)
    grad_norm = jnp.sqrt(total)
    factor = clip_norm / jnp.maximum(grad_norm, clip_norm)
    wide_new, wide_moment_new, wide_average_new = advance(
        wide_weight, wide_moment, wide_average, wide_grad, factor, decay_rate
    )
    down_new, down_moment_new, down_average_new = advance(
        down_weight, down_moment, down_average, down_grad, factor, decay_rate
    )
    vector_new, vector_moment_new, vector_average_new = advance(
        vector_weight, vector_moment, vector_average, vector_grad, factor, 0.0
    )
    return (
        block_output,
        input_grad,
        grad_norm,
        wide_new,
        wide_moment_new,
        wide_average_new,
        down_new,
        down_moment_new,
        down_average_new,
        vector_new,
        vector_moment_new,
        vector_average_new,
    )


def flips(devices, mask):
    return [(i, i ^ mask) for i in range(devices)]


def shifts(devices, step):
    return [(i, (i + PLANE * step) % devices) for i in range(devices)]


def place():
    me = lax.axis_index("dev")
    return jnp.stack([me // PLANE, (me // 4) % 2, (me // 2) % 2, me % 2]).astype(jnp.int32)


def core_order(core, mine, theirs):
    first = jnp.where(core == 0, mine, theirs)
    second = jnp.where(core == 0, theirs, mine)
    return first, second


def stack_along_z(block):
    devices = lax.axis_size("dev")
    depth = devices // PLANE
    return jnp.stack(
        [block] + [lax.ppermute(block, "dev", shifts(devices, k)) for k in range(1, depth)], 0
    )


def gather_pieces(own):
    devices = lax.axis_size("dev")
    half = own.shape[2] // 2
    from_x = lax.ppermute(own, "dev", flips(devices, 2))
    from_y = lax.ppermute(own, "dev", flips(devices, 4))
    diag_a = lax.ppermute(from_x[:, :, :half], "dev", flips(devices, 4))
    diag_b = lax.ppermute(from_y[:, :, half:], "dev", flips(devices, 2))
    mine = (own, from_x, from_y, diag_a, diag_b)
    return mine + tuple(lax.ppermute(piece, "dev", flips(devices, 1)) for piece in mine)


def wide_sum(first, second):
    return (first.astype(jnp.float32) + second.astype(jnp.float32)).astype(jnp.bfloat16)


def scatter_blocks(mine, theirs):
    devices = lax.axis_size("dev")
    depth = devices // PLANE
    half = mine.shape[-1] // 2
    mine = wide_sum(mine, lax.ppermute(theirs, "dev", flips(devices, 1)))
    got_a = lax.ppermute(mine[3, :, :, :half], "dev", flips(devices, 4))
    got_b = lax.ppermute(mine[3, :, :, half:], "dev", flips(devices, 2))
    to_x = jnp.concatenate([wide_sum(mine[1, :, :, :half], got_a), mine[1, :, :, half:]], -1)
    to_y = jnp.concatenate([mine[2, :, :, :half], wide_sum(mine[2, :, :, half:], got_b)], -1)
    got_x = lax.ppermute(to_x, "dev", flips(devices, 2)).astype(jnp.float32)
    got_y = lax.ppermute(to_y, "dev", flips(devices, 4)).astype(jnp.float32)
    total = mine[0].astype(jnp.float32) + got_x + got_y
    result = total[0]
    for k in range(1, depth):
        result = result + lax.ppermute(
            total[k].astype(jnp.bfloat16), "dev", shifts(devices, k)
        ).astype(jnp.float32)
    return result


def join_columns(core, block):
    devices = lax.axis_size("dev")
    rows = block.shape[0] // 2
    keep, give = core_order(core, block[:rows], block[rows:])
    got = lax.ppermute(give, "dev", flips(devices, 1))
    return jnp.concatenate(core_order(core, keep, got), 1)


def exchange(rows):
    return lax.all_to_all(rows, "dev", split_axis=0, concat_axis=0, tiled=True)


ANYWHERE = pl.BlockSpec(memory_space=pl.ANY)
SCALARS = pl.BlockSpec(memory_space=pltpu.SMEM)


def whole(*shape):
    return pl.BlockSpec(shape, lambda *_: (0,) * len(shape))


def settings(limit):
    return pltpu.CompilerParams(vmem_limit_bytes=limit * MIB)


def cost(flops, moved, exps=0):
    return pl.CostEstimate(flops=int(flops), bytes_accessed=int(moved), transcendentals=int(exps))


def shaped(shape, dtype):
    return jax.ShapeDtypeStruct(shape, dtype)


def by_rows(matrix, other):
    return lax.dot_general(
        matrix, other, (((1,), (1,)), ((), ())), preferred_element_type=jnp.float32
    )


def by_columns(matrix, other):
    return lax.dot_general(
        matrix, other, (((0,), (0,)), ((), ())), preferred_element_type=jnp.float32
    )


def normed(values):
    center = values - jnp.mean(values, -1, keepdims=True)
    scale = lax.rsqrt(jnp.mean(center * center, -1, keepdims=True) + epsilon)
    return center * scale, scale


def norm_back(grad, gain, unit, scale):
    inner = grad * gain
    return scale * (
        inner
        - jnp.mean(inner, -1, keepdims=True)
        - unit * jnp.mean(inner * unit, -1, keepdims=True)
    )


def iota(shape, axis):
    return lax.broadcasted_iota(jnp.int32, shape, axis)


def slots_of(ids_row, capacity, groups):
    count = ids_row.shape[1]
    square = (count, count)
    ids = jnp.sum(
        jnp.where(iota(square, 0) == iota(square, 1), ids_row, 0), axis=1, keepdims=True
    )
    group = jnp.right_shift(ids, DOCS_DEV.bit_length() - 1)
    lanes = max(128, groups)
    onehot = jnp.where(group == iota((count, lanes), 1), 1.0, 0.0)
    lower = jnp.where(iota(square, 0) > iota(square, 1), 1.0, 0.0).astype(jnp.bfloat16)
    earlier = product(lower, onehot.astype(jnp.bfloat16))
    within = jnp.sum(earlier * onehot, axis=1, keepdims=True).astype(jnp.int32)
    return jnp.where(ids >= 0, group * capacity + within, -1)


def route(ids_row, tokens, cotangent, devices):
    count, feature = tokens.shape

    def kernel(ids_ref, tokens_ref, cotangent_ref, rows_ref, grads_ref, code_ref, slot_ref):
        ids = ids_ref[...]
        slot = slots_of(ids, count // devices, devices)
        slot_ref[...] = slot
        move = jnp.where(slot == iota((count, count), 1), 1.0, 0.0).astype(jnp.bfloat16)
        rows_ref[...] = by_columns(move, tokens_ref[...]).astype(jnp.bfloat16)
        grads_ref[...] = by_columns(move, cotangent_ref[...]).astype(jnp.bfloat16)
        code = jnp.where(ids >= 0, jnp.bitwise_and(ids, DOCS_DEV - 1) + 1, 0)
        code = jnp.broadcast_to(code.astype(jnp.float32), (8, count)).astype(jnp.bfloat16)
        code_ref[...] = product(code, move)[:1].astype(jnp.int32)

    rows = shaped((count, feature), jnp.bfloat16)
    return pl.pallas_call(
        kernel,
        out_shape=[rows, rows, shaped((1, count), jnp.int32), shaped((count, 1), jnp.int32)],
        compiler_params=settings(24),
        cost_estimate=cost(4 * count * count * feature, 8 * count * feature),
    )(ids_row, tokens, cotangent)


def give_back(slot, rows):
    count, feature = rows.shape

    def kernel(slot_ref, rows_ref, out_ref):
        move = jnp.where(slot_ref[...] == iota((count, count), 1), 1.0, 0.0).astype(jnp.bfloat16)
        out_ref[...] = product(move, rows_ref[...]).astype(jnp.bfloat16)

    return pl.pallas_call(
        kernel,
        out_shape=shaped((count, feature), jnp.bfloat16),
        compiler_params=settings(16),
        cost_estimate=cost(2 * count * count * feature, 4 * count * feature),
    )(slot, rows)


def wide_copies(where_ref, pieces, buffer, sems):
    z, y, x, core = where_ref[0], where_ref[1], where_ref[2], where_ref[3]
    copies = []
    for half_index, (own, from_x, from_y, diag_a, diag_b) in (
        (core, pieces[:5]),
        (1 - core, pieces[5:]),
    ):
        depth, rows, columns = own.shape
        half = columns // 2
        for step in range(depth):
            zz = lax.rem(z - step + depth, depth)
            for source, yy, xx, offset, width in (
                (own, y, x, 0, columns),
                (from_x, y, 1 - x, 0, columns),
                (from_y, 1 - y, x, 0, columns),
                (diag_a, 1 - y, 1 - x, 0, half),
                (diag_b, 1 - y, 1 - x, half, half),
            ):
                row = pl.multiple_of(((zz * 2 + yy) * 2 + xx) * rows, 16)
                column = pl.multiple_of(half_index * columns + offset, 128)
                copies.append(
                    pltpu.make_async_copy(
                        source.at[step],
                        buffer.at[pl.ds(row, rows), pl.ds(column, width)],
                        sems.at[len(copies)],
                    )
                )
    return copies


def down_copies(where_ref, pieces, buffer, sems):
    z, y, x, core = where_ref[0], where_ref[1], where_ref[2], where_ref[3]
    copies = []
    for part, (own, from_x, from_y, diag_a, diag_b) in (
        (core, pieces[:5]),
        (1 - core, pieces[5:]),
    ):
        depth, rows, columns = own.shape
        half = columns // 2
        for step in range(depth):
            zz = lax.rem(z - step + depth, depth)
            for source, yy, xx, offset, width in (
                (own, y, x, 0, columns),
                (from_x, y, 1 - x, 0, columns),
                (from_y, 1 - y, x, 0, columns),
                (diag_a, 1 - y, 1 - x, 0, half),
                (diag_b, 1 - y, 1 - x, half, half),
            ):
                row = pl.multiple_of((((zz * 2 + yy) * 2 + xx) * 2 + part) * rows, 16)
                copies.append(
                    pltpu.make_async_copy(
                        source.at[step],
                        buffer.at[pl.ds(row, rows), pl.ds(offset, width)],
                        sems.at[len(copies)],
                    )
                )
    return copies


def project(where, work, vector, pieces):
    count, feature = work.shape
    depth = pieces[0].shape[0]
    chunk = 2 * pieces[0].shape[2]
    tile = 256

    def kernel(where_ref, work_ref, vector_ref, *refs):
        low_ref, out_ref, weights_ref, buffer, sems, out_sem = refs[10:]
        copies = wide_copies(where_ref, refs[:10], buffer, sems)
        for copy in copies:
            copy.start()

        def rows_of(index, carry):
            rows = pl.ds(pl.multiple_of(index * 64, 64), 64)
            unit, _ = normed(work_ref[rows, :].astype(jnp.float32))
            low_ref[rows, :] = (unit * vector_ref[0:1, :] + vector_ref[1:2, :]).astype(
                jnp.bfloat16
            )
            return carry

        lax.fori_loop(0, count // 64, rows_of, 0)
        for copy in copies:
            copy.wait()
        store = pltpu.make_async_copy(buffer, weights_ref, out_sem)
        store.start()
        for part, bias in ((0, 4), (1, None), (2, 5)):

            def columns_of(index, carry):
                inner = pl.ds(pl.multiple_of(index * tile, tile), tile)
                columns = pl.ds(pl.multiple_of(part * feature + index * tile, tile), tile)
                value = product(low_ref[...], buffer[:, columns])
                if bias is not None:
                    value = value + vector_ref[bias : bias + 1, inner]
                out_ref[:, columns] = value.astype(jnp.bfloat16)
                return carry

            lax.fori_loop(0, feature // tile, columns_of, 0)
        store.wait()

    return pl.pallas_call(
        kernel,
        out_shape=[
            shaped((count, feature), jnp.bfloat16),
            shaped((count, 3 * feature), jnp.bfloat16),
            shaped((feature, chunk), jnp.bfloat16),
        ],
        in_specs=[SCALARS, whole(*work.shape), whole(*vector.shape)] + [ANYWHERE] * 10,
        out_specs=[whole(count, feature), whole(count, 3 * feature), ANYWHERE],
        scratch_shapes=[
            pltpu.VMEM((feature, chunk), jnp.bfloat16),
            pltpu.SemaphoreType.DMA((10 * depth,)),
            pltpu.SemaphoreType.DMA,
        ],
        compiler_params=settings(32),
        cost_estimate=cost(6 * count * feature * feature, 12 * feature * feature),
    )(where, work, vector, *pieces)


def code_column(code_ref):
    count = code_ref.shape[1]
    square = (count, count)
    return jnp.sum(
        jnp.where(iota(square, 0) == iota(square, 1), code_ref[...], 0.0), axis=1, keepdims=True
    )


def one_head(values, head):
    lanes = iota(values.shape, 1)
    inside = (lanes >= head * HEAD) & (lanes < (head + 1) * HEAD)
    return jnp.where(inside, values, 0.0).astype(jnp.bfloat16)


def attend(projected, code, work, vector, weights):
    count, feature = work.shape
    pairs = feature // 128
    tile = 256

    def kernel(
        q_ref, k_ref, v_ref, weight_ref, code_ref, work_ref, vector_ref,
        attended_ref, resid_ref, low_ref, stat_ref, total, column,
    ):
        pair = pl.program_id(0)

        @pl.when(pair == 0)
        def _():
            column[...] = code_column(code_ref)
            total[...] = jnp.zeros_like(total)

        keys = k_ref[...]
        values = v_ref[...].astype(jnp.float32).T.astype(jnp.bfloat16)
        scaled = q_ref[...].astype(jnp.float32) * 0.125
        heads = []
        for head in range(2):
            query = one_head(scaled, head)
            parts = []
            for start in range(0, count, tile):
                span = slice(start, start + tile)
                scores = by_rows(keys, query[span])
                same = column[...] == code_ref[:, span]
                scores = jnp.where(same, scores, masked_value)
                most = jnp.max(scores, 0, keepdims=True)
                powers = jnp.exp(scores - most)
                sums = jnp.sum(powers, 0, keepdims=True)
                low = (powers * (1.0 / sums)).astype(jnp.bfloat16)
                stat_ref[0, head : head + 1, span] = most + jnp.log(sums)
                parts.append(product(values[head * HEAD : (head + 1) * HEAD], low))
            heads.append(jnp.concatenate(parts, 1))
        low = jnp.concatenate(heads, 0).T.astype(jnp.bfloat16)
        attended_ref[...] = low
        total[...] += product(low, weight_ref[...])

        @pl.when(pair == pairs - 1)
        def _():
            def rows_of(index, carry):
                rows = pl.ds(pl.multiple_of(index * 64, 64), 64)
                resid = (
                    work_ref[rows, :].astype(jnp.float32) + total[rows, :] + vector_ref[6:7, :]
                )
                resid_ref[rows, :] = resid
                unit, _ = normed(resid)
                low_ref[rows, :] = (unit * vector_ref[2:3, :] + vector_ref[3:4, :]).astype(
                    jnp.bfloat16
                )
                return carry

            lax.fori_loop(0, count // 64, rows_of, 0)

    def columns_at(first):
        return pl.BlockSpec((count, 128), lambda pair: (0, first + pair))

    return pl.pallas_call(
        kernel,
        grid=(pairs,),
        out_shape=[
            shaped((count, feature), jnp.bfloat16),
            shaped((count, feature), jnp.float32),
            shaped((count, feature), jnp.bfloat16),
            shaped((pairs, 8, count), jnp.float32),
        ],
        in_specs=[
            columns_at(0),
            columns_at(pairs),
            columns_at(2 * pairs),
            pl.BlockSpec((128, feature), lambda pair: (pair, 3)),
            whole(1, count),
            whole(count, feature),
            whole(*vector.shape),
        ],
        out_specs=[
            columns_at(0),
            whole(count, feature),
            whole(count, feature),
            pl.BlockSpec((1, 8, count), lambda pair: (pair, 0, 0)),
        ],
        scratch_shapes=[
            pltpu.VMEM((count, feature), jnp.float32),
            pltpu.VMEM((count, 1), jnp.float32),
        ],
        compiler_params=settings(32),
        cost_estimate=cost(
            8 * count * count * feature, 14 * count * feature, HEADS * count * count
        ),
    )(projected, projected, projected, weights, code, work, vector)


def widen(where, low, bias_row, pieces):
    count, feature = low.shape
    depth = pieces[0].shape[0]
    chunk = 2 * pieces[0].shape[2]
    tile = 512
    steps = chunk // tile

    def kernel(where_ref, low_ref, bias_ref, *refs):
        hidden_ref, slope_ref, weights_ref, buffer, sems, out_sem = refs[10:]
        step = pl.program_id(0)
        store = pltpu.make_async_copy(buffer, weights_ref, out_sem)

        @pl.when(step == 0)
        def _():
            copies = wide_copies(where_ref, refs[:10], buffer, sems)
            for copy in copies:
                copy.start()
            for copy in copies:
                copy.wait()
            store.start()

        columns = pl.ds(pl.multiple_of(step * tile, tile), tile)
        up = product(low_ref[...], buffer[:, columns]) + bias_ref[...]
        below = 0.5 * (1.0 + lax.erf(up * (0.5**0.5)))
        hidden_ref[...] = (up * below).astype(jnp.bfloat16)
        slope_ref[...] = below + up * (jnp.exp(-0.5 * up * up) * ((2.0 * math.pi) ** -0.5))

        @pl.when(step == steps - 1)
        def _():
            store.wait()

    block = pl.BlockSpec((count, tile), lambda step: (0, step))
    return pl.pallas_call(
        kernel,
        grid=(steps,),
        out_shape=[
            shaped((count, chunk), jnp.bfloat16),
            shaped((count, chunk), jnp.float32),
            shaped((feature, chunk), jnp.bfloat16),
        ],
        in_specs=[
            SCALARS,
            whole(count, feature),
            pl.BlockSpec((1, tile), lambda step: (0, step)),
        ]
        + [ANYWHERE] * 10,
        out_specs=[block, block, ANYWHERE],
        scratch_shapes=[
            pltpu.VMEM((feature, chunk), jnp.bfloat16),
            pltpu.SemaphoreType.DMA((10 * depth,)),
            pltpu.SemaphoreType.DMA,
        ],
        compiler_params=settings(32),
        cost_estimate=cost(
            2 * count * feature * chunk, 4 * feature * chunk + 6 * count * chunk, count * chunk
        ),
    )(where, low, bias_row, *pieces)


def down_gradient(where, hidden, grads, depth):
    count, wide = hidden.shape
    feature = grads.shape[1]
    rows = wide // (depth * PLANE)
    part = wide // depth

    def kernel(where_ref, hidden_ref, grads_ref, mine_ref, theirs_ref, result):
        y, x, core = where_ref[1], where_ref[2], where_ref[3]
        result[...] = by_columns(hidden_ref[...], grads_ref[...])
        for yy in range(2):
            for xx in range(2):
                spot = jnp.bitwise_xor(y, yy) * 2 + jnp.bitwise_xor(x, xx)
                first = (yy * 2 + xx) * 2
                for target, side in ((mine_ref, core), (theirs_ref, 1 - core)):
                    row = pl.multiple_of((first + side) * rows, 16)
                    target[spot, 0] = result[pl.ds(row, rows), :].astype(jnp.bfloat16)

    shape = shaped((4, depth, rows, feature), jnp.bfloat16)
    block = pl.BlockSpec((4, 1, rows, feature), lambda step, where_ref: (0, step, 0, 0))
    return pl.pallas_call(
        kernel,
        out_shape=[shape, shape],
        grid_spec=pltpu.PrefetchScalarGridSpec(
            num_scalar_prefetch=1,
            grid=(depth,),
            in_specs=[
                pl.BlockSpec(
                    (count, part),
                    lambda step, where_ref: (0, lax.rem(where_ref[0] + step, depth)),
                ),
                whole(count, feature),
            ],
            out_specs=[block, block],
            scratch_shapes=[pltpu.VMEM((part, feature), jnp.float32)],
        ),
        compiler_params=settings(24),
        cost_estimate=cost(2 * count * wide * feature, 2 * wide * (count + feature)),
    )(where, hidden, grads)


def put_wide(where_ref, result, half, offset, mine_ref, theirs_ref):
    z, y, x, core = where_ref[0], where_ref[1], where_ref[2], where_ref[3]
    _, depth, rows, _ = mine_ref.shape
    width = result.shape[1]
    columns = pl.ds(pl.multiple_of(offset, 128), width)
    for is_mine, target in ((True, mine_ref), (False, theirs_ref)):

        @pl.when((half == core) == is_mine)
        def _():
            for chip in range(4 * depth):
                zz, yy, xx = chip // 4, (chip // 2) % 2, chip % 2
                step = lax.rem(zz - z + depth, depth)
                spot = jnp.bitwise_xor(y, yy) * 2 + jnp.bitwise_xor(x, xx)
                target[spot, step, :, columns] = result[chip * rows : (chip + 1) * rows].astype(
                    jnp.bfloat16
                )


def feed_back(where, hidden, slope, low, grads, resid, vector, up_weights, pieces):
    count, wide = hidden.shape
    feature = grads.shape[1]
    depth, rows, _ = pieces[0].shape
    tile = 512
    steps = wide // tile
    chip_rows = feature // (4 * depth)

    def kernel(where_ref, hidden_ref, slope_ref, low_ref, grads_ref, resid_ref, vector_ref, up_ref, *refs):
        (
            out_ref, mine_ref, theirs_ref, dresid_ref, dlow_ref, sums_ref, bias_ref,
            buffer, sems, total, back, flipped, result,
        ) = refs[10:]
        step = pl.program_id(0)

        @pl.when(step == 0)
        def _():
            copies = down_copies(where_ref, refs[:10], buffer, sems)
            for copy in copies:
                copy.start()
            flipped[...] = low_ref[...].astype(jnp.float32).T.astype(jnp.bfloat16)
            total[...] = jnp.zeros_like(total)
            back[...] = jnp.zeros_like(back)
            for copy in copies:
                copy.wait()

        weights = buffer[pl.ds(pl.multiple_of(step * tile, tile), tile), :]
        total[...] += product(hidden_ref[...], weights)
        dup = (slope_ref[...] * by_rows(grads_ref[...], weights)).astype(jnp.bfloat16)
        bias_ref[...] = jnp.sum(dup.astype(jnp.float32), 0, keepdims=True)
        back[...] += by_rows(dup, up_ref[...])
        result[...] = product(flipped[...], dup)
        per_half = wide // 2 // tile
        put_wide(
            where_ref, result, step // per_half, lax.rem(step, per_half) * tile, mine_ref, theirs_ref
        )

        @pl.when(step == steps - 1)
        def _():
            sums_ref[...] = jnp.zeros_like(sums_ref)

            def rows_of(index, carry):
                rows = pl.ds(pl.multiple_of(index * 64, 64), 64)
                resid = resid_ref[rows, :]
                out_ref[rows, :] = (resid + (total[rows, :] + vector_ref[7:8, :])).astype(
                    jnp.bfloat16
                )
                unit, scale = normed(resid)
                da = back[rows, :]
                dy = grads_ref[rows, :].astype(jnp.float32)
                dresid = dy + norm_back(da, vector_ref[2:3, :], unit, scale)
                dresid_ref[rows, :] = dresid
                dlow = dresid.astype(jnp.bfloat16)
                dlow_ref[rows, :] = dlow
                for row, value in enumerate((da * unit, da, dlow.astype(jnp.float32), dy)):
                    sums_ref[row : row + 1, :] += jnp.sum(value, 0, keepdims=True)
                return carry

            lax.fori_loop(0, count // 64, rows_of, 0)

    block = pl.BlockSpec((count, tile), lambda step: (0, step))
    split = (4, depth, chip_rows, wide // 2)
    return pl.pallas_call(
        kernel,
        grid=(steps,),
        out_shape=[
            shaped((count, feature), jnp.bfloat16),
            shaped(split, jnp.bfloat16),
            shaped(split, jnp.bfloat16),
            shaped((count, feature), jnp.float32),
            shaped((count, feature), jnp.bfloat16),
            shaped((8, feature), jnp.float32),
            shaped((1, wide), jnp.float32),
        ],
        in_specs=[
            SCALARS,
            block,
            block,
            whole(count, feature),
            whole(count, feature),
            whole(count, feature),
            whole(*vector.shape),
            pl.BlockSpec((feature, tile), lambda step: (0, step)),
        ]
        + [ANYWHERE] * 10,
        out_specs=[
            whole(count, feature),
            whole(*split),
            whole(*split),
            whole(count, feature),
            whole(count, feature),
            whole(8, feature),
            pl.BlockSpec((1, tile), lambda step: (0, step)),
        ],
        scratch_shapes=[
            pltpu.VMEM((wide, feature), jnp.bfloat16),
            pltpu.SemaphoreType.DMA((10 * depth,)),
            pltpu.VMEM((count, feature), jnp.float32),
            pltpu.VMEM((count, feature), jnp.float32),
            pltpu.VMEM((feature, count), jnp.bfloat16),
            pltpu.VMEM((feature, tile), jnp.float32),
        ],
        compiler_params=settings(48),
        cost_estimate=cost(8 * count * wide * feature, 6 * wide * feature + 6 * count * wide),
    )(where, hidden, slope, low, grads, resid, vector, up_weights, *pieces)


def attend_back(projected, code, stats, dlow, weights):
    count, feature = dlow.shape
    pairs = feature // 128
    tile = 256

    def kernel(
        q_ref, k_ref, v_ref, code_ref, stat_ref, dlow_ref, weight_ref, out_ref, sums_ref, douts, column
    ):
        pair = pl.program_id(0)

        @pl.when(pair == 0)
        def _():
            column[...] = code_column(code_ref)
            for start in range(0, feature, tile):
                span = slice(start, start + tile)
                douts[:, span] = by_rows(dlow_ref[...], weight_ref[span, :]).astype(jnp.bfloat16)

        keys, values = k_ref[...], v_ref[...]
        flipped = keys.astype(jnp.float32).T.astype(jnp.bfloat16)
        scaled = q_ref[...].astype(jnp.float32) * 0.125
        dout = douts[:, pl.ds(pl.multiple_of(pair * 128, 128), 128)].astype(jnp.float32)
        dkey = jnp.zeros((count, 128), jnp.float32)
        dvalue = jnp.zeros((count, 128), jnp.float32)
        heads = []
        for head in range(2):
            query = one_head(scaled, head)
            dhead = one_head(dout, head)
            parts = []
            for start in range(0, count, tile):
                span = slice(start, start + tile)
                scores = by_rows(keys, query[span])
                same = column[...] == code_ref[:, span]
                probs = jnp.exp(
                    jnp.where(same, scores, masked_value) - stat_ref[0, head : head + 1, span]
                )
                dprob = by_rows(values, dhead[span])
                inner = jnp.sum(probs * dprob, 0, keepdims=True)
                dscore = (probs * (dprob - inner)).astype(jnp.bfloat16)
                dvalue = dvalue + product(probs.astype(jnp.bfloat16), dhead[span])
                dkey = dkey + product(dscore, query[span])
                parts.append(product(flipped[head * HEAD : (head + 1) * HEAD], dscore))
            heads.append(jnp.concatenate(parts, 1))
        dquery = (jnp.concatenate(heads, 0).T * 0.125).astype(jnp.bfloat16)
        dvalue = dvalue.astype(jnp.bfloat16)
        out_ref[0] = dquery
        out_ref[1] = dkey.astype(jnp.bfloat16)
        out_ref[2] = dvalue
        sums_ref[0:1, :] = jnp.sum(dquery.astype(jnp.float32), 0, keepdims=True)
        sums_ref[1:2, :] = jnp.sum(dvalue.astype(jnp.float32), 0, keepdims=True)

    def columns_at(first):
        return pl.BlockSpec((count, 128), lambda pair: (0, first + pair))

    return pl.pallas_call(
        kernel,
        grid=(pairs,),
        out_shape=[
            shaped((3, count, feature), jnp.bfloat16),
            shaped((8, feature), jnp.float32),
        ],
        in_specs=[
            columns_at(0),
            columns_at(pairs),
            columns_at(2 * pairs),
            whole(1, count),
            pl.BlockSpec((1, 8, count), lambda pair: (pair, 0, 0)),
            whole(count, feature),
            pl.BlockSpec((feature, feature), lambda pair: (0, 3)),
        ],
        out_specs=[
            pl.BlockSpec((3, count, 128), lambda pair: (0, 0, pair)),
            pl.BlockSpec((8, 128), lambda pair: (0, pair)),
        ],
        scratch_shapes=[
            pltpu.VMEM((count, feature), jnp.bfloat16),
            pltpu.VMEM((count, 1), jnp.float32),
        ],
        compiler_params=settings(32),
        cost_estimate=cost(
            14 * count * count * feature, 16 * count * feature, HEADS * count * count
        ),
    )(projected, projected, projected, code, stats, dlow, weights)


def first_gradient(where, low, dprojected, attended, dlow, depth):
    count, feature = low.shape
    split = (4, depth, feature // (4 * depth), 2 * feature)

    def kernel(where_ref, low_ref, dprojected_ref, attended_ref, dlow_ref, mine_ref, theirs_ref, result):
        step = pl.program_id(0)

        @pl.when(step < 3)
        def _():
            result[...] = by_columns(low_ref[...], dprojected_ref[0])

        @pl.when(step == 3)
        def _():
            result[...] = by_columns(attended_ref[...], dlow_ref[...])

        put_wide(where_ref, result, step // 2, lax.rem(step, 2) * feature, mine_ref, theirs_ref)

    return pl.pallas_call(
        kernel,
        grid=(4,),
        out_shape=[shaped(split, jnp.bfloat16)] * 2,
        in_specs=[
            SCALARS,
            whole(count, feature),
            pl.BlockSpec((1, count, feature), lambda step: (jnp.minimum(step, 2), 0, 0)),
            whole(count, feature),
            whole(count, feature),
        ],
        out_specs=[whole(*split)] * 2,
        scratch_shapes=[pltpu.VMEM((feature, feature), jnp.float32)],
        compiler_params=settings(32),
        cost_estimate=cost(8 * count * feature * feature, 8 * feature * feature),
    )(where, low, dprojected, attended, dlow)


def project_back(work, dprojected, dresid, vector, weights):
    count, feature = work.shape
    tile = 128

    def kernel(work_ref, dprojected_ref, dresid_ref, vector_ref, weight_ref, out_ref, sums_ref):
        sums_ref[...] = jnp.zeros_like(sums_ref)

        def rows_of(index, carry):
            rows = pl.ds(pl.multiple_of(index * tile, tile), tile)
            da = by_rows(dprojected_ref[0, rows, :], weight_ref[:, :feature])
            da += by_rows(dprojected_ref[1, rows, :], weight_ref[:, feature : 2 * feature])
            da += by_rows(dprojected_ref[2, rows, :], weight_ref[:, 2 * feature :])
            unit, scale = normed(work_ref[rows, :].astype(jnp.float32))
            out_ref[rows, :] = (
                dresid_ref[rows, :] + norm_back(da, vector_ref[0:1, :], unit, scale)
            ).astype(jnp.bfloat16)
            sums_ref[0:1, :] += jnp.sum(da * unit, 0, keepdims=True)
            sums_ref[1:2, :] += jnp.sum(da, 0, keepdims=True)
            return carry

        lax.fori_loop(0, count // tile, rows_of, 0)

    return pl.pallas_call(
        kernel,
        grid=(1,),
        out_shape=[shaped((count, feature), jnp.bfloat16), shaped((8, feature), jnp.float32)],
        in_specs=[
            whole(count, feature),
            whole(3, count, feature),
            whole(count, feature),
            whole(*vector.shape),
            whole(feature, 3 * feature),
        ],
        out_specs=[whole(count, feature), whole(8, feature)],
        compiler_params=settings(32),
        cost_estimate=cost(6 * count * feature * feature, 6 * feature * feature),
    )(work, dprojected, dresid, vector, weights)


def structured(devices, feature):
    rows = feature // devices
    return devices % PLANE == 0 and feature % devices == 0 and (2 * rows) % 16 == 0


def body(
    tokens,
    cotangent,
    segment_ids,
    wide_weight,
    wide_moment,
    wide_average,
    down_weight,
    down_moment,
    down_average,
    vector_weight,
    vector_moment,
    vector_average,
):
    devices = lax.axis_size("dev")
    count, feature = tokens.shape
    if not structured(devices, feature):
        return plain_body(
            tokens,
            cotangent,
            segment_ids,
            wide_weight,
            wide_moment,
            wide_average,
            down_weight,
            down_moment,
            down_average,
            vector_weight,
            vector_moment,
            vector_average,
        )
    depth = devices // PLANE
    capacity = count // devices
    where = place()
    core = where[3]

    wide_low, down_low = wide_weight.astype(jnp.bfloat16), down_weight.astype(jnp.bfloat16)
    rows, columns = wide_low.shape
    parts = wide_low.reshape(rows, 2, 2, columns // 4)
    keep, give = core_order(core, parts[:, :, 0], parts[:, :, 1])
    got = lax.ppermute(give, "dev", flips(devices, 1))
    pair = jnp.concatenate(core_order(core, keep, got), 0)

    send_rows, send_grads, send_code, slot = route(
        segment_ids.reshape(1, count), tokens, cotangent, devices
    )
    work = exchange(send_rows.reshape(devices, capacity, feature)).reshape(count, feature)
    code = exchange(send_code.reshape(devices, 1, capacity)).reshape(1, count)
    code = code.astype(jnp.float32)

    first_own = stack_along_z(pair[:, 0])
    up_block, first_own = lax.optimization_barrier((pair[:, 1], first_own))
    first_pieces = gather_pieces(first_own)
    up_own = stack_along_z(up_block)
    down_block, up_own = lax.optimization_barrier((down_low, up_own))
    up_pieces = gather_pieces(up_own)
    down_pieces = gather_pieces(stack_along_z(down_block))

    grads = exchange(send_grads.reshape(devices, capacity, feature)).reshape(count, feature)

    low_one, projected, first_weights = project(where, work, vector_weight, first_pieces)
    attended, resid, low_two, stats = attend(projected, code, work, vector_weight, first_weights)
    hidden, slope, up_weights = widen(
        where, low_two, vector_weight[8:].reshape(1, FF), up_pieces
    )
    down_mine, down_theirs = down_gradient(where, hidden, grads, depth)
    down_grad = scatter_blocks(down_mine, down_theirs)
    output, up_mine, up_theirs, dresid, dlow, sums_two, bias_up_grad = feed_back(
        where, hidden, slope, low_two, grads, resid, vector_weight, up_weights, down_pieces
    )
    up_grad = join_columns(core, scatter_blocks(up_mine, up_theirs))
    dprojected, sums_attend = attend_back(projected, code, stats, dlow, first_weights)
    first_mine, first_theirs = first_gradient(where, low_one, dprojected, attended, dlow, depth)
    first_grad = join_columns(core, scatter_blocks(first_mine, first_theirs))
    dinput, sums_one = project_back(work, dprojected, dresid, vector_weight, first_weights)

    back_out = exchange(output.reshape(devices, capacity, feature)).reshape(count, feature)
    back_grad = exchange(dinput.reshape(devices, capacity, feature)).reshape(count, feature)
    block_output = give_back(slot, back_out)
    input_grad = give_back(slot, back_grad)

    vector_partial = jnp.concatenate(
        [
            sums_one[0:2],
            sums_two[0:2],
            sums_attend[0:2],
            sums_two[2:4],
            bias_up_grad.reshape(FF // feature, feature),
            jnp.zeros((4, feature), jnp.float32),
        ],
        0,
    )
    share = vector_partial.size // devices // 128
    vector_share = jnp.sum(exchange(vector_partial.reshape(devices, share, 128)), 0)
    wide_grad = jnp.concatenate([first_grad, up_grad], 1)
    shard_squares = jnp.sum(wide_grad * wide_grad) + jnp.sum(down_grad * down_grad)
    packet = jnp.concatenate([vector_share, jnp.full((1, 128), shard_squares)], 0)
    packets = exchange(jnp.broadcast_to(packet[None], (devices, share + 1, 128)))
    vector_grad = packets[:, :share].reshape(-1, feature)[: vector_weight.shape[0]]
    total = jnp.sum(packets[:, share, 0]) + jnp.sum(vector_grad * vector_grad)
    grad_norm = jnp.sqrt(total)
    factor = clip_norm / jnp.maximum(grad_norm, clip_norm)
    wide_new, wide_moment_new, wide_average_new = advance(
        wide_weight, wide_moment, wide_average, wide_grad, factor, decay_rate
    )
    down_new, down_moment_new, down_average_new = advance(
        down_weight, down_moment, down_average, down_grad, factor, decay_rate
    )
    vector_new, vector_moment_new, vector_average_new = advance(
        vector_weight, vector_moment, vector_average, vector_grad, factor, 0.0
    )
    return (
        block_output,
        input_grad,
        grad_norm,
        wide_new,
        wide_moment_new,
        wide_average_new,
        down_new,
        down_moment_new,
        down_average_new,
        vector_new,
        vector_moment_new,
        vector_average_new,
    )


def solution(mesh):
    placed = (
        P("dev", None),
        P("dev", None),
        P("dev"),
        P("dev", None),
        P("dev", None),
        P("dev", None),
        P("dev", None),
        P("dev", None),
        P("dev", None),
        P(),
        P(),
        P(),
    )
    return jax.shard_map(
        body,
        mesh=mesh,
        in_specs=placed,
        out_specs=(
            P("dev", None),
            P("dev", None),
            P(),
            P("dev", None),
            P("dev", None),
            P("dev", None),
            P("dev", None),
            P("dev", None),
            P("dev", None),
            P(),
            P(),
            P(),
        ),
        check_vma=False,
    )
```

```python
import math

import jax
import jax.numpy as jnp
from jax import lax
from jax.experimental import pallas as pl
from jax.experimental.pallas import tpu as pltpu
from jax.sharding import PartitionSpec as P

HEADS = 12
HEAD = 64
FF = 3072
DOCS_DEV = 4
PLANE = 8
MIB = 1 << 20


epsilon = 1e-05
masked_value = -1e30
momentum = 0.9
learn_rate = 0.01
decay_rate = 0.0001
average_rate = 0.8
clip_norm = 2048.0


def norm_rows(values, gain_row, shift_row):
    center = values - jnp.mean(values, -1, keepdims=True)
    spread = jnp.mean(center * center, -1, keepdims=True)
    return center * lax.rsqrt(spread + epsilon) * gain_row + shift_row


def gelu_exact(values):
    return jax.nn.gelu(values, approximate=False)


def product(matrix, other):
    return jnp.dot(matrix, other, preferred_element_type=jnp.float32)


def against(matrix, other):
    return lax.dot_general(
        matrix, other, (((1,), (1,)), ((), ())), preferred_element_type=jnp.float32
    )


def inner_rows(matrix, other):
    return lax.dot_general(
        matrix, other, (((0,), (0,)), ((), ())), preferred_element_type=jnp.float32
    )


def advance(weight, moment, average, gradient, factor, decay_term):
    update = factor * gradient + decay_term * weight
    new_moment = momentum * moment + update
    new_weight = weight - learn_rate * (update + momentum * new_moment)
    new_average = average_rate * average + (1.0 - average_rate) * new_weight
    return (new_weight, new_moment, new_average)


def routing(segment_ids, devices, capacity):
    row_count = segment_ids.shape[0]
    is_live = segment_ids >= 0
    target = jnp.where(is_live, segment_ids // DOCS_DEV, devices)
    onehot = (target[:, None] == jnp.arange(devices, dtype=jnp.int32)[None, :]).astype(jnp.int32)
    earlier = jnp.cumsum(onehot, axis=0) - onehot
    within = jnp.sum(earlier * onehot, axis=1)
    slot_of = jnp.where(is_live, target * capacity + within, row_count)
    anchor = (
        jnp.full((row_count,), row_count, jnp.int32)
        .at[slot_of]
        .set(jnp.arange(row_count, dtype=jnp.int32), mode="drop")
    )
    return (is_live, jnp.minimum(slot_of, row_count - 1), anchor)


def plain_body(
    tokens,
    cotangent,
    segment_ids,
    wide_weight,
    wide_moment,
    wide_average,
    down_weight,
    down_moment,
    down_average,
    vector_weight,
    vector_moment,
    vector_average,
):
    wide_full, down_full = (
        lax.all_gather(wide_weight.astype(jnp.bfloat16), "dev", axis=0, tiled=True),
        lax.all_gather(down_weight.astype(jnp.bfloat16), "dev", axis=0, tiled=True),
    )
    devices = lax.axis_size("dev")
    row_count, feature = tokens.shape
    capacity = row_count // devices
    is_live, slot_of, anchor = routing(segment_ids, devices, capacity)
    blank_row = jnp.zeros((1, feature), jnp.bfloat16)
    send_rows = jnp.concatenate([tokens, blank_row], 0)[anchor].reshape(devices, capacity, feature)
    send_grads = jnp.concatenate([cotangent, blank_row], 0)[anchor].reshape(
        devices, capacity, feature
    )
    send_ids = jnp.concatenate([segment_ids, jnp.full((1,), -1, jnp.int32)], 0)[anchor].reshape(
        devices, capacity
    )
    work_rows, work_grads, work_ids = (
        lax.all_to_all(send_rows, "dev", split_axis=0, concat_axis=0, tiled=True),
        lax.all_to_all(send_grads, "dev", split_axis=0, concat_axis=0, tiled=True),
        lax.all_to_all(send_ids, "dev", split_axis=0, concat_axis=0, tiled=True),
    )
    work_rows = work_rows.reshape(row_count, feature)
    work_grads = work_grads.reshape(row_count, feature)
    work_ids = work_ids.reshape(row_count)
    gain_one, shift_one, gain_two, shift_two, bias_query, bias_value, bias_out, bias_down = [
        vector_weight[row_index] for row_index in range(8)
    ]
    bias_up = vector_weight[8:].reshape(FF)
    w_qkv = wide_full[:, : 3 * feature]
    w_out = wide_full[:, 3 * feature : 4 * feature]
    w_up = wide_full[:, 4 * feature :]
    work_float = work_rows.astype(jnp.float32)
    low_one = norm_rows(work_float, gain_one, shift_one).astype(jnp.bfloat16)
    bias_all = jnp.concatenate([bias_query, jnp.zeros_like(bias_query), bias_value])
    projected = (product(low_one, w_qkv) + bias_all).astype(jnp.bfloat16)
    queries = projected[:, :feature].reshape(row_count, HEADS, HEAD)
    key_rows = projected[:, feature : 2 * feature].reshape(row_count, HEADS, HEAD)
    value_rows = projected[:, 2 * feature :].reshape(row_count, HEADS, HEAD)
    same_seg = work_ids[:, None] == work_ids[None, :]
    block_rows = min(512, row_count)
    group_size = math.gcd(HEADS, 4)
    group_count = HEADS // group_size

    def scores_of(offset, first_head):
        query_part = queries[offset : offset + block_rows, first_head : first_head + group_size]
        raw_scores = (
            jnp.einsum(
                "qhd,khd->hqk",
                query_part,
                key_rows[:, first_head : first_head + group_size],
                preferred_element_type=jnp.float32,
            )
            * 0.125
        )
        return jnp.where(same_seg[None], raw_scores, masked_value)

    stored = []
    offset = 0
    head_outs = []
    for group in range(group_count):
        first_head = group * group_size
        scores = scores_of(offset, first_head)
        row_max = jnp.max(scores, -1, keepdims=True)
        powers = jnp.exp(scores - row_max)
        row_sums = jnp.sum(powers, -1, keepdims=True)
        prob_low = (powers / row_sums).astype(jnp.bfloat16)
        head_outs.append(
            jnp.einsum(
                "hqk,khd->qhd",
                prob_low,
                value_rows[:, first_head : first_head + group_size],
                preferred_element_type=jnp.float32,
            )
        )
        stored.append((row_max, row_sums))
    out_blocks = jnp.concatenate(head_outs, 1)
    attended = out_blocks.reshape(row_count, feature).astype(jnp.bfloat16)
    resid = work_float + product(attended, w_out) + bias_out
    low_two = norm_rows(resid, gain_two, shift_two).astype(jnp.bfloat16)
    up_float = product(low_two, w_up) + bias_up
    hidden = gelu_exact(up_float).astype(jnp.bfloat16)
    output_low = (resid + product(hidden, down_full) + bias_down).astype(jnp.bfloat16)
    dy_float = work_grads.astype(jnp.float32)
    dhidden = against(work_grads, down_full)
    gelu_pull = jax.vjp(gelu_exact, up_float)[1]
    dup_low = gelu_pull(dhidden)[0].astype(jnp.bfloat16)
    da_two = against(dup_low, w_up)
    norm_two_pull = jax.vjp(norm_rows, resid, gain_two, shift_two)[1]
    dres_norm, dgain_two, dshift_two = norm_two_pull(da_two)
    dresid = dy_float + dres_norm
    dres_low = dresid.astype(jnp.bfloat16)
    dattended = against(dres_low, w_out).astype(jnp.bfloat16).reshape(row_count, HEADS, HEAD)
    dkey_parts = [
        jnp.zeros((row_count, group_size, HEAD), jnp.float32) for group in range(group_count)
    ]
    dvalue_parts = [
        jnp.zeros((row_count, group_size, HEAD), jnp.float32) for group in range(group_count)
    ]
    position = 0
    offset = 0
    pieces = []
    for group in range(group_count):
        first_head = group * group_size
        scores = scores_of(offset, first_head)
        row_max, row_sums = stored[position]
        position += 1
        prob_float = jnp.exp(scores - row_max) / row_sums
        prob_low = prob_float.astype(jnp.bfloat16)
        dout_part = dattended[offset : offset + block_rows, first_head : first_head + group_size]
        value_part = value_rows[:, first_head : first_head + group_size]
        dvalue_parts[group] = jnp.einsum(
            "hqk,qhd->khd", prob_low, dout_part, preferred_element_type=jnp.float32
        )
        dprob = jnp.einsum(
            "qhd,khd->hqk", dout_part, value_part, preferred_element_type=jnp.float32
        )
        dscore = (prob_float * (dprob - jnp.sum(prob_float * dprob, -1, keepdims=True))).astype(
            jnp.bfloat16
        )
        pieces.append(
            jnp.einsum(
                "hqk,khd->qhd",
                dscore,
                key_rows[:, first_head : first_head + group_size],
                preferred_element_type=jnp.float32,
            )
            * 0.125
        )
        query_part = queries[offset : offset + block_rows, first_head : first_head + group_size]
        dkey_parts[group] = (
            jnp.einsum("hqk,qhd->khd", dscore, query_part, preferred_element_type=jnp.float32)
            * 0.125
        )
    dquery_blocks = jnp.concatenate(pieces, 1)
    dquery_low = dquery_blocks.reshape(row_count, feature).astype(jnp.bfloat16)
    dkey_low = jnp.concatenate(dkey_parts, 1).reshape(row_count, feature).astype(jnp.bfloat16)
    dvalue_low = jnp.concatenate(dvalue_parts, 1).reshape(row_count, feature).astype(jnp.bfloat16)
    dqkv_low = jnp.concatenate([dquery_low, dkey_low, dvalue_low], 1)
    da_one = against(dqkv_low, w_qkv)
    norm_one_pull = jax.vjp(norm_rows, work_float, gain_one, shift_one)[1]
    dinput_norm, dgain_one, dshift_one = norm_one_pull(da_one)
    dinput_low = (dresid + dinput_norm).astype(jnp.bfloat16)
    back_out, back_grad = (
        lax.all_to_all(
            output_low.reshape(devices, capacity, feature),
            "dev",
            split_axis=0,
            concat_axis=0,
            tiled=True,
        ),
        lax.all_to_all(
            dinput_low.reshape(devices, capacity, feature),
            "dev",
            split_axis=0,
            concat_axis=0,
            tiled=True,
        ),
    )
    block_output = jnp.where(
        is_live[:, None], back_out.reshape(row_count, feature)[slot_of], jnp.zeros_like(tokens)
    )
    input_grad = jnp.where(
        is_live[:, None], back_grad.reshape(row_count, feature)[slot_of], jnp.zeros_like(tokens)
    )
    vector_rows = jnp.stack(
        [
            dgain_one,
            dshift_one,
            dgain_two,
            dshift_two,
            jnp.sum(dquery_low.astype(jnp.float32), 0),
            jnp.sum(dvalue_low.astype(jnp.float32), 0),
            jnp.sum(dres_low.astype(jnp.float32), 0),
            jnp.sum(dy_float, 0),
        ],
        0,
    )
    bias_up_grad = jnp.sum(dup_low.astype(jnp.float32), 0).reshape(FF // feature, feature)
    vector_partial = jnp.concatenate([vector_rows, bias_up_grad], 0)
    down_grad = lax.psum_scatter(
        inner_rows(hidden, work_grads), "dev", scatter_dimension=0, tiled=True
    )
    wide_grad = lax.psum_scatter(
        jnp.concatenate(
            [
                inner_rows(low_one, dqkv_low),
                jnp.concatenate([inner_rows(attended, dres_low), inner_rows(low_two, dup_low)], 1),
            ],
            1,
        ),
        "dev",
        scatter_dimension=0,
        tiled=True,
    )
    shard_squares = jnp.sum(wide_grad * wide_grad) + jnp.sum(down_grad * down_grad)
    vector_grad = lax.psum(vector_partial, "dev")
    total = lax.psum(shard_squares, "dev") + jnp.sum(vector_grad * vector_grad)
    grad_norm = jnp.sqrt(total)
    factor = clip_norm / jnp.maximum(grad_norm, clip_norm)
    wide_new, wide_moment_new, wide_average_new = advance(
        wide_weight, wide_moment, wide_average, wide_grad, factor, decay_rate
    )
    down_new, down_moment_new, down_average_new = advance(
        down_weight, down_moment, down_average, down_grad, factor, decay_rate
    )
    vector_new, vector_moment_new, vector_average_new = advance(
        vector_weight, vector_moment, vector_average, vector_grad, factor, 0.0
    )
    return (
        block_output,
        input_grad,
        grad_norm,
        wide_new,
        wide_moment_new,
        wide_average_new,
        down_new,
        down_moment_new,
        down_average_new,
        vector_new,
        vector_moment_new,
        vector_average_new,
    )


def flips(devices, mask):
    return [(i, i ^ mask) for i in range(devices)]


def shifts(devices, step):
    return [(i, (i + PLANE * step) % devices) for i in range(devices)]


def place():
    me = lax.axis_index("dev")
    return jnp.stack([me // PLANE, (me // 4) % 2, (me // 2) % 2, me % 2]).astype(jnp.int32)


def core_order(core, mine, theirs):
    first = jnp.where(core == 0, mine, theirs)
    second = jnp.where(core == 0, theirs, mine)
    return first, second


def pin(*values):
    return lax.optimization_barrier(values)


def send(value, mask):
    return lax.ppermute(value, "dev", flips(lax.axis_size("dev"), mask))


def along_z(block):
    devices = lax.axis_size("dev")
    depth = devices // PLANE
    return jnp.stack(
        [block] + [lax.ppermute(block, "dev", shifts(devices, k)) for k in range(1, depth)], 0
    )


def to_neighbours(own):
    return send(own, 2), send(own, 4)


def to_diagonal(from_x, from_y):
    half = from_x.shape[0] // 2
    return send(from_x[:half], 4), send(from_y[half:], 2)


def to_partner(*pieces):
    return tuple(send(piece, 1) for piece in pieces)


def total_of(*terms):
    return sum(term.astype(jnp.float32) for term in terms)


def low_sum(*terms):
    return total_of(*terms).astype(jnp.bfloat16)


class Fold:
    def __init__(self, mine, got):
        self.mine, self.got = mine, got
        self.half = mine.shape[1] // 2

    def pair(self, spot, steps):
        return self.mine[spot, steps], self.got[spot, steps]

    def diagonal(self):
        first, last = slice(None, self.half), slice(self.half, None)
        return low_sum(*self.pair(3, first)), low_sum(*self.pair(3, last))

    def neighbours(self, got_a, got_b):
        first, last = slice(None, self.half), slice(self.half, None)
        to_x = (low_sum(*self.pair(1, first), got_a), low_sum(*self.pair(1, last)))
        to_y = (low_sum(*self.pair(2, first)), low_sum(*self.pair(2, last), got_b))
        return jnp.concatenate(to_x, 0), jnp.concatenate(to_y, 0)

    def column(self, got_x, got_y):
        total = total_of(*self.pair(0, slice(None)), got_x, got_y)
        return (total[0],) + tuple(
            total[k].astype(jnp.bfloat16) for k in range(1, total.shape[0])
        )


def over_diagonal(to_a, to_b):
    return send(to_a, 4), send(to_b, 2)


def over_plane(to_x, to_y):
    return send(to_x, 2), send(to_y, 4)


def over_column(sums):
    devices = lax.axis_size("dev")
    return tuple(lax.ppermute(sums[k], "dev", shifts(devices, k)) for k in range(1, len(sums)))


def exchange(rows):
    return lax.all_to_all(rows, "dev", split_axis=0, concat_axis=0, tiled=True)


FAR = pl.BlockSpec(memory_space=pltpu.HBM)
SCALARS = pl.BlockSpec(memory_space=pltpu.SMEM)


def whole(*shape):
    return pl.BlockSpec(shape, lambda *_: (0,) * len(shape))


LIMIT = 48


def settings(limit):
    return pltpu.CompilerParams(vmem_limit_bytes=limit * MIB)


def cost(flops, moved, exps=0):
    return pl.CostEstimate(flops=int(flops), bytes_accessed=int(moved), transcendentals=int(exps))


def shaped(shape, dtype):
    return jax.ShapeDtypeStruct(shape, dtype)


def by_rows(matrix, other):
    return lax.dot_general(
        matrix, other, (((1,), (1,)), ((), ())), preferred_element_type=jnp.float32
    )


def by_columns(matrix, other):
    return lax.dot_general(
        matrix, other, (((0,), (0,)), ((), ())), preferred_element_type=jnp.float32
    )


def normed(values):
    center = values - jnp.mean(values, -1, keepdims=True)
    scale = lax.rsqrt(jnp.mean(center * center, -1, keepdims=True) + epsilon)
    return center * scale, scale


def norm_back(grad, gain, unit, scale):
    inner = grad * gain
    return scale * (
        inner
        - jnp.mean(inner, -1, keepdims=True)
        - unit * jnp.mean(inner * unit, -1, keepdims=True)
    )


def iota(shape, axis):
    return lax.broadcasted_iota(jnp.int32, shape, axis)


def slots_of(ids_row, capacity, groups):
    count = ids_row.shape[1]
    square = (count, count)
    ids = jnp.sum(
        jnp.where(iota(square, 0) == iota(square, 1), ids_row, 0), axis=1, keepdims=True
    )
    group = jnp.right_shift(ids, DOCS_DEV.bit_length() - 1)
    lanes = max(128, groups)
    onehot = jnp.where(group == iota((count, lanes), 1), 1.0, 0.0)
    lower = jnp.where(iota(square, 0) > iota(square, 1), 1.0, 0.0).astype(jnp.bfloat16)
    earlier = product(lower, onehot.astype(jnp.bfloat16))
    within = jnp.sum(earlier * onehot, axis=1, keepdims=True).astype(jnp.int32)
    return ids, jnp.where(ids >= 0, group * capacity + within, -1)


def route(ids_row, tokens, cotangent, devices):
    count, feature = tokens.shape

    def kernel(ids_ref, tokens_ref, cotangent_ref, rows_ref, grads_ref, slot_ref):
        ids, slot = slots_of(ids_ref[...], count // devices, devices)
        slot_ref[...] = slot
        move = jnp.where(slot == iota((count, count), 1), 1.0, 0.0).astype(jnp.bfloat16)
        code = jnp.where(ids >= 0, jnp.bitwise_and(ids, DOCS_DEV - 1) + 1, 0)
        code = jnp.broadcast_to(code.astype(jnp.float32), (count, 128)).astype(jnp.bfloat16)
        rows_ref[:, :feature] = by_columns(move, tokens_ref[...]).astype(jnp.bfloat16)
        rows_ref[:, feature:] = by_columns(move, code).astype(jnp.bfloat16)
        grads_ref[...] = by_columns(move, cotangent_ref[...]).astype(jnp.bfloat16)

    return pl.pallas_call(
        kernel,
        out_shape=[
            shaped((count, feature + 128), jnp.bfloat16),
            shaped((count, feature), jnp.bfloat16),
            shaped((count, 1), jnp.int32),
        ],
        compiler_params=settings(LIMIT),
        cost_estimate=cost(4 * count * count * feature, 8 * count * feature),
    )(ids_row, tokens, cotangent)


def give_back(slot, rows):
    count, feature = rows.shape[0], rows.shape[1] // 256 * 256

    def kernel(slot_ref, rows_ref, out_ref):
        move = jnp.where(slot_ref[...] == iota((count, count), 1), 1.0, 0.0).astype(jnp.bfloat16)
        out_ref[...] = product(move, rows_ref[...]).astype(jnp.bfloat16)

    return pl.pallas_call(
        kernel,
        grid=(1,),
        out_shape=shaped((count, feature), jnp.bfloat16),
        in_specs=[whole(count, 1), whole(count, feature)],
        out_specs=whole(count, feature),
        compiler_params=settings(LIMIT),
        cost_estimate=cost(2 * count * count * feature, 4 * count * feature),
    )(slot, rows)


PIECES = 10


def pieces_of(where_ref, pieces):
    z, y, x, core = where_ref[0], where_ref[1], where_ref[2], where_ref[3]
    for part, group in ((core, pieces[: PIECES // 2]), (1 - core, pieces[PIECES // 2 :])):
        depth = group[0].shape[0]
        firsts = (0, 0, 0, 0, depth // 2)
        columns = ((y, x), (y, 1 - x), (1 - y, x), (1 - y, 1 - x), (1 - y, 1 - x))
        for piece, first, (yy, xx) in zip(group, firsts, columns, strict=True):
            for index in range(piece.shape[0]):
                step = first + index
                zz = lax.rem(z - step + depth, depth)
                yield piece.at[index], step, (zz * 2 + yy) * 2 + xx, part


def wide_copies(where_ref, pieces, buffer, sems):
    copies = []
    for source, _, chip, part in pieces_of(where_ref, pieces):
        rows, columns = source.shape
        target = buffer.at[
            pl.ds(pl.multiple_of(chip * rows, 16), rows),
            pl.ds(pl.multiple_of(part * columns, 128), columns),
        ]
        copies.append(pltpu.make_async_copy(source, target, sems.at[len(copies)]))
    return copies


def down_copies(where_ref, pieces, buffer, sems):
    copies = []
    for source, _, chip, part in pieces_of(where_ref, pieces):
        rows = source.shape[0]
        row = pl.multiple_of((chip * 2 + part) * rows, 16)
        copies.append(
            pltpu.make_async_copy(source, buffer.at[pl.ds(row, rows)], sems.at[len(copies)])
        )
    return copies


def project(where, work, vector, pieces):
    count, feature = work.shape[0], vector.shape[1]
    copies_count = 8 * pieces[0].shape[0]
    tile = 256

    def kernel(where_ref, work_ref, vector_ref, *refs):
        (
            flipped_ref, out_ref, weights_ref, output_ref, low, buffer, sems, store_sems
        ) = refs[PIECES:]
        copies = wide_copies(where_ref, refs[:PIECES], buffer, sems)
        for copy in copies:
            copy.start()

        def rows_of(index, carry):
            rows = pl.ds(pl.multiple_of(index * 64, 64), 64)
            unit, _ = normed(work_ref[rows, :].astype(jnp.float32))
            low[rows, :] = (unit * vector_ref[0:1, :] + vector_ref[1:2, :]).astype(jnp.bfloat16)
            return carry

        lax.fori_loop(0, count // 64, rows_of, 0)
        flipped_ref[...] = low[...].astype(jnp.float32).T.astype(jnp.bfloat16)
        for copy in copies:
            copy.wait()
        stores = [
            pltpu.make_async_copy(
                buffer.at[:, pl.ds(0, 3 * feature)], weights_ref, store_sems.at[0]
            ),
            pltpu.make_async_copy(
                buffer.at[:, pl.ds(3 * feature, feature)], output_ref, store_sems.at[1]
            ),
        ]
        for store in stores:
            store.start()
        for part, bias in ((0, 4), (1, None), (2, 5)):

            def columns_of(index, carry):
                inner = pl.ds(pl.multiple_of(index * tile, tile), tile)
                columns = pl.ds(pl.multiple_of(part * feature + index * tile, tile), tile)
                value = product(low[...], buffer[:, columns])
                if bias is not None:
                    value = value + vector_ref[bias : bias + 1, inner]
                out_ref[:, columns] = value.astype(jnp.bfloat16)
                return carry

            lax.fori_loop(0, feature // tile, columns_of, 0)
        for store in stores:
            store.wait()

    return pl.pallas_call(
        kernel,
        grid=(1,),
        out_shape=[
            shaped((feature, count), jnp.bfloat16),
            shaped((count, 3 * feature), jnp.bfloat16),
            shaped((feature, 3 * feature), jnp.bfloat16),
            shaped((feature, feature), jnp.bfloat16),
        ],
        in_specs=[SCALARS, whole(count, feature), whole(*vector.shape)] + [FAR] * PIECES,
        out_specs=[whole(feature, count), whole(count, 3 * feature), FAR, FAR],
        scratch_shapes=[
            pltpu.VMEM((count, feature), jnp.bfloat16),
            pltpu.VMEM((feature, 4 * feature), jnp.bfloat16),
            pltpu.SemaphoreType.DMA((copies_count,)),
            pltpu.SemaphoreType.DMA((2,)),
        ],
        compiler_params=settings(60),
        cost_estimate=cost(6 * count * feature * feature, 12 * feature * feature),
    )(where, work, vector, *pieces)


def code_both(code_ref, column, row):
    code = code_ref[...].astype(jnp.float32)
    column[...] = code[:, :1]
    row[...] = code.T[:1]


def one_head(values, head):
    lanes = iota(values.shape, 1)
    inside = (lanes >= head * HEAD) & (lanes < (head + 1) * HEAD)
    return jnp.where(inside, values, 0.0).astype(jnp.bfloat16)


def attend(projected, work, vector, weights, first, pairs, carried=None):
    count, feature = work.shape[0], vector.shape[1]
    all_pairs = feature // 128
    tile = 256
    ends = carried is not None

    def kernel(q_ref, k_ref, v_ref, weight_ref, code_ref, work_ref, vector_ref, *refs):
        if ends:
            carried_ref, attended_ref, stat_ref, resid_ref, low_ref, total, column, row = refs
        else:
            attended_ref, stat_ref, total, column, row = refs
        pair = pl.program_id(0)

        @pl.when(pair == 0)
        def _():
            code_both(code_ref, column, row)
            total[...] = carried_ref[...] if ends else jnp.zeros_like(total)

        keys = k_ref[...]
        values = v_ref[...].astype(jnp.float32).T.astype(jnp.bfloat16)
        scaled = q_ref[...].astype(jnp.float32) * 0.125
        heads = []
        for head in range(2):
            query = one_head(scaled, head)
            parts = []
            for start in range(0, count, tile):
                span = slice(start, start + tile)
                scores = by_rows(keys, query[span])
                same = column[...] == row[:, span]
                scores = jnp.where(same, scores, masked_value)
                most = jnp.max(scores, 0, keepdims=True)
                powers = jnp.exp(scores - most)
                sums = jnp.sum(powers, 0, keepdims=True)
                low = (powers * (1.0 / sums)).astype(jnp.bfloat16)
                stat_ref[0, head : head + 1, span] = most + jnp.log(sums)
                parts.append(product(values[head * HEAD : (head + 1) * HEAD], low))
            heads.append(jnp.concatenate(parts, 1))
        both = jnp.concatenate(heads, 0)
        attended_ref[...] = both.astype(jnp.bfloat16)
        total[...] += product(both.T.astype(jnp.bfloat16), weight_ref[...])

        if ends:

            @pl.when(pair == pairs - 1)
            def _():
                def rows_of(index, carry):
                    rows = pl.ds(pl.multiple_of(index * 64, 64), 64)
                    resid = (
                        work_ref[rows, :].astype(jnp.float32) + total[rows, :] + vector_ref[6:7, :]
                    )
                    resid_ref[rows, :] = resid
                    unit, _ = normed(resid)
                    low_ref[rows, :] = (unit * vector_ref[2:3, :] + vector_ref[3:4, :]).astype(
                        jnp.bfloat16
                    )
                    return carry

                lax.fori_loop(0, count // 64, rows_of, 0)

    def columns_at(offset):
        return pl.BlockSpec((count, 128), lambda pair: (0, offset + pair))

    wide = whole(count, feature)
    return pl.pallas_call(
        kernel,
        grid=(pairs,),
        out_shape=[
            shaped((pairs * 128, count), jnp.bfloat16),
            shaped((pairs, 8, count), jnp.float32),
        ]
        + (
            [shaped((count, feature), jnp.float32), shaped((count, feature), jnp.bfloat16)]
            if ends
            else [shaped((count, feature), jnp.float32)]
        ),
        in_specs=[
            columns_at(first),
            columns_at(all_pairs + first),
            columns_at(2 * all_pairs + first),
            pl.BlockSpec((128, feature), lambda pair: (first + pair, 0)),
            pl.BlockSpec((count, 128), lambda pair: (0, all_pairs)),
            wide,
            whole(*vector.shape),
        ]
        + ([wide] if ends else []),
        out_specs=[
            pl.BlockSpec((128, count), lambda pair: (pair, 0)),
            pl.BlockSpec((1, 8, count), lambda pair: (pair, 0, 0)),
        ]
        + ([wide, wide] if ends else [wide]),
        scratch_shapes=([pltpu.VMEM((count, feature), jnp.float32)] if ends else [])
        + [pltpu.VMEM((count, 1), jnp.float32), pltpu.VMEM((1, count), jnp.float32)],
        compiler_params=settings(LIMIT),
        cost_estimate=cost(
            8 * count * count * pairs * 128, 14 * count * feature, 2 * pairs * count * count
        ),
    )(
        projected, projected, projected, weights, work, work, vector,
        *([carried] if ends else []),
    )


def widen(where, low, bias_row, pieces):
    count, feature = low.shape
    wide = bias_row.shape[1]
    tile = feature
    steps = wide // tile

    def kernel(where_ref, low_ref, bias_ref, *refs):
        hidden_ref, slope_ref, weights_ref, buffer, sems, store_sem = refs[PIECES:]
        step = pl.program_id(0)
        store = pltpu.make_async_copy(buffer, weights_ref, store_sem)

        @pl.when(step == 0)
        def _():
            copies = wide_copies(where_ref, refs[:PIECES], buffer, sems)
            for copy in copies:
                copy.start()
            for copy in copies:
                copy.wait()
            store.start()

        columns = pl.ds(pl.multiple_of(step * tile, tile), tile)
        up = product(low_ref[...], buffer[:, columns]) + bias_ref[...]
        below = 0.5 * (1.0 + lax.erf(up * (0.5**0.5)))
        hidden_ref[...] = (up * below).astype(jnp.bfloat16)
        slope_ref[...] = below + up * (jnp.exp(-0.5 * up * up) * ((2.0 * math.pi) ** -0.5))

        @pl.when(step == steps - 1)
        def _():
            store.wait()

    block = pl.BlockSpec((count, tile), lambda step: (0, step))
    return pl.pallas_call(
        kernel,
        grid=(steps,),
        out_shape=[
            shaped((count, wide), jnp.bfloat16),
            shaped((count, wide), jnp.float32),
            shaped((feature, wide), jnp.bfloat16),
        ],
        in_specs=[
            SCALARS,
            whole(count, feature),
            pl.BlockSpec((1, tile), lambda step: (0, step)),
        ]
        + [FAR] * PIECES,
        out_specs=[block, block, FAR],
        scratch_shapes=[
            pltpu.VMEM((feature, wide), jnp.bfloat16),
            pltpu.SemaphoreType.DMA((8 * pieces[0].shape[0],)),
            pltpu.SemaphoreType.DMA,
        ],
        compiler_params=settings(60),
        cost_estimate=cost(
            2 * count * feature * wide, 2 * feature * wide + 6 * count * wide, count * wide
        ),
    )(where, low, bias_row, *pieces)


def down_gradient(where, hidden, grads, depth):
    count, wide = hidden.shape
    feature = grads.shape[1]
    rows = wide // (depth * PLANE)
    part = wide // depth

    def kernel(where_ref, hidden_ref, grads_ref, mine_ref, theirs_ref, result):
        y, x, core = where_ref[1], where_ref[2], where_ref[3]
        result[...] = by_columns(hidden_ref[...], grads_ref[...])
        for yy in range(2):
            for xx in range(2):
                spot = jnp.bitwise_xor(y, yy) * 2 + jnp.bitwise_xor(x, xx)
                first = (yy * 2 + xx) * 2
                for target, side in ((mine_ref, core), (theirs_ref, 1 - core)):
                    row = pl.multiple_of((first + side) * rows, 16)
                    target[spot, 0] = result[pl.ds(row, rows), :].astype(jnp.bfloat16)

    shape = shaped((4, depth, rows, feature), jnp.bfloat16)
    block = pl.BlockSpec((4, 1, rows, feature), lambda step, where_ref: (0, step, 0, 0))
    return pl.pallas_call(
        kernel,
        out_shape=[shape, shape],
        grid_spec=pltpu.PrefetchScalarGridSpec(
            num_scalar_prefetch=1,
            grid=(depth,),
            in_specs=[
                pl.BlockSpec(
                    (count, part),
                    lambda step, where_ref: (0, lax.rem(where_ref[0] + step, depth)),
                ),
                whole(count, feature),
            ],
            out_specs=[block, block],
            scratch_shapes=[pltpu.VMEM((part, feature), jnp.float32)],
        ),
        compiler_params=settings(LIMIT),
        cost_estimate=cost(2 * count * wide * feature, 2 * wide * (count + feature)),
    )(where, hidden, grads)


def put_wide(where_ref, result, mine_ref, theirs_ref):
    z, y, x, core = where_ref[0], where_ref[1], where_ref[2], where_ref[3]
    _, depth, rows, _ = mine_ref.shape
    for chip in range(4 * depth):
        zz, yy, xx = chip // 4, (chip // 2) % 2, chip % 2
        step = lax.rem(zz - z + depth, depth)
        spot = jnp.bitwise_xor(y, yy) * 2 + jnp.bitwise_xor(x, xx)
        for target, side in ((mine_ref, core), (theirs_ref, 1 - core)):
            row = pl.multiple_of((chip * 2 + side) * rows, 8)
            target[spot, step] = result[pl.ds(row, rows), :].astype(jnp.bfloat16)


def narrow(where, hidden, resid, vector, pieces):
    count, wide = hidden.shape
    feature = resid.shape[1]
    tile = 256

    def kernel(where_ref, hidden_ref, resid_ref, vector_ref, *refs):
        out_ref, weights_ref, buffer, sems, store_sem = refs[PIECES:]
        copies = down_copies(where_ref, refs[:PIECES], buffer, sems)
        for copy in copies:
            copy.start()
        for copy in copies:
            copy.wait()
        store = pltpu.make_async_copy(buffer, weights_ref, store_sem)
        store.start()

        def columns_of(index, carry):
            columns = pl.ds(pl.multiple_of(index * tile, tile), tile)
            value = product(hidden_ref[...], buffer[:, columns])
            out_ref[:, columns] = (
                resid_ref[:, columns] + (value + vector_ref[7:8, columns])
            ).astype(jnp.bfloat16)
            return carry

        lax.fori_loop(0, feature // tile, columns_of, 0)
        store.wait()

    return pl.pallas_call(
        kernel,
        grid=(1,),
        out_shape=[
            shaped((count, feature), jnp.bfloat16),
            shaped((wide, feature), jnp.bfloat16),
        ],
        in_specs=[SCALARS, whole(count, wide), whole(count, feature), whole(*vector.shape)]
        + [FAR] * PIECES,
        out_specs=[whole(count, feature), FAR],
        scratch_shapes=[
            pltpu.VMEM((wide, feature), jnp.bfloat16),
            pltpu.SemaphoreType.DMA((8 * pieces[0].shape[0],)),
            pltpu.SemaphoreType.DMA,
        ],
        compiler_params=settings(LIMIT),
        cost_estimate=cost(2 * count * wide * feature, 6 * wide * feature),
    )(where, hidden, resid, vector, *pieces)


def feed_back(where, slope, low, grads, resid, vector, up_weights, down_weights, attended, depth):
    count, wide = slope.shape
    feature = resid.shape[1]
    tile = feature
    steps = wide // tile
    half = feature // 2
    chip_rows = feature // (PLANE * depth)

    def kernel(
        where_ref, slope_ref, low_ref, grads_ref, resid_ref, vector_ref, up_ref, down_ref, left_ref, right_ref,
        dresid_ref, dlow_ref, sums_ref, bias_ref, mine_ref, theirs_ref, back, flipped, result,
    ):
        step = pl.program_id(0)

        @pl.when(step == 0)
        def _():
            flipped[...] = low_ref[...].astype(jnp.float32).T.astype(jnp.bfloat16)
            back[...] = jnp.zeros_like(back)

        @pl.when(step < steps)
        def _():
            dup = (slope_ref[...] * by_rows(grads_ref[...], down_ref[...])).astype(jnp.bfloat16)
            bias_ref[...] = jnp.sum(dup.astype(jnp.float32), 0, keepdims=True)
            back[...] += by_rows(dup, up_ref[...])
            result[...] = product(flipped[...], dup)

        @pl.when(step == steps)
        def _():
            sums_ref[...] = jnp.zeros_like(sums_ref)

            def rows_of(index, carry):
                rows = pl.ds(pl.multiple_of(index * 64, 64), 64)
                unit, scale = normed(resid_ref[rows, :])
                da = back[rows, :]
                dy = grads_ref[rows, :].astype(jnp.float32)
                dresid = dy + norm_back(da, vector_ref[2:3, :], unit, scale)
                dresid_ref[rows, :] = dresid
                dlow = dresid.astype(jnp.bfloat16)
                dlow_ref[rows, :] = dlow
                for row, value in enumerate((da * unit, da, dlow.astype(jnp.float32), dy)):
                    sums_ref[row : row + 1, :] += jnp.sum(value, 0, keepdims=True)
                return carry

            lax.fori_loop(0, count // 64, rows_of, 0)
            result[:half, :] = product(left_ref[...], dlow_ref[...])
            result[half:, :] = product(right_ref[...], dlow_ref[...])

        put_wide(where_ref, result, mine_ref, theirs_ref)

    def at(step):
        return jnp.minimum(step, steps - 1)

    def columns_at(rows):
        return pl.BlockSpec((rows, tile), lambda step: (0, at(step)))

    all_rows = whole(count, feature)
    split = shaped((4, depth, chip_rows, (steps + 1) * feature), jnp.bfloat16)
    block = pl.BlockSpec((4, depth, chip_rows, feature), lambda step: (0, 0, 0, step))
    return pl.pallas_call(
        kernel,
        grid=(steps + 1,),
        out_shape=[
            shaped((count, feature), jnp.float32),
            shaped((count, feature), jnp.bfloat16),
            shaped((8, feature), jnp.float32),
            shaped((1, wide), jnp.float32),
            split,
            split,
        ],
        in_specs=[
            SCALARS,
            columns_at(count),
            all_rows,
            all_rows,
            all_rows,
            whole(*vector.shape),
            columns_at(feature),
            pl.BlockSpec((tile, feature), lambda step: (at(step), 0)),
            whole(half, count),
            whole(half, count),
        ],
        out_specs=[all_rows, all_rows, whole(8, feature), columns_at(1), block, block],
        scratch_shapes=[
            pltpu.VMEM((count, feature), jnp.float32),
            pltpu.VMEM((feature, count), jnp.bfloat16),
            pltpu.VMEM((feature, feature), jnp.float32),
        ],
        compiler_params=settings(LIMIT),
        cost_estimate=cost(6 * count * wide * feature, 8 * wide * feature + 10 * count * wide),
    )(where, slope, low, grads, resid, vector, up_weights, down_weights, *attended)


def attend_back(projected, work, stats, dlow, weights, first, pairs, gradient=None):
    count, feature = dlow.shape
    all_pairs = feature // 128
    tile = 256
    wide = pairs * 128

    def kernel(q_ref, k_ref, v_ref, code_ref, stat_ref, dlow_ref, weight_ref, *refs):
        if gradient is None:
            out_ref, sums_ref, douts, column, row = refs
        else:
            (
                where_ref, flipped_ref, left_ref, out_ref, sums_ref, mine_ref, theirs_ref,
                douts, column, row, right, result,
            ) = refs
        pair = pl.program_id(0)

        @pl.when(pair == 0)
        def _():
            code_both(code_ref, column, row)
            for start in range(0, wide, 128):
                span = slice(start, start + 128)
                douts[start // 128] = by_rows(dlow_ref[...], weight_ref[span, :]).astype(
                    jnp.bfloat16
                )

        @pl.when(pair < pairs)
        def _():
            keys, values = k_ref[...], v_ref[...]
            flipped = keys.astype(jnp.float32).T.astype(jnp.bfloat16)
            scaled = q_ref[...].astype(jnp.float32) * 0.125
            dout = douts[pair].astype(jnp.float32)
            dkey = jnp.zeros((count, 128), jnp.float32)
            dvalue = jnp.zeros((count, 128), jnp.float32)
            heads = []
            for head in range(2):
                query = one_head(scaled, head)
                dhead = one_head(dout, head)
                parts = []
                for start in range(0, count, tile):
                    span = slice(start, start + tile)
                    scores = by_rows(keys, query[span])
                    same = column[...] == row[:, span]
                    probs = jnp.exp(
                        jnp.where(same, scores, masked_value) - stat_ref[0, head : head + 1, span]
                    )
                    dprob = by_rows(values, dhead[span])
                    inner = jnp.sum(probs * dprob, 0, keepdims=True)
                    dscore = (probs * (dprob - inner)).astype(jnp.bfloat16)
                    dvalue = dvalue + product(probs.astype(jnp.bfloat16), dhead[span])
                    dkey = dkey + product(dscore, query[span])
                    parts.append(product(flipped[head * HEAD : (head + 1) * HEAD], dscore))
                heads.append(jnp.concatenate(parts, 1))
            dquery = (jnp.concatenate(heads, 0).T * 0.125).astype(jnp.bfloat16)
            dvalue = dvalue.astype(jnp.bfloat16)
            out_ref[0] = dquery
            out_ref[1] = dkey.astype(jnp.bfloat16)
            out_ref[2] = dvalue
            sums_ref[0:1, :] = jnp.sum(dquery.astype(jnp.float32), 0, keepdims=True)
            sums_ref[1:2, :] = jnp.sum(dvalue.astype(jnp.float32), 0, keepdims=True)
            if gradient is not None:
                right[0, pair] = dquery
                right[1, pair] = dkey.astype(jnp.bfloat16)
                right[2, pair] = dvalue

        if gradient is not None:

            @pl.when(pair >= pairs)
            def _():
                flipped = flipped_ref[...]
                result[:, :wide] = product(flipped, left_ref[0])
                for index in range(pairs):
                    span = slice(wide + index * 128, wide + (index + 1) * 128)
                    result[:, span] = product(flipped, right[pair - pairs, index])
                put_wide(where_ref, result, mine_ref, theirs_ref)

    def at(pair):
        return jnp.minimum(pair, pairs - 1)

    def part_at(pair):
        return jnp.maximum(pair - pairs, 0)

    def columns_at(offset):
        return pl.BlockSpec((count, 128), lambda pair: (0, offset + at(pair)))

    out_shape = [shaped((3, count, wide), jnp.bfloat16), shaped((8, wide), jnp.float32)]
    in_specs = [
        columns_at(first),
        columns_at(all_pairs + first),
        columns_at(2 * all_pairs + first),
        pl.BlockSpec((count, 128), lambda pair: (0, all_pairs)),
        pl.BlockSpec((1, 8, count), lambda pair: (at(pair), 0, 0)),
        whole(count, feature),
        pl.BlockSpec((wide, feature), lambda pair: (first // pairs, 0)),
    ]
    out_specs = [
        pl.BlockSpec((3, count, 128), lambda pair: (0, 0, at(pair))),
        pl.BlockSpec((8, 128), lambda pair: (0, at(pair))),
    ]
    scratch = [
        pltpu.VMEM((pairs, count, 128), jnp.bfloat16),
        pltpu.VMEM((count, 1), jnp.float32),
        pltpu.VMEM((1, count), jnp.float32),
    ]
    extra = ()
    if gradient is not None:
        where, flipped, left, depth = gradient
        rows = feature // (PLANE * depth)
        extra = (where, flipped, left)
        out_shape += [shaped((4, depth, rows, 3 * feature), jnp.bfloat16)] * 2
        in_specs += [
            SCALARS,
            whole(feature, count),
            pl.BlockSpec((1, count, wide), lambda pair: (part_at(pair), 0, 0)),
        ]
        out_specs += [
            pl.BlockSpec((4, depth, rows, feature), lambda pair: (0, 0, 0, part_at(pair)))
        ] * 2
        scratch += [
            pltpu.VMEM((3, pairs, count, 128), jnp.bfloat16),
            pltpu.VMEM((feature, feature), jnp.float32),
        ]
    return pl.pallas_call(
        kernel,
        grid=(pairs if gradient is None else pairs + 3,),
        out_shape=out_shape,
        in_specs=in_specs,
        out_specs=out_specs,
        scratch_shapes=scratch,
        compiler_params=settings(LIMIT),
        cost_estimate=cost(
            14 * count * count * wide, 16 * count * feature, 2 * pairs * count * count
        ),
    )(projected, projected, projected, work, stats, dlow, weights, *extra)


def project_back(work, dprojected, dresid, vector, weights, sums_two, sums_attend, bias_up, devices):
    count, feature = dresid.shape
    tile = 128
    half = feature // 2
    lanes = 16 * feature // devices // 128
    capacity = count // devices

    def kernel(
        work_ref, d_ref, e_ref, dresid_ref, vector_ref, weight_ref, two_ref, left_ref, right_ref, bias_ref,
        out_ref, sums,
    ):
        sums[...] = jnp.zeros_like(sums)

        def rows_of(index, carry):
            rows = pl.ds(pl.multiple_of(index * tile, tile), tile)
            da = jnp.zeros((tile, feature), jnp.float32)
            for part in range(3):
                middle = part * feature + half
                da += by_rows(d_ref[part, rows, :], weight_ref[:, middle - half : middle])
                da += by_rows(e_ref[part, rows, :], weight_ref[:, middle : middle + half])
            unit, scale = normed(work_ref[rows, :].astype(jnp.float32))
            out_ref[rows, :feature] = (
                dresid_ref[rows, :] + norm_back(da, vector_ref[0:1, :], unit, scale)
            ).astype(jnp.bfloat16)
            sums[0:1, :] += jnp.sum(da * unit, 0, keepdims=True)
            sums[1:2, :] += jnp.sum(da, 0, keepdims=True)
            return carry

        lax.fori_loop(0, count // tile, rows_of, 0)
        sums[2:4, :] = two_ref[0:2, :]
        sums[4:6, :half] = left_ref[0:2, :]
        sums[4:6, half:] = right_ref[0:2, :]
        sums[6:8, :] = two_ref[2:4, :]
        for row in range(FF // feature):
            sums[8 + row : 9 + row, :] = bias_ref[0:1, row * feature : (row + 1) * feature]
        place_in = iota((capacity, 128), 0)
        for device in range(devices):
            block = jnp.zeros((capacity, 128), jnp.float32)
            for lane in range(lanes):
                first = device * lanes + lane
                row, column = divmod(first * 128, feature)
                value = sums[row : row + 1, column : column + 128]
                high = value.astype(jnp.bfloat16).astype(jnp.float32)
                block = jnp.where(place_in == lane, high, block)
                block = jnp.where(place_in == lanes + lane, value - high, block)
            out_ref[device * capacity : (device + 1) * capacity, feature:] = block.astype(
                jnp.bfloat16
            )

    return pl.pallas_call(
        kernel,
        grid=(1,),
        out_shape=shaped((count, feature + 128), jnp.bfloat16),
        in_specs=[
            whole(count, feature),
            whole(3, count, half),
            whole(3, count, half),
            whole(count, feature),
            whole(*vector.shape),
            whole(feature, 3 * feature),
            whole(8, feature),
            whole(8, half),
            whole(8, half),
            whole(1, FF),
        ],
        out_specs=whole(count, feature + 128),
        scratch_shapes=[pltpu.VMEM((16, feature), jnp.float32)],
        compiler_params=settings(LIMIT),
        cost_estimate=cost(6 * count * feature * feature, 6 * feature * feature),
    )(work, *dprojected, dresid, vector, weights, sums_two, *sums_attend, bias_up)


def structured(devices, feature):
    rows = feature // devices
    return devices % PLANE == 0 and feature % devices == 0 and (2 * rows) % 16 == 0


def body(
    tokens,
    cotangent,
    segment_ids,
    wide_weight,
    wide_moment,
    wide_average,
    down_weight,
    down_moment,
    down_average,
    vector_weight,
    vector_moment,
    vector_average,
):
    devices = lax.axis_size("dev")
    count, feature = tokens.shape
    if not structured(devices, feature):
        return plain_body(
            tokens,
            cotangent,
            segment_ids,
            wide_weight,
            wide_moment,
            wide_average,
            down_weight,
            down_moment,
            down_average,
            vector_weight,
            vector_moment,
            vector_average,
        )
    depth = devices // PLANE
    capacity = count // devices
    where = place()
    core = where[3]

    wide_low, down_low = wide_weight.astype(jnp.bfloat16), down_weight.astype(jnp.bfloat16)
    rows, columns = wide_low.shape
    parts = wide_low.reshape(rows, 2, 2, columns // 4)
    keep, give = core_order(core, parts[:, :, 0], parts[:, :, 1])
    got = lax.ppermute(give, "dev", flips(devices, 1))
    pair = jnp.concatenate(core_order(core, keep, got), 0)

    send_rows, send_grads, slot = route(segment_ids.reshape(1, count), tokens, cotangent, devices)
    first_own = along_z(pair[:, 0])
    send_rows, first_own = pin(send_rows, first_own)

    work = exchange(send_rows.reshape(devices, capacity, -1)).reshape(count, -1)
    first_near = to_neighbours(first_own)
    first_near, up_block = pin(first_near, pair[:, 1])

    first_far = to_diagonal(*first_near)
    first_got = to_partner(first_own, *first_near)
    first_far, first_got = pin(first_far, first_got)
    first_got = first_got + to_partner(*first_far)
    first_got, work, up_block = pin(first_got, work, up_block)

    up_own = along_z(up_block)
    flipped_one, projected, first_weights, out_weights = project(
        where, work, vector_weight, (first_own, *first_near, *first_far, *first_got)
    )
    projected, up_own, down_block, send_grads = pin(projected, up_own, down_low, send_grads)

    up_near = to_neighbours(up_own)
    down_own = along_z(down_block)
    pairs = feature // 256
    attended_a, stats_a, carried = attend(projected, work, vector_weight, out_weights, 0, pairs)
    carried, up_near, down_own, send_grads = pin(carried, up_near, down_own, send_grads)

    up_far = to_diagonal(*up_near)
    up_got = to_partner(up_own, *up_near)
    grads = exchange(send_grads.reshape(devices, capacity, feature)).reshape(count, feature)
    attended_b, stats_b, resid, low_two = attend(
        projected, work, vector_weight, out_weights, pairs, pairs, carried
    )
    low_two, up_far, up_got = pin(low_two, up_far, up_got)
    up_got = up_got + to_partner(*up_far)
    low_two, up_got, down_own = pin(low_two, up_got, down_own)

    down_near = to_neighbours(down_own)
    hidden, slope, up_weights = widen(
        where, low_two, vector_weight[8:].reshape(1, FF), (up_own, *up_near, *up_far, *up_got)
    )
    hidden, down_near = pin(hidden, down_near)

    down_far = to_diagonal(*down_near)
    down_got = to_partner(down_own, *down_near)
    down_mine, down_theirs = down_gradient(where, hidden, grads, depth)
    down_far, down_got, down_mine, down_theirs = pin(down_far, down_got, down_mine, down_theirs)

    down_got = pin(*down_got, *to_partner(*down_far))
    got = send(down_theirs, 1)
    output, down_weights = narrow(
        where, hidden, resid, vector_weight, (down_own, *down_near, *down_far, *down_got)
    )
    output, down_weights, got = pin(output, down_weights, got)

    down_fold = Fold(down_mine, got)
    down_to = pin(*down_fold.diagonal())
    back_out = exchange(output.reshape(devices, capacity, feature)).reshape(count, feature)
    got = over_diagonal(*down_to)
    dresid, dlow, sums_two, bias_up_grad, up_mine, up_theirs = feed_back(
        where, slope, low_two, grads, resid, vector_weight, up_weights, down_weights,
        (attended_a, attended_b), depth,
    )
    dlow, got, up_mine, up_theirs, back_out = pin(dlow, got, up_mine, up_theirs, back_out)
    down_to, dlow, up_theirs = pin(down_fold.neighbours(*got), dlow, up_theirs)

    down_got = over_plane(*down_to)
    up_got = send(up_theirs, 1)
    dleft, sums_left = attend_back(projected, work, stats_a, dlow, out_weights, 0, pairs)
    up_got, dleft, dlow = pin(up_got, dleft, dlow)
    up_fold = Fold(up_mine, up_got)
    up_to, dlow = pin(up_fold.diagonal(), dlow)

    up_got = over_diagonal(*up_to)
    dright, sums_right, first_mine, first_theirs = attend_back(
        projected, work, stats_b, dlow, out_weights, pairs, pairs,
        (where, flipped_one, dleft, depth),
    )
    up_got, down_got, dright, first_mine, first_theirs = pin(
        up_got, down_got, dright, first_mine, first_theirs
    )
    up_to, down_sums, dright, first_theirs = pin(
        up_fold.neighbours(*up_got), down_fold.column(*down_got), dright, first_theirs
    )

    up_got = over_plane(*up_to)
    down_got = over_column(down_sums)
    first_got = send(first_theirs, 1)
    block_output = give_back(slot, back_out)
    first_got, dright, block_output = pin(first_got, dright, block_output)
    first_fold = Fold(first_mine, first_got)
    first_to, dright = pin(first_fold.diagonal(), dright)

    got = over_diagonal(*first_to)
    both = project_back(
        work, (dleft, dright), dresid, vector_weight, first_weights,
        sums_two, (sums_left, sums_right), bias_up_grad, devices,
    )
    both, got, up_got, down_got = pin(both, got, up_got, down_got)
    first_to, up_sums = pin(first_fold.neighbours(*got), up_fold.column(*up_got))

    back = exchange(both.reshape(devices, capacity, -1))
    got = over_plane(*first_to)
    up_got = over_column(up_sums)
    down_grad = total_of(down_sums[0], *down_got)
    got, down_grad = pin(got, down_grad)
    first_sums = pin(*first_fold.column(*got))

    first_got = over_column(first_sums)
    up_grad = total_of(up_sums[0], *up_got)
    first_got, up_grad = pin(first_got, up_grad)
    first_grad = total_of(first_sums[0], *first_got)
    back, first_grad = pin(back, first_grad)
    input_grad = give_back(slot, back.reshape(count, -1))

    lanes = 16 * feature // devices // 128
    vector_share = total_of(back[:, :lanes, feature:], back[:, lanes : 2 * lanes, feature:])
    vector_share = jnp.sum(vector_share, 0)
    wide_grad = jnp.concatenate([first_grad, up_grad[:, FF:], up_grad[:, :FF]], 1)
    shard_squares = sum(jnp.sum(grad * grad) for grad in (down_grad, up_grad, first_grad))
    packet = jnp.concatenate([vector_share, jnp.full((1, 128), shard_squares)], 0)
    packets = exchange(jnp.broadcast_to(packet[None], (devices, lanes + 1, 128)))
    vector_grad = packets[:, :lanes].reshape(-1, feature)[: vector_weight.shape[0]]
    total = jnp.sum(packets[:, lanes, 0]) + jnp.sum(vector_grad * vector_grad)
    grad_norm = jnp.sqrt(total)
    factor = clip_norm / jnp.maximum(grad_norm, clip_norm)
    wide_new, wide_moment_new, wide_average_new = advance(
        wide_weight, wide_moment, wide_average, wide_grad, factor, decay_rate
    )
    down_new, down_moment_new, down_average_new = advance(
        down_weight, down_moment, down_average, down_grad, factor, decay_rate
    )
    vector_new, vector_moment_new, vector_average_new = advance(
        vector_weight, vector_moment, vector_average, vector_grad, factor, 0.0
    )
    return (
        block_output,
        input_grad,
        grad_norm,
        wide_new,
        wide_moment_new,
        wide_average_new,
        down_new,
        down_moment_new,
        down_average_new,
        vector_new,
        vector_moment_new,
        vector_average_new,
    )


def solution(mesh):
    placed = (
        P("dev", None),
        P("dev", None),
        P("dev"),
        P("dev", None),
        P("dev", None),
        P("dev", None),
        P("dev", None),
        P("dev", None),
        P("dev", None),
        P(),
        P(),
        P(),
    )
    return jax.shard_map(
        body,
        mesh=mesh,
        in_specs=placed,
        out_specs=(
            P("dev", None),
            P("dev", None),
            P(),
            P("dev", None),
            P("dev", None),
            P("dev", None),
            P("dev", None),
            P("dev", None),
            P("dev", None),
            P(),
            P(),
            P(),
        ),
        check_vma=False,
    )
```

```python
import math

import jax
import jax.numpy as jnp
from jax import lax
from jax.experimental import pallas as pl
from jax.experimental.pallas import tpu as pltpu
from jax.sharding import PartitionSpec as P

HEADS = 12
HEAD = 64
FF = 3072
DOCS_DEV = 4
PLANE = 8
MIB = 1 << 20


epsilon = 1e-05
masked_value = -1e30
momentum = 0.9
learn_rate = 0.01
decay_rate = 0.0001
average_rate = 0.8
clip_norm = 2048.0


def norm_rows(values, gain_row, shift_row):
    center = values - jnp.mean(values, -1, keepdims=True)
    spread = jnp.mean(center * center, -1, keepdims=True)
    return center * lax.rsqrt(spread + epsilon) * gain_row + shift_row


def gelu_exact(values):
    return jax.nn.gelu(values, approximate=False)


def product(matrix, other):
    return jnp.dot(matrix, other, preferred_element_type=jnp.float32)


def against(matrix, other):
    return lax.dot_general(
        matrix, other, (((1,), (1,)), ((), ())), preferred_element_type=jnp.float32
    )


def inner_rows(matrix, other):
    return lax.dot_general(
        matrix, other, (((0,), (0,)), ((), ())), preferred_element_type=jnp.float32
    )


def advance(weight, moment, average, gradient, factor, decay_term):
    update = factor * gradient + decay_term * weight
    new_moment = momentum * moment + update
    new_weight = weight - learn_rate * (update + momentum * new_moment)
    new_average = average_rate * average + (1.0 - average_rate) * new_weight
    return (new_weight, new_moment, new_average)


def routing(segment_ids, devices, capacity):
    row_count = segment_ids.shape[0]
    is_live = segment_ids >= 0
    target = jnp.where(is_live, segment_ids // DOCS_DEV, devices)
    onehot = (target[:, None] == jnp.arange(devices, dtype=jnp.int32)[None, :]).astype(jnp.int32)
    earlier = jnp.cumsum(onehot, axis=0) - onehot
    within = jnp.sum(earlier * onehot, axis=1)
    slot_of = jnp.where(is_live, target * capacity + within, row_count)
    anchor = (
        jnp.full((row_count,), row_count, jnp.int32)
        .at[slot_of]
        .set(jnp.arange(row_count, dtype=jnp.int32), mode="drop")
    )
    return (is_live, jnp.minimum(slot_of, row_count - 1), anchor)


def plain_body(
    tokens,
    cotangent,
    segment_ids,
    wide_weight,
    wide_moment,
    wide_average,
    down_weight,
    down_moment,
    down_average,
    vector_weight,
    vector_moment,
    vector_average,
):
    wide_full, down_full = (
        lax.all_gather(wide_weight.astype(jnp.bfloat16), "dev", axis=0, tiled=True),
        lax.all_gather(down_weight.astype(jnp.bfloat16), "dev", axis=0, tiled=True),
    )
    devices = lax.axis_size("dev")
    row_count, feature = tokens.shape
    capacity = row_count // devices
    is_live, slot_of, anchor = routing(segment_ids, devices, capacity)
    blank_row = jnp.zeros((1, feature), jnp.bfloat16)
    send_rows = jnp.concatenate([tokens, blank_row], 0)[anchor].reshape(devices, capacity, feature)
    send_grads = jnp.concatenate([cotangent, blank_row], 0)[anchor].reshape(
        devices, capacity, feature
    )
    send_ids = jnp.concatenate([segment_ids, jnp.full((1,), -1, jnp.int32)], 0)[anchor].reshape(
        devices, capacity
    )
    work_rows, work_grads, work_ids = (
        lax.all_to_all(send_rows, "dev", split_axis=0, concat_axis=0, tiled=True),
        lax.all_to_all(send_grads, "dev", split_axis=0, concat_axis=0, tiled=True),
        lax.all_to_all(send_ids, "dev", split_axis=0, concat_axis=0, tiled=True),
    )
    work_rows = work_rows.reshape(row_count, feature)
    work_grads = work_grads.reshape(row_count, feature)
    work_ids = work_ids.reshape(row_count)
    gain_one, shift_one, gain_two, shift_two, bias_query, bias_value, bias_out, bias_down = [
        vector_weight[row_index] for row_index in range(8)
    ]
    bias_up = vector_weight[8:].reshape(FF)
    w_qkv = wide_full[:, : 3 * feature]
    w_out = wide_full[:, 3 * feature : 4 * feature]
    w_up = wide_full[:, 4 * feature :]
    work_float = work_rows.astype(jnp.float32)
    low_one = norm_rows(work_float, gain_one, shift_one).astype(jnp.bfloat16)
    bias_all = jnp.concatenate([bias_query, jnp.zeros_like(bias_query), bias_value])
    projected = (product(low_one, w_qkv) + bias_all).astype(jnp.bfloat16)
    queries = projected[:, :feature].reshape(row_count, HEADS, HEAD)
    key_rows = projected[:, feature : 2 * feature].reshape(row_count, HEADS, HEAD)
    value_rows = projected[:, 2 * feature :].reshape(row_count, HEADS, HEAD)
    same_seg = work_ids[:, None] == work_ids[None, :]
    block_rows = min(512, row_count)
    group_size = math.gcd(HEADS, 4)
    group_count = HEADS // group_size

    def scores_of(offset, first_head):
        query_part = queries[offset : offset + block_rows, first_head : first_head + group_size]
        raw_scores = (
            jnp.einsum(
                "qhd,khd->hqk",
                query_part,
                key_rows[:, first_head : first_head + group_size],
                preferred_element_type=jnp.float32,
            )
            * 0.125
        )
        return jnp.where(same_seg[None], raw_scores, masked_value)

    stored = []
    offset = 0
    head_outs = []
    for group in range(group_count):
        first_head = group * group_size
        scores = scores_of(offset, first_head)
        row_max = jnp.max(scores, -1, keepdims=True)
        powers = jnp.exp(scores - row_max)
        row_sums = jnp.sum(powers, -1, keepdims=True)
        prob_low = (powers / row_sums).astype(jnp.bfloat16)
        head_outs.append(
            jnp.einsum(
                "hqk,khd->qhd",
                prob_low,
                value_rows[:, first_head : first_head + group_size],
                preferred_element_type=jnp.float32,
            )
        )
        stored.append((row_max, row_sums))
    out_blocks = jnp.concatenate(head_outs, 1)
    attended = out_blocks.reshape(row_count, feature).astype(jnp.bfloat16)
    resid = work_float + product(attended, w_out) + bias_out
    low_two = norm_rows(resid, gain_two, shift_two).astype(jnp.bfloat16)
    up_float = product(low_two, w_up) + bias_up
    hidden = gelu_exact(up_float).astype(jnp.bfloat16)
    output_low = (resid + product(hidden, down_full) + bias_down).astype(jnp.bfloat16)
    dy_float = work_grads.astype(jnp.float32)
    dhidden = against(work_grads, down_full)
    gelu_pull = jax.vjp(gelu_exact, up_float)[1]
    dup_low = gelu_pull(dhidden)[0].astype(jnp.bfloat16)
    da_two = against(dup_low, w_up)
    norm_two_pull = jax.vjp(norm_rows, resid, gain_two, shift_two)[1]
    dres_norm, dgain_two, dshift_two = norm_two_pull(da_two)
    dresid = dy_float + dres_norm
    dres_low = dresid.astype(jnp.bfloat16)
    dattended = against(dres_low, w_out).astype(jnp.bfloat16).reshape(row_count, HEADS, HEAD)
    dkey_parts = [
        jnp.zeros((row_count, group_size, HEAD), jnp.float32) for group in range(group_count)
    ]
    dvalue_parts = [
        jnp.zeros((row_count, group_size, HEAD), jnp.float32) for group in range(group_count)
    ]
    position = 0
    offset = 0
    pieces = []
    for group in range(group_count):
        first_head = group * group_size
        scores = scores_of(offset, first_head)
        row_max, row_sums = stored[position]
        position += 1
        prob_float = jnp.exp(scores - row_max) / row_sums
        prob_low = prob_float.astype(jnp.bfloat16)
        dout_part = dattended[offset : offset + block_rows, first_head : first_head + group_size]
        value_part = value_rows[:, first_head : first_head + group_size]
        dvalue_parts[group] = jnp.einsum(
            "hqk,qhd->khd", prob_low, dout_part, preferred_element_type=jnp.float32
        )
        dprob = jnp.einsum(
            "qhd,khd->hqk", dout_part, value_part, preferred_element_type=jnp.float32
        )
        dscore = (prob_float * (dprob - jnp.sum(prob_float * dprob, -1, keepdims=True))).astype(
            jnp.bfloat16
        )
        pieces.append(
            jnp.einsum(
                "hqk,khd->qhd",
                dscore,
                key_rows[:, first_head : first_head + group_size],
                preferred_element_type=jnp.float32,
            )
            * 0.125
        )
        query_part = queries[offset : offset + block_rows, first_head : first_head + group_size]
        dkey_parts[group] = (
            jnp.einsum("hqk,qhd->khd", dscore, query_part, preferred_element_type=jnp.float32)
            * 0.125
        )
    dquery_blocks = jnp.concatenate(pieces, 1)
    dquery_low = dquery_blocks.reshape(row_count, feature).astype(jnp.bfloat16)
    dkey_low = jnp.concatenate(dkey_parts, 1).reshape(row_count, feature).astype(jnp.bfloat16)
    dvalue_low = jnp.concatenate(dvalue_parts, 1).reshape(row_count, feature).astype(jnp.bfloat16)
    dqkv_low = jnp.concatenate([dquery_low, dkey_low, dvalue_low], 1)
    da_one = against(dqkv_low, w_qkv)
    norm_one_pull = jax.vjp(norm_rows, work_float, gain_one, shift_one)[1]
    dinput_norm, dgain_one, dshift_one = norm_one_pull(da_one)
    dinput_low = (dresid + dinput_norm).astype(jnp.bfloat16)
    back_out, back_grad = (
        lax.all_to_all(
            output_low.reshape(devices, capacity, feature),
            "dev",
            split_axis=0,
            concat_axis=0,
            tiled=True,
        ),
        lax.all_to_all(
            dinput_low.reshape(devices, capacity, feature),
            "dev",
            split_axis=0,
            concat_axis=0,
            tiled=True,
        ),
    )
    block_output = jnp.where(
        is_live[:, None], back_out.reshape(row_count, feature)[slot_of], jnp.zeros_like(tokens)
    )
    input_grad = jnp.where(
        is_live[:, None], back_grad.reshape(row_count, feature)[slot_of], jnp.zeros_like(tokens)
    )
    vector_rows = jnp.stack(
        [
            dgain_one,
            dshift_one,
            dgain_two,
            dshift_two,
            jnp.sum(dquery_low.astype(jnp.float32), 0),
            jnp.sum(dvalue_low.astype(jnp.float32), 0),
            jnp.sum(dres_low.astype(jnp.float32), 0),
            jnp.sum(dy_float, 0),
        ],
        0,
    )
    bias_up_grad = jnp.sum(dup_low.astype(jnp.float32), 0).reshape(FF // feature, feature)
    vector_partial = jnp.concatenate([vector_rows, bias_up_grad], 0)
    down_grad = lax.psum_scatter(
        inner_rows(hidden, work_grads), "dev", scatter_dimension=0, tiled=True
    )
    wide_grad = lax.psum_scatter(
        jnp.concatenate(
            [
                inner_rows(low_one, dqkv_low),
                jnp.concatenate([inner_rows(attended, dres_low), inner_rows(low_two, dup_low)], 1),
            ],
            1,
        ),
        "dev",
        scatter_dimension=0,
        tiled=True,
    )
    shard_squares = jnp.sum(wide_grad * wide_grad) + jnp.sum(down_grad * down_grad)
    vector_grad = lax.psum(vector_partial, "dev")
    total = lax.psum(shard_squares, "dev") + jnp.sum(vector_grad * vector_grad)
    grad_norm = jnp.sqrt(total)
    factor = clip_norm / jnp.maximum(grad_norm, clip_norm)
    wide_new, wide_moment_new, wide_average_new = advance(
        wide_weight, wide_moment, wide_average, wide_grad, factor, decay_rate
    )
    down_new, down_moment_new, down_average_new = advance(
        down_weight, down_moment, down_average, down_grad, factor, decay_rate
    )
    vector_new, vector_moment_new, vector_average_new = advance(
        vector_weight, vector_moment, vector_average, vector_grad, factor, 0.0
    )
    return (
        block_output,
        input_grad,
        grad_norm,
        wide_new,
        wide_moment_new,
        wide_average_new,
        down_new,
        down_moment_new,
        down_average_new,
        vector_new,
        vector_moment_new,
        vector_average_new,
    )


def flips(devices, mask):
    return [(i, i ^ mask) for i in range(devices)]


def shifts(devices, step):
    return [(i, (i + PLANE * step) % devices) for i in range(devices)]


def place():
    me = lax.axis_index("dev")
    return jnp.stack([me // PLANE, (me // 4) % 2, (me // 2) % 2, me % 2]).astype(jnp.int32)


def core_order(core, mine, theirs):
    first = jnp.where(core == 0, mine, theirs)
    second = jnp.where(core == 0, theirs, mine)
    return first, second


def pin(*values):
    return lax.optimization_barrier(values)


def send(value, mask):
    return lax.ppermute(value, "dev", flips(lax.axis_size("dev"), mask))


def along_z(block, stacks):
    devices = lax.axis_size("dev")
    depth = devices // PLANE
    blocks = [block] + [lax.ppermute(block, "dev", shifts(devices, k)) for k in range(1, depth)]
    each = depth // stacks
    return tuple(jnp.stack(blocks[k : k + each], 0) for k in range(0, depth, each))


def to_neighbours(*own):
    return tuple(send(stack, 2) for stack in own) + tuple(send(stack, 4) for stack in own)


def to_diagonal(*near):
    if len(near) == 4:
        return send(near[0], 4), send(near[3], 2)
    half = near[0].shape[0] // 2
    return send(near[0][:half], 4), send(near[1][half:], 2)


def to_partner(*pieces):
    return tuple(send(piece, 1) for piece in pieces)


def total_of(*terms):
    return sum(term.astype(jnp.float32) for term in terms)


def low_sum(*terms):
    return total_of(*terms).astype(jnp.bfloat16)


class Fold:
    def __init__(self, mine, got):
        self.mine, self.got = mine, got
        self.half = mine.shape[1] // 2

    def pair(self, spot, steps):
        return self.mine[spot, steps], self.got[spot, steps]

    def diagonal(self):
        first, last = slice(None, self.half), slice(self.half, None)
        return low_sum(*self.pair(3, first)), low_sum(*self.pair(3, last))

    def neighbours(self, got_a, got_b):
        first, last = slice(None, self.half), slice(self.half, None)
        to_x = (low_sum(*self.pair(1, first), got_a), low_sum(*self.pair(1, last)))
        to_y = (low_sum(*self.pair(2, first)), low_sum(*self.pair(2, last), got_b))
        return jnp.concatenate(to_x, 0), jnp.concatenate(to_y, 0)

    def column(self, got_x, got_y):
        total = total_of(*self.pair(0, slice(None)), got_x, got_y)
        return (total[0],) + tuple(
            total[k].astype(jnp.bfloat16) for k in range(1, total.shape[0])
        )


def over_diagonal(to_a, to_b):
    return send(to_a, 4), send(to_b, 2)


def over_plane(to_x, to_y):
    return send(to_x, 2), send(to_y, 4)


def over_column(sums):
    devices = lax.axis_size("dev")
    return tuple(lax.ppermute(sums[k], "dev", shifts(devices, k)) for k in range(1, len(sums)))


def exchange(rows):
    return lax.all_to_all(rows, "dev", split_axis=0, concat_axis=0, tiled=True)


FAR = pl.BlockSpec(memory_space=pltpu.HBM)
SCALARS = pl.BlockSpec(memory_space=pltpu.SMEM)


def whole(*shape):
    return pl.BlockSpec(shape, lambda *_: (0,) * len(shape))


LIMIT = 48


def settings(limit):
    return pltpu.CompilerParams(vmem_limit_bytes=limit * MIB)


def cost(flops, moved, exps=0):
    return pl.CostEstimate(flops=int(flops), bytes_accessed=int(moved), transcendentals=int(exps))


def shaped(shape, dtype):
    return jax.ShapeDtypeStruct(shape, dtype)


def by_rows(matrix, other):
    return lax.dot_general(
        matrix, other, (((1,), (1,)), ((), ())), preferred_element_type=jnp.float32
    )


def by_columns(matrix, other):
    return lax.dot_general(
        matrix, other, (((0,), (0,)), ((), ())), preferred_element_type=jnp.float32
    )


def normed(values):
    center = values - jnp.mean(values, -1, keepdims=True)
    scale = lax.rsqrt(jnp.mean(center * center, -1, keepdims=True) + epsilon)
    return center * scale, scale


def norm_back(grad, gain, unit, scale):
    inner = grad * gain
    return scale * (
        inner
        - jnp.mean(inner, -1, keepdims=True)
        - unit * jnp.mean(inner * unit, -1, keepdims=True)
    )


def iota(shape, axis):
    return lax.broadcasted_iota(jnp.int32, shape, axis)


def slots_of(ids_row, capacity, groups):
    count = ids_row.shape[1]
    square = (count, count)
    ids = jnp.sum(
        jnp.where(iota(square, 0) == iota(square, 1), ids_row, 0), axis=1, keepdims=True
    )
    group = jnp.right_shift(ids, DOCS_DEV.bit_length() - 1)
    lanes = max(128, groups)
    onehot = jnp.where(group == iota((count, lanes), 1), 1.0, 0.0)
    lower = jnp.where(iota(square, 0) > iota(square, 1), 1.0, 0.0).astype(jnp.bfloat16)
    earlier = product(lower, onehot.astype(jnp.bfloat16))
    within = jnp.sum(earlier * onehot, axis=1, keepdims=True).astype(jnp.int32)
    return ids, jnp.where(ids >= 0, group * capacity + within, -1)


def route(ids_row, tokens, cotangent, devices):
    count, feature = tokens.shape

    def kernel(ids_ref, tokens_ref, cotangent_ref, rows_ref, grads_ref, slot_ref):
        ids, slot = slots_of(ids_ref[...], count // devices, devices)
        slot_ref[...] = slot
        move = jnp.where(slot == iota((count, count), 1), 1.0, 0.0).astype(jnp.bfloat16)
        code = jnp.where(ids >= 0, jnp.bitwise_and(ids, DOCS_DEV - 1) + 1, 0)
        code = jnp.broadcast_to(code.astype(jnp.float32), (count, 128)).astype(jnp.bfloat16)
        rows_ref[:, :feature] = by_columns(move, tokens_ref[...]).astype(jnp.bfloat16)
        rows_ref[:, feature:] = by_columns(move, code).astype(jnp.bfloat16)
        grads_ref[...] = by_columns(move, cotangent_ref[...]).astype(jnp.bfloat16)

    return pl.pallas_call(
        kernel,
        out_shape=[
            shaped((count, feature + 128), jnp.bfloat16),
            shaped((count, feature), jnp.bfloat16),
            shaped((count, 1), jnp.int32),
        ],
        compiler_params=settings(LIMIT),
        cost_estimate=cost(4 * count * count * feature, 8 * count * feature),
    )(ids_row, tokens, cotangent)


def give_back(slot, rows):
    count, feature = rows.shape[0], rows.shape[1] // 256 * 256

    def kernel(slot_ref, rows_ref, out_ref):
        move = jnp.where(slot_ref[...] == iota((count, count), 1), 1.0, 0.0).astype(jnp.bfloat16)
        out_ref[...] = product(move, rows_ref[...]).astype(jnp.bfloat16)

    return pl.pallas_call(
        kernel,
        grid=(1,),
        out_shape=shaped((count, feature), jnp.bfloat16),
        in_specs=[whole(count, 1), whole(count, feature)],
        out_specs=whole(count, feature),
        compiler_params=settings(LIMIT),
        cost_estimate=cost(2 * count * count * feature, 4 * count * feature),
    )(slot, rows)


def pieces_of(where_ref, pieces):
    z, y, x, core = where_ref[0], where_ref[1], where_ref[2], where_ref[3]
    count = len(pieces) // 2
    depth = 2 * pieces[count - 1].shape[0]
    columns = ((y, x), (y, 1 - x), (1 - y, x), (1 - y, 1 - x))
    for part, group in ((core, pieces[:count]), (1 - core, pieces[count:])):
        reached = 0
        for piece in group:
            for index in range(piece.shape[0]):
                yy, xx = columns[reached // depth]
                step = reached % depth
                zz = lax.rem(z - step + depth, depth)
                yield piece.at[index], step, (zz * 2 + yy) * 2 + xx, part
                reached += 1


def wide_copies(where_ref, pieces, buffer, sems):
    copies = []
    for source, _, chip, part in pieces_of(where_ref, pieces):
        rows, columns = source.shape
        target = buffer.at[
            pl.ds(pl.multiple_of(chip * rows, 16), rows),
            pl.ds(pl.multiple_of(part * columns, 128), columns),
        ]
        copies.append(pltpu.make_async_copy(source, target, sems.at[len(copies)]))
    return copies


def down_copies(where_ref, pieces, buffer, sems):
    copies = []
    for source, _, chip, part in pieces_of(where_ref, pieces):
        rows = source.shape[0]
        row = pl.multiple_of((chip * 2 + part) * rows, 16)
        copies.append(
            pltpu.make_async_copy(source, buffer.at[pl.ds(row, rows)], sems.at[len(copies)])
        )
    return copies


def project(where, work, vector, pieces):
    count, feature = work.shape[0], vector.shape[1]
    copies_count = sum(piece.shape[0] for piece in pieces)
    tile = 256

    def kernel(where_ref, work_ref, vector_ref, *refs):
        (
            flipped_ref, out_ref, weights_ref, output_ref, low, buffer, sems, store_sems
        ) = refs[len(pieces):]
        copies = wide_copies(where_ref, refs[:len(pieces)], buffer, sems)
        for copy in copies:
            copy.start()

        def rows_of(index, carry):
            rows = pl.ds(pl.multiple_of(index * 64, 64), 64)
            unit, _ = normed(work_ref[rows, :].astype(jnp.float32))
            low[rows, :] = (unit * vector_ref[0:1, :] + vector_ref[1:2, :]).astype(jnp.bfloat16)
            return carry

        lax.fori_loop(0, count // 64, rows_of, 0)
        flipped_ref[...] = low[...].astype(jnp.float32).T.astype(jnp.bfloat16)
        for copy in copies:
            copy.wait()
        stores = [
            pltpu.make_async_copy(
                buffer.at[:, pl.ds(0, 3 * feature)], weights_ref, store_sems.at[0]
            ),
            pltpu.make_async_copy(
                buffer.at[:, pl.ds(3 * feature, feature)], output_ref, store_sems.at[1]
            ),
        ]
        for store in stores:
            store.start()
        for part, bias in ((0, 4), (1, None), (2, 5)):

            def columns_of(index, carry):
                inner = pl.ds(pl.multiple_of(index * tile, tile), tile)
                columns = pl.ds(pl.multiple_of(part * feature + index * tile, tile), tile)
                value = product(low[...], buffer[:, columns])
                if bias is not None:
                    value = value + vector_ref[bias : bias + 1, inner]
                out_ref[:, columns] = value.astype(jnp.bfloat16)
                return carry

            lax.fori_loop(0, feature // tile, columns_of, 0)
        for store in stores:
            store.wait()

    return pl.pallas_call(
        kernel,
        grid=(1,),
        out_shape=[
            shaped((feature, count), jnp.bfloat16),
            shaped((count, 3 * feature), jnp.bfloat16),
            shaped((feature, 3 * feature), jnp.bfloat16),
            shaped((feature, feature), jnp.bfloat16),
        ],
        in_specs=[SCALARS, whole(count, feature), whole(*vector.shape)] + [FAR] * len(pieces),
        out_specs=[whole(feature, count), whole(count, 3 * feature), FAR, FAR],
        scratch_shapes=[
            pltpu.VMEM((count, feature), jnp.bfloat16),
            pltpu.VMEM((feature, 4 * feature), jnp.bfloat16),
            pltpu.SemaphoreType.DMA((copies_count,)),
            pltpu.SemaphoreType.DMA((2,)),
        ],
        compiler_params=settings(60),
        cost_estimate=cost(6 * count * feature * feature, 12 * feature * feature),
    )(where, work, vector, *pieces)


def fill_cap(code_ref, cap):
    code = code_ref[...].astype(jnp.float32)
    cap[...] = jnp.where(code[:, :1] == code.T[:1], -masked_value, masked_value)


def one_head(values, head):
    lanes = iota(values.shape, 1)
    inside = (lanes >= head * HEAD) & (lanes < (head + 1) * HEAD)
    return jnp.where(inside, values, 0.0).astype(jnp.bfloat16)


def attend(projected, work, vector, weights, first, pairs, carried=None):
    count, feature = work.shape[0], vector.shape[1]
    all_pairs = feature // 128
    tile = 512
    ends = carried is not None

    def kernel(q_ref, k_ref, v_ref, weight_ref, code_ref, work_ref, vector_ref, *refs):
        if ends:
            carried_ref, attended_ref, stat_ref, resid_ref, low_ref, total, cap = refs
        else:
            attended_ref, stat_ref, total, cap = refs
        pair = pl.program_id(0)

        @pl.when(pair == 0)
        def _():
            fill_cap(code_ref, cap)
            total[...] = carried_ref[...] if ends else jnp.zeros_like(total)

        keys = k_ref[...]
        values = v_ref[...].astype(jnp.float32).T.astype(jnp.bfloat16)
        scaled = q_ref[...].astype(jnp.float32) * 0.125
        heads = []
        for head in range(2):
            query = one_head(scaled, head)
            parts = []
            for start in range(0, count, tile):
                span = slice(start, start + tile)
                scores = jnp.minimum(by_rows(keys, query[span]), cap[:, span])
                most = jnp.max(scores, 0, keepdims=True)
                powers = jnp.exp(scores - most)
                sums = jnp.sum(powers, 0, keepdims=True)
                stat_ref[0, head : head + 1, span] = most + jnp.log(sums)
                mixed = product(
                    values[head * HEAD : (head + 1) * HEAD], powers.astype(jnp.bfloat16)
                )
                parts.append(mixed * (1.0 / sums))
            heads.append(jnp.concatenate(parts, 1))
        both = jnp.concatenate(heads, 0)
        attended_ref[...] = both.astype(jnp.bfloat16)
        total[...] += product(both.T.astype(jnp.bfloat16), weight_ref[...])

        if ends:

            @pl.when(pair == pairs - 1)
            def _():
                def rows_of(index, carry):
                    rows = pl.ds(pl.multiple_of(index * 64, 64), 64)
                    resid = (
                        work_ref[rows, :].astype(jnp.float32) + total[rows, :] + vector_ref[6:7, :]
                    )
                    resid_ref[rows, :] = resid
                    unit, _ = normed(resid)
                    low_ref[rows, :] = (unit * vector_ref[2:3, :] + vector_ref[3:4, :]).astype(
                        jnp.bfloat16
                    )
                    return carry

                lax.fori_loop(0, count // 64, rows_of, 0)

    def columns_at(offset):
        return pl.BlockSpec((count, 128), lambda pair: (0, offset + pair))

    wide = whole(count, feature)
    return pl.pallas_call(
        kernel,
        grid=(pairs,),
        out_shape=[
            shaped((pairs * 128, count), jnp.bfloat16),
            shaped((pairs, 8, count), jnp.float32),
        ]
        + (
            [shaped((count, feature), jnp.float32), shaped((count, feature), jnp.bfloat16)]
            if ends
            else [shaped((count, feature), jnp.float32)]
        ),
        in_specs=[
            columns_at(first),
            columns_at(all_pairs + first),
            columns_at(2 * all_pairs + first),
            pl.BlockSpec((128, feature), lambda pair: (first + pair, 0)),
            pl.BlockSpec((count, 128), lambda pair: (0, all_pairs)),
            wide,
            whole(*vector.shape),
        ]
        + ([wide] if ends else []),
        out_specs=[
            pl.BlockSpec((128, count), lambda pair: (pair, 0)),
            pl.BlockSpec((1, 8, count), lambda pair: (pair, 0, 0)),
        ]
        + ([wide, wide] if ends else [wide]),
        scratch_shapes=([pltpu.VMEM((count, feature), jnp.float32)] if ends else [])
        + [pltpu.VMEM((count, count), jnp.float32)],
        compiler_params=settings(LIMIT),
        cost_estimate=cost(
            8 * count * count * pairs * 128, 14 * count * feature, 2 * pairs * count * count
        ),
    )(
        projected, projected, projected, weights, work, work, vector,
        *([carried] if ends else []),
    )


def widen(where, low, bias_row, pieces):
    count, feature = low.shape
    wide = bias_row.shape[1]
    tile = feature
    steps = wide // tile

    def kernel(where_ref, low_ref, bias_ref, *refs):
        hidden_ref, slope_ref, weights_ref, buffer, sems, store_sem = refs[len(pieces):]
        step = pl.program_id(0)
        store = pltpu.make_async_copy(buffer, weights_ref, store_sem)

        @pl.when(step == 0)
        def _():
            copies = wide_copies(where_ref, refs[:len(pieces)], buffer, sems)
            for copy in copies:
                copy.start()
            for copy in copies:
                copy.wait()
            store.start()

        columns = pl.ds(pl.multiple_of(step * tile, tile), tile)
        up = product(low_ref[...], buffer[:, columns]) + bias_ref[...]
        below = 0.5 * (1.0 + lax.erf(up * (0.5**0.5)))
        hidden_ref[...] = (up * below).astype(jnp.bfloat16)
        slope_ref[...] = below + up * (jnp.exp(-0.5 * up * up) * ((2.0 * math.pi) ** -0.5))

        @pl.when(step == steps - 1)
        def _():
            store.wait()

    block = pl.BlockSpec((count, tile), lambda step: (0, step))
    return pl.pallas_call(
        kernel,
        grid=(steps,),
        out_shape=[
            shaped((count, wide), jnp.bfloat16),
            shaped((count, wide), jnp.float32),
            shaped((feature, wide), jnp.bfloat16),
        ],
        in_specs=[
            SCALARS,
            whole(count, feature),
            pl.BlockSpec((1, tile), lambda step: (0, step)),
        ]
        + [FAR] * len(pieces),
        out_specs=[block, block, FAR],
        scratch_shapes=[
            pltpu.VMEM((feature, wide), jnp.bfloat16),
            pltpu.SemaphoreType.DMA((sum(piece.shape[0] for piece in pieces),)),
            pltpu.SemaphoreType.DMA,
        ],
        compiler_params=settings(60),
        cost_estimate=cost(
            2 * count * feature * wide, 2 * feature * wide + 6 * count * wide, count * wide
        ),
    )(where, low, bias_row, *pieces)


def down_gradient(where, hidden, grads, depth):
    count, wide = hidden.shape
    feature = grads.shape[1]
    rows = wide // (depth * PLANE)
    part = wide // depth

    def kernel(where_ref, hidden_ref, grads_ref, mine_ref, theirs_ref, result):
        y, x, core = where_ref[1], where_ref[2], where_ref[3]
        result[...] = by_columns(hidden_ref[...], grads_ref[...])
        for yy in range(2):
            for xx in range(2):
                spot = jnp.bitwise_xor(y, yy) * 2 + jnp.bitwise_xor(x, xx)
                first = (yy * 2 + xx) * 2
                for target, side in ((mine_ref, core), (theirs_ref, 1 - core)):
                    row = pl.multiple_of((first + side) * rows, 16)
                    target[spot, 0] = result[pl.ds(row, rows), :].astype(jnp.bfloat16)

    shape = shaped((4, depth, rows, feature), jnp.bfloat16)
    block = pl.BlockSpec((4, 1, rows, feature), lambda step, where_ref: (0, step, 0, 0))
    return pl.pallas_call(
        kernel,
        out_shape=[shape, shape],
        grid_spec=pltpu.PrefetchScalarGridSpec(
            num_scalar_prefetch=1,
            grid=(depth,),
            in_specs=[
                pl.BlockSpec(
                    (count, part),
                    lambda step, where_ref: (0, lax.rem(where_ref[0] + step, depth)),
                ),
                whole(count, feature),
            ],
            out_specs=[block, block],
            scratch_shapes=[pltpu.VMEM((part, feature), jnp.float32)],
        ),
        compiler_params=settings(LIMIT),
        cost_estimate=cost(2 * count * wide * feature, 2 * wide * (count + feature)),
    )(where, hidden, grads)


def put_wide(where_ref, result, mine_ref, theirs_ref):
    z, y, x, core = where_ref[0], where_ref[1], where_ref[2], where_ref[3]
    _, depth, rows, _ = mine_ref.shape
    for chip in range(4 * depth):
        zz, yy, xx = chip // 4, (chip // 2) % 2, chip % 2
        step = lax.rem(zz - z + depth, depth)
        spot = jnp.bitwise_xor(y, yy) * 2 + jnp.bitwise_xor(x, xx)
        for target, side in ((mine_ref, core), (theirs_ref, 1 - core)):
            row = pl.multiple_of((chip * 2 + side) * rows, 8)
            target[spot, step] = result[pl.ds(row, rows), :].astype(jnp.bfloat16)


def narrow(where, hidden, resid, vector, pieces):
    count, wide = hidden.shape
    feature = resid.shape[1]
    tile = 256

    def kernel(where_ref, hidden_ref, resid_ref, vector_ref, *refs):
        out_ref, weights_ref, buffer, sems, store_sem = refs[len(pieces):]
        copies = down_copies(where_ref, refs[:len(pieces)], buffer, sems)
        for copy in copies:
            copy.start()
        for copy in copies:
            copy.wait()
        store = pltpu.make_async_copy(buffer, weights_ref, store_sem)
        store.start()

        def columns_of(index, carry):
            columns = pl.ds(pl.multiple_of(index * tile, tile), tile)
            value = product(hidden_ref[...], buffer[:, columns])
            out_ref[:, columns] = (
                resid_ref[:, columns] + (value + vector_ref[7:8, columns])
            ).astype(jnp.bfloat16)
            return carry

        lax.fori_loop(0, feature // tile, columns_of, 0)
        store.wait()

    return pl.pallas_call(
        kernel,
        grid=(1,),
        out_shape=[
            shaped((count, feature), jnp.bfloat16),
            shaped((wide, feature), jnp.bfloat16),
        ],
        in_specs=[SCALARS, whole(count, wide), whole(count, feature), whole(*vector.shape)]
        + [FAR] * len(pieces),
        out_specs=[whole(count, feature), FAR],
        scratch_shapes=[
            pltpu.VMEM((wide, feature), jnp.bfloat16),
            pltpu.SemaphoreType.DMA((sum(piece.shape[0] for piece in pieces),)),
            pltpu.SemaphoreType.DMA,
        ],
        compiler_params=settings(LIMIT),
        cost_estimate=cost(2 * count * wide * feature, 6 * wide * feature),
    )(where, hidden, resid, vector, *pieces)


def feed_back(where, slope, low, grads, resid, vector, up_weights, down_weights, attended, depth):
    count, wide = slope.shape
    feature = resid.shape[1]
    tile = feature
    steps = wide // tile
    half = feature // 2
    chip_rows = feature // (PLANE * depth)

    def kernel(
        where_ref, slope_ref, low_ref, grads_ref, resid_ref, vector_ref, up_ref, down_ref, left_ref, right_ref,
        dresid_ref, dlow_ref, sums_ref, bias_ref, mine_ref, theirs_ref, back, flipped, result,
    ):
        step = pl.program_id(0)

        @pl.when(step == 0)
        def _():
            flipped[...] = low_ref[...].astype(jnp.float32).T.astype(jnp.bfloat16)
            back[...] = jnp.zeros_like(back)

        @pl.when(step < steps)
        def _():
            dup = (slope_ref[...] * by_rows(grads_ref[...], down_ref[...])).astype(jnp.bfloat16)
            bias_ref[...] = jnp.sum(dup.astype(jnp.float32), 0, keepdims=True)
            back[...] += by_rows(dup, up_ref[...])
            result[...] = product(flipped[...], dup)

        @pl.when(step == steps)
        def _():
            sums_ref[...] = jnp.zeros_like(sums_ref)

            def rows_of(index, carry):
                rows = pl.ds(pl.multiple_of(index * 64, 64), 64)
                unit, scale = normed(resid_ref[rows, :])
                da = back[rows, :]
                dy = grads_ref[rows, :].astype(jnp.float32)
                dresid = dy + norm_back(da, vector_ref[2:3, :], unit, scale)
                dresid_ref[rows, :] = dresid
                dlow = dresid.astype(jnp.bfloat16)
                dlow_ref[rows, :] = dlow
                for row, value in enumerate((da * unit, da, dlow.astype(jnp.float32), dy)):
                    sums_ref[row : row + 1, :] += jnp.sum(value, 0, keepdims=True)
                return carry

            lax.fori_loop(0, count // 64, rows_of, 0)
            result[:half, :] = product(left_ref[...], dlow_ref[...])
            result[half:, :] = product(right_ref[...], dlow_ref[...])

        put_wide(where_ref, result, mine_ref, theirs_ref)

    def at(step):
        return jnp.minimum(step, steps - 1)

    def columns_at(rows):
        return pl.BlockSpec((rows, tile), lambda step: (0, at(step)))

    all_rows = whole(count, feature)
    split = shaped((4, depth, chip_rows, (steps + 1) * feature), jnp.bfloat16)
    block = pl.BlockSpec((4, depth, chip_rows, feature), lambda step: (0, 0, 0, step))
    return pl.pallas_call(
        kernel,
        grid=(steps + 1,),
        out_shape=[
            shaped((count, feature), jnp.float32),
            shaped((count, feature), jnp.bfloat16),
            shaped((8, feature), jnp.float32),
            shaped((1, wide), jnp.float32),
            split,
            split,
        ],
        in_specs=[
            SCALARS,
            columns_at(count),
            all_rows,
            all_rows,
            all_rows,
            whole(*vector.shape),
            columns_at(feature),
            pl.BlockSpec((tile, feature), lambda step: (at(step), 0)),
            whole(half, count),
            whole(half, count),
        ],
        out_specs=[all_rows, all_rows, whole(8, feature), columns_at(1), block, block],
        scratch_shapes=[
            pltpu.VMEM((count, feature), jnp.float32),
            pltpu.VMEM((feature, count), jnp.bfloat16),
            pltpu.VMEM((feature, feature), jnp.float32),
        ],
        compiler_params=settings(60),
        cost_estimate=cost(6 * count * wide * feature, 8 * wide * feature + 10 * count * wide),
    )(where, slope, low, grads, resid, vector, up_weights, down_weights, *attended)


def attend_back(projected, work, stats, dlow, weights, first, pairs, gradient=None):
    count, feature = dlow.shape
    all_pairs = feature // 128
    tile = 512
    wide = pairs * 128

    def kernel(q_ref, k_ref, v_ref, code_ref, stat_ref, dlow_ref, weight_ref, *refs):
        if gradient is None:
            out_ref, sums_ref, douts, cap = refs
        else:
            (
                where_ref, flipped_ref, left_ref, out_ref, sums_ref, mine_ref, theirs_ref,
                douts, cap, right, result,
            ) = refs
        pair = pl.program_id(0)

        @pl.when(pair == 0)
        def _():
            fill_cap(code_ref, cap)
            for start in range(0, wide, 128):
                span = slice(start, start + 128)
                douts[start // 128] = by_rows(dlow_ref[...], weight_ref[span, :]).astype(
                    jnp.bfloat16
                )

        @pl.when(pair < pairs)
        def _():
            keys, values = k_ref[...], v_ref[...]
            wide_keys = keys.astype(jnp.float32)
            dquery = jnp.zeros((count, 128), jnp.float32)
            scaled = q_ref[...].astype(jnp.float32) * 0.125
            dout = douts[pair].astype(jnp.float32)
            dkey = jnp.zeros((count, 128), jnp.float32)
            dvalue = jnp.zeros((count, 128), jnp.float32)
            for head in range(2):
                query = one_head(scaled, head)
                dhead = one_head(dout, head)
                for start in range(0, count, tile):
                    span = slice(start, start + tile)
                    scores = jnp.minimum(by_rows(keys, query[span]), cap[:, span])
                    probs = jnp.exp(scores - stat_ref[0, head : head + 1, span])
                    dprob = by_rows(values, dhead[span])
                    inner = jnp.sum(probs * dprob, 0, keepdims=True)
                    dscore = (probs * (dprob - inner)).astype(jnp.bfloat16)
                    dvalue = dvalue + product(probs.astype(jnp.bfloat16), dhead[span])
                    dkey = dkey + product(dscore, query[span])
                    dquery = dquery + by_columns(dscore, one_head(wide_keys, head))
            dquery = (dquery * 0.125).astype(jnp.bfloat16)
            dvalue = dvalue.astype(jnp.bfloat16)
            out_ref[0] = dquery
            out_ref[1] = dkey.astype(jnp.bfloat16)
            out_ref[2] = dvalue
            sums_ref[0:1, :] = jnp.sum(dquery.astype(jnp.float32), 0, keepdims=True)
            sums_ref[1:2, :] = jnp.sum(dvalue.astype(jnp.float32), 0, keepdims=True)
            if gradient is not None:
                right[0, pair] = dquery
                right[1, pair] = dkey.astype(jnp.bfloat16)
                right[2, pair] = dvalue

        if gradient is not None:

            @pl.when(pair >= pairs)
            def _():
                flipped = flipped_ref[...]
                result[:, :wide] = product(flipped, left_ref[0])
                for index in range(pairs):
                    span = slice(wide + index * 128, wide + (index + 1) * 128)
                    result[:, span] = product(flipped, right[pair - pairs, index])
                put_wide(where_ref, result, mine_ref, theirs_ref)

    def at(pair):
        return jnp.minimum(pair, pairs - 1)

    def part_at(pair):
        return jnp.maximum(pair - pairs, 0)

    def columns_at(offset):
        return pl.BlockSpec((count, 128), lambda pair: (0, offset + at(pair)))

    out_shape = [shaped((3, count, wide), jnp.bfloat16), shaped((8, wide), jnp.float32)]
    in_specs = [
        columns_at(first),
        columns_at(all_pairs + first),
        columns_at(2 * all_pairs + first),
        pl.BlockSpec((count, 128), lambda pair: (0, all_pairs)),
        pl.BlockSpec((1, 8, count), lambda pair: (at(pair), 0, 0)),
        whole(count, feature),
        pl.BlockSpec((wide, feature), lambda pair: (first // pairs, 0)),
    ]
    out_specs = [
        pl.BlockSpec((3, count, 128), lambda pair: (0, 0, at(pair))),
        pl.BlockSpec((8, 128), lambda pair: (0, at(pair))),
    ]
    scratch = [
        pltpu.VMEM((pairs, count, 128), jnp.bfloat16),
        pltpu.VMEM((count, count), jnp.float32),
    ]
    extra = ()
    if gradient is not None:
        where, flipped, left, depth = gradient
        rows = feature // (PLANE * depth)
        extra = (where, flipped, left)
        out_shape += [shaped((4, depth, rows, 3 * feature), jnp.bfloat16)] * 2
        in_specs += [
            SCALARS,
            whole(feature, count),
            pl.BlockSpec((1, count, wide), lambda pair: (part_at(pair), 0, 0)),
        ]
        out_specs += [
            pl.BlockSpec((4, depth, rows, feature), lambda pair: (0, 0, 0, part_at(pair)))
        ] * 2
        scratch += [
            pltpu.VMEM((3, pairs, count, 128), jnp.bfloat16),
            pltpu.VMEM((feature, feature), jnp.float32),
        ]
    return pl.pallas_call(
        kernel,
        grid=(pairs if gradient is None else pairs + 3,),
        out_shape=out_shape,
        in_specs=in_specs,
        out_specs=out_specs,
        scratch_shapes=scratch,
        compiler_params=settings(LIMIT),
        cost_estimate=cost(
            14 * count * count * wide, 16 * count * feature, 2 * pairs * count * count
        ),
    )(projected, projected, projected, work, stats, dlow, weights, *extra)


def project_back(work, dprojected, dresid, vector, weights, sums_two, sums_attend, bias_up, devices):
    count, feature = dresid.shape
    tile = 128
    half = feature // 2
    lanes = 16 * feature // devices // 128
    capacity = count // devices

    def kernel(
        work_ref, d_ref, e_ref, dresid_ref, vector_ref, weight_ref, two_ref, left_ref, right_ref, bias_ref,
        out_ref, sums,
    ):
        sums[...] = jnp.zeros_like(sums)

        def rows_of(index, carry):
            rows = pl.ds(pl.multiple_of(index * tile, tile), tile)
            da = jnp.zeros((tile, feature), jnp.float32)
            for part in range(3):
                middle = part * feature + half
                da += by_rows(d_ref[part, rows, :], weight_ref[:, middle - half : middle])
                da += by_rows(e_ref[part, rows, :], weight_ref[:, middle : middle + half])
            unit, scale = normed(work_ref[rows, :].astype(jnp.float32))
            out_ref[rows, :feature] = (
                dresid_ref[rows, :] + norm_back(da, vector_ref[0:1, :], unit, scale)
            ).astype(jnp.bfloat16)
            sums[0:1, :] += jnp.sum(da * unit, 0, keepdims=True)
            sums[1:2, :] += jnp.sum(da, 0, keepdims=True)
            return carry

        lax.fori_loop(0, count // tile, rows_of, 0)
        sums[2:4, :] = two_ref[0:2, :]
        sums[4:6, :half] = left_ref[0:2, :]
        sums[4:6, half:] = right_ref[0:2, :]
        sums[6:8, :] = two_ref[2:4, :]
        for row in range(FF // feature):
            sums[8 + row : 9 + row, :] = bias_ref[0:1, row * feature : (row + 1) * feature]
        place_in = iota((capacity, 128), 0)
        for device in range(devices):
            block = jnp.zeros((capacity, 128), jnp.float32)
            for lane in range(lanes):
                first = device * lanes + lane
                row, column = divmod(first * 128, feature)
                value = sums[row : row + 1, column : column + 128]
                high = value.astype(jnp.bfloat16).astype(jnp.float32)
                block = jnp.where(place_in == lane, high, block)
                block = jnp.where(place_in == lanes + lane, value - high, block)
            out_ref[device * capacity : (device + 1) * capacity, feature:] = block.astype(
                jnp.bfloat16
            )

    return pl.pallas_call(
        kernel,
        grid=(1,),
        out_shape=shaped((count, feature + 128), jnp.bfloat16),
        in_specs=[
            whole(count, feature),
            whole(3, count, half),
            whole(3, count, half),
            whole(count, feature),
            whole(*vector.shape),
            whole(feature, 3 * feature),
            whole(8, feature),
            whole(8, half),
            whole(8, half),
            whole(1, FF),
        ],
        out_specs=whole(count, feature + 128),
        scratch_shapes=[pltpu.VMEM((16, feature), jnp.float32)],
        compiler_params=settings(LIMIT),
        cost_estimate=cost(6 * count * feature * feature, 6 * feature * feature),
    )(work, *dprojected, dresid, vector, weights, sums_two, *sums_attend, bias_up)


def settle(own, got, back, squares, devices, feature):
    rows, columns = own.shape
    lanes = 16 * feature // devices // 128
    capacity = back.shape[1]

    def kernel(squares_ref, own_ref, *refs):
        got_refs, (back_ref, grad_ref, packet_ref) = refs[: len(got)], refs[len(got) :]
        grad = own_ref[...]
        for ref in got_refs:
            grad += ref[...].astype(jnp.float32)
        grad_ref[...] = grad
        total = squares_ref[0, 0] + jnp.sum(grad * grad)
        sums = jnp.sum(back_ref[...].astype(jnp.float32), 0)
        packet_ref[:, :lanes, :] = jnp.broadcast_to(
            (sums[:lanes] + sums[lanes : 2 * lanes])[None], (devices, lanes, 128)
        )
        packet_ref[:, lanes:, :] = jnp.full((devices, 1, 128), total, jnp.float32)

    return pl.pallas_call(
        kernel,
        grid=(1,),
        out_shape=[
            shaped((rows, columns), jnp.float32),
            shaped((devices, lanes + 1, 128), jnp.float32),
        ],
        in_specs=[SCALARS, whole(rows, columns)]
        + [whole(rows, columns)] * len(got)
        + [pl.BlockSpec((devices, capacity, 128), lambda step: (0, 0, feature // 128))],
        out_specs=[whole(rows, columns), whole(devices, lanes + 1, 128)],
        compiler_params=settings(60),
        cost_estimate=cost(8 * rows * columns, 16 * rows * columns),
    )(squares.reshape(1, 1), own, *got, back)


def finish(packets, first_grad, up_grad, down_grad, wide, down, vector):
    devices, lanes, _ = packets.shape
    lanes -= 1
    rows, columns = wide[0].shape
    down_rows, feature = down[0].shape
    vector_rows = vector[0].shape[0]
    steps = 4
    tile, down_tile = columns // steps, down_rows // steps
    first_columns = first_grad.shape[1]

    def kernel(packets_ref, first_ref, up_ref, down_grad_ref, *refs):
        wide_refs, down_refs, vector_refs = refs[:3], refs[3:6], refs[6:9]
        norm_ref, wide_new, down_new, vector_new = refs[9], refs[10:13], refs[13:16], refs[16:19]
        sums, factor_ref = refs[19:]
        step = pl.program_id(0)

        def put(new, old, gradient, decay):
            for ref, value in zip(
                new, advance(*(ref[...] for ref in old), gradient, factor_ref[0], decay), strict=True
            ):
                ref[...] = value

        @pl.when(step == 0)
        def _():
            for place_of in range(vector_rows * feature // 128):
                device, lane = divmod(place_of, lanes)
                row, column = divmod(place_of * 128, feature)
                sums[row : row + 1, column : column + 128] = packets_ref[device, lane : lane + 1]
            gradient = sums[...]
            shares = packets_ref[:, lanes, :1]
            total = jnp.sum(shares) + jnp.sum(gradient * gradient)
            norm = jnp.sqrt(jnp.full((1, 1), total))
            norm_ref[...] = norm
            factor_ref[0] = jnp.sum(clip_norm / jnp.maximum(norm, clip_norm))
            put(vector_new, vector_refs, gradient, 0.0)

        for index in range(steps):

            @pl.when(step == index)
            def _():
                first = index * tile
                parts = []
                if first < first_columns:
                    parts.append(first_ref[:, first : min(first + tile, first_columns)])
                if first + tile > first_columns:
                    low = max(first - first_columns, 0)
                    high = first + tile - first_columns
                    if low < feature:
                        parts.append(up_ref[:, FF + low : FF + min(high, feature)])
                    if high > feature:
                        parts.append(up_ref[:, max(low - feature, 0) : high - feature])
                gradient = parts[0] if len(parts) == 1 else jnp.concatenate(parts, 1)
                put(wide_new, wide_refs, gradient, decay_rate)

        put(down_new, down_refs, down_grad_ref[...], decay_rate)

    def tiles(shape):
        return pl.BlockSpec(shape, lambda step: (0, step))

    wide_specs = [tiles((rows, tile))] * 3
    down_specs = [pl.BlockSpec((down_tile, feature), lambda step: (step, 0))] * 3
    vector_specs = [whole(vector_rows, feature)] * 3
    return pl.pallas_call(
        kernel,
        grid=(steps,),
        out_shape=[shaped((1, 1), jnp.float32)]
        + [shaped(part.shape, jnp.float32) for part in (*wide, *down, *vector)],
        in_specs=[
            whole(*packets.shape),
            whole(*first_grad.shape),
            whole(*up_grad.shape),
            down_specs[0],
        ]
        + wide_specs
        + down_specs
        + vector_specs,
        out_specs=[whole(1, 1)] + wide_specs + down_specs + vector_specs,
        scratch_shapes=[
            pltpu.VMEM((vector_rows, feature), jnp.float32),
            pltpu.SMEM((1,), jnp.float32),
        ],
        compiler_params=settings(60),
        cost_estimate=cost(20 * rows * columns, 40 * rows * columns),
    )(packets, first_grad, up_grad, down_grad, *wide, *down, *vector)


def structured(devices, feature):
    rows = feature // devices
    return devices % PLANE == 0 and feature % devices == 0 and (2 * rows) % 16 == 0


def body(
    tokens,
    cotangent,
    segment_ids,
    wide_weight,
    wide_moment,
    wide_average,
    down_weight,
    down_moment,
    down_average,
    vector_weight,
    vector_moment,
    vector_average,
):
    devices = lax.axis_size("dev")
    count, feature = tokens.shape
    if not structured(devices, feature):
        return plain_body(
            tokens,
            cotangent,
            segment_ids,
            wide_weight,
            wide_moment,
            wide_average,
            down_weight,
            down_moment,
            down_average,
            vector_weight,
            vector_moment,
            vector_average,
        )
    depth = devices // PLANE
    capacity = count // devices
    where = place()
    core = where[3]

    wide_low, down_low = wide_weight.astype(jnp.bfloat16), down_weight.astype(jnp.bfloat16)
    rows, columns = wide_low.shape
    parts = wide_low.reshape(rows, 2, 2, columns // 4)
    keep, give = core_order(core, parts[:, :, 0], parts[:, :, 1])
    got = lax.ppermute(give, "dev", flips(devices, 1))
    pair = jnp.concatenate(core_order(core, keep, got), 0)

    send_rows, send_grads, slot = route(segment_ids.reshape(1, count), tokens, cotangent, devices)
    first_own = along_z(pair[:, 0], 2)
    send_rows, first_own = pin(send_rows, first_own)

    work = exchange(send_rows.reshape(devices, capacity, -1)).reshape(count, -1)
    first_near = pin(*to_neighbours(*first_own))

    first_far = to_diagonal(*first_near)
    first_got = to_partner(*first_own, *first_near)
    first_far, first_got = pin(first_far, first_got)
    first_got = first_got + to_partner(*first_far)
    first_got, work, up_block = pin(first_got, work, pair[:, 1])

    up_own = along_z(up_block, 1)
    flipped_one, projected, first_weights, out_weights = project(
        where, work, vector_weight, (*first_own, *first_near, *first_far, *first_got)
    )
    projected, up_own, down_block, send_grads = pin(projected, up_own, down_low, send_grads)

    up_near = to_neighbours(*up_own)
    down_own = along_z(down_block, 2)
    pairs = feature // 256
    attended_a, stats_a, carried = attend(projected, work, vector_weight, out_weights, 0, pairs)
    carried, up_near, down_own, send_grads = pin(carried, up_near, down_own, send_grads)

    up_far = to_diagonal(*up_near)
    up_got = to_partner(*up_own, *up_near)
    grads = exchange(send_grads.reshape(devices, capacity, feature)).reshape(count, feature)
    attended_b, stats_b, resid, low_two = attend(
        projected, work, vector_weight, out_weights, pairs, pairs, carried
    )
    low_two, up_far, up_got = pin(low_two, up_far, up_got)
    up_got = up_got + to_partner(*up_far)
    low_two, up_got, down_own = pin(low_two, up_got, down_own)

    down_near = to_neighbours(*down_own)
    hidden, slope, up_weights = widen(
        where, low_two, vector_weight[8:].reshape(1, FF), (*up_own, *up_near, *up_far, *up_got)
    )
    hidden, down_near = pin(hidden, down_near)

    down_far = to_diagonal(*down_near)
    down_got = to_partner(*down_own, *down_near)
    down_mine, down_theirs = down_gradient(where, hidden, grads, depth)
    down_far, down_got, down_mine, down_theirs = pin(down_far, down_got, down_mine, down_theirs)

    got = send(down_theirs, 1)
    down_got = down_got + to_partner(*down_far)
    down_got, got = pin(down_got, got)
    down_fold = Fold(down_mine, got)
    down_to, down_got = pin(down_fold.diagonal(), down_got)

    got = over_diagonal(*down_to)
    output, down_weights = narrow(
        where, hidden, resid, vector_weight, (*down_own, *down_near, *down_far, *down_got)
    )
    output, down_weights, got = pin(output, down_weights, got)
    down_to, output = pin(down_fold.neighbours(*got), output)

    back_out = exchange(output.reshape(devices, capacity, feature)).reshape(count, feature)
    got = over_plane(*down_to)
    dresid, dlow, sums_two, bias_up_grad, up_mine, up_theirs = feed_back(
        where, slope, low_two, grads, resid, vector_weight, up_weights, down_weights,
        (attended_a, attended_b), depth,
    )
    dlow, got, up_mine, up_theirs, back_out = pin(dlow, got, up_mine, up_theirs, back_out)
    down_sums, dlow, up_theirs = pin(down_fold.column(*got), dlow, up_theirs)

    down_got = over_column(down_sums)
    up_got = send(up_theirs, 1)
    dleft, sums_left = attend_back(projected, work, stats_a, dlow, out_weights, 0, pairs)
    up_got, dleft, dlow = pin(up_got, dleft, dlow)
    up_fold = Fold(up_mine, up_got)
    up_to, dlow = pin(up_fold.diagonal(), dlow)

    up_got = over_diagonal(*up_to)
    dright, sums_right, first_mine, first_theirs = attend_back(
        projected, work, stats_b, dlow, out_weights, pairs, pairs,
        (where, flipped_one, dleft, depth),
    )
    up_got, dright, first_mine, first_theirs, down_got = pin(
        up_got, dright, first_mine, first_theirs, down_got
    )
    up_to, dright, first_theirs = pin(up_fold.neighbours(*up_got), dright, first_theirs)

    first_got = send(first_theirs, 1)
    first_got, dright, up_to = pin(first_got, dright, up_to)
    first_fold = Fold(first_mine, first_got)
    first_to, dright, up_to = pin(first_fold.diagonal(), dright, up_to)

    got = over_diagonal(*first_to)
    up_got = over_plane(*up_to)
    both = project_back(
        work, (dleft, dright), dresid, vector_weight, first_weights,
        sums_two, (sums_left, sums_right), bias_up_grad, devices,
    )
    both, got = pin(both, got)
    first_to = pin(*first_fold.neighbours(*got))

    back = exchange(both.reshape(devices, capacity, -1))
    got = over_plane(*first_to)
    up_sums = pin(*up_fold.column(*up_got))
    up_got = over_column(up_sums)
    got, up_first, back = pin(got, up_got[0], back)
    down_grad = total_of(down_sums[0], *down_got)
    first_sums, back_out = pin(first_fold.column(*got), back_out)

    first_got = over_column(first_sums)
    up_grad = total_of(up_sums[0], up_first, *up_got[1:])
    squares = jnp.sum(up_grad * up_grad) + jnp.sum(down_grad * down_grad)
    block_output = give_back(slot, back_out)
    first_got, up_grad, block_output, down_grad, squares = pin(
        first_got, up_grad, block_output, down_grad, squares
    )
    first_grad, packet = settle(first_sums[0], first_got, back, squares, devices, feature)
    packets = exchange(packet)
    input_grad = give_back(slot, back.reshape(count, -1))
    grad_norm, *new = finish(
        packets, first_grad, up_grad, down_grad,
        (wide_weight, wide_moment, wide_average),
        (down_weight, down_moment, down_average),
        (vector_weight, vector_moment, vector_average),
    )
    return (block_output, input_grad, grad_norm.reshape(()), *new)


def solution(mesh):
    placed = (
        P("dev", None),
        P("dev", None),
        P("dev"),
        P("dev", None),
        P("dev", None),
        P("dev", None),
        P("dev", None),
        P("dev", None),
        P("dev", None),
        P(),
        P(),
        P(),
    )
    return jax.shard_map(
        body,
        mesh=mesh,
        in_specs=placed,
        out_specs=(
            P("dev", None),
            P("dev", None),
            P(),
            P("dev", None),
            P("dev", None),
            P("dev", None),
            P("dev", None),
            P("dev", None),
            P("dev", None),
            P(),
            P(),
            P(),
        ),
        check_vma=False,
    )
```

```python
import math

import jax
import jax.numpy as jnp
from jax import lax
from jax.experimental import pallas as pl
from jax.experimental.pallas import tpu as pltpu
from jax.sharding import PartitionSpec as P

HEADS = 12
HEAD = 64
FF = 3072
DOCS_DEV = 4
PLANE = 8
MIB = 1 << 20


epsilon = 1e-05
masked_value = -1e30
momentum = 0.9
learn_rate = 0.01
decay_rate = 0.0001
average_rate = 0.8
clip_norm = 2048.0


def norm_rows(values, gain_row, shift_row):
    center = values - jnp.mean(values, -1, keepdims=True)
    spread = jnp.mean(center * center, -1, keepdims=True)
    return center * lax.rsqrt(spread + epsilon) * gain_row + shift_row


def gelu_exact(values):
    return jax.nn.gelu(values, approximate=False)


def product(matrix, other):
    return jnp.dot(matrix, other, preferred_element_type=jnp.float32)


def against(matrix, other):
    return lax.dot_general(
        matrix, other, (((1,), (1,)), ((), ())), preferred_element_type=jnp.float32
    )


def inner_rows(matrix, other):
    return lax.dot_general(
        matrix, other, (((0,), (0,)), ((), ())), preferred_element_type=jnp.float32
    )


def advance(weight, moment, average, gradient, factor, decay_term):
    update = factor * gradient + decay_term * weight
    new_moment = momentum * moment + update
    new_weight = weight - learn_rate * (update + momentum * new_moment)
    new_average = average_rate * average + (1.0 - average_rate) * new_weight
    return (new_weight, new_moment, new_average)


def routing(segment_ids, devices, capacity):
    row_count = segment_ids.shape[0]
    is_live = segment_ids >= 0
    target = jnp.where(is_live, segment_ids // DOCS_DEV, devices)
    onehot = (target[:, None] == jnp.arange(devices, dtype=jnp.int32)[None, :]).astype(jnp.int32)
    earlier = jnp.cumsum(onehot, axis=0) - onehot
    within = jnp.sum(earlier * onehot, axis=1)
    slot_of = jnp.where(is_live, target * capacity + within, row_count)
    anchor = (
        jnp.full((row_count,), row_count, jnp.int32)
        .at[slot_of]
        .set(jnp.arange(row_count, dtype=jnp.int32), mode="drop")
    )
    return (is_live, jnp.minimum(slot_of, row_count - 1), anchor)


def plain_body(
    tokens,
    cotangent,
    segment_ids,
    wide_weight,
    wide_moment,
    wide_average,
    down_weight,
    down_moment,
    down_average,
    vector_weight,
    vector_moment,
    vector_average,
):
    wide_full, down_full = (
        lax.all_gather(wide_weight.astype(jnp.bfloat16), "dev", axis=0, tiled=True),
        lax.all_gather(down_weight.astype(jnp.bfloat16), "dev", axis=0, tiled=True),
    )
    devices = lax.axis_size("dev")
    row_count, feature = tokens.shape
    capacity = row_count // devices
    is_live, slot_of, anchor = routing(segment_ids, devices, capacity)
    blank_row = jnp.zeros((1, feature), jnp.bfloat16)
    send_rows = jnp.concatenate([tokens, blank_row], 0)[anchor].reshape(devices, capacity, feature)
    send_grads = jnp.concatenate([cotangent, blank_row], 0)[anchor].reshape(
        devices, capacity, feature
    )
    send_ids = jnp.concatenate([segment_ids, jnp.full((1,), -1, jnp.int32)], 0)[anchor].reshape(
        devices, capacity
    )
    work_rows, work_grads, work_ids = (
        lax.all_to_all(send_rows, "dev", split_axis=0, concat_axis=0, tiled=True),
        lax.all_to_all(send_grads, "dev", split_axis=0, concat_axis=0, tiled=True),
        lax.all_to_all(send_ids, "dev", split_axis=0, concat_axis=0, tiled=True),
    )
    work_rows = work_rows.reshape(row_count, feature)
    work_grads = work_grads.reshape(row_count, feature)
    work_ids = work_ids.reshape(row_count)
    gain_one, shift_one, gain_two, shift_two, bias_query, bias_value, bias_out, bias_down = [
        vector_weight[row_index] for row_index in range(8)
    ]
    bias_up = vector_weight[8:].reshape(FF)
    w_qkv = wide_full[:, : 3 * feature]
    w_out = wide_full[:, 3 * feature : 4 * feature]
    w_up = wide_full[:, 4 * feature :]
    work_float = work_rows.astype(jnp.float32)
    low_one = norm_rows(work_float, gain_one, shift_one).astype(jnp.bfloat16)
    bias_all = jnp.concatenate([bias_query, jnp.zeros_like(bias_query), bias_value])
    projected = (product(low_one, w_qkv) + bias_all).astype(jnp.bfloat16)
    queries = projected[:, :feature].reshape(row_count, HEADS, HEAD)
    key_rows = projected[:, feature : 2 * feature].reshape(row_count, HEADS, HEAD)
    value_rows = projected[:, 2 * feature :].reshape(row_count, HEADS, HEAD)
    same_seg = work_ids[:, None] == work_ids[None, :]
    block_rows = min(512, row_count)
    group_size = math.gcd(HEADS, 4)
    group_count = HEADS // group_size

    def scores_of(offset, first_head):
        query_part = queries[offset : offset + block_rows, first_head : first_head + group_size]
        raw_scores = (
            jnp.einsum(
                "qhd,khd->hqk",
                query_part,
                key_rows[:, first_head : first_head + group_size],
                preferred_element_type=jnp.float32,
            )
            * 0.125
        )
        return jnp.where(same_seg[None], raw_scores, masked_value)

    stored = []
    offset = 0
    head_outs = []
    for group in range(group_count):
        first_head = group * group_size
        scores = scores_of(offset, first_head)
        row_max = jnp.max(scores, -1, keepdims=True)
        powers = jnp.exp(scores - row_max)
        row_sums = jnp.sum(powers, -1, keepdims=True)
        prob_low = (powers / row_sums).astype(jnp.bfloat16)
        head_outs.append(
            jnp.einsum(
                "hqk,khd->qhd",
                prob_low,
                value_rows[:, first_head : first_head + group_size],
                preferred_element_type=jnp.float32,
            )
        )
        stored.append((row_max, row_sums))
    out_blocks = jnp.concatenate(head_outs, 1)
    attended = out_blocks.reshape(row_count, feature).astype(jnp.bfloat16)
    resid = work_float + product(attended, w_out) + bias_out
    low_two = norm_rows(resid, gain_two, shift_two).astype(jnp.bfloat16)
    up_float = product(low_two, w_up) + bias_up
    hidden = gelu_exact(up_float).astype(jnp.bfloat16)
    output_low = (resid + product(hidden, down_full) + bias_down).astype(jnp.bfloat16)
    dy_float = work_grads.astype(jnp.float32)
    dhidden = against(work_grads, down_full)
    gelu_pull = jax.vjp(gelu_exact, up_float)[1]
    dup_low = gelu_pull(dhidden)[0].astype(jnp.bfloat16)
    da_two = against(dup_low, w_up)
    norm_two_pull = jax.vjp(norm_rows, resid, gain_two, shift_two)[1]
    dres_norm, dgain_two, dshift_two = norm_two_pull(da_two)
    dresid = dy_float + dres_norm
    dres_low = dresid.astype(jnp.bfloat16)
    dattended = against(dres_low, w_out).astype(jnp.bfloat16).reshape(row_count, HEADS, HEAD)
    dkey_parts = [
        jnp.zeros((row_count, group_size, HEAD), jnp.float32) for group in range(group_count)
    ]
    dvalue_parts = [
        jnp.zeros((row_count, group_size, HEAD), jnp.float32) for group in range(group_count)
    ]
    position = 0
    offset = 0
    pieces = []
    for group in range(group_count):
        first_head = group * group_size
        scores = scores_of(offset, first_head)
        row_max, row_sums = stored[position]
        position += 1
        prob_float = jnp.exp(scores - row_max) / row_sums
        prob_low = prob_float.astype(jnp.bfloat16)
        dout_part = dattended[offset : offset + block_rows, first_head : first_head + group_size]
        value_part = value_rows[:, first_head : first_head + group_size]
        dvalue_parts[group] = jnp.einsum(
            "hqk,qhd->khd", prob_low, dout_part, preferred_element_type=jnp.float32
        )
        dprob = jnp.einsum(
            "qhd,khd->hqk", dout_part, value_part, preferred_element_type=jnp.float32
        )
        dscore = (prob_float * (dprob - jnp.sum(prob_float * dprob, -1, keepdims=True))).astype(
            jnp.bfloat16
        )
        pieces.append(
            jnp.einsum(
                "hqk,khd->qhd",
                dscore,
                key_rows[:, first_head : first_head + group_size],
                preferred_element_type=jnp.float32,
            )
            * 0.125
        )
        query_part = queries[offset : offset + block_rows, first_head : first_head + group_size]
        dkey_parts[group] = (
            jnp.einsum("hqk,qhd->khd", dscore, query_part, preferred_element_type=jnp.float32)
            * 0.125
        )
    dquery_blocks = jnp.concatenate(pieces, 1)
    dquery_low = dquery_blocks.reshape(row_count, feature).astype(jnp.bfloat16)
    dkey_low = jnp.concatenate(dkey_parts, 1).reshape(row_count, feature).astype(jnp.bfloat16)
    dvalue_low = jnp.concatenate(dvalue_parts, 1).reshape(row_count, feature).astype(jnp.bfloat16)
    dqkv_low = jnp.concatenate([dquery_low, dkey_low, dvalue_low], 1)
    da_one = against(dqkv_low, w_qkv)
    norm_one_pull = jax.vjp(norm_rows, work_float, gain_one, shift_one)[1]
    dinput_norm, dgain_one, dshift_one = norm_one_pull(da_one)
    dinput_low = (dresid + dinput_norm).astype(jnp.bfloat16)
    back_out, back_grad = (
        lax.all_to_all(
            output_low.reshape(devices, capacity, feature),
            "dev",
            split_axis=0,
            concat_axis=0,
            tiled=True,
        ),
        lax.all_to_all(
            dinput_low.reshape(devices, capacity, feature),
            "dev",
            split_axis=0,
            concat_axis=0,
            tiled=True,
        ),
    )
    block_output = jnp.where(
        is_live[:, None], back_out.reshape(row_count, feature)[slot_of], jnp.zeros_like(tokens)
    )
    input_grad = jnp.where(
        is_live[:, None], back_grad.reshape(row_count, feature)[slot_of], jnp.zeros_like(tokens)
    )
    vector_rows = jnp.stack(
        [
            dgain_one,
            dshift_one,
            dgain_two,
            dshift_two,
            jnp.sum(dquery_low.astype(jnp.float32), 0),
            jnp.sum(dvalue_low.astype(jnp.float32), 0),
            jnp.sum(dres_low.astype(jnp.float32), 0),
            jnp.sum(dy_float, 0),
        ],
        0,
    )
    bias_up_grad = jnp.sum(dup_low.astype(jnp.float32), 0).reshape(FF // feature, feature)
    vector_partial = jnp.concatenate([vector_rows, bias_up_grad], 0)
    down_grad = lax.psum_scatter(
        inner_rows(hidden, work_grads), "dev", scatter_dimension=0, tiled=True
    )
    wide_grad = lax.psum_scatter(
        jnp.concatenate(
            [
                inner_rows(low_one, dqkv_low),
                jnp.concatenate([inner_rows(attended, dres_low), inner_rows(low_two, dup_low)], 1),
            ],
            1,
        ),
        "dev",
        scatter_dimension=0,
        tiled=True,
    )
    shard_squares = jnp.sum(wide_grad * wide_grad) + jnp.sum(down_grad * down_grad)
    vector_grad = lax.psum(vector_partial, "dev")
    total = lax.psum(shard_squares, "dev") + jnp.sum(vector_grad * vector_grad)
    grad_norm = jnp.sqrt(total)
    factor = clip_norm / jnp.maximum(grad_norm, clip_norm)
    wide_new, wide_moment_new, wide_average_new = advance(
        wide_weight, wide_moment, wide_average, wide_grad, factor, decay_rate
    )
    down_new, down_moment_new, down_average_new = advance(
        down_weight, down_moment, down_average, down_grad, factor, decay_rate
    )
    vector_new, vector_moment_new, vector_average_new = advance(
        vector_weight, vector_moment, vector_average, vector_grad, factor, 0.0
    )
    return (
        block_output,
        input_grad,
        grad_norm,
        wide_new,
        wide_moment_new,
        wide_average_new,
        down_new,
        down_moment_new,
        down_average_new,
        vector_new,
        vector_moment_new,
        vector_average_new,
    )


def flips(devices, mask):
    return [(i, i ^ mask) for i in range(devices)]


def shifts(devices, step):
    return [(i, (i + PLANE * step) % devices) for i in range(devices)]


def place():
    me = lax.axis_index("dev")
    return jnp.stack([me // PLANE, (me // 4) % 2, (me // 2) % 2, me % 2]).astype(jnp.int32)


def core_order(core, mine, theirs):
    first = jnp.where(core == 0, mine, theirs)
    second = jnp.where(core == 0, theirs, mine)
    return first, second


def pin(*values):
    return lax.optimization_barrier(values)


def send(value, mask):
    return lax.ppermute(value, "dev", flips(lax.axis_size("dev"), mask))


def along_z(block, stacks):
    devices = lax.axis_size("dev")
    depth = devices // PLANE
    blocks = [block] + [lax.ppermute(block, "dev", shifts(devices, k)) for k in range(1, depth)]
    each = depth // stacks
    return tuple(jnp.stack(blocks[k : k + each], 0) for k in range(0, depth, each))


def to_neighbours(*own):
    return tuple(send(stack, 2) for stack in own) + tuple(send(stack, 4) for stack in own)


def to_diagonal(*near):
    if len(near) == 4:
        return send(near[0], 4), send(near[3], 2)
    half = near[0].shape[0] // 2
    return send(near[0][:half], 4), send(near[1][half:], 2)


def to_partner(*pieces):
    return tuple(send(piece, 1) for piece in pieces)


def total_of(*terms):
    return sum(term.astype(jnp.float32) for term in terms)


def low_sum(*terms):
    return total_of(*terms).astype(jnp.bfloat16)


class Fold:
    def __init__(self, mine, got):
        self.mine, self.got = mine, got
        self.half = mine.shape[1] // 2

    def pair(self, spot, steps):
        return self.mine[spot, steps], self.got[spot, steps]

    def diagonal(self):
        first, last = slice(None, self.half), slice(self.half, None)
        return low_sum(*self.pair(3, first)), low_sum(*self.pair(3, last))

    def neighbours(self, got_a, got_b):
        first, last = slice(None, self.half), slice(self.half, None)
        to_x = (low_sum(*self.pair(1, first), got_a), low_sum(*self.pair(1, last)))
        to_y = (low_sum(*self.pair(2, first)), low_sum(*self.pair(2, last), got_b))
        return jnp.concatenate(to_x, 0), jnp.concatenate(to_y, 0)

    def column(self, got_x, got_y):
        total = total_of(*self.pair(0, slice(None)), got_x, got_y)
        return (total[0],) + tuple(
            total[k].astype(jnp.bfloat16) for k in range(1, total.shape[0])
        )


def over_diagonal(to_a, to_b):
    return send(to_a, 4), send(to_b, 2)


def over_plane(to_x, to_y):
    return send(to_x, 2), send(to_y, 4)


def over_column(sums):
    devices = lax.axis_size("dev")
    return tuple(lax.ppermute(sums[k], "dev", shifts(devices, k)) for k in range(1, len(sums)))


def exchange(rows):
    return lax.all_to_all(rows, "dev", split_axis=0, concat_axis=0, tiled=True)


FAR = pl.BlockSpec(memory_space=pltpu.HBM)
SCALARS = pl.BlockSpec(memory_space=pltpu.SMEM)


def whole(*shape):
    return pl.BlockSpec(shape, lambda *_: (0,) * len(shape))


LIMIT = 48


def settings(limit):
    return pltpu.CompilerParams(vmem_limit_bytes=limit * MIB)


def cost(flops, moved, exps=0):
    return pl.CostEstimate(flops=int(flops), bytes_accessed=int(moved), transcendentals=int(exps))


def shaped(shape, dtype):
    return jax.ShapeDtypeStruct(shape, dtype)


def by_rows(matrix, other):
    return lax.dot_general(
        matrix, other, (((1,), (1,)), ((), ())), preferred_element_type=jnp.float32
    )


def by_columns(matrix, other):
    return lax.dot_general(
        matrix, other, (((0,), (0,)), ((), ())), preferred_element_type=jnp.float32
    )


def normed(values):
    center = values - jnp.mean(values, -1, keepdims=True)
    scale = lax.rsqrt(jnp.mean(center * center, -1, keepdims=True) + epsilon)
    return center * scale, scale


def norm_back(grad, gain, unit, scale):
    inner = grad * gain
    return scale * (
        inner
        - jnp.mean(inner, -1, keepdims=True)
        - unit * jnp.mean(inner * unit, -1, keepdims=True)
    )


def iota(shape, axis):
    return lax.broadcasted_iota(jnp.int32, shape, axis)


def slots_of(ids_row, capacity, groups):
    count = ids_row.shape[1]
    square = (count, count)
    ids = jnp.sum(
        jnp.where(iota(square, 0) == iota(square, 1), ids_row, 0), axis=1, keepdims=True
    )
    group = jnp.right_shift(ids, DOCS_DEV.bit_length() - 1)
    lanes = max(128, groups)
    onehot = jnp.where(group == iota((count, lanes), 1), 1.0, 0.0)
    lower = jnp.where(iota(square, 0) > iota(square, 1), 1.0, 0.0).astype(jnp.bfloat16)
    earlier = product(lower, onehot.astype(jnp.bfloat16))
    within = jnp.sum(earlier * onehot, axis=1, keepdims=True).astype(jnp.int32)
    return ids, jnp.where(ids >= 0, group * capacity + within, -1)


def route(ids_row, tokens, cotangent, devices):
    count, feature = tokens.shape

    def kernel(ids_ref, tokens_ref, cotangent_ref, rows_ref, grads_ref, slot_ref):
        ids, slot = slots_of(ids_ref[...], count // devices, devices)
        slot_ref[...] = slot
        move = jnp.where(slot == iota((count, count), 1), 1.0, 0.0).astype(jnp.bfloat16)
        code = jnp.where(ids >= 0, jnp.bitwise_and(ids, DOCS_DEV - 1) + 1, 0)
        code = jnp.broadcast_to(code.astype(jnp.float32), (count, 128)).astype(jnp.bfloat16)
        rows_ref[:, :feature] = by_columns(move, tokens_ref[...]).astype(jnp.bfloat16)
        rows_ref[:, feature:] = by_columns(move, code).astype(jnp.bfloat16)
        grads_ref[...] = by_columns(move, cotangent_ref[...]).astype(jnp.bfloat16)

    return pl.pallas_call(
        kernel,
        out_shape=[
            shaped((count, feature + 128), jnp.bfloat16),
            shaped((count, feature), jnp.bfloat16),
            shaped((count, 1), jnp.int32),
        ],
        compiler_params=settings(LIMIT),
        cost_estimate=cost(4 * count * count * feature, 8 * count * feature),
    )(ids_row, tokens, cotangent)


def give_back(slot, rows):
    count, feature = rows.shape[0], rows.shape[1] // 256 * 256

    def kernel(slot_ref, rows_ref, out_ref):
        move = jnp.where(slot_ref[...] == iota((count, count), 1), 1.0, 0.0).astype(jnp.bfloat16)
        out_ref[...] = product(move, rows_ref[...]).astype(jnp.bfloat16)

    return pl.pallas_call(
        kernel,
        grid=(1,),
        out_shape=shaped((count, feature), jnp.bfloat16),
        in_specs=[whole(count, 1), whole(count, feature)],
        out_specs=whole(count, feature),
        compiler_params=settings(LIMIT),
        cost_estimate=cost(2 * count * count * feature, 4 * count * feature),
    )(slot, rows)


def pieces_of(where_ref, pieces):
    z, y, x, core = where_ref[0], where_ref[1], where_ref[2], where_ref[3]
    count = len(pieces) // 2
    depth = 2 * pieces[count - 1].shape[0]
    columns = ((y, x), (y, 1 - x), (1 - y, x), (1 - y, 1 - x))
    for part, group in ((core, pieces[:count]), (1 - core, pieces[count:])):
        reached = 0
        for piece in group:
            for index in range(piece.shape[0]):
                yy, xx = columns[reached // depth]
                step = reached % depth
                zz = lax.rem(z - step + depth, depth)
                yield piece.at[index], step, (zz * 2 + yy) * 2 + xx, part
                reached += 1


def wide_copies(where_ref, pieces, buffer, sems):
    copies = []
    for source, _, chip, part in pieces_of(where_ref, pieces):
        rows, columns = source.shape
        target = buffer.at[
            pl.ds(pl.multiple_of(chip * rows, 16), rows),
            pl.ds(pl.multiple_of(part * columns, 128), columns),
        ]
        copies.append(pltpu.make_async_copy(source, target, sems.at[len(copies)]))
    return copies


def down_copies(where_ref, pieces, buffer, sems):
    copies = []
    for source, _, chip, part in pieces_of(where_ref, pieces):
        rows = source.shape[0]
        row = pl.multiple_of((chip * 2 + part) * rows, 16)
        copies.append(
            pltpu.make_async_copy(source, buffer.at[pl.ds(row, rows)], sems.at[len(copies)])
        )
    return copies


def project(where, work, vector, pieces):
    count, feature = work.shape[0], vector.shape[1]
    copies_count = sum(piece.shape[0] for piece in pieces)
    tile = 256

    def kernel(where_ref, work_ref, vector_ref, *refs):
        (
            flipped_ref, out_ref, weights_ref, output_ref, low, buffer, sems, store_sems
        ) = refs[len(pieces):]
        copies = wide_copies(where_ref, refs[:len(pieces)], buffer, sems)
        for copy in copies:
            copy.start()

        def rows_of(index, carry):
            rows = pl.ds(pl.multiple_of(index * 64, 64), 64)
            unit, _ = normed(work_ref[rows, :].astype(jnp.float32))
            low[rows, :] = (unit * vector_ref[0:1, :] + vector_ref[1:2, :]).astype(jnp.bfloat16)
            return carry

        lax.fori_loop(0, count // 64, rows_of, 0)
        flipped_ref[...] = low[...].astype(jnp.float32).T.astype(jnp.bfloat16)
        for copy in copies:
            copy.wait()
        stores = [
            pltpu.make_async_copy(
                buffer.at[:, pl.ds(0, 3 * feature)], weights_ref, store_sems.at[0]
            ),
            pltpu.make_async_copy(
                buffer.at[:, pl.ds(3 * feature, feature)], output_ref, store_sems.at[1]
            ),
        ]
        for store in stores:
            store.start()
        for part, bias in ((0, 4), (1, None), (2, 5)):

            def columns_of(index, carry):
                inner = pl.ds(pl.multiple_of(index * tile, tile), tile)
                columns = pl.ds(pl.multiple_of(part * feature + index * tile, tile), tile)
                value = product(low[...], buffer[:, columns])
                if bias is not None:
                    value = value + vector_ref[bias : bias + 1, inner]
                out_ref[:, columns] = value.astype(jnp.bfloat16)
                return carry

            lax.fori_loop(0, feature // tile, columns_of, 0)
        for store in stores:
            store.wait()

    return pl.pallas_call(
        kernel,
        grid=(1,),
        out_shape=[
            shaped((feature, count), jnp.bfloat16),
            shaped((count, 3 * feature), jnp.bfloat16),
            shaped((feature, 3 * feature), jnp.bfloat16),
            shaped((feature, feature), jnp.bfloat16),
        ],
        in_specs=[SCALARS, whole(count, feature), whole(*vector.shape)] + [FAR] * len(pieces),
        out_specs=[whole(feature, count), whole(count, 3 * feature), FAR, FAR],
        scratch_shapes=[
            pltpu.VMEM((count, feature), jnp.bfloat16),
            pltpu.VMEM((feature, 4 * feature), jnp.bfloat16),
            pltpu.SemaphoreType.DMA((copies_count,)),
            pltpu.SemaphoreType.DMA((2,)),
        ],
        compiler_params=settings(60),
        cost_estimate=cost(6 * count * feature * feature, 12 * feature * feature),
    )(where, work, vector, *pieces)


def fill_cap(code_ref, cap):
    code = code_ref[...].astype(jnp.float32)
    cap[...] = jnp.where(code[:, :1] == code.T[:1], -masked_value, masked_value)


def one_head(values, head):
    lanes = iota(values.shape, 1)
    inside = (lanes >= head * HEAD) & (lanes < (head + 1) * HEAD)
    return jnp.where(inside, values, 0.0).astype(jnp.bfloat16)


def attend(projected, work, vector, weights, first, pairs, left=None):
    count, feature = work.shape[0], vector.shape[1]
    all_pairs = feature // 128
    tile = 512
    ends = left is not None

    def kernel(q_ref, k_ref, v_ref, code_ref, *refs):
        if ends:
            (
                weight_ref, work_ref, vector_ref, left_ref, flipped_ref, stat_ref, resid_ref, low_ref,
                cap, right, total,
            ) = refs
        else:
            flipped_ref, stat_ref, attended_ref, cap = refs
        pair = pl.program_id(0)

        @pl.when(pair == 0)
        def _():
            fill_cap(code_ref, cap)

        keys = k_ref[...]
        values = v_ref[...].astype(jnp.float32).T.astype(jnp.bfloat16)
        scaled = q_ref[...].astype(jnp.float32) * 0.125
        heads = []
        for head in range(2):
            query = one_head(scaled, head)
            parts = []
            for start in range(0, count, tile):
                span = slice(start, start + tile)
                scores = jnp.minimum(by_rows(keys, query[span]), cap[:, span])
                most = jnp.max(scores, 0, keepdims=True)
                powers = jnp.exp(scores - most)
                sums = jnp.sum(powers, 0, keepdims=True)
                stat_ref[0, head : head + 1, span] = most + jnp.log(sums)
                mixed = product(
                    values[head * HEAD : (head + 1) * HEAD], powers.astype(jnp.bfloat16)
                )
                parts.append(mixed * (1.0 / sums))
            heads.append(jnp.concatenate(parts, 1))
        both = jnp.concatenate(heads, 0)
        flipped_ref[...] = both.astype(jnp.bfloat16)
        attended = both.T.astype(jnp.bfloat16)
        if ends:
            right[pair] = attended
        else:
            attended_ref[...] = attended

        if ends:

            @pl.when(pair == pairs - 1)
            def _():
                middle = feature - pairs * 128
                for start in range(0, feature, 256):
                    span = slice(start, start + 256)
                    value = product(left_ref[...], weight_ref[:middle, span])
                    for index in range(pairs):
                        rows = slice(middle + index * 128, middle + (index + 1) * 128)
                        value = value + product(right[index], weight_ref[rows, span])
                    total[:, span] = value

                def rows_of(index, carry):
                    rows = pl.ds(pl.multiple_of(index * 64, 64), 64)
                    resid = (
                        work_ref[rows, :].astype(jnp.float32) + total[rows, :] + vector_ref[6:7, :]
                    )
                    resid_ref[rows, :] = resid
                    unit, _ = normed(resid)
                    low_ref[rows, :] = (unit * vector_ref[2:3, :] + vector_ref[3:4, :]).astype(
                        jnp.bfloat16
                    )
                    return carry

                lax.fori_loop(0, count // 64, rows_of, 0)

    def columns_at(offset):
        return pl.BlockSpec((count, 128), lambda pair: (0, offset + pair))

    wide = whole(count, feature)
    return pl.pallas_call(
        kernel,
        grid=(pairs,),
        out_shape=[
            shaped((pairs * 128, count), jnp.bfloat16),
            shaped((pairs, 8, count), jnp.float32),
        ]
        + (
            [shaped((count, feature), jnp.float32), shaped((count, feature), jnp.bfloat16)]
            if ends
            else [shaped((count, pairs * 128), jnp.bfloat16)]
        ),
        in_specs=[
            columns_at(first),
            columns_at(all_pairs + first),
            columns_at(2 * all_pairs + first),
            pl.BlockSpec((count, 128), lambda pair: (0, all_pairs)),
        ]
        + (
            [whole(feature, feature), wide, whole(*vector.shape), whole(*left.shape)]
            if ends
            else []
        ),
        out_specs=[
            pl.BlockSpec((128, count), lambda pair: (pair, 0)),
            pl.BlockSpec((1, 8, count), lambda pair: (pair, 0, 0)),
        ]
        + ([wide, wide] if ends else [columns_at(0)]),
        scratch_shapes=[pltpu.VMEM((count, count), jnp.float32)]
        + (
            [
                pltpu.VMEM((pairs, count, 128), jnp.bfloat16),
                pltpu.VMEM((count, feature), jnp.float32),
            ]
            if ends
            else []
        ),
        compiler_params=settings(60),
        cost_estimate=cost(
            8 * count * count * pairs * 128, 14 * count * feature, 2 * pairs * count * count
        ),
    )(
        projected, projected, projected, work,
        *([weights, work, vector, left] if ends else []),
    )


def widen(where, low, bias_row, pieces):
    count, feature = low.shape
    wide = bias_row.shape[1]
    tile = feature
    steps = wide // tile

    def kernel(where_ref, low_ref, bias_ref, *refs):
        hidden_ref, slope_ref, weights_ref, buffer, sems, store_sem = refs[len(pieces):]
        step = pl.program_id(0)
        store = pltpu.make_async_copy(buffer, weights_ref, store_sem)

        @pl.when(step == 0)
        def _():
            copies = wide_copies(where_ref, refs[:len(pieces)], buffer, sems)
            for copy in copies:
                copy.start()
            for copy in copies:
                copy.wait()
            store.start()

        columns = pl.ds(pl.multiple_of(step * tile, tile), tile)
        up = product(low_ref[...], buffer[:, columns]) + bias_ref[...]
        below = 0.5 * (1.0 + lax.erf(up * (0.5**0.5)))
        hidden_ref[...] = (up * below).astype(jnp.bfloat16)
        slope_ref[...] = below + up * (jnp.exp(-0.5 * up * up) * ((2.0 * math.pi) ** -0.5))

        @pl.when(step == steps - 1)
        def _():
            store.wait()

    block = pl.BlockSpec((count, tile), lambda step: (0, step))
    return pl.pallas_call(
        kernel,
        grid=(steps,),
        out_shape=[
            shaped((count, wide), jnp.bfloat16),
            shaped((count, wide), jnp.float32),
            shaped((feature, wide), jnp.bfloat16),
        ],
        in_specs=[
            SCALARS,
            whole(count, feature),
            pl.BlockSpec((1, tile), lambda step: (0, step)),
        ]
        + [FAR] * len(pieces),
        out_specs=[block, block, FAR],
        scratch_shapes=[
            pltpu.VMEM((feature, wide), jnp.bfloat16),
            pltpu.SemaphoreType.DMA((sum(piece.shape[0] for piece in pieces),)),
            pltpu.SemaphoreType.DMA,
        ],
        compiler_params=settings(60),
        cost_estimate=cost(
            2 * count * feature * wide, 2 * feature * wide + 6 * count * wide, count * wide
        ),
    )(where, low, bias_row, *pieces)


def down_gradient(where, hidden, grads, depth):
    count, wide = hidden.shape
    feature = grads.shape[1]
    rows = wide // (depth * PLANE)
    part = wide // depth

    def kernel(where_ref, hidden_ref, grads_ref, mine_ref, theirs_ref, result):
        y, x, core = where_ref[1], where_ref[2], where_ref[3]
        result[...] = by_columns(hidden_ref[...], grads_ref[...])
        for yy in range(2):
            for xx in range(2):
                spot = jnp.bitwise_xor(y, yy) * 2 + jnp.bitwise_xor(x, xx)
                first = (yy * 2 + xx) * 2
                for target, side in ((mine_ref, core), (theirs_ref, 1 - core)):
                    row = pl.multiple_of((first + side) * rows, 16)
                    target[spot, 0] = result[pl.ds(row, rows), :].astype(jnp.bfloat16)

    shape = shaped((4, depth, rows, feature), jnp.bfloat16)
    block = pl.BlockSpec((4, 1, rows, feature), lambda step, where_ref: (0, step, 0, 0))
    return pl.pallas_call(
        kernel,
        out_shape=[shape, shape],
        grid_spec=pltpu.PrefetchScalarGridSpec(
            num_scalar_prefetch=1,
            grid=(depth,),
            in_specs=[
                pl.BlockSpec(
                    (count, part),
                    lambda step, where_ref: (0, lax.rem(where_ref[0] + step, depth)),
                ),
                whole(count, feature),
            ],
            out_specs=[block, block],
            scratch_shapes=[pltpu.VMEM((part, feature), jnp.float32)],
        ),
        compiler_params=settings(LIMIT),
        cost_estimate=cost(2 * count * wide * feature, 2 * wide * (count + feature)),
    )(where, hidden, grads)


def put_wide(where_ref, result, mine_ref, theirs_ref):
    z, y, x, core = where_ref[0], where_ref[1], where_ref[2], where_ref[3]
    _, depth, rows, _ = mine_ref.shape
    for chip in range(4 * depth):
        zz, yy, xx = chip // 4, (chip // 2) % 2, chip % 2
        step = lax.rem(zz - z + depth, depth)
        spot = jnp.bitwise_xor(y, yy) * 2 + jnp.bitwise_xor(x, xx)
        for target, side in ((mine_ref, core), (theirs_ref, 1 - core)):
            row = pl.multiple_of((chip * 2 + side) * rows, 8)
            target[spot, step] = result[pl.ds(row, rows), :].astype(jnp.bfloat16)


def narrow(where, hidden, resid, vector, pieces):
    count, wide = hidden.shape
    feature = resid.shape[1]
    tile = 256

    def kernel(where_ref, hidden_ref, resid_ref, vector_ref, *refs):
        out_ref, weights_ref, buffer, sems, store_sem = refs[len(pieces):]
        copies = down_copies(where_ref, refs[:len(pieces)], buffer, sems)
        for copy in copies:
            copy.start()
        for copy in copies:
            copy.wait()
        store = pltpu.make_async_copy(buffer, weights_ref, store_sem)
        store.start()

        def columns_of(index, carry):
            columns = pl.ds(pl.multiple_of(index * tile, tile), tile)
            value = product(hidden_ref[...], buffer[:, columns])
            out_ref[:, columns] = (
                resid_ref[:, columns] + (value + vector_ref[7:8, columns])
            ).astype(jnp.bfloat16)
            return carry

        lax.fori_loop(0, feature // tile, columns_of, 0)
        store.wait()

    return pl.pallas_call(
        kernel,
        grid=(1,),
        out_shape=[
            shaped((count, feature), jnp.bfloat16),
            shaped((wide, feature), jnp.bfloat16),
        ],
        in_specs=[SCALARS, whole(count, wide), whole(count, feature), whole(*vector.shape)]
        + [FAR] * len(pieces),
        out_specs=[whole(count, feature), FAR],
        scratch_shapes=[
            pltpu.VMEM((wide, feature), jnp.bfloat16),
            pltpu.SemaphoreType.DMA((sum(piece.shape[0] for piece in pieces),)),
            pltpu.SemaphoreType.DMA,
        ],
        compiler_params=settings(LIMIT),
        cost_estimate=cost(2 * count * wide * feature, 6 * wide * feature),
    )(where, hidden, resid, vector, *pieces)


def feed_back(where, slope, low, grads, resid, vector, up_weights, down_weights, attended, depth):
    count, wide = slope.shape
    feature = resid.shape[1]
    tile = feature
    steps = wide // tile
    half = feature // 2
    chip_rows = feature // (PLANE * depth)

    def kernel(
        where_ref, slope_ref, low_ref, grads_ref, resid_ref, vector_ref, up_ref, down_ref, left_ref, right_ref,
        dresid_ref, dlow_ref, sums_ref, bias_ref, mine_ref, theirs_ref, back, flipped, result,
    ):
        step = pl.program_id(0)

        @pl.when(step == 0)
        def _():
            flipped[...] = low_ref[...].astype(jnp.float32).T.astype(jnp.bfloat16)
            back[...] = jnp.zeros_like(back)

        @pl.when(step < steps)
        def _():
            dup = (slope_ref[...] * by_rows(grads_ref[...], down_ref[...])).astype(jnp.bfloat16)
            bias_ref[...] = jnp.sum(dup.astype(jnp.float32), 0, keepdims=True)
            back[...] += by_rows(dup, up_ref[...])
            result[...] = product(flipped[...], dup)

        @pl.when(step == steps)
        def _():
            sums_ref[...] = jnp.zeros_like(sums_ref)

            def rows_of(index, carry):
                rows = pl.ds(pl.multiple_of(index * 64, 64), 64)
                unit, scale = normed(resid_ref[rows, :])
                da = back[rows, :]
                dy = grads_ref[rows, :].astype(jnp.float32)
                dresid = dy + norm_back(da, vector_ref[2:3, :], unit, scale)
                dresid_ref[rows, :] = dresid
                dlow = dresid.astype(jnp.bfloat16)
                dlow_ref[rows, :] = dlow
                for row, value in enumerate((da * unit, da, dlow.astype(jnp.float32), dy)):
                    sums_ref[row : row + 1, :] += jnp.sum(value, 0, keepdims=True)
                return carry

            lax.fori_loop(0, count // 64, rows_of, 0)
            result[:half, :] = product(left_ref[...], dlow_ref[...])
            result[half:, :] = product(right_ref[...], dlow_ref[...])

        put_wide(where_ref, result, mine_ref, theirs_ref)

    def at(step):
        return jnp.minimum(step, steps - 1)

    def columns_at(rows):
        return pl.BlockSpec((rows, tile), lambda step: (0, at(step)))

    all_rows = whole(count, feature)
    split = shaped((4, depth, chip_rows, (steps + 1) * feature), jnp.bfloat16)
    block = pl.BlockSpec((4, depth, chip_rows, feature), lambda step: (0, 0, 0, step))
    return pl.pallas_call(
        kernel,
        grid=(steps + 1,),
        out_shape=[
            shaped((count, feature), jnp.float32),
            shaped((count, feature), jnp.bfloat16),
            shaped((8, feature), jnp.float32),
            shaped((1, wide), jnp.float32),
            split,
            split,
        ],
        in_specs=[
            SCALARS,
            columns_at(count),
            all_rows,
            all_rows,
            all_rows,
            whole(*vector.shape),
            columns_at(feature),
            pl.BlockSpec((tile, feature), lambda step: (at(step), 0)),
            whole(half, count),
            whole(half, count),
        ],
        out_specs=[all_rows, all_rows, whole(8, feature), columns_at(1), block, block],
        scratch_shapes=[
            pltpu.VMEM((count, feature), jnp.float32),
            pltpu.VMEM((feature, count), jnp.bfloat16),
            pltpu.VMEM((feature, feature), jnp.float32),
        ],
        compiler_params=settings(60),
        cost_estimate=cost(6 * count * wide * feature, 8 * wide * feature + 10 * count * wide),
    )(where, slope, low, grads, resid, vector, up_weights, down_weights, *attended)


def attend_back(projected, work, stats, dlow, weights, first, pairs):
    count, feature = dlow.shape
    all_pairs = feature // 128
    tile = 512
    wide = pairs * 128

    def kernel(
        q_ref, k_ref, v_ref, code_ref, stat_ref, dlow_ref, weight_ref, out_ref, sums_ref, douts, cap
    ):
        pair = pl.program_id(0)

        @pl.when(pair == 0)
        def _():
            fill_cap(code_ref, cap)
            for start in range(0, wide, 128):
                span = slice(start, start + 128)
                douts[start // 128] = by_rows(dlow_ref[...], weight_ref[span, :]).astype(
                    jnp.bfloat16
                )

        keys, values = k_ref[...], v_ref[...]
        wide_keys = keys.astype(jnp.float32)
        dquery = jnp.zeros((count, 128), jnp.float32)
        scaled = q_ref[...].astype(jnp.float32) * 0.125
        dout = douts[pair].astype(jnp.float32)
        dkey = jnp.zeros((count, 128), jnp.float32)
        dvalue = jnp.zeros((count, 128), jnp.float32)
        for head in range(2):
            query = one_head(scaled, head)
            dhead = one_head(dout, head)
            for start in range(0, count, tile):
                span = slice(start, start + tile)
                scores = jnp.minimum(by_rows(keys, query[span]), cap[:, span])
                probs = jnp.exp(scores - stat_ref[0, head : head + 1, span])
                dprob = by_rows(values, dhead[span])
                inner = jnp.sum(probs * dprob, 0, keepdims=True)
                dscore = (probs * (dprob - inner)).astype(jnp.bfloat16)
                dvalue = dvalue + product(probs.astype(jnp.bfloat16), dhead[span])
                dkey = dkey + product(dscore, query[span])
                dquery = dquery + by_columns(dscore, one_head(wide_keys, head))
        dquery = (dquery * 0.125).astype(jnp.bfloat16)
        dvalue = dvalue.astype(jnp.bfloat16)
        out_ref[0] = dquery
        out_ref[1] = dkey.astype(jnp.bfloat16)
        out_ref[2] = dvalue
        sums_ref[0:1, :] = jnp.sum(dquery.astype(jnp.float32), 0, keepdims=True)
        sums_ref[1:2, :] = jnp.sum(dvalue.astype(jnp.float32), 0, keepdims=True)

    def columns_at(offset):
        return pl.BlockSpec((count, 128), lambda pair: (0, offset + pair))

    return pl.pallas_call(
        kernel,
        grid=(pairs,),
        out_shape=[
            shaped((3, count, wide), jnp.bfloat16),
            shaped((8, wide), jnp.float32),
        ],
        in_specs=[
            columns_at(first),
            columns_at(all_pairs + first),
            columns_at(2 * all_pairs + first),
            pl.BlockSpec((count, 128), lambda pair: (0, all_pairs)),
            pl.BlockSpec((1, 8, count), lambda pair: (pair, 0, 0)),
            whole(count, feature),
            pl.BlockSpec((wide, feature), lambda pair: (first // pairs, 0)),
        ],
        out_specs=[
            pl.BlockSpec((3, count, 128), lambda pair: (0, 0, pair)),
            pl.BlockSpec((8, 128), lambda pair: (0, pair)),
        ],
        scratch_shapes=[
            pltpu.VMEM((pairs, count, 128), jnp.bfloat16),
            pltpu.VMEM((count, count), jnp.float32),
        ],
        compiler_params=settings(LIMIT),
        cost_estimate=cost(
            14 * count * count * wide, 16 * count * feature, 2 * pairs * count * count
        ),
    )(projected, projected, projected, work, stats, dlow, weights)


def first_gradient(where, flipped, dprojected, depth):
    feature, count = flipped.shape
    half = feature // 2
    rows = feature // (PLANE * depth)

    def kernel(where_ref, flipped_ref, d_ref, e_ref, mine_ref, theirs_ref, result):
        result[:, :half] = product(flipped_ref[...], d_ref[0])
        result[:, half:] = product(flipped_ref[...], e_ref[0])
        put_wide(where_ref, result, mine_ref, theirs_ref)

    shape = shaped((4, depth, rows, 3 * feature), jnp.bfloat16)
    block = pl.BlockSpec((4, depth, rows, feature), lambda step: (0, 0, 0, step))
    part = pl.BlockSpec((1, count, half), lambda step: (step, 0, 0))
    return pl.pallas_call(
        kernel,
        grid=(3,),
        out_shape=[shape, shape],
        in_specs=[SCALARS, whole(feature, count), part, part],
        out_specs=[block, block],
        scratch_shapes=[pltpu.VMEM((feature, feature), jnp.float32)],
        compiler_params=settings(60),
        cost_estimate=cost(6 * count * feature * feature, 16 * feature * feature),
    )(where, flipped, *dprojected)


def project_back(work, dprojected, dresid, vector, weights, sums_two, sums_attend, bias_up, devices):
    count, feature = dresid.shape
    tile = 128
    half = feature // 2
    lanes = 16 * feature // devices // 128
    capacity = count // devices

    def kernel(
        work_ref, d_ref, e_ref, dresid_ref, vector_ref, weight_ref, two_ref, left_ref, right_ref, bias_ref,
        out_ref, sums,
    ):
        sums[...] = jnp.zeros_like(sums)

        def rows_of(index, carry):
            rows = pl.ds(pl.multiple_of(index * tile, tile), tile)
            da = jnp.zeros((tile, feature), jnp.float32)
            for part in range(3):
                middle = part * feature + half
                da += by_rows(d_ref[part, rows, :], weight_ref[:, middle - half : middle])
                da += by_rows(e_ref[part, rows, :], weight_ref[:, middle : middle + half])
            unit, scale = normed(work_ref[rows, :].astype(jnp.float32))
            out_ref[rows, :feature] = (
                dresid_ref[rows, :] + norm_back(da, vector_ref[0:1, :], unit, scale)
            ).astype(jnp.bfloat16)
            sums[0:1, :] += jnp.sum(da * unit, 0, keepdims=True)
            sums[1:2, :] += jnp.sum(da, 0, keepdims=True)
            return carry

        lax.fori_loop(0, count // tile, rows_of, 0)
        sums[2:4, :] = two_ref[0:2, :]
        sums[4:6, :half] = left_ref[0:2, :]
        sums[4:6, half:] = right_ref[0:2, :]
        sums[6:8, :] = two_ref[2:4, :]
        for row in range(FF // feature):
            sums[8 + row : 9 + row, :] = bias_ref[0:1, row * feature : (row + 1) * feature]
        place_in = iota((capacity, 128), 0)
        for device in range(devices):
            block = jnp.zeros((capacity, 128), jnp.float32)
            for lane in range(lanes):
                first = device * lanes + lane
                row, column = divmod(first * 128, feature)
                value = sums[row : row + 1, column : column + 128]
                high = value.astype(jnp.bfloat16).astype(jnp.float32)
                block = jnp.where(place_in == lane, high, block)
                block = jnp.where(place_in == lanes + lane, value - high, block)
            out_ref[device * capacity : (device + 1) * capacity, feature:] = block.astype(
                jnp.bfloat16
            )

    return pl.pallas_call(
        kernel,
        grid=(1,),
        out_shape=shaped((count, feature + 128), jnp.bfloat16),
        in_specs=[
            whole(count, feature),
            whole(3, count, half),
            whole(3, count, half),
            whole(count, feature),
            whole(*vector.shape),
            whole(feature, 3 * feature),
            whole(8, feature),
            whole(8, half),
            whole(8, half),
            whole(1, FF),
        ],
        out_specs=whole(count, feature + 128),
        scratch_shapes=[pltpu.VMEM((16, feature), jnp.float32)],
        compiler_params=settings(LIMIT),
        cost_estimate=cost(6 * count * feature * feature, 6 * feature * feature),
    )(work, *dprojected, dresid, vector, weights, sums_two, *sums_attend, bias_up)


def settle(own, got, back, squares, devices, feature):
    rows, columns = own.shape
    lanes = 16 * feature // devices // 128
    capacity = back.shape[1]

    def kernel(squares_ref, own_ref, *refs):
        got_refs, (back_ref, grad_ref, packet_ref) = refs[: len(got)], refs[len(got) :]
        grad = own_ref[...]
        for ref in got_refs:
            grad += ref[...].astype(jnp.float32)
        grad_ref[...] = grad
        total = squares_ref[0, 0] + jnp.sum(grad * grad)
        sums = jnp.sum(back_ref[...].astype(jnp.float32), 0)
        packet_ref[:, :lanes, :] = jnp.broadcast_to(
            (sums[:lanes] + sums[lanes : 2 * lanes])[None], (devices, lanes, 128)
        )
        packet_ref[:, lanes:, :] = jnp.full((devices, 1, 128), total, jnp.float32)

    return pl.pallas_call(
        kernel,
        grid=(1,),
        out_shape=[
            shaped((rows, columns), jnp.float32),
            shaped((devices, lanes + 1, 128), jnp.float32),
        ],
        in_specs=[SCALARS, whole(rows, columns)]
        + [whole(rows, columns)] * len(got)
        + [pl.BlockSpec((devices, capacity, 128), lambda step: (0, 0, feature // 128))],
        out_specs=[whole(rows, columns), whole(devices, lanes + 1, 128)],
        compiler_params=settings(60),
        cost_estimate=cost(8 * rows * columns, 16 * rows * columns),
    )(squares.reshape(1, 1), own, *got, back)


def finish(packets, first_grad, up_grad, down_grad, wide, down, vector):
    devices, lanes, _ = packets.shape
    lanes -= 1
    rows, columns = wide[0].shape
    down_rows, feature = down[0].shape
    vector_rows = vector[0].shape[0]
    steps = 4
    tile, down_tile = columns // steps, down_rows // steps
    first_columns = first_grad.shape[1]

    def kernel(packets_ref, first_ref, up_ref, down_grad_ref, *refs):
        wide_refs, down_refs, vector_refs = refs[:3], refs[3:6], refs[6:9]
        norm_ref, wide_new, down_new, vector_new = refs[9], refs[10:13], refs[13:16], refs[16:19]
        sums, factor_ref = refs[19:]
        step = pl.program_id(0)

        def put(new, old, gradient, decay):
            for ref, value in zip(
                new, advance(*(ref[...] for ref in old), gradient, factor_ref[0], decay), strict=True
            ):
                ref[...] = value

        @pl.when(step == 0)
        def _():
            for place_of in range(vector_rows * feature // 128):
                device, lane = divmod(place_of, lanes)
                row, column = divmod(place_of * 128, feature)
                sums[row : row + 1, column : column + 128] = packets_ref[device, lane : lane + 1]
            gradient = sums[...]
            shares = packets_ref[:, lanes, :1]
            total = jnp.sum(shares) + jnp.sum(gradient * gradient)
            norm = jnp.sqrt(jnp.full((1, 1), total))
            norm_ref[...] = norm
            factor_ref[0] = jnp.sum(clip_norm / jnp.maximum(norm, clip_norm))
            put(vector_new, vector_refs, gradient, 0.0)

        for index in range(steps):

            @pl.when(step == index)
            def _():
                first = index * tile
                parts = []
                if first < first_columns:
                    parts.append(first_ref[:, first : min(first + tile, first_columns)])
                if first + tile > first_columns:
                    low = max(first - first_columns, 0)
                    high = first + tile - first_columns
                    if low < feature:
                        parts.append(up_ref[:, FF + low : FF + min(high, feature)])
                    if high > feature:
                        parts.append(up_ref[:, max(low - feature, 0) : high - feature])
                gradient = parts[0] if len(parts) == 1 else jnp.concatenate(parts, 1)
                put(wide_new, wide_refs, gradient, decay_rate)

        put(down_new, down_refs, down_grad_ref[...], decay_rate)

    def tiles(shape):
        return pl.BlockSpec(shape, lambda step: (0, step))

    wide_specs = [tiles((rows, tile))] * 3
    down_specs = [pl.BlockSpec((down_tile, feature), lambda step: (step, 0))] * 3
    vector_specs = [whole(vector_rows, feature)] * 3
    return pl.pallas_call(
        kernel,
        grid=(steps,),
        out_shape=[shaped((1, 1), jnp.float32)]
        + [shaped(part.shape, jnp.float32) for part in (*wide, *down, *vector)],
        in_specs=[
            whole(*packets.shape),
            whole(*first_grad.shape),
            whole(*up_grad.shape),
            down_specs[0],
        ]
        + wide_specs
        + down_specs
        + vector_specs,
        out_specs=[whole(1, 1)] + wide_specs + down_specs + vector_specs,
        scratch_shapes=[
            pltpu.VMEM((vector_rows, feature), jnp.float32),
            pltpu.SMEM((1,), jnp.float32),
        ],
        compiler_params=settings(60),
        cost_estimate=cost(20 * rows * columns, 40 * rows * columns),
    )(packets, first_grad, up_grad, down_grad, *wide, *down, *vector)


def structured(devices, feature):
    rows = feature // devices
    return devices % PLANE == 0 and feature % devices == 0 and (2 * rows) % 16 == 0


def body(
    tokens,
    cotangent,
    segment_ids,
    wide_weight,
    wide_moment,
    wide_average,
    down_weight,
    down_moment,
    down_average,
    vector_weight,
    vector_moment,
    vector_average,
):
    devices = lax.axis_size("dev")
    count, feature = tokens.shape
    if not structured(devices, feature):
        return plain_body(
            tokens,
            cotangent,
            segment_ids,
            wide_weight,
            wide_moment,
            wide_average,
            down_weight,
            down_moment,
            down_average,
            vector_weight,
            vector_moment,
            vector_average,
        )
    depth = devices // PLANE
    capacity = count // devices
    where = place()
    core = where[3]

    wide_low, down_low = wide_weight.astype(jnp.bfloat16), down_weight.astype(jnp.bfloat16)
    rows, columns = wide_low.shape
    parts = wide_low.reshape(rows, 2, 2, columns // 4)
    keep, give = core_order(core, parts[:, :, 0], parts[:, :, 1])
    got = lax.ppermute(give, "dev", flips(devices, 1))
    pair = jnp.concatenate(core_order(core, keep, got), 0)

    send_rows, send_grads, slot = route(segment_ids.reshape(1, count), tokens, cotangent, devices)
    first_own = along_z(pair[:, 0], 2)
    send_rows, first_own = pin(send_rows, first_own)

    work = exchange(send_rows.reshape(devices, capacity, -1)).reshape(count, -1)
    first_near = pin(*to_neighbours(*first_own))

    first_far = to_diagonal(*first_near)
    first_got = to_partner(*first_own, *first_near)
    first_far, first_got = pin(first_far, first_got)
    first_got = first_got + to_partner(*first_far)
    first_got, work, up_block = pin(first_got, work, pair[:, 1])

    up_own = along_z(up_block, 1)
    flipped_one, projected, first_weights, out_weights = project(
        where, work, vector_weight, (*first_own, *first_near, *first_far, *first_got)
    )
    projected, up_own, down_block, send_grads = pin(projected, up_own, down_low, send_grads)

    up_near = to_neighbours(*up_own)
    down_own = along_z(down_block, 2)
    pairs = feature // 256
    attended_a, stats_a, carried = attend(projected, work, vector_weight, out_weights, 0, pairs)
    carried, up_near, down_own, send_grads = pin(carried, up_near, down_own, send_grads)

    up_far = to_diagonal(*up_near)
    up_got = to_partner(*up_own, *up_near)
    grads = exchange(send_grads.reshape(devices, capacity, feature)).reshape(count, feature)
    attended_b, stats_b, resid, low_two = attend(
        projected, work, vector_weight, out_weights, pairs, pairs, carried
    )
    low_two, up_far, up_got = pin(low_two, up_far, up_got)
    up_got = up_got + to_partner(*up_far)
    low_two, up_got, down_own = pin(low_two, up_got, down_own)

    down_near = to_neighbours(*down_own)
    hidden, slope, up_weights = widen(
        where, low_two, vector_weight[8:].reshape(1, FF), (*up_own, *up_near, *up_far, *up_got)
    )
    hidden, down_near = pin(hidden, down_near)

    down_far = to_diagonal(*down_near)
    down_got = to_partner(*down_own, *down_near)
    down_mine, down_theirs = down_gradient(where, hidden, grads, depth)
    down_far, down_got, down_mine, down_theirs = pin(down_far, down_got, down_mine, down_theirs)

    got = send(down_theirs, 1)
    down_got = down_got + to_partner(*down_far)
    down_got, got = pin(down_got, got)
    down_fold = Fold(down_mine, got)
    down_to, down_got = pin(down_fold.diagonal(), down_got)

    got = over_diagonal(*down_to)
    output, down_weights = narrow(
        where, hidden, resid, vector_weight, (*down_own, *down_near, *down_far, *down_got)
    )
    output, down_weights, got = pin(output, down_weights, got)
    down_to, output = pin(down_fold.neighbours(*got), output)

    back_out = exchange(output.reshape(devices, capacity, feature)).reshape(count, feature)
    got = over_plane(*down_to)
    dresid, dlow, sums_two, bias_up_grad, up_mine, up_theirs = feed_back(
        where, slope, low_two, grads, resid, vector_weight, up_weights, down_weights,
        (attended_a, attended_b), depth,
    )
    dlow, got, up_mine, up_theirs, back_out = pin(dlow, got, up_mine, up_theirs, back_out)
    down_sums, dlow, up_theirs = pin(down_fold.column(*got), dlow, up_theirs)

    down_got = over_column(down_sums)
    up_got = send(up_theirs, 1)
    dleft, sums_left = attend_back(projected, work, stats_a, dlow, out_weights, 0, pairs)
    up_got, dleft, dlow = pin(up_got, dleft, dlow)
    up_fold = Fold(up_mine, up_got)
    up_to, dlow = pin(up_fold.diagonal(), dlow)

    up_got = over_diagonal(*up_to)
    dright, sums_right = attend_back(projected, work, stats_b, dlow, out_weights, pairs, pairs)
    up_got, dright, down_got = pin(up_got, dright, down_got)
    up_to, dright = pin(up_fold.neighbours(*up_got), dright)

    up_got = over_plane(*up_to)
    both = project_back(
        work, (dleft, dright), dresid, vector_weight, first_weights,
        sums_two, (sums_left, sums_right), bias_up_grad, devices,
    )
    both, dright = pin(both, dright)

    back = exchange(both.reshape(devices, capacity, -1))
    first_mine, first_theirs = first_gradient(where, flipped_one, (dleft, dright), depth)
    first_mine, first_theirs, up_got = pin(first_mine, first_theirs, up_got)

    first_got = send(first_theirs, 1)
    up_sums = up_fold.column(*up_got)
    first_got, up_sums = pin(first_got, up_sums)
    first_fold = Fold(first_mine, first_got)
    first_to, up_sums = pin(first_fold.diagonal(), up_sums)

    up_got = over_column(up_sums)
    got, back = pin(over_diagonal(*first_to), back)
    first_to = pin(*first_fold.neighbours(*got))

    got = over_plane(*first_to)
    got, up_first = pin(got, up_got[0])
    down_grad = total_of(down_sums[0], *down_got)
    first_sums, back_out = pin(first_fold.column(*got), back_out)

    first_got = over_column(first_sums)
    up_grad = total_of(up_sums[0], up_first, *up_got[1:])
    squares = jnp.sum(up_grad * up_grad) + jnp.sum(down_grad * down_grad)
    block_output = give_back(slot, back_out)
    first_got, up_grad, block_output, down_grad, squares = pin(
        first_got, up_grad, block_output, down_grad, squares
    )
    first_grad, packet = settle(first_sums[0], first_got, back, squares, devices, feature)
    packets = exchange(packet)
    input_grad = give_back(slot, back.reshape(count, -1))
    grad_norm, *new = finish(
        packets, first_grad, up_grad, down_grad,
        (wide_weight, wide_moment, wide_average),
        (down_weight, down_moment, down_average),
        (vector_weight, vector_moment, vector_average),
    )
    return (block_output, input_grad, grad_norm.reshape(()), *new)


def solution(mesh):
    placed = (
        P("dev", None),
        P("dev", None),
        P("dev"),
        P("dev", None),
        P("dev", None),
        P("dev", None),
        P("dev", None),
        P("dev", None),
        P("dev", None),
        P(),
        P(),
        P(),
    )
    return jax.shard_map(
        body,
        mesh=mesh,
        in_specs=placed,
        out_specs=(
            P("dev", None),
            P("dev", None),
            P(),
            P("dev", None),
            P("dev", None),
            P("dev", None),
            P("dev", None),
            P("dev", None),
            P("dev", None),
            P(),
            P(),
            P(),
        ),
        check_vma=False,
    )
```

```python
import math

import jax
import jax.numpy as jnp
from jax import lax
from jax.experimental import pallas as pl
from jax.experimental.pallas import tpu as pltpu
from jax.sharding import PartitionSpec as P

HEADS = 12
HEAD = 64
FF = 3072
DOCS_DEV = 4
PLANE = 8
MIB = 1 << 20


epsilon = 1e-05
masked_value = -1e30
momentum = 0.9
learn_rate = 0.01
decay_rate = 0.0001
average_rate = 0.8
clip_norm = 2048.0


def norm_rows(values, gain_row, shift_row):
    center = values - jnp.mean(values, -1, keepdims=True)
    spread = jnp.mean(center * center, -1, keepdims=True)
    return center * lax.rsqrt(spread + epsilon) * gain_row + shift_row


def gelu_exact(values):
    return jax.nn.gelu(values, approximate=False)


def product(matrix, other):
    return jnp.dot(matrix, other, preferred_element_type=jnp.float32)


def against(matrix, other):
    return lax.dot_general(
        matrix, other, (((1,), (1,)), ((), ())), preferred_element_type=jnp.float32
    )


def inner_rows(matrix, other):
    return lax.dot_general(
        matrix, other, (((0,), (0,)), ((), ())), preferred_element_type=jnp.float32
    )


def advance(weight, moment, average, gradient, factor, decay_term):
    update = factor * gradient + decay_term * weight
    new_moment = momentum * moment + update
    new_weight = weight - learn_rate * (update + momentum * new_moment)
    new_average = average_rate * average + (1.0 - average_rate) * new_weight
    return (new_weight, new_moment, new_average)


def routing(segment_ids, devices, capacity):
    row_count = segment_ids.shape[0]
    is_live = segment_ids >= 0
    target = jnp.where(is_live, segment_ids // DOCS_DEV, devices)
    onehot = (target[:, None] == jnp.arange(devices, dtype=jnp.int32)[None, :]).astype(jnp.int32)
    earlier = jnp.cumsum(onehot, axis=0) - onehot
    within = jnp.sum(earlier * onehot, axis=1)
    slot_of = jnp.where(is_live, target * capacity + within, row_count)
    anchor = (
        jnp.full((row_count,), row_count, jnp.int32)
        .at[slot_of]
        .set(jnp.arange(row_count, dtype=jnp.int32), mode="drop")
    )
    return (is_live, jnp.minimum(slot_of, row_count - 1), anchor)


def plain_body(
    tokens,
    cotangent,
    segment_ids,
    wide_weight,
    wide_moment,
    wide_average,
    down_weight,
    down_moment,
    down_average,
    vector_weight,
    vector_moment,
    vector_average,
):
    wide_full, down_full = (
        lax.all_gather(wide_weight.astype(jnp.bfloat16), "dev", axis=0, tiled=True),
        lax.all_gather(down_weight.astype(jnp.bfloat16), "dev", axis=0, tiled=True),
    )
    devices = lax.axis_size("dev")
    row_count, feature = tokens.shape
    capacity = row_count // devices
    is_live, slot_of, anchor = routing(segment_ids, devices, capacity)
    blank_row = jnp.zeros((1, feature), jnp.bfloat16)
    send_rows = jnp.concatenate([tokens, blank_row], 0)[anchor].reshape(devices, capacity, feature)
    send_grads = jnp.concatenate([cotangent, blank_row], 0)[anchor].reshape(
        devices, capacity, feature
    )
    send_ids = jnp.concatenate([segment_ids, jnp.full((1,), -1, jnp.int32)], 0)[anchor].reshape(
        devices, capacity
    )
    work_rows, work_grads, work_ids = (
        lax.all_to_all(send_rows, "dev", split_axis=0, concat_axis=0, tiled=True),
        lax.all_to_all(send_grads, "dev", split_axis=0, concat_axis=0, tiled=True),
        lax.all_to_all(send_ids, "dev", split_axis=0, concat_axis=0, tiled=True),
    )
    work_rows = work_rows.reshape(row_count, feature)
    work_grads = work_grads.reshape(row_count, feature)
    work_ids = work_ids.reshape(row_count)
    gain_one, shift_one, gain_two, shift_two, bias_query, bias_value, bias_out, bias_down = [
        vector_weight[row_index] for row_index in range(8)
    ]
    bias_up = vector_weight[8:].reshape(FF)
    w_qkv = wide_full[:, : 3 * feature]
    w_out = wide_full[:, 3 * feature : 4 * feature]
    w_up = wide_full[:, 4 * feature :]
    work_float = work_rows.astype(jnp.float32)
    low_one = norm_rows(work_float, gain_one, shift_one).astype(jnp.bfloat16)
    bias_all = jnp.concatenate([bias_query, jnp.zeros_like(bias_query), bias_value])
    projected = (product(low_one, w_qkv) + bias_all).astype(jnp.bfloat16)
    queries = projected[:, :feature].reshape(row_count, HEADS, HEAD)
    key_rows = projected[:, feature : 2 * feature].reshape(row_count, HEADS, HEAD)
    value_rows = projected[:, 2 * feature :].reshape(row_count, HEADS, HEAD)
    same_seg = work_ids[:, None] == work_ids[None, :]
    block_rows = min(512, row_count)
    group_size = math.gcd(HEADS, 4)
    group_count = HEADS // group_size

    def scores_of(offset, first_head):
        query_part = queries[offset : offset + block_rows, first_head : first_head + group_size]
        raw_scores = (
            jnp.einsum(
                "qhd,khd->hqk",
                query_part,
                key_rows[:, first_head : first_head + group_size],
                preferred_element_type=jnp.float32,
            )
            * 0.125
        )
        return jnp.where(same_seg[None], raw_scores, masked_value)

    stored = []
    offset = 0
    head_outs = []
    for group in range(group_count):
        first_head = group * group_size
        scores = scores_of(offset, first_head)
        row_max = jnp.max(scores, -1, keepdims=True)
        powers = jnp.exp(scores - row_max)
        row_sums = jnp.sum(powers, -1, keepdims=True)
        prob_low = (powers / row_sums).astype(jnp.bfloat16)
        head_outs.append(
            jnp.einsum(
                "hqk,khd->qhd",
                prob_low,
                value_rows[:, first_head : first_head + group_size],
                preferred_element_type=jnp.float32,
            )
        )
        stored.append((row_max, row_sums))
    out_blocks = jnp.concatenate(head_outs, 1)
    attended = out_blocks.reshape(row_count, feature).astype(jnp.bfloat16)
    resid = work_float + product(attended, w_out) + bias_out
    low_two = norm_rows(resid, gain_two, shift_two).astype(jnp.bfloat16)
    up_float = product(low_two, w_up) + bias_up
    hidden = gelu_exact(up_float).astype(jnp.bfloat16)
    output_low = (resid + product(hidden, down_full) + bias_down).astype(jnp.bfloat16)
    dy_float = work_grads.astype(jnp.float32)
    dhidden = against(work_grads, down_full)
    gelu_pull = jax.vjp(gelu_exact, up_float)[1]
    dup_low = gelu_pull(dhidden)[0].astype(jnp.bfloat16)
    da_two = against(dup_low, w_up)
    norm_two_pull = jax.vjp(norm_rows, resid, gain_two, shift_two)[1]
    dres_norm, dgain_two, dshift_two = norm_two_pull(da_two)
    dresid = dy_float + dres_norm
    dres_low = dresid.astype(jnp.bfloat16)
    dattended = against(dres_low, w_out).astype(jnp.bfloat16).reshape(row_count, HEADS, HEAD)
    dkey_parts = [
        jnp.zeros((row_count, group_size, HEAD), jnp.float32) for group in range(group_count)
    ]
    dvalue_parts = [
        jnp.zeros((row_count, group_size, HEAD), jnp.float32) for group in range(group_count)
    ]
    position = 0
    offset = 0
    pieces = []
    for group in range(group_count):
        first_head = group * group_size
        scores = scores_of(offset, first_head)
        row_max, row_sums = stored[position]
        position += 1
        prob_float = jnp.exp(scores - row_max) / row_sums
        prob_low = prob_float.astype(jnp.bfloat16)
        dout_part = dattended[offset : offset + block_rows, first_head : first_head + group_size]
        value_part = value_rows[:, first_head : first_head + group_size]
        dvalue_parts[group] = jnp.einsum(
            "hqk,qhd->khd", prob_low, dout_part, preferred_element_type=jnp.float32
        )
        dprob = jnp.einsum(
            "qhd,khd->hqk", dout_part, value_part, preferred_element_type=jnp.float32
        )
        dscore = (prob_float * (dprob - jnp.sum(prob_float * dprob, -1, keepdims=True))).astype(
            jnp.bfloat16
        )
        pieces.append(
            jnp.einsum(
                "hqk,khd->qhd",
                dscore,
                key_rows[:, first_head : first_head + group_size],
                preferred_element_type=jnp.float32,
            )
            * 0.125
        )
        query_part = queries[offset : offset + block_rows, first_head : first_head + group_size]
        dkey_parts[group] = (
            jnp.einsum("hqk,qhd->khd", dscore, query_part, preferred_element_type=jnp.float32)
            * 0.125
        )
    dquery_blocks = jnp.concatenate(pieces, 1)
    dquery_low = dquery_blocks.reshape(row_count, feature).astype(jnp.bfloat16)
    dkey_low = jnp.concatenate(dkey_parts, 1).reshape(row_count, feature).astype(jnp.bfloat16)
    dvalue_low = jnp.concatenate(dvalue_parts, 1).reshape(row_count, feature).astype(jnp.bfloat16)
    dqkv_low = jnp.concatenate([dquery_low, dkey_low, dvalue_low], 1)
    da_one = against(dqkv_low, w_qkv)
    norm_one_pull = jax.vjp(norm_rows, work_float, gain_one, shift_one)[1]
    dinput_norm, dgain_one, dshift_one = norm_one_pull(da_one)
    dinput_low = (dresid + dinput_norm).astype(jnp.bfloat16)
    back_out, back_grad = (
        lax.all_to_all(
            output_low.reshape(devices, capacity, feature),
            "dev",
            split_axis=0,
            concat_axis=0,
            tiled=True,
        ),
        lax.all_to_all(
            dinput_low.reshape(devices, capacity, feature),
            "dev",
            split_axis=0,
            concat_axis=0,
            tiled=True,
        ),
    )
    block_output = jnp.where(
        is_live[:, None], back_out.reshape(row_count, feature)[slot_of], jnp.zeros_like(tokens)
    )
    input_grad = jnp.where(
        is_live[:, None], back_grad.reshape(row_count, feature)[slot_of], jnp.zeros_like(tokens)
    )
    vector_rows = jnp.stack(
        [
            dgain_one,
            dshift_one,
            dgain_two,
            dshift_two,
            jnp.sum(dquery_low.astype(jnp.float32), 0),
            jnp.sum(dvalue_low.astype(jnp.float32), 0),
            jnp.sum(dres_low.astype(jnp.float32), 0),
            jnp.sum(dy_float, 0),
        ],
        0,
    )
    bias_up_grad = jnp.sum(dup_low.astype(jnp.float32), 0).reshape(FF // feature, feature)
    vector_partial = jnp.concatenate([vector_rows, bias_up_grad], 0)
    down_grad = lax.psum_scatter(
        inner_rows(hidden, work_grads), "dev", scatter_dimension=0, tiled=True
    )
    wide_grad = lax.psum_scatter(
        jnp.concatenate(
            [
                inner_rows(low_one, dqkv_low),
                jnp.concatenate([inner_rows(attended, dres_low), inner_rows(low_two, dup_low)], 1),
            ],
            1,
        ),
        "dev",
        scatter_dimension=0,
        tiled=True,
    )
    shard_squares = jnp.sum(wide_grad * wide_grad) + jnp.sum(down_grad * down_grad)
    vector_grad = lax.psum(vector_partial, "dev")
    total = lax.psum(shard_squares, "dev") + jnp.sum(vector_grad * vector_grad)
    grad_norm = jnp.sqrt(total)
    factor = clip_norm / jnp.maximum(grad_norm, clip_norm)
    wide_new, wide_moment_new, wide_average_new = advance(
        wide_weight, wide_moment, wide_average, wide_grad, factor, decay_rate
    )
    down_new, down_moment_new, down_average_new = advance(
        down_weight, down_moment, down_average, down_grad, factor, decay_rate
    )
    vector_new, vector_moment_new, vector_average_new = advance(
        vector_weight, vector_moment, vector_average, vector_grad, factor, 0.0
    )
    return (
        block_output,
        input_grad,
        grad_norm,
        wide_new,
        wide_moment_new,
        wide_average_new,
        down_new,
        down_moment_new,
        down_average_new,
        vector_new,
        vector_moment_new,
        vector_average_new,
    )


def flips(devices, mask):
    return [(i, i ^ mask) for i in range(devices)]


def shifts(devices, step):
    return [(i, (i + PLANE * step) % devices) for i in range(devices)]


def place():
    me = lax.axis_index("dev")
    return jnp.stack([me // PLANE, (me // 4) % 2, (me // 2) % 2, me % 2]).astype(jnp.int32)


def core_order(core, mine, theirs):
    first = jnp.where(core == 0, mine, theirs)
    second = jnp.where(core == 0, theirs, mine)
    return first, second


def pin(*values):
    return lax.optimization_barrier(values)


def send(value, mask):
    return lax.ppermute(value, "dev", flips(lax.axis_size("dev"), mask))


def along_z(block):
    devices = lax.axis_size("dev")
    return [block] + [
        lax.ppermute(block, "dev", shifts(devices, k)) for k in range(1, devices // PLANE)
    ]


def stacked(blocks, stacks):
    depth = len(blocks)
    each = depth // stacks
    return tuple(jnp.stack(blocks[k : k + each], 0) for k in range(0, depth, each))


def to_neighbours(*own):
    return tuple(send(stack, 2) for stack in own) + tuple(send(stack, 4) for stack in own)


def to_diagonal(*near):
    if len(near) == 4:
        return send(near[0], 4), send(near[3], 2)
    half = near[0].shape[0] // 2
    return send(near[0][:half], 4), send(near[1][half:], 2)


def to_partner(*pieces):
    return tuple(send(piece, 1) for piece in pieces)


def total_of(*terms):
    return sum(term.astype(jnp.float32) for term in terms)


def low_sum(*terms):
    return total_of(*terms).astype(jnp.bfloat16)


class Fold:
    def __init__(self, mine, got):
        self.mine, self.got = mine, got
        self.half = mine.shape[1] // 2

    def pair(self, spot, steps):
        return self.mine[spot, steps], self.got[spot, steps]

    def diagonal(self):
        first, last = slice(None, self.half), slice(self.half, None)
        return low_sum(*self.pair(3, first)), low_sum(*self.pair(3, last))

    def neighbours(self, got_a, got_b):
        first, last = slice(None, self.half), slice(self.half, None)
        to_x = (low_sum(*self.pair(1, first), got_a), low_sum(*self.pair(1, last)))
        to_y = (low_sum(*self.pair(2, first)), low_sum(*self.pair(2, last), got_b))
        return jnp.concatenate(to_x, 0), jnp.concatenate(to_y, 0)

    def column(self, got_x, got_y):
        total = total_of(*self.pair(0, slice(None)), got_x, got_y)
        return (total[0],) + tuple(
            total[k].astype(jnp.bfloat16) for k in range(1, total.shape[0])
        )


def over_diagonal(to_a, to_b):
    return send(to_a, 4), send(to_b, 2)


def over_plane(to_x, to_y):
    return send(to_x, 2), send(to_y, 4)


def over_column(sums):
    devices = lax.axis_size("dev")
    return tuple(lax.ppermute(sums[k], "dev", shifts(devices, k)) for k in range(1, len(sums)))


def exchange(rows):
    return lax.all_to_all(rows, "dev", split_axis=0, concat_axis=0, tiled=True)


FAR = pl.BlockSpec(memory_space=pltpu.HBM)
SCALARS = pl.BlockSpec(memory_space=pltpu.SMEM)


def whole(*shape):
    return pl.BlockSpec(shape, lambda *_: (0,) * len(shape))


LIMIT = 48


def settings(limit):
    return pltpu.CompilerParams(vmem_limit_bytes=limit * MIB)


def cost(flops, moved, exps=0):
    return pl.CostEstimate(flops=int(flops), bytes_accessed=int(moved), transcendentals=int(exps))


def shaped(shape, dtype):
    return jax.ShapeDtypeStruct(shape, dtype)


def by_rows(matrix, other):
    return lax.dot_general(
        matrix, other, (((1,), (1,)), ((), ())), preferred_element_type=jnp.float32
    )


def by_columns(matrix, other):
    return lax.dot_general(
        matrix, other, (((0,), (0,)), ((), ())), preferred_element_type=jnp.float32
    )


def normed(values):
    center = values - jnp.mean(values, -1, keepdims=True)
    scale = lax.rsqrt(jnp.mean(center * center, -1, keepdims=True) + epsilon)
    return center * scale, scale


def norm_back(grad, gain, unit, scale):
    inner = grad * gain
    return scale * (
        inner
        - jnp.mean(inner, -1, keepdims=True)
        - unit * jnp.mean(inner * unit, -1, keepdims=True)
    )


def iota(shape, axis):
    return lax.broadcasted_iota(jnp.int32, shape, axis)


def slots_of(ids_row, capacity, groups):
    count = ids_row.shape[1]
    square = (count, count)
    ids = jnp.sum(
        jnp.where(iota(square, 0) == iota(square, 1), ids_row, 0), axis=1, keepdims=True
    )
    group = jnp.right_shift(ids, DOCS_DEV.bit_length() - 1)
    lanes = max(128, groups)
    onehot = jnp.where(group == iota((count, lanes), 1), 1.0, 0.0)
    lower = jnp.where(iota(square, 0) > iota(square, 1), 1.0, 0.0).astype(jnp.bfloat16)
    earlier = product(lower, onehot.astype(jnp.bfloat16))
    within = jnp.sum(earlier * onehot, axis=1, keepdims=True).astype(jnp.int32)
    return ids, jnp.where(ids >= 0, group * capacity + within, -1)


def route(ids_row, tokens, cotangent, devices):
    count, feature = tokens.shape

    def kernel(ids_ref, tokens_ref, cotangent_ref, rows_ref, grads_ref, slot_ref):
        ids, slot = slots_of(ids_ref[...], count // devices, devices)
        slot_ref[...] = slot
        move = jnp.where(slot == iota((count, count), 1), 1.0, 0.0).astype(jnp.bfloat16)
        code = jnp.where(ids >= 0, jnp.bitwise_and(ids, DOCS_DEV - 1) + 1, 0)
        code = jnp.broadcast_to(code.astype(jnp.float32), (count, 128)).astype(jnp.bfloat16)
        rows_ref[:, :feature] = by_columns(move, tokens_ref[...]).astype(jnp.bfloat16)
        rows_ref[:, feature:] = by_columns(move, code).astype(jnp.bfloat16)
        grads_ref[...] = by_columns(move, cotangent_ref[...]).astype(jnp.bfloat16)

    return pl.pallas_call(
        kernel,
        out_shape=[
            shaped((count, feature + 128), jnp.bfloat16),
            shaped((count, feature), jnp.bfloat16),
            shaped((count, 1), jnp.int32),
        ],
        compiler_params=settings(LIMIT),
        cost_estimate=cost(4 * count * count * feature, 8 * count * feature),
    )(ids_row, tokens, cotangent)


def give_back(slot, rows):
    count, feature = rows.shape[0], rows.shape[1] // 256 * 256

    def kernel(slot_ref, rows_ref, out_ref):
        move = jnp.where(slot_ref[...] == iota((count, count), 1), 1.0, 0.0).astype(jnp.bfloat16)
        out_ref[...] = product(move, rows_ref[...]).astype(jnp.bfloat16)

    return pl.pallas_call(
        kernel,
        grid=(1,),
        out_shape=shaped((count, feature), jnp.bfloat16),
        in_specs=[whole(count, 1), whole(count, feature)],
        out_specs=whole(count, feature),
        compiler_params=settings(LIMIT),
        cost_estimate=cost(2 * count * count * feature, 4 * count * feature),
    )(slot, rows)


def pieces_of(where_ref, pieces):
    z, y, x, core = where_ref[0], where_ref[1], where_ref[2], where_ref[3]
    count = len(pieces) // 2
    depth = 2 * pieces[count - 1].shape[0]
    columns = ((y, x), (y, 1 - x), (1 - y, x), (1 - y, 1 - x))
    for part, group in ((core, pieces[:count]), (1 - core, pieces[count:])):
        reached = 0
        for piece in group:
            for index in range(piece.shape[0]):
                yy, xx = columns[reached // depth]
                step = reached % depth
                zz = lax.rem(z - step + depth, depth)
                yield piece.at[index], step, (zz * 2 + yy) * 2 + xx, part
                reached += 1


def wide_copies(where_ref, pieces, buffer, sems):
    copies = []
    for source, _, chip, part in pieces_of(where_ref, pieces):
        rows, columns = source.shape
        target = buffer.at[
            pl.ds(pl.multiple_of(chip * rows, 16), rows),
            pl.ds(pl.multiple_of(part * columns, 128), columns),
        ]
        copies.append(pltpu.make_async_copy(source, target, sems.at[len(copies)]))
    return copies


def down_copies(where_ref, pieces, buffer, sems):
    copies = []
    for source, _, chip, part in pieces_of(where_ref, pieces):
        rows = source.shape[0]
        row = pl.multiple_of((chip * 2 + part) * rows, 16)
        copies.append(
            pltpu.make_async_copy(source, buffer.at[pl.ds(row, rows)], sems.at[len(copies)])
        )
    return copies


def project(where, work, vector, pieces):
    count, feature = work.shape[0], vector.shape[1]
    copies_count = sum(piece.shape[0] for piece in pieces)
    tile = 256

    def kernel(where_ref, work_ref, vector_ref, *refs):
        (
            flipped_ref, out_ref, weights_ref, output_ref, low, buffer, sems, store_sems
        ) = refs[len(pieces):]
        copies = wide_copies(where_ref, refs[:len(pieces)], buffer, sems)
        for copy in copies:
            copy.start()

        def rows_of(index, carry):
            rows = pl.ds(pl.multiple_of(index * 64, 64), 64)
            unit, _ = normed(work_ref[rows, :].astype(jnp.float32))
            low[rows, :] = (unit * vector_ref[0:1, :] + vector_ref[1:2, :]).astype(jnp.bfloat16)
            return carry

        lax.fori_loop(0, count // 64, rows_of, 0)
        flipped_ref[...] = low[...].astype(jnp.float32).T.astype(jnp.bfloat16)
        for copy in copies:
            copy.wait()
        stores = [
            pltpu.make_async_copy(
                buffer.at[:, pl.ds(0, 3 * feature)], weights_ref, store_sems.at[0]
            ),
            pltpu.make_async_copy(
                buffer.at[:, pl.ds(3 * feature, feature)], output_ref, store_sems.at[1]
            ),
        ]
        for store in stores:
            store.start()
        for part, bias in ((0, 4), (1, None), (2, 5)):

            def columns_of(index, carry):
                inner = pl.ds(pl.multiple_of(index * tile, tile), tile)
                columns = pl.ds(pl.multiple_of(part * feature + index * tile, tile), tile)
                value = product(low[...], buffer[:, columns])
                if bias is not None:
                    value = value + vector_ref[bias : bias + 1, inner]
                out_ref[:, columns] = value.astype(jnp.bfloat16)
                return carry

            lax.fori_loop(0, feature // tile, columns_of, 0)
        for store in stores:
            store.wait()

    return pl.pallas_call(
        kernel,
        grid=(1,),
        out_shape=[
            shaped((feature, count), jnp.bfloat16),
            shaped((count, 3 * feature), jnp.bfloat16),
            shaped((feature, 3 * feature), jnp.bfloat16),
            shaped((feature, feature), jnp.bfloat16),
        ],
        in_specs=[SCALARS, whole(count, feature), whole(*vector.shape)] + [FAR] * len(pieces),
        out_specs=[whole(feature, count), whole(count, 3 * feature), FAR, FAR],
        scratch_shapes=[
            pltpu.VMEM((count, feature), jnp.bfloat16),
            pltpu.VMEM((feature, 4 * feature), jnp.bfloat16),
            pltpu.SemaphoreType.DMA((copies_count,)),
            pltpu.SemaphoreType.DMA((2,)),
        ],
        compiler_params=settings(60),
        cost_estimate=cost(6 * count * feature * feature, 12 * feature * feature),
    )(where, work, vector, *pieces)


def fill_cap(code_ref, cap):
    code = code_ref[...].astype(jnp.float32)
    cap[...] = jnp.where(code[:, :1] == code.T[:1], -masked_value, masked_value)


def one_head(values, head):
    lanes = iota(values.shape, 1)
    inside = (lanes >= head * HEAD) & (lanes < (head + 1) * HEAD)
    return jnp.where(inside, values, 0.0).astype(jnp.bfloat16)


def attend(projected, work, vector, weights, first, pairs, left=None):
    count, feature = work.shape[0], vector.shape[1]
    all_pairs = feature // 128
    tile = 512
    ends = left is not None

    def kernel(q_ref, k_ref, v_ref, code_ref, *refs):
        if ends:
            (
                weight_ref, work_ref, vector_ref, left_ref, flipped_ref, stat_ref, resid_ref, low_ref,
                cap, right, total,
            ) = refs
        else:
            flipped_ref, stat_ref, attended_ref, cap = refs
        pair = pl.program_id(0)

        @pl.when(pair == 0)
        def _():
            fill_cap(code_ref, cap)

        keys = k_ref[...]
        values = v_ref[...].astype(jnp.float32).T.astype(jnp.bfloat16)
        scaled = q_ref[...].astype(jnp.float32) * 0.125
        heads = []
        for head in range(2):
            query = one_head(scaled, head)
            parts = []
            for start in range(0, count, tile):
                span = slice(start, start + tile)
                scores = jnp.minimum(by_rows(keys, query[span]), cap[:, span])
                most = jnp.max(scores, 0, keepdims=True)
                powers = jnp.exp(scores - most)
                sums = jnp.sum(powers, 0, keepdims=True)
                stat_ref[0, head : head + 1, span] = most + jnp.log(sums)
                mixed = product(
                    values[head * HEAD : (head + 1) * HEAD], powers.astype(jnp.bfloat16)
                )
                parts.append(mixed * (1.0 / sums))
            heads.append(jnp.concatenate(parts, 1))
        both = jnp.concatenate(heads, 0)
        flipped_ref[...] = both.astype(jnp.bfloat16)
        attended = both.T.astype(jnp.bfloat16)
        if ends:
            right[pair] = attended
        else:
            attended_ref[...] = attended

        if ends:

            @pl.when(pair == pairs - 1)
            def _():
                middle = feature - pairs * 128
                for start in range(0, feature, 256):
                    span = slice(start, start + 256)
                    value = product(left_ref[...], weight_ref[:middle, span])
                    for index in range(pairs):
                        rows = slice(middle + index * 128, middle + (index + 1) * 128)
                        value = value + product(right[index], weight_ref[rows, span])
                    total[:, span] = value

                def rows_of(index, carry):
                    rows = pl.ds(pl.multiple_of(index * 64, 64), 64)
                    resid = (
                        work_ref[rows, :].astype(jnp.float32) + total[rows, :] + vector_ref[6:7, :]
                    )
                    resid_ref[rows, :] = resid
                    unit, _ = normed(resid)
                    low_ref[rows, :] = (unit * vector_ref[2:3, :] + vector_ref[3:4, :]).astype(
                        jnp.bfloat16
                    )
                    return carry

                lax.fori_loop(0, count // 64, rows_of, 0)

    def columns_at(offset):
        return pl.BlockSpec((count, 128), lambda pair: (0, offset + pair))

    wide = whole(count, feature)
    return pl.pallas_call(
        kernel,
        grid=(pairs,),
        out_shape=[
            shaped((pairs * 128, count), jnp.bfloat16),
            shaped((pairs, 8, count), jnp.float32),
        ]
        + (
            [shaped((count, feature), jnp.float32), shaped((count, feature), jnp.bfloat16)]
            if ends
            else [shaped((count, pairs * 128), jnp.bfloat16)]
        ),
        in_specs=[
            columns_at(first),
            columns_at(all_pairs + first),
            columns_at(2 * all_pairs + first),
            pl.BlockSpec((count, 128), lambda pair: (0, all_pairs)),
        ]
        + (
            [whole(feature, feature), wide, whole(*vector.shape), whole(*left.shape)]
            if ends
            else []
        ),
        out_specs=[
            pl.BlockSpec((128, count), lambda pair: (pair, 0)),
            pl.BlockSpec((1, 8, count), lambda pair: (pair, 0, 0)),
        ]
        + ([wide, wide] if ends else [columns_at(0)]),
        scratch_shapes=[pltpu.VMEM((count, count), jnp.float32)]
        + (
            [
                pltpu.VMEM((pairs, count, 128), jnp.bfloat16),
                pltpu.VMEM((count, feature), jnp.float32),
            ]
            if ends
            else []
        ),
        compiler_params=settings(60),
        cost_estimate=cost(
            8 * count * count * pairs * 128, 14 * count * feature, 2 * pairs * count * count
        ),
    )(
        projected, projected, projected, work,
        *([weights, work, vector, left] if ends else []),
    )


def widen(where, low, bias_row, pieces):
    count, feature = low.shape
    wide = bias_row.shape[1]
    tile = feature
    steps = wide // tile

    def kernel(where_ref, low_ref, bias_ref, *refs):
        hidden_ref, slope_ref, weights_ref, buffer, sems, store_sem = refs[len(pieces):]
        step = pl.program_id(0)
        store = pltpu.make_async_copy(buffer, weights_ref, store_sem)

        @pl.when(step == 0)
        def _():
            copies = wide_copies(where_ref, refs[:len(pieces)], buffer, sems)
            for copy in copies:
                copy.start()
            for copy in copies:
                copy.wait()
            store.start()

        columns = pl.ds(pl.multiple_of(step * tile, tile), tile)
        up = product(low_ref[...], buffer[:, columns]) + bias_ref[...]
        below = 0.5 * (1.0 + lax.erf(up * (0.5**0.5)))
        hidden_ref[...] = (up * below).astype(jnp.bfloat16)
        slope_ref[...] = below + up * (jnp.exp(-0.5 * up * up) * ((2.0 * math.pi) ** -0.5))

        @pl.when(step == steps - 1)
        def _():
            store.wait()

    block = pl.BlockSpec((count, tile), lambda step: (0, step))
    return pl.pallas_call(
        kernel,
        grid=(steps,),
        out_shape=[
            shaped((count, wide), jnp.bfloat16),
            shaped((count, wide), jnp.float32),
            shaped((feature, wide), jnp.bfloat16),
        ],
        in_specs=[
            SCALARS,
            whole(count, feature),
            pl.BlockSpec((1, tile), lambda step: (0, step)),
        ]
        + [FAR] * len(pieces),
        out_specs=[block, block, FAR],
        scratch_shapes=[
            pltpu.VMEM((feature, wide), jnp.bfloat16),
            pltpu.SemaphoreType.DMA((sum(piece.shape[0] for piece in pieces),)),
            pltpu.SemaphoreType.DMA,
        ],
        compiler_params=settings(60),
        cost_estimate=cost(
            2 * count * feature * wide, 2 * feature * wide + 6 * count * wide, count * wide
        ),
    )(where, low, bias_row, *pieces)


def down_gradient(where, hidden, grads, depth):
    count, wide = hidden.shape
    feature = grads.shape[1]
    rows = wide // (depth * PLANE)
    part = wide // depth

    def kernel(where_ref, hidden_ref, grads_ref, mine_ref, theirs_ref, result):
        y, x, core = where_ref[1], where_ref[2], where_ref[3]
        result[...] = by_columns(hidden_ref[...], grads_ref[...])
        for yy in range(2):
            for xx in range(2):
                spot = jnp.bitwise_xor(y, yy) * 2 + jnp.bitwise_xor(x, xx)
                first = (yy * 2 + xx) * 2
                for target, side in ((mine_ref, core), (theirs_ref, 1 - core)):
                    row = pl.multiple_of((first + side) * rows, 16)
                    target[spot, 0] = result[pl.ds(row, rows), :].astype(jnp.bfloat16)

    shape = shaped((4, depth, rows, feature), jnp.bfloat16)
    block = pl.BlockSpec((4, 1, rows, feature), lambda step, where_ref: (0, step, 0, 0))
    return pl.pallas_call(
        kernel,
        out_shape=[shape, shape],
        grid_spec=pltpu.PrefetchScalarGridSpec(
            num_scalar_prefetch=1,
            grid=(depth,),
            in_specs=[
                pl.BlockSpec(
                    (count, part),
                    lambda step, where_ref: (0, lax.rem(where_ref[0] + step, depth)),
                ),
                whole(count, feature),
            ],
            out_specs=[block, block],
            scratch_shapes=[pltpu.VMEM((part, feature), jnp.float32)],
        ),
        compiler_params=settings(LIMIT),
        cost_estimate=cost(2 * count * wide * feature, 2 * wide * (count + feature)),
    )(where, hidden, grads)


def put_wide(where_ref, result, mine_ref, theirs_ref):
    z, y, x, core = where_ref[0], where_ref[1], where_ref[2], where_ref[3]
    _, depth, rows, _ = mine_ref.shape
    for chip in range(4 * depth):
        zz, yy, xx = chip // 4, (chip // 2) % 2, chip % 2
        step = lax.rem(zz - z + depth, depth)
        spot = jnp.bitwise_xor(y, yy) * 2 + jnp.bitwise_xor(x, xx)
        for target, side in ((mine_ref, core), (theirs_ref, 1 - core)):
            row = pl.multiple_of((chip * 2 + side) * rows, 8)
            target[spot, step] = result[pl.ds(row, rows), :].astype(jnp.bfloat16)


def narrow(where, hidden, resid, vector, pieces):
    count, wide = hidden.shape
    feature = resid.shape[1]
    tile = 256

    def kernel(where_ref, hidden_ref, resid_ref, vector_ref, *refs):
        out_ref, weights_ref, buffer, sems, store_sem = refs[len(pieces):]
        copies = down_copies(where_ref, refs[:len(pieces)], buffer, sems)
        for copy in copies:
            copy.start()
        for copy in copies:
            copy.wait()
        store = pltpu.make_async_copy(buffer, weights_ref, store_sem)
        store.start()

        def columns_of(index, carry):
            columns = pl.ds(pl.multiple_of(index * tile, tile), tile)
            value = product(hidden_ref[...], buffer[:, columns])
            out_ref[:, columns] = (
                resid_ref[:, columns] + (value + vector_ref[7:8, columns])
            ).astype(jnp.bfloat16)
            return carry

        lax.fori_loop(0, feature // tile, columns_of, 0)
        store.wait()

    return pl.pallas_call(
        kernel,
        grid=(1,),
        out_shape=[
            shaped((count, feature), jnp.bfloat16),
            shaped((wide, feature), jnp.bfloat16),
        ],
        in_specs=[SCALARS, whole(count, wide), whole(count, feature), whole(*vector.shape)]
        + [FAR] * len(pieces),
        out_specs=[whole(count, feature), FAR],
        scratch_shapes=[
            pltpu.VMEM((wide, feature), jnp.bfloat16),
            pltpu.SemaphoreType.DMA((sum(piece.shape[0] for piece in pieces),)),
            pltpu.SemaphoreType.DMA,
        ],
        compiler_params=settings(LIMIT),
        cost_estimate=cost(2 * count * wide * feature, 6 * wide * feature),
    )(where, hidden, resid, vector, *pieces)


def feed_back(where, slope, low, grads, resid, vector, up_weights, down_weights, attended, depth):
    count, wide = slope.shape
    feature = resid.shape[1]
    tile = feature
    steps = wide // tile
    half = feature // 2
    chip_rows = feature // (PLANE * depth)

    def kernel(
        where_ref, slope_ref, low_ref, grads_ref, resid_ref, vector_ref, up_ref, down_ref, left_ref, right_ref,
        dresid_ref, dlow_ref, sums_ref, bias_ref, mine_ref, theirs_ref, back, flipped, result,
    ):
        step = pl.program_id(0)

        @pl.when(step == 0)
        def _():
            flipped[...] = low_ref[...].astype(jnp.float32).T.astype(jnp.bfloat16)
            back[...] = jnp.zeros_like(back)

        @pl.when(step < steps)
        def _():
            dup = (slope_ref[...] * by_rows(grads_ref[...], down_ref[...])).astype(jnp.bfloat16)
            bias_ref[...] = jnp.sum(dup.astype(jnp.float32), 0, keepdims=True)
            back[...] += by_rows(dup, up_ref[...])
            result[...] = product(flipped[...], dup)

        @pl.when(step == steps)
        def _():
            sums_ref[...] = jnp.zeros_like(sums_ref)

            def rows_of(index, carry):
                rows = pl.ds(pl.multiple_of(index * 64, 64), 64)
                unit, scale = normed(resid_ref[rows, :])
                da = back[rows, :]
                dy = grads_ref[rows, :].astype(jnp.float32)
                dresid = dy + norm_back(da, vector_ref[2:3, :], unit, scale)
                dresid_ref[rows, :] = dresid
                dlow = dresid.astype(jnp.bfloat16)
                dlow_ref[rows, :] = dlow
                for row, value in enumerate((da * unit, da, dlow.astype(jnp.float32), dy)):
                    sums_ref[row : row + 1, :] += jnp.sum(value, 0, keepdims=True)
                return carry

            lax.fori_loop(0, count // 64, rows_of, 0)
            result[:half, :] = product(left_ref[...], dlow_ref[...])
            result[half:, :] = product(right_ref[...], dlow_ref[...])

        put_wide(where_ref, result, mine_ref, theirs_ref)

    def at(step):
        return jnp.minimum(step, steps - 1)

    def columns_at(rows):
        return pl.BlockSpec((rows, tile), lambda step: (0, at(step)))

    all_rows = whole(count, feature)
    split = shaped((4, depth, chip_rows, (steps + 1) * feature), jnp.bfloat16)
    block = pl.BlockSpec((4, depth, chip_rows, feature), lambda step: (0, 0, 0, step))
    return pl.pallas_call(
        kernel,
        grid=(steps + 1,),
        out_shape=[
            shaped((count, feature), jnp.float32),
            shaped((count, feature), jnp.bfloat16),
            shaped((8, feature), jnp.float32),
            shaped((1, wide), jnp.float32),
            split,
            split,
        ],
        in_specs=[
            SCALARS,
            columns_at(count),
            all_rows,
            all_rows,
            all_rows,
            whole(*vector.shape),
            columns_at(feature),
            pl.BlockSpec((tile, feature), lambda step: (at(step), 0)),
            whole(half, count),
            whole(half, count),
        ],
        out_specs=[all_rows, all_rows, whole(8, feature), columns_at(1), block, block],
        scratch_shapes=[
            pltpu.VMEM((count, feature), jnp.float32),
            pltpu.VMEM((feature, count), jnp.bfloat16),
            pltpu.VMEM((feature, feature), jnp.float32),
        ],
        compiler_params=settings(60),
        cost_estimate=cost(6 * count * wide * feature, 8 * wide * feature + 10 * count * wide),
    )(where, slope, low, grads, resid, vector, up_weights, down_weights, *attended)


def attend_back(projected, work, stats, dlow, weights, first, pairs):
    count, feature = dlow.shape
    all_pairs = feature // 128
    tile = 512
    wide = pairs * 128

    def kernel(
        q_ref, k_ref, v_ref, code_ref, stat_ref, dlow_ref, weight_ref, out_ref, sums_ref, douts, cap
    ):
        pair = pl.program_id(0)

        @pl.when(pair == 0)
        def _():
            fill_cap(code_ref, cap)
            for start in range(0, wide, 128):
                span = slice(start, start + 128)
                douts[start // 128] = by_rows(dlow_ref[...], weight_ref[span, :]).astype(
                    jnp.bfloat16
                )

        keys, values = k_ref[...], v_ref[...]
        wide_keys = keys.astype(jnp.float32)
        dquery = jnp.zeros((count, 128), jnp.float32)
        scaled = q_ref[...].astype(jnp.float32) * 0.125
        dout = douts[pair].astype(jnp.float32)
        dkey = jnp.zeros((count, 128), jnp.float32)
        dvalue = jnp.zeros((count, 128), jnp.float32)
        for head in range(2):
            query = one_head(scaled, head)
            dhead = one_head(dout, head)
            for start in range(0, count, tile):
                span = slice(start, start + tile)
                scores = jnp.minimum(by_rows(keys, query[span]), cap[:, span])
                probs = jnp.exp(scores - stat_ref[0, head : head + 1, span])
                dprob = by_rows(values, dhead[span])
                inner = jnp.sum(probs * dprob, 0, keepdims=True)
                dscore = (probs * (dprob - inner)).astype(jnp.bfloat16)
                dvalue = dvalue + product(probs.astype(jnp.bfloat16), dhead[span])
                dkey = dkey + product(dscore, query[span])
                dquery = dquery + by_columns(dscore, one_head(wide_keys, head))
        dquery = (dquery * 0.125).astype(jnp.bfloat16)
        dvalue = dvalue.astype(jnp.bfloat16)
        out_ref[0] = dquery
        out_ref[1] = dkey.astype(jnp.bfloat16)
        out_ref[2] = dvalue
        sums_ref[0:1, :] = jnp.sum(dquery.astype(jnp.float32), 0, keepdims=True)
        sums_ref[1:2, :] = jnp.sum(dvalue.astype(jnp.float32), 0, keepdims=True)

    def columns_at(offset):
        return pl.BlockSpec((count, 128), lambda pair: (0, offset + pair))

    return pl.pallas_call(
        kernel,
        grid=(pairs,),
        out_shape=[
            shaped((3, count, wide), jnp.bfloat16),
            shaped((8, wide), jnp.float32),
        ],
        in_specs=[
            columns_at(first),
            columns_at(all_pairs + first),
            columns_at(2 * all_pairs + first),
            pl.BlockSpec((count, 128), lambda pair: (0, all_pairs)),
            pl.BlockSpec((1, 8, count), lambda pair: (pair, 0, 0)),
            whole(count, feature),
            pl.BlockSpec((wide, feature), lambda pair: (first // pairs, 0)),
        ],
        out_specs=[
            pl.BlockSpec((3, count, 128), lambda pair: (0, 0, pair)),
            pl.BlockSpec((8, 128), lambda pair: (0, pair)),
        ],
        scratch_shapes=[
            pltpu.VMEM((pairs, count, 128), jnp.bfloat16),
            pltpu.VMEM((count, count), jnp.float32),
        ],
        compiler_params=settings(LIMIT),
        cost_estimate=cost(
            14 * count * count * wide, 16 * count * feature, 2 * pairs * count * count
        ),
    )(projected, projected, projected, work, stats, dlow, weights)


def first_gradient(where, flipped, dprojected, depth):
    feature, count = flipped.shape
    half = feature // 2
    rows = feature // (PLANE * depth)

    def kernel(where_ref, flipped_ref, d_ref, e_ref, mine_ref, theirs_ref, result):
        result[:, :half] = product(flipped_ref[...], d_ref[0])
        result[:, half:] = product(flipped_ref[...], e_ref[0])
        put_wide(where_ref, result, mine_ref, theirs_ref)

    shape = shaped((4, depth, rows, 3 * feature), jnp.bfloat16)
    block = pl.BlockSpec((4, depth, rows, feature), lambda step: (0, 0, 0, step))
    part = pl.BlockSpec((1, count, half), lambda step: (step, 0, 0))
    return pl.pallas_call(
        kernel,
        grid=(3,),
        out_shape=[shape, shape],
        in_specs=[SCALARS, whole(feature, count), part, part],
        out_specs=[block, block],
        scratch_shapes=[pltpu.VMEM((feature, feature), jnp.float32)],
        compiler_params=settings(60),
        cost_estimate=cost(6 * count * feature * feature, 16 * feature * feature),
    )(where, flipped, *dprojected)


def project_back(work, dprojected, dresid, vector, weights, sums_two, sums_attend, bias_up, devices):
    count, feature = dresid.shape
    tile = 128
    half = feature // 2
    lanes = 16 * feature // devices // 128
    capacity = count // devices

    def kernel(
        work_ref, d_ref, e_ref, dresid_ref, vector_ref, weight_ref, two_ref, left_ref, right_ref, bias_ref,
        out_ref, sums,
    ):
        sums[...] = jnp.zeros_like(sums)

        def rows_of(index, carry):
            rows = pl.ds(pl.multiple_of(index * tile, tile), tile)
            da = jnp.zeros((tile, feature), jnp.float32)
            for part in range(3):
                middle = part * feature + half
                da += by_rows(d_ref[part, rows, :], weight_ref[:, middle - half : middle])
                da += by_rows(e_ref[part, rows, :], weight_ref[:, middle : middle + half])
            unit, scale = normed(work_ref[rows, :].astype(jnp.float32))
            out_ref[rows, :feature] = (
                dresid_ref[rows, :] + norm_back(da, vector_ref[0:1, :], unit, scale)
            ).astype(jnp.bfloat16)
            sums[0:1, :] += jnp.sum(da * unit, 0, keepdims=True)
            sums[1:2, :] += jnp.sum(da, 0, keepdims=True)
            return carry

        lax.fori_loop(0, count // tile, rows_of, 0)
        sums[2:4, :] = two_ref[0:2, :]
        sums[4:6, :half] = left_ref[0:2, :]
        sums[4:6, half:] = right_ref[0:2, :]
        sums[6:8, :] = two_ref[2:4, :]
        for row in range(FF // feature):
            sums[8 + row : 9 + row, :] = bias_ref[0:1, row * feature : (row + 1) * feature]
        place_in = iota((capacity, 128), 0)
        for device in range(devices):
            block = jnp.zeros((capacity, 128), jnp.float32)
            for lane in range(lanes):
                first = device * lanes + lane
                row, column = divmod(first * 128, feature)
                value = sums[row : row + 1, column : column + 128]
                high = value.astype(jnp.bfloat16).astype(jnp.float32)
                block = jnp.where(place_in == lane, high, block)
                block = jnp.where(place_in == lanes + lane, value - high, block)
            out_ref[device * capacity : (device + 1) * capacity, feature:] = block.astype(
                jnp.bfloat16
            )

    return pl.pallas_call(
        kernel,
        grid=(1,),
        out_shape=shaped((count, feature + 128), jnp.bfloat16),
        in_specs=[
            whole(count, feature),
            whole(3, count, half),
            whole(3, count, half),
            whole(count, feature),
            whole(*vector.shape),
            whole(feature, 3 * feature),
            whole(8, feature),
            whole(8, half),
            whole(8, half),
            whole(1, FF),
        ],
        out_specs=whole(count, feature + 128),
        scratch_shapes=[pltpu.VMEM((16, feature), jnp.float32)],
        compiler_params=settings(LIMIT),
        cost_estimate=cost(6 * count * feature * feature, 6 * feature * feature),
    )(work, *dprojected, dresid, vector, weights, sums_two, *sums_attend, bias_up)


def settle(own, got, back, squares, devices, feature):
    rows, columns = own.shape
    lanes = 16 * feature // devices // 128
    capacity = back.shape[1]

    def kernel(squares_ref, own_ref, *refs):
        got_refs, (back_ref, grad_ref, packet_ref) = refs[: len(got)], refs[len(got) :]
        grad = own_ref[...]
        for ref in got_refs:
            grad += ref[...].astype(jnp.float32)
        grad_ref[...] = grad
        total = squares_ref[0, 0] + jnp.sum(grad * grad)
        sums = jnp.sum(back_ref[...].astype(jnp.float32), 0)
        packet_ref[:, :lanes, :] = jnp.broadcast_to(
            (sums[:lanes] + sums[lanes : 2 * lanes])[None], (devices, lanes, 128)
        )
        packet_ref[:, lanes:, :] = jnp.full((devices, 1, 128), total, jnp.float32)

    return pl.pallas_call(
        kernel,
        grid=(1,),
        out_shape=[
            shaped((rows, columns), jnp.float32),
            shaped((devices, lanes + 1, 128), jnp.float32),
        ],
        in_specs=[SCALARS, whole(rows, columns)]
        + [whole(rows, columns)] * len(got)
        + [pl.BlockSpec((devices, capacity, 128), lambda step: (0, 0, feature // 128))],
        out_specs=[whole(rows, columns), whole(devices, lanes + 1, 128)],
        compiler_params=settings(60),
        cost_estimate=cost(8 * rows * columns, 16 * rows * columns),
    )(squares.reshape(1, 1), own, *got, back)


def finish(packets, first_grad, up_grad, down_grad, wide, down, vector):
    devices, lanes, _ = packets.shape
    lanes -= 1
    rows, columns = wide[0].shape
    down_rows, feature = down[0].shape
    vector_rows = vector[0].shape[0]
    steps = 4
    tile, down_tile = columns // steps, down_rows // steps
    first_columns = first_grad.shape[1]

    def kernel(packets_ref, first_ref, up_ref, down_grad_ref, *refs):
        wide_refs, down_refs, vector_refs = refs[:3], refs[3:6], refs[6:9]
        norm_ref, wide_new, down_new, vector_new = refs[9], refs[10:13], refs[13:16], refs[16:19]
        sums, factor_ref = refs[19:]
        step = pl.program_id(0)

        def put(new, old, gradient, decay):
            for ref, value in zip(
                new, advance(*(ref[...] for ref in old), gradient, factor_ref[0], decay), strict=True
            ):
                ref[...] = value

        @pl.when(step == 0)
        def _():
            for place_of in range(vector_rows * feature // 128):
                device, lane = divmod(place_of, lanes)
                row, column = divmod(place_of * 128, feature)
                sums[row : row + 1, column : column + 128] = packets_ref[device, lane : lane + 1]
            gradient = sums[...]
            shares = packets_ref[:, lanes, :1]
            total = jnp.sum(shares) + jnp.sum(gradient * gradient)
            norm = jnp.sqrt(jnp.full((1, 1), total))
            norm_ref[...] = norm
            factor_ref[0] = jnp.sum(clip_norm / jnp.maximum(norm, clip_norm))
            put(vector_new, vector_refs, gradient, 0.0)

        for index in range(steps):

            @pl.when(step == index)
            def _():
                first = index * tile
                parts = []
                if first < first_columns:
                    parts.append(first_ref[:, first : min(first + tile, first_columns)])
                if first + tile > first_columns:
                    low = max(first - first_columns, 0)
                    high = first + tile - first_columns
                    if low < feature:
                        parts.append(up_ref[:, FF + low : FF + min(high, feature)])
                    if high > feature:
                        parts.append(up_ref[:, max(low - feature, 0) : high - feature])
                gradient = parts[0] if len(parts) == 1 else jnp.concatenate(parts, 1)
                put(wide_new, wide_refs, gradient, decay_rate)

        put(down_new, down_refs, down_grad_ref[...], decay_rate)

    def tiles(shape):
        return pl.BlockSpec(shape, lambda step: (0, step))

    wide_specs = [tiles((rows, tile))] * 3
    down_specs = [pl.BlockSpec((down_tile, feature), lambda step: (step, 0))] * 3
    vector_specs = [whole(vector_rows, feature)] * 3
    return pl.pallas_call(
        kernel,
        grid=(steps,),
        out_shape=[shaped((1, 1), jnp.float32)]
        + [shaped(part.shape, jnp.float32) for part in (*wide, *down, *vector)],
        in_specs=[
            whole(*packets.shape),
            whole(*first_grad.shape),
            whole(*up_grad.shape),
            down_specs[0],
        ]
        + wide_specs
        + down_specs
        + vector_specs,
        out_specs=[whole(1, 1)] + wide_specs + down_specs + vector_specs,
        scratch_shapes=[
            pltpu.VMEM((vector_rows, feature), jnp.float32),
            pltpu.SMEM((1,), jnp.float32),
        ],
        compiler_params=settings(60),
        cost_estimate=cost(20 * rows * columns, 40 * rows * columns),
    )(packets, first_grad, up_grad, down_grad, *wide, *down, *vector)


def structured(devices, feature):
    rows = feature // devices
    return devices % PLANE == 0 and feature % devices == 0 and (2 * rows) % 16 == 0


def body(
    tokens,
    cotangent,
    segment_ids,
    wide_weight,
    wide_moment,
    wide_average,
    down_weight,
    down_moment,
    down_average,
    vector_weight,
    vector_moment,
    vector_average,
):
    devices = lax.axis_size("dev")
    count, feature = tokens.shape
    if not structured(devices, feature):
        return plain_body(
            tokens,
            cotangent,
            segment_ids,
            wide_weight,
            wide_moment,
            wide_average,
            down_weight,
            down_moment,
            down_average,
            vector_weight,
            vector_moment,
            vector_average,
        )
    depth = devices // PLANE
    capacity = count // devices
    where = place()
    core = where[3]

    wide_low, down_low = wide_weight.astype(jnp.bfloat16), down_weight.astype(jnp.bfloat16)
    rows, columns = wide_low.shape
    parts = wide_low.reshape(rows, 2, 2, columns // 4)
    keep, give = core_order(core, parts[:, :, 0], parts[:, :, 1])
    got = lax.ppermute(give, "dev", flips(devices, 1))
    pair = jnp.concatenate(core_order(core, keep, got), 0)

    send_rows, send_grads, slot = route(segment_ids.reshape(1, count), tokens, cotangent, devices)
    first_own = along_z(pair[:, 0])
    send_rows, first_own[1] = pin(send_rows, first_own[1])
    first_own = stacked(first_own, 2)

    work = exchange(send_rows.reshape(devices, capacity, -1)).reshape(count, -1)
    first_near = pin(*to_neighbours(*first_own))

    first_far = to_diagonal(*first_near)
    first_got = to_partner(*first_own, *first_near)
    first_far, first_got = pin(first_far, first_got)
    first_got = first_got + to_partner(*first_far)
    first_got, work, up_block = pin(first_got, work, pair[:, 1])

    up_own = stacked(along_z(up_block), 1)
    flipped_one, projected, first_weights, out_weights = project(
        where, work, vector_weight, (*first_own, *first_near, *first_far, *first_got)
    )
    projected, up_own, down_block, send_grads = pin(projected, up_own, down_low, send_grads)

    up_near = to_neighbours(*up_own)
    down_own = stacked(along_z(down_block), 2)
    pairs = feature // 256
    attended_a, stats_a, carried = attend(projected, work, vector_weight, out_weights, 0, pairs)
    carried, up_near, down_own, send_grads = pin(carried, up_near, down_own, send_grads)

    up_far = to_diagonal(*up_near)
    up_got = to_partner(*up_own, *up_near)
    grads = exchange(send_grads.reshape(devices, capacity, feature)).reshape(count, feature)
    attended_b, stats_b, resid, low_two = attend(
        projected, work, vector_weight, out_weights, pairs, pairs, carried
    )
    low_two, up_far, up_got = pin(low_two, up_far, up_got)
    up_got = up_got + to_partner(*up_far)
    low_two, up_got, down_own = pin(low_two, up_got, down_own)

    down_near = to_neighbours(*down_own)
    hidden, slope, up_weights = widen(
        where, low_two, vector_weight[8:].reshape(1, FF), (*up_own, *up_near, *up_far, *up_got)
    )
    hidden, down_near = pin(hidden, down_near)

    down_far = to_diagonal(*down_near)
    down_got = to_partner(*down_own, *down_near)
    down_mine, down_theirs = down_gradient(where, hidden, grads, depth)
    down_far, down_got, down_mine, down_theirs = pin(down_far, down_got, down_mine, down_theirs)

    got = send(down_theirs, 1)
    down_got = down_got + to_partner(*down_far)
    down_got, got = pin(down_got, got)
    down_fold = Fold(down_mine, got)
    down_to, down_got = pin(down_fold.diagonal(), down_got)

    got = over_diagonal(*down_to)
    output, down_weights = narrow(
        where, hidden, resid, vector_weight, (*down_own, *down_near, *down_far, *down_got)
    )
    output, down_weights, got = pin(output, down_weights, got)
    down_to, output = pin(down_fold.neighbours(*got), output)

    back_out = exchange(output.reshape(devices, capacity, feature)).reshape(count, feature)
    got = over_plane(*down_to)
    dresid, dlow, sums_two, bias_up_grad, up_mine, up_theirs = feed_back(
        where, slope, low_two, grads, resid, vector_weight, up_weights, down_weights,
        (attended_a, attended_b), depth,
    )
    dlow, got, up_mine, up_theirs, back_out = pin(dlow, got, up_mine, up_theirs, back_out)
    down_sums, dlow, up_theirs = pin(down_fold.column(*got), dlow, up_theirs)

    down_got = over_column(down_sums)
    up_got = send(up_theirs, 1)
    dleft, sums_left = attend_back(projected, work, stats_a, dlow, out_weights, 0, pairs)
    up_got, dleft, dlow = pin(up_got, dleft, dlow)
    up_fold = Fold(up_mine, up_got)
    up_to, dlow = pin(up_fold.diagonal(), dlow)

    up_got = over_diagonal(*up_to)
    dright, sums_right = attend_back(projected, work, stats_b, dlow, out_weights, pairs, pairs)
    up_got, dright, down_got = pin(up_got, dright, down_got)
    up_to, dright = pin(up_fold.neighbours(*up_got), dright)

    up_got = over_plane(*up_to)
    both = project_back(
        work, (dleft, dright), dresid, vector_weight, first_weights,
        sums_two, (sums_left, sums_right), bias_up_grad, devices,
    )
    both, dright = pin(both, dright)

    back = exchange(both.reshape(devices, capacity, -1))
    first_mine, first_theirs = first_gradient(where, flipped_one, (dleft, dright), depth)
    first_mine, first_theirs, up_got = pin(first_mine, first_theirs, up_got)

    first_got = send(first_theirs, 1)
    up_sums = up_fold.column(*up_got)
    first_got, up_sums = pin(first_got, up_sums)
    first_fold = Fold(first_mine, first_got)
    first_to, up_sums = pin(first_fold.diagonal(), up_sums)

    got = pin(*over_diagonal(*first_to))
    first_to, back, up_sums = pin(first_fold.neighbours(*got), back, up_sums)
    up_got = over_column(up_sums)

    got = over_plane(*first_to)
    got, up_first = pin(got, up_got[0])
    down_grad = total_of(down_sums[0], *down_got)
    first_sums, back_out = pin(first_fold.column(*got), back_out)

    first_got = over_column(first_sums)
    up_grad = total_of(up_sums[0], up_first, *up_got[1:])
    squares = jnp.sum(up_grad * up_grad) + jnp.sum(down_grad * down_grad)
    block_output = give_back(slot, back_out)
    first_got, up_grad, block_output, down_grad, squares = pin(
        first_got, up_grad, block_output, down_grad, squares
    )
    first_grad, packet = settle(first_sums[0], first_got, back, squares, devices, feature)
    packets = exchange(packet)
    input_grad = give_back(slot, back.reshape(count, -1))
    grad_norm, *new = finish(
        packets, first_grad, up_grad, down_grad,
        (wide_weight, wide_moment, wide_average),
        (down_weight, down_moment, down_average),
        (vector_weight, vector_moment, vector_average),
    )
    return (block_output, input_grad, grad_norm.reshape(()), *new)


def solution(mesh):
    placed = (
        P("dev", None),
        P("dev", None),
        P("dev"),
        P("dev", None),
        P("dev", None),
        P("dev", None),
        P("dev", None),
        P("dev", None),
        P("dev", None),
        P(),
        P(),
        P(),
    )
    return jax.shard_map(
        body,
        mesh=mesh,
        in_specs=placed,
        out_specs=(
            P("dev", None),
            P("dev", None),
            P(),
            P("dev", None),
            P("dev", None),
            P("dev", None),
            P("dev", None),
            P("dev", None),
            P("dev", None),
            P(),
            P(),
            P(),
        ),
        check_vma=False,
    )
```

```python
import math

import jax
import jax.numpy as jnp
from jax import lax
from jax.experimental import pallas as pl
from jax.experimental.pallas import tpu as pltpu
from jax.sharding import PartitionSpec as P

HEADS = 12
HEAD = 64
FF = 3072
DOCS_DEV = 4
PLANE = 8
MIB = 1 << 20


epsilon = 1e-05
masked_value = -1e30
momentum = 0.9
learn_rate = 0.01
decay_rate = 0.0001
average_rate = 0.8
clip_norm = 2048.0


def norm_rows(values, gain_row, shift_row):
    center = values - jnp.mean(values, -1, keepdims=True)
    spread = jnp.mean(center * center, -1, keepdims=True)
    return center * lax.rsqrt(spread + epsilon) * gain_row + shift_row


def gelu_exact(values):
    return jax.nn.gelu(values, approximate=False)


def product(matrix, other):
    return jnp.dot(matrix, other, preferred_element_type=jnp.float32)


def against(matrix, other):
    return lax.dot_general(
        matrix, other, (((1,), (1,)), ((), ())), preferred_element_type=jnp.float32
    )


def inner_rows(matrix, other):
    return lax.dot_general(
        matrix, other, (((0,), (0,)), ((), ())), preferred_element_type=jnp.float32
    )


def advance(weight, moment, average, gradient, factor, decay_term):
    update = factor * gradient + decay_term * weight
    new_moment = momentum * moment + update
    new_weight = weight - learn_rate * (update + momentum * new_moment)
    new_average = average_rate * average + (1.0 - average_rate) * new_weight
    return (new_weight, new_moment, new_average)


def routing(segment_ids, devices, capacity):
    row_count = segment_ids.shape[0]
    is_live = segment_ids >= 0
    target = jnp.where(is_live, segment_ids // DOCS_DEV, devices)
    onehot = (target[:, None] == jnp.arange(devices, dtype=jnp.int32)[None, :]).astype(jnp.int32)
    earlier = jnp.cumsum(onehot, axis=0) - onehot
    within = jnp.sum(earlier * onehot, axis=1)
    slot_of = jnp.where(is_live, target * capacity + within, row_count)
    anchor = (
        jnp.full((row_count,), row_count, jnp.int32)
        .at[slot_of]
        .set(jnp.arange(row_count, dtype=jnp.int32), mode="drop")
    )
    return (is_live, jnp.minimum(slot_of, row_count - 1), anchor)


def plain_body(
    tokens,
    cotangent,
    segment_ids,
    wide_weight,
    wide_moment,
    wide_average,
    down_weight,
    down_moment,
    down_average,
    vector_weight,
    vector_moment,
    vector_average,
):
    wide_full, down_full = (
        lax.all_gather(wide_weight.astype(jnp.bfloat16), "dev", axis=0, tiled=True),
        lax.all_gather(down_weight.astype(jnp.bfloat16), "dev", axis=0, tiled=True),
    )
    devices = lax.axis_size("dev")
    row_count, feature = tokens.shape
    capacity = row_count // devices
    is_live, slot_of, anchor = routing(segment_ids, devices, capacity)
    blank_row = jnp.zeros((1, feature), jnp.bfloat16)
    send_rows = jnp.concatenate([tokens, blank_row], 0)[anchor].reshape(devices, capacity, feature)
    send_grads = jnp.concatenate([cotangent, blank_row], 0)[anchor].reshape(
        devices, capacity, feature
    )
    send_ids = jnp.concatenate([segment_ids, jnp.full((1,), -1, jnp.int32)], 0)[anchor].reshape(
        devices, capacity
    )
    work_rows, work_grads, work_ids = (
        lax.all_to_all(send_rows, "dev", split_axis=0, concat_axis=0, tiled=True),
        lax.all_to_all(send_grads, "dev", split_axis=0, concat_axis=0, tiled=True),
        lax.all_to_all(send_ids, "dev", split_axis=0, concat_axis=0, tiled=True),
    )
    work_rows = work_rows.reshape(row_count, feature)
    work_grads = work_grads.reshape(row_count, feature)
    work_ids = work_ids.reshape(row_count)
    gain_one, shift_one, gain_two, shift_two, bias_query, bias_value, bias_out, bias_down = [
        vector_weight[row_index] for row_index in range(8)
    ]
    bias_up = vector_weight[8:].reshape(FF)
    w_qkv = wide_full[:, : 3 * feature]
    w_out = wide_full[:, 3 * feature : 4 * feature]
    w_up = wide_full[:, 4 * feature :]
    work_float = work_rows.astype(jnp.float32)
    low_one = norm_rows(work_float, gain_one, shift_one).astype(jnp.bfloat16)
    bias_all = jnp.concatenate([bias_query, jnp.zeros_like(bias_query), bias_value])
    projected = (product(low_one, w_qkv) + bias_all).astype(jnp.bfloat16)
    queries = projected[:, :feature].reshape(row_count, HEADS, HEAD)
    key_rows = projected[:, feature : 2 * feature].reshape(row_count, HEADS, HEAD)
    value_rows = projected[:, 2 * feature :].reshape(row_count, HEADS, HEAD)
    same_seg = work_ids[:, None] == work_ids[None, :]
    block_rows = min(512, row_count)
    group_size = math.gcd(HEADS, 4)
    group_count = HEADS // group_size

    def scores_of(offset, first_head):
        query_part = queries[offset : offset + block_rows, first_head : first_head + group_size]
        raw_scores = (
            jnp.einsum(
                "qhd,khd->hqk",
                query_part,
                key_rows[:, first_head : first_head + group_size],
                preferred_element_type=jnp.float32,
            )
            * 0.125
        )
        return jnp.where(same_seg[None], raw_scores, masked_value)

    stored = []
    offset = 0
    head_outs = []
    for group in range(group_count):
        first_head = group * group_size
        scores = scores_of(offset, first_head)
        row_max = jnp.max(scores, -1, keepdims=True)
        powers = jnp.exp(scores - row_max)
        row_sums = jnp.sum(powers, -1, keepdims=True)
        prob_low = (powers / row_sums).astype(jnp.bfloat16)
        head_outs.append(
            jnp.einsum(
                "hqk,khd->qhd",
                prob_low,
                value_rows[:, first_head : first_head + group_size],
                preferred_element_type=jnp.float32,
            )
        )
        stored.append((row_max, row_sums))
    out_blocks = jnp.concatenate(head_outs, 1)
    attended = out_blocks.reshape(row_count, feature).astype(jnp.bfloat16)
    resid = work_float + product(attended, w_out) + bias_out
    low_two = norm_rows(resid, gain_two, shift_two).astype(jnp.bfloat16)
    up_float = product(low_two, w_up) + bias_up
    hidden = gelu_exact(up_float).astype(jnp.bfloat16)
    output_low = (resid + product(hidden, down_full) + bias_down).astype(jnp.bfloat16)
    dy_float = work_grads.astype(jnp.float32)
    dhidden = against(work_grads, down_full)
    gelu_pull = jax.vjp(gelu_exact, up_float)[1]
    dup_low = gelu_pull(dhidden)[0].astype(jnp.bfloat16)
    da_two = against(dup_low, w_up)
    norm_two_pull = jax.vjp(norm_rows, resid, gain_two, shift_two)[1]
    dres_norm, dgain_two, dshift_two = norm_two_pull(da_two)
    dresid = dy_float + dres_norm
    dres_low = dresid.astype(jnp.bfloat16)
    dattended = against(dres_low, w_out).astype(jnp.bfloat16).reshape(row_count, HEADS, HEAD)
    dkey_parts = [
        jnp.zeros((row_count, group_size, HEAD), jnp.float32) for group in range(group_count)
    ]
    dvalue_parts = [
        jnp.zeros((row_count, group_size, HEAD), jnp.float32) for group in range(group_count)
    ]
    position = 0
    offset = 0
    pieces = []
    for group in range(group_count):
        first_head = group * group_size
        scores = scores_of(offset, first_head)
        row_max, row_sums = stored[position]
        position += 1
        prob_float = jnp.exp(scores - row_max) / row_sums
        prob_low = prob_float.astype(jnp.bfloat16)
        dout_part = dattended[offset : offset + block_rows, first_head : first_head + group_size]
        value_part = value_rows[:, first_head : first_head + group_size]
        dvalue_parts[group] = jnp.einsum(
            "hqk,qhd->khd", prob_low, dout_part, preferred_element_type=jnp.float32
        )
        dprob = jnp.einsum(
            "qhd,khd->hqk", dout_part, value_part, preferred_element_type=jnp.float32
        )
        dscore = (prob_float * (dprob - jnp.sum(prob_float * dprob, -1, keepdims=True))).astype(
            jnp.bfloat16
        )
        pieces.append(
            jnp.einsum(
                "hqk,khd->qhd",
                dscore,
                key_rows[:, first_head : first_head + group_size],
                preferred_element_type=jnp.float32,
            )
            * 0.125
        )
        query_part = queries[offset : offset + block_rows, first_head : first_head + group_size]
        dkey_parts[group] = (
            jnp.einsum("hqk,qhd->khd", dscore, query_part, preferred_element_type=jnp.float32)
            * 0.125
        )
    dquery_blocks = jnp.concatenate(pieces, 1)
    dquery_low = dquery_blocks.reshape(row_count, feature).astype(jnp.bfloat16)
    dkey_low = jnp.concatenate(dkey_parts, 1).reshape(row_count, feature).astype(jnp.bfloat16)
    dvalue_low = jnp.concatenate(dvalue_parts, 1).reshape(row_count, feature).astype(jnp.bfloat16)
    dqkv_low = jnp.concatenate([dquery_low, dkey_low, dvalue_low], 1)
    da_one = against(dqkv_low, w_qkv)
    norm_one_pull = jax.vjp(norm_rows, work_float, gain_one, shift_one)[1]
    dinput_norm, dgain_one, dshift_one = norm_one_pull(da_one)
    dinput_low = (dresid + dinput_norm).astype(jnp.bfloat16)
    back_out, back_grad = (
        lax.all_to_all(
            output_low.reshape(devices, capacity, feature),
            "dev",
            split_axis=0,
            concat_axis=0,
            tiled=True,
        ),
        lax.all_to_all(
            dinput_low.reshape(devices, capacity, feature),
            "dev",
            split_axis=0,
            concat_axis=0,
            tiled=True,
        ),
    )
    block_output = jnp.where(
        is_live[:, None], back_out.reshape(row_count, feature)[slot_of], jnp.zeros_like(tokens)
    )
    input_grad = jnp.where(
        is_live[:, None], back_grad.reshape(row_count, feature)[slot_of], jnp.zeros_like(tokens)
    )
    vector_rows = jnp.stack(
        [
            dgain_one,
            dshift_one,
            dgain_two,
            dshift_two,
            jnp.sum(dquery_low.astype(jnp.float32), 0),
            jnp.sum(dvalue_low.astype(jnp.float32), 0),
            jnp.sum(dres_low.astype(jnp.float32), 0),
            jnp.sum(dy_float, 0),
        ],
        0,
    )
    bias_up_grad = jnp.sum(dup_low.astype(jnp.float32), 0).reshape(FF // feature, feature)
    vector_partial = jnp.concatenate([vector_rows, bias_up_grad], 0)
    down_grad = lax.psum_scatter(
        inner_rows(hidden, work_grads), "dev", scatter_dimension=0, tiled=True
    )
    wide_grad = lax.psum_scatter(
        jnp.concatenate(
            [
                inner_rows(low_one, dqkv_low),
                jnp.concatenate([inner_rows(attended, dres_low), inner_rows(low_two, dup_low)], 1),
            ],
            1,
        ),
        "dev",
        scatter_dimension=0,
        tiled=True,
    )
    shard_squares = jnp.sum(wide_grad * wide_grad) + jnp.sum(down_grad * down_grad)
    vector_grad = lax.psum(vector_partial, "dev")
    total = lax.psum(shard_squares, "dev") + jnp.sum(vector_grad * vector_grad)
    grad_norm = jnp.sqrt(total)
    factor = clip_norm / jnp.maximum(grad_norm, clip_norm)
    wide_new, wide_moment_new, wide_average_new = advance(
        wide_weight, wide_moment, wide_average, wide_grad, factor, decay_rate
    )
    down_new, down_moment_new, down_average_new = advance(
        down_weight, down_moment, down_average, down_grad, factor, decay_rate
    )
    vector_new, vector_moment_new, vector_average_new = advance(
        vector_weight, vector_moment, vector_average, vector_grad, factor, 0.0
    )
    return (
        block_output,
        input_grad,
        grad_norm,
        wide_new,
        wide_moment_new,
        wide_average_new,
        down_new,
        down_moment_new,
        down_average_new,
        vector_new,
        vector_moment_new,
        vector_average_new,
    )


def flips(devices, mask):
    return [(i, i ^ mask) for i in range(devices)]


def shifts(devices, step):
    return [(i, (i + PLANE * step) % devices) for i in range(devices)]


def place():
    me = lax.axis_index("dev")
    return jnp.stack([me // PLANE, (me // 4) % 2, (me // 2) % 2, me % 2]).astype(jnp.int32)


def core_order(core, mine, theirs):
    first = jnp.where(core == 0, mine, theirs)
    second = jnp.where(core == 0, theirs, mine)
    return first, second


def pin(*values):
    return lax.optimization_barrier(values)


def send(value, mask):
    return lax.ppermute(value, "dev", flips(lax.axis_size("dev"), mask))


def along_z(block):
    devices = lax.axis_size("dev")
    return [block] + [
        lax.ppermute(block, "dev", shifts(devices, k)) for k in range(1, devices // PLANE)
    ]


def stacked(blocks, stacks):
    depth = len(blocks)
    each = depth // stacks
    return tuple(jnp.stack(blocks[k : k + each], 0) for k in range(0, depth, each))


def to_neighbours(*own):
    return tuple(send(stack, 2) for stack in own) + tuple(send(stack, 4) for stack in own)


def to_diagonal(*near):
    if len(near) == 4:
        return send(near[0], 4), send(near[3], 2)
    half = near[0].shape[0] // 2
    return send(near[0][:half], 4), send(near[1][half:], 2)


def to_partner(*pieces):
    return tuple(send(piece, 1) for piece in pieces)


def total_of(*terms):
    return sum(term.astype(jnp.float32) for term in terms)


def low_sum(*terms):
    return total_of(*terms).astype(jnp.bfloat16)


class Fold:
    def __init__(self, mine, got):
        self.mine, self.got = mine, got
        self.half = mine.shape[1] // 2

    def pair(self, spot, steps):
        return self.mine[spot, steps], self.got[spot, steps]

    def diagonal(self):
        first, last = slice(None, self.half), slice(self.half, None)
        return low_sum(*self.pair(3, first)), low_sum(*self.pair(3, last))

    def neighbours(self, got_a, got_b):
        first, last = slice(None, self.half), slice(self.half, None)
        to_x = (low_sum(*self.pair(1, first), got_a), low_sum(*self.pair(1, last)))
        to_y = (low_sum(*self.pair(2, first)), low_sum(*self.pair(2, last), got_b))
        return jnp.concatenate(to_x, 0), jnp.concatenate(to_y, 0)

    def column(self, got_x, got_y):
        total = total_of(*self.pair(0, slice(None)), got_x, got_y)
        return (total[0],) + tuple(
            total[k].astype(jnp.bfloat16) for k in range(1, total.shape[0])
        )


def over_diagonal(to_a, to_b):
    return send(to_a, 4), send(to_b, 2)


def over_plane(to_x, to_y):
    return send(to_x, 2), send(to_y, 4)


def over_column(sums):
    devices = lax.axis_size("dev")
    return tuple(lax.ppermute(sums[k], "dev", shifts(devices, k)) for k in range(1, len(sums)))


def exchange(rows):
    return lax.all_to_all(rows, "dev", split_axis=0, concat_axis=0, tiled=True)


FAR = pl.BlockSpec(memory_space=pltpu.HBM)
SCALARS = pl.BlockSpec(memory_space=pltpu.SMEM)


def whole(*shape):
    return pl.BlockSpec(shape, lambda *_: (0,) * len(shape))


LIMIT = 48


def settings(limit):
    return pltpu.CompilerParams(vmem_limit_bytes=limit * MIB)


def cost(flops, moved, exps=0):
    return pl.CostEstimate(flops=int(flops), bytes_accessed=int(moved), transcendentals=int(exps))


def shaped(shape, dtype):
    return jax.ShapeDtypeStruct(shape, dtype)


def by_rows(matrix, other):
    return lax.dot_general(
        matrix, other, (((1,), (1,)), ((), ())), preferred_element_type=jnp.float32
    )


def by_columns(matrix, other):
    return lax.dot_general(
        matrix, other, (((0,), (0,)), ((), ())), preferred_element_type=jnp.float32
    )


def normed(values):
    center = values - jnp.mean(values, -1, keepdims=True)
    scale = lax.rsqrt(jnp.mean(center * center, -1, keepdims=True) + epsilon)
    return center * scale, scale


def norm_back(grad, gain, unit, scale):
    inner = grad * gain
    return scale * (
        inner
        - jnp.mean(inner, -1, keepdims=True)
        - unit * jnp.mean(inner * unit, -1, keepdims=True)
    )


def iota(shape, axis):
    return lax.broadcasted_iota(jnp.int32, shape, axis)


def slots_of(ids_row, capacity, groups):
    count = ids_row.shape[1]
    square = (count, count)
    ids = jnp.sum(
        jnp.where(iota(square, 0) == iota(square, 1), ids_row, 0), axis=1, keepdims=True
    )
    group = jnp.right_shift(ids, DOCS_DEV.bit_length() - 1)
    lanes = max(128, groups)
    onehot = jnp.where(group == iota((count, lanes), 1), 1.0, 0.0)
    lower = jnp.where(iota(square, 0) > iota(square, 1), 1.0, 0.0).astype(jnp.bfloat16)
    earlier = product(lower, onehot.astype(jnp.bfloat16))
    within = jnp.sum(earlier * onehot, axis=1, keepdims=True).astype(jnp.int32)
    return ids, jnp.where(ids >= 0, group * capacity + within, -1)


def route(ids_row, tokens, cotangent, devices):
    count, feature = tokens.shape

    def kernel(ids_ref, tokens_ref, cotangent_ref, rows_ref, grads_ref, slot_ref):
        ids, slot = slots_of(ids_ref[...], count // devices, devices)
        slot_ref[...] = slot
        move = jnp.where(slot == iota((count, count), 1), 1.0, 0.0).astype(jnp.bfloat16)
        code = jnp.where(ids >= 0, jnp.bitwise_and(ids, DOCS_DEV - 1) + 1, 0)
        code = jnp.broadcast_to(code.astype(jnp.float32), (count, 128)).astype(jnp.bfloat16)
        rows_ref[:, :feature] = by_columns(move, tokens_ref[...]).astype(jnp.bfloat16)
        rows_ref[:, feature:] = by_columns(move, code).astype(jnp.bfloat16)
        grads_ref[...] = by_columns(move, cotangent_ref[...]).astype(jnp.bfloat16)

    return pl.pallas_call(
        kernel,
        out_shape=[
            shaped((count, feature + 128), jnp.bfloat16),
            shaped((count, feature), jnp.bfloat16),
            shaped((count, 1), jnp.int32),
        ],
        compiler_params=settings(LIMIT),
        cost_estimate=cost(4 * count * count * feature, 8 * count * feature),
    )(ids_row, tokens, cotangent)


def give_back(slot, rows):
    count, feature = rows.shape[0], rows.shape[1] // 256 * 256

    def kernel(slot_ref, rows_ref, out_ref):
        move = jnp.where(slot_ref[...] == iota((count, count), 1), 1.0, 0.0).astype(jnp.bfloat16)
        out_ref[...] = product(move, rows_ref[...]).astype(jnp.bfloat16)

    return pl.pallas_call(
        kernel,
        grid=(1,),
        out_shape=shaped((count, feature), jnp.bfloat16),
        in_specs=[whole(count, 1), whole(count, feature)],
        out_specs=whole(count, feature),
        compiler_params=settings(LIMIT),
        cost_estimate=cost(2 * count * count * feature, 4 * count * feature),
    )(slot, rows)


def pieces_of(where_ref, pieces):
    z, y, x, core = where_ref[0], where_ref[1], where_ref[2], where_ref[3]
    count = len(pieces) // 2
    depth = 2 * pieces[count - 1].shape[0]
    columns = ((y, x), (y, 1 - x), (1 - y, x), (1 - y, 1 - x))
    for part, group in ((core, pieces[:count]), (1 - core, pieces[count:])):
        reached = 0
        for piece in group:
            for index in range(piece.shape[0]):
                yy, xx = columns[reached // depth]
                step = reached % depth
                zz = lax.rem(z - step + depth, depth)
                yield piece.at[index], step, (zz * 2 + yy) * 2 + xx, part
                reached += 1


def wide_copies(where_ref, pieces, buffer, sems):
    copies = []
    for source, _, chip, part in pieces_of(where_ref, pieces):
        rows, columns = source.shape
        target = buffer.at[
            pl.ds(pl.multiple_of(chip * rows, 16), rows),
            pl.ds(pl.multiple_of(part * columns, 128), columns),
        ]
        copies.append(pltpu.make_async_copy(source, target, sems.at[len(copies)]))
    return copies


def down_copies(where_ref, pieces, buffer, sems):
    copies = []
    for source, _, chip, part in pieces_of(where_ref, pieces):
        rows = source.shape[0]
        row = pl.multiple_of((chip * 2 + part) * rows, 16)
        copies.append(
            pltpu.make_async_copy(source, buffer.at[pl.ds(row, rows)], sems.at[len(copies)])
        )
    return copies


def project(where, work, vector, pieces):
    count, feature = work.shape[0], vector.shape[1]
    copies_count = sum(piece.shape[0] for piece in pieces)
    tile = 256

    def kernel(where_ref, work_ref, vector_ref, *refs):
        (
            flipped_ref, out_ref, weights_ref, output_ref, low, buffer, sems, store_sems
        ) = refs[len(pieces):]
        copies = wide_copies(where_ref, refs[:len(pieces)], buffer, sems)
        for copy in copies:
            copy.start()

        def rows_of(index, carry):
            rows = pl.ds(pl.multiple_of(index * 64, 64), 64)
            unit, _ = normed(work_ref[rows, :].astype(jnp.float32))
            low[rows, :] = (unit * vector_ref[0:1, :] + vector_ref[1:2, :]).astype(jnp.bfloat16)
            return carry

        lax.fori_loop(0, count // 64, rows_of, 0)
        flipped_ref[...] = low[...].astype(jnp.float32).T.astype(jnp.bfloat16)
        for copy in copies:
            copy.wait()
        stores = [
            pltpu.make_async_copy(
                buffer.at[:, pl.ds(0, 3 * feature)], weights_ref, store_sems.at[0]
            ),
            pltpu.make_async_copy(
                buffer.at[:, pl.ds(3 * feature, feature)], output_ref, store_sems.at[1]
            ),
        ]
        for store in stores:
            store.start()
        for part, bias in ((0, 4), (1, None), (2, 5)):

            def columns_of(index, carry):
                inner = pl.ds(pl.multiple_of(index * tile, tile), tile)
                columns = pl.ds(pl.multiple_of(part * feature + index * tile, tile), tile)
                value = product(low[...], buffer[:, columns])
                if bias is not None:
                    value = value + vector_ref[bias : bias + 1, inner]
                out_ref[:, columns] = value.astype(jnp.bfloat16)
                return carry

            lax.fori_loop(0, feature // tile, columns_of, 0)
        for store in stores:
            store.wait()

    return pl.pallas_call(
        kernel,
        grid=(1,),
        out_shape=[
            shaped((feature, count), jnp.bfloat16),
            shaped((count, 3 * feature), jnp.bfloat16),
            shaped((feature, 3 * feature), jnp.bfloat16),
            shaped((feature, feature), jnp.bfloat16),
        ],
        in_specs=[SCALARS, whole(count, feature), whole(*vector.shape)] + [FAR] * len(pieces),
        out_specs=[whole(feature, count), whole(count, 3 * feature), FAR, FAR],
        scratch_shapes=[
            pltpu.VMEM((count, feature), jnp.bfloat16),
            pltpu.VMEM((feature, 4 * feature), jnp.bfloat16),
            pltpu.SemaphoreType.DMA((copies_count,)),
            pltpu.SemaphoreType.DMA((2,)),
        ],
        compiler_params=settings(60),
        cost_estimate=cost(6 * count * feature * feature, 12 * feature * feature),
    )(where, work, vector, *pieces)


def fill_cap(code_ref, cap):
    code = code_ref[...].astype(jnp.float32)
    cap[...] = jnp.where(code[:, :1] == code.T[:1], -masked_value, masked_value)


def one_head(values, head):
    lanes = iota(values.shape, 1)
    inside = (lanes >= head * HEAD) & (lanes < (head + 1) * HEAD)
    return jnp.where(inside, values, 0.0).astype(jnp.bfloat16)


def attend(projected, work, vector, weights, first, pairs, left=None):
    count, feature = work.shape[0], vector.shape[1]
    all_pairs = feature // 128
    tile = 512
    ends = left is not None

    def kernel(q_ref, k_ref, v_ref, code_ref, *refs):
        if ends:
            (
                weight_ref, work_ref, vector_ref, left_ref, flipped_ref, stat_ref, resid_ref, low_ref,
                cap, right, total,
            ) = refs
        else:
            flipped_ref, stat_ref, attended_ref, cap = refs
        pair = pl.program_id(0)

        @pl.when(pair == 0)
        def _():
            fill_cap(code_ref, cap)

        keys = k_ref[...]
        values = v_ref[...].astype(jnp.float32).T.astype(jnp.bfloat16)
        scaled = q_ref[...].astype(jnp.float32) * 0.125
        heads = []
        for head in range(2):
            query = one_head(scaled, head)
            parts = []
            for start in range(0, count, tile):
                span = slice(start, start + tile)
                scores = jnp.minimum(by_rows(keys, query[span]), cap[:, span])
                most = jnp.max(scores, 0, keepdims=True)
                powers = jnp.exp(scores - most)
                sums = jnp.sum(powers, 0, keepdims=True)
                stat_ref[0, head : head + 1, span] = most + jnp.log(sums)
                mixed = product(
                    values[head * HEAD : (head + 1) * HEAD], powers.astype(jnp.bfloat16)
                )
                parts.append(mixed * (1.0 / sums))
            heads.append(jnp.concatenate(parts, 1))
        both = jnp.concatenate(heads, 0)
        flipped_ref[...] = both.astype(jnp.bfloat16)
        attended = both.T.astype(jnp.bfloat16)
        if ends:
            right[pair] = attended
        else:
            attended_ref[...] = attended

        if ends:

            @pl.when(pair == pairs - 1)
            def _():
                middle = feature - pairs * 128
                for start in range(0, feature, 256):
                    span = slice(start, start + 256)
                    value = product(left_ref[...], weight_ref[:middle, span])
                    for index in range(pairs):
                        rows = slice(middle + index * 128, middle + (index + 1) * 128)
                        value = value + product(right[index], weight_ref[rows, span])
                    total[:, span] = value

                def rows_of(index, carry):
                    rows = pl.ds(pl.multiple_of(index * 64, 64), 64)
                    resid = (
                        work_ref[rows, :].astype(jnp.float32) + total[rows, :] + vector_ref[6:7, :]
                    )
                    resid_ref[rows, :] = resid
                    unit, _ = normed(resid)
                    low_ref[rows, :] = (unit * vector_ref[2:3, :] + vector_ref[3:4, :]).astype(
                        jnp.bfloat16
                    )
                    return carry

                lax.fori_loop(0, count // 64, rows_of, 0)

    def columns_at(offset):
        return pl.BlockSpec((count, 128), lambda pair: (0, offset + pair))

    wide = whole(count, feature)
    return pl.pallas_call(
        kernel,
        grid=(pairs,),
        out_shape=[
            shaped((pairs * 128, count), jnp.bfloat16),
            shaped((pairs, 8, count), jnp.float32),
        ]
        + (
            [shaped((count, feature), jnp.float32), shaped((count, feature), jnp.bfloat16)]
            if ends
            else [shaped((count, pairs * 128), jnp.bfloat16)]
        ),
        in_specs=[
            columns_at(first),
            columns_at(all_pairs + first),
            columns_at(2 * all_pairs + first),
            pl.BlockSpec((count, 128), lambda pair: (0, all_pairs)),
        ]
        + (
            [whole(feature, feature), wide, whole(*vector.shape), whole(*left.shape)]
            if ends
            else []
        ),
        out_specs=[
            pl.BlockSpec((128, count), lambda pair: (pair, 0)),
            pl.BlockSpec((1, 8, count), lambda pair: (pair, 0, 0)),
        ]
        + ([wide, wide] if ends else [columns_at(0)]),
        scratch_shapes=[pltpu.VMEM((count, count), jnp.float32)]
        + (
            [
                pltpu.VMEM((pairs, count, 128), jnp.bfloat16),
                pltpu.VMEM((count, feature), jnp.float32),
            ]
            if ends
            else []
        ),
        compiler_params=settings(60),
        cost_estimate=cost(
            8 * count * count * pairs * 128, 14 * count * feature, 2 * pairs * count * count
        ),
    )(
        projected, projected, projected, work,
        *([weights, work, vector, left] if ends else []),
    )


def widen(where, low, bias_row, pieces):
    count, feature = low.shape
    wide = bias_row.shape[1]
    tile = feature
    steps = wide // tile

    def kernel(where_ref, low_ref, bias_ref, *refs):
        hidden_ref, slope_ref, weights_ref, buffer, sems, store_sem = refs[len(pieces):]
        step = pl.program_id(0)
        store = pltpu.make_async_copy(buffer, weights_ref, store_sem)

        @pl.when(step == 0)
        def _():
            copies = wide_copies(where_ref, refs[:len(pieces)], buffer, sems)
            for copy in copies:
                copy.start()
            for copy in copies:
                copy.wait()
            store.start()

        columns = pl.ds(pl.multiple_of(step * tile, tile), tile)
        up = product(low_ref[...], buffer[:, columns]) + bias_ref[...]
        below = 0.5 * (1.0 + lax.erf(up * (0.5**0.5)))
        hidden_ref[...] = (up * below).astype(jnp.bfloat16)
        slope_ref[...] = below + up * (jnp.exp(-0.5 * up * up) * ((2.0 * math.pi) ** -0.5))

        @pl.when(step == steps - 1)
        def _():
            store.wait()

    block = pl.BlockSpec((count, tile), lambda step: (0, step))
    return pl.pallas_call(
        kernel,
        grid=(steps,),
        out_shape=[
            shaped((count, wide), jnp.bfloat16),
            shaped((count, wide), jnp.float32),
            shaped((feature, wide), jnp.bfloat16),
        ],
        in_specs=[
            SCALARS,
            whole(count, feature),
            pl.BlockSpec((1, tile), lambda step: (0, step)),
        ]
        + [FAR] * len(pieces),
        out_specs=[block, block, FAR],
        scratch_shapes=[
            pltpu.VMEM((feature, wide), jnp.bfloat16),
            pltpu.SemaphoreType.DMA((sum(piece.shape[0] for piece in pieces),)),
            pltpu.SemaphoreType.DMA,
        ],
        compiler_params=settings(60),
        cost_estimate=cost(
            2 * count * feature * wide, 2 * feature * wide + 6 * count * wide, count * wide
        ),
    )(where, low, bias_row, *pieces)


def down_gradient(where, hidden, grads, depth):
    count, wide = hidden.shape
    feature = grads.shape[1]
    rows = wide // (depth * PLANE)
    part = wide // depth

    def kernel(where_ref, hidden_ref, grads_ref, mine_ref, theirs_ref, result):
        y, x, core = where_ref[1], where_ref[2], where_ref[3]
        result[...] = by_columns(hidden_ref[...], grads_ref[...])
        for yy in range(2):
            for xx in range(2):
                spot = jnp.bitwise_xor(y, yy) * 2 + jnp.bitwise_xor(x, xx)
                first = (yy * 2 + xx) * 2
                for target, side in ((mine_ref, core), (theirs_ref, 1 - core)):
                    row = pl.multiple_of((first + side) * rows, 16)
                    target[spot, 0] = result[pl.ds(row, rows), :].astype(jnp.bfloat16)

    shape = shaped((4, depth, rows, feature), jnp.bfloat16)
    block = pl.BlockSpec((4, 1, rows, feature), lambda step, where_ref: (0, step, 0, 0))
    return pl.pallas_call(
        kernel,
        out_shape=[shape, shape],
        grid_spec=pltpu.PrefetchScalarGridSpec(
            num_scalar_prefetch=1,
            grid=(depth,),
            in_specs=[
                pl.BlockSpec(
                    (count, part),
                    lambda step, where_ref: (0, lax.rem(where_ref[0] + step, depth)),
                ),
                whole(count, feature),
            ],
            out_specs=[block, block],
            scratch_shapes=[pltpu.VMEM((part, feature), jnp.float32)],
        ),
        compiler_params=settings(LIMIT),
        cost_estimate=cost(2 * count * wide * feature, 2 * wide * (count + feature)),
    )(where, hidden, grads)


def put_wide(where_ref, result, mine_ref, theirs_ref):
    z, y, x, core = where_ref[0], where_ref[1], where_ref[2], where_ref[3]
    _, depth, rows, _ = mine_ref.shape
    for chip in range(4 * depth):
        zz, yy, xx = chip // 4, (chip // 2) % 2, chip % 2
        step = lax.rem(zz - z + depth, depth)
        spot = jnp.bitwise_xor(y, yy) * 2 + jnp.bitwise_xor(x, xx)
        for target, side in ((mine_ref, core), (theirs_ref, 1 - core)):
            row = pl.multiple_of((chip * 2 + side) * rows, 8)
            target[spot, step] = result[pl.ds(row, rows), :].astype(jnp.bfloat16)


def narrow(where, hidden, resid, vector, pieces):
    count, wide = hidden.shape
    feature = resid.shape[1]
    tile = 256

    def kernel(where_ref, hidden_ref, resid_ref, vector_ref, *refs):
        out_ref, weights_ref, buffer, sems, store_sem = refs[len(pieces):]
        copies = down_copies(where_ref, refs[:len(pieces)], buffer, sems)
        for copy in copies:
            copy.start()
        for copy in copies:
            copy.wait()
        store = pltpu.make_async_copy(buffer, weights_ref, store_sem)
        store.start()

        def columns_of(index, carry):
            columns = pl.ds(pl.multiple_of(index * tile, tile), tile)
            value = product(hidden_ref[...], buffer[:, columns])
            out_ref[:, columns] = (
                resid_ref[:, columns] + (value + vector_ref[7:8, columns])
            ).astype(jnp.bfloat16)
            return carry

        lax.fori_loop(0, feature // tile, columns_of, 0)
        store.wait()

    return pl.pallas_call(
        kernel,
        grid=(1,),
        out_shape=[
            shaped((count, feature), jnp.bfloat16),
            shaped((wide, feature), jnp.bfloat16),
        ],
        in_specs=[SCALARS, whole(count, wide), whole(count, feature), whole(*vector.shape)]
        + [FAR] * len(pieces),
        out_specs=[whole(count, feature), FAR],
        scratch_shapes=[
            pltpu.VMEM((wide, feature), jnp.bfloat16),
            pltpu.SemaphoreType.DMA((sum(piece.shape[0] for piece in pieces),)),
            pltpu.SemaphoreType.DMA,
        ],
        compiler_params=settings(LIMIT),
        cost_estimate=cost(2 * count * wide * feature, 6 * wide * feature),
    )(where, hidden, resid, vector, *pieces)


def feed_back(where, slope, low, grads, resid, vector, up_weights, down_weights, attended, depth):
    count, wide = slope.shape
    feature = resid.shape[1]
    tile = feature
    steps = wide // tile
    half = feature // 2
    chip_rows = feature // (PLANE * depth)

    def kernel(
        where_ref, slope_ref, low_ref, grads_ref, resid_ref, vector_ref, up_ref, down_ref, left_ref, right_ref,
        dresid_ref, dlow_ref, sums_ref, bias_ref, mine_ref, theirs_ref, back, flipped, result,
    ):
        step = pl.program_id(0)

        @pl.when(step == 0)
        def _():
            flipped[...] = low_ref[...].astype(jnp.float32).T.astype(jnp.bfloat16)
            back[...] = jnp.zeros_like(back)

        @pl.when(step < steps)
        def _():
            dup = (slope_ref[...] * by_rows(grads_ref[...], down_ref[...])).astype(jnp.bfloat16)
            bias_ref[...] = jnp.sum(dup.astype(jnp.float32), 0, keepdims=True)
            back[...] += by_rows(dup, up_ref[...])
            result[...] = product(flipped[...], dup)

        @pl.when(step == steps)
        def _():
            sums_ref[...] = jnp.zeros_like(sums_ref)

            def rows_of(index, carry):
                rows = pl.ds(pl.multiple_of(index * 64, 64), 64)
                unit, scale = normed(resid_ref[rows, :])
                da = back[rows, :]
                dy = grads_ref[rows, :].astype(jnp.float32)
                dresid = dy + norm_back(da, vector_ref[2:3, :], unit, scale)
                dresid_ref[rows, :] = dresid
                dlow = dresid.astype(jnp.bfloat16)
                dlow_ref[rows, :] = dlow
                for row, value in enumerate((da * unit, da, dlow.astype(jnp.float32), dy)):
                    sums_ref[row : row + 1, :] += jnp.sum(value, 0, keepdims=True)
                return carry

            lax.fori_loop(0, count // 64, rows_of, 0)
            result[:half, :] = product(left_ref[...], dlow_ref[...])
            result[half:, :] = product(right_ref[...], dlow_ref[...])

        put_wide(where_ref, result, mine_ref, theirs_ref)

    def at(step):
        return jnp.minimum(step, steps - 1)

    def columns_at(rows):
        return pl.BlockSpec((rows, tile), lambda step: (0, at(step)))

    all_rows = whole(count, feature)
    split = shaped((4, depth, chip_rows, (steps + 1) * feature), jnp.bfloat16)
    block = pl.BlockSpec((4, depth, chip_rows, feature), lambda step: (0, 0, 0, step))
    return pl.pallas_call(
        kernel,
        grid=(steps + 1,),
        out_shape=[
            shaped((count, feature), jnp.float32),
            shaped((count, feature), jnp.bfloat16),
            shaped((8, feature), jnp.float32),
            shaped((1, wide), jnp.float32),
            split,
            split,
        ],
        in_specs=[
            SCALARS,
            columns_at(count),
            all_rows,
            all_rows,
            all_rows,
            whole(*vector.shape),
            columns_at(feature),
            pl.BlockSpec((tile, feature), lambda step: (at(step), 0)),
            whole(half, count),
            whole(half, count),
        ],
        out_specs=[all_rows, all_rows, whole(8, feature), columns_at(1), block, block],
        scratch_shapes=[
            pltpu.VMEM((count, feature), jnp.float32),
            pltpu.VMEM((feature, count), jnp.bfloat16),
            pltpu.VMEM((feature, feature), jnp.float32),
        ],
        compiler_params=settings(60),
        cost_estimate=cost(6 * count * wide * feature, 8 * wide * feature + 10 * count * wide),
    )(where, slope, low, grads, resid, vector, up_weights, down_weights, *attended)


def attend_back(projected, work, stats, dlow, weights, first, pairs):
    count, feature = dlow.shape
    all_pairs = feature // 128
    tile = 512
    wide = pairs * 128

    def kernel(
        q_ref, k_ref, v_ref, code_ref, stat_ref, dlow_ref, weight_ref, out_ref, sums_ref, douts, cap
    ):
        pair = pl.program_id(0)

        @pl.when(pair == 0)
        def _():
            fill_cap(code_ref, cap)
            for start in range(0, wide, 128):
                span = slice(start, start + 128)
                douts[start // 128] = by_rows(dlow_ref[...], weight_ref[span, :]).astype(
                    jnp.bfloat16
                )

        keys, values = k_ref[...], v_ref[...]
        wide_keys = keys.astype(jnp.float32)
        dquery = jnp.zeros((count, 128), jnp.float32)
        scaled = q_ref[...].astype(jnp.float32) * 0.125
        dout = douts[pair].astype(jnp.float32)
        dkey = jnp.zeros((count, 128), jnp.float32)
        dvalue = jnp.zeros((count, 128), jnp.float32)
        for head in range(2):
            query = one_head(scaled, head)
            dhead = one_head(dout, head)
            for start in range(0, count, tile):
                span = slice(start, start + tile)
                scores = jnp.minimum(by_rows(keys, query[span]), cap[:, span])
                probs = jnp.exp(scores - stat_ref[0, head : head + 1, span])
                dprob = by_rows(values, dhead[span])
                inner = jnp.sum(probs * dprob, 0, keepdims=True)
                dscore = (probs * (dprob - inner)).astype(jnp.bfloat16)
                dvalue = dvalue + product(probs.astype(jnp.bfloat16), dhead[span])
                dkey = dkey + product(dscore, query[span])
                dquery = dquery + by_columns(dscore, one_head(wide_keys, head))
        dquery = (dquery * 0.125).astype(jnp.bfloat16)
        dvalue = dvalue.astype(jnp.bfloat16)
        out_ref[0] = dquery
        out_ref[1] = dkey.astype(jnp.bfloat16)
        out_ref[2] = dvalue
        sums_ref[0:1, :] = jnp.sum(dquery.astype(jnp.float32), 0, keepdims=True)
        sums_ref[1:2, :] = jnp.sum(dvalue.astype(jnp.float32), 0, keepdims=True)

    def columns_at(offset):
        return pl.BlockSpec((count, 128), lambda pair: (0, offset + pair))

    return pl.pallas_call(
        kernel,
        grid=(pairs,),
        out_shape=[
            shaped((3, count, wide), jnp.bfloat16),
            shaped((8, wide), jnp.float32),
        ],
        in_specs=[
            columns_at(first),
            columns_at(all_pairs + first),
            columns_at(2 * all_pairs + first),
            pl.BlockSpec((count, 128), lambda pair: (0, all_pairs)),
            pl.BlockSpec((1, 8, count), lambda pair: (pair, 0, 0)),
            whole(count, feature),
            pl.BlockSpec((wide, feature), lambda pair: (first // pairs, 0)),
        ],
        out_specs=[
            pl.BlockSpec((3, count, 128), lambda pair: (0, 0, pair)),
            pl.BlockSpec((8, 128), lambda pair: (0, pair)),
        ],
        scratch_shapes=[
            pltpu.VMEM((pairs, count, 128), jnp.bfloat16),
            pltpu.VMEM((count, count), jnp.float32),
        ],
        compiler_params=settings(LIMIT),
        cost_estimate=cost(
            14 * count * count * wide, 16 * count * feature, 2 * pairs * count * count
        ),
    )(projected, projected, projected, work, stats, dlow, weights)


def first_gradient(where, flipped, dprojected, depth):
    feature, count = flipped.shape
    half = feature // 2
    rows = feature // (PLANE * depth)

    def kernel(where_ref, flipped_ref, d_ref, e_ref, mine_ref, theirs_ref, result):
        result[:, :half] = product(flipped_ref[...], d_ref[0])
        result[:, half:] = product(flipped_ref[...], e_ref[0])
        put_wide(where_ref, result, mine_ref, theirs_ref)

    shape = shaped((4, depth, rows, 3 * feature), jnp.bfloat16)
    block = pl.BlockSpec((4, depth, rows, feature), lambda step: (0, 0, 0, step))
    part = pl.BlockSpec((1, count, half), lambda step: (step, 0, 0))
    return pl.pallas_call(
        kernel,
        grid=(3,),
        out_shape=[shape, shape],
        in_specs=[SCALARS, whole(feature, count), part, part],
        out_specs=[block, block],
        scratch_shapes=[pltpu.VMEM((feature, feature), jnp.float32)],
        compiler_params=settings(60),
        cost_estimate=cost(6 * count * feature * feature, 16 * feature * feature),
    )(where, flipped, *dprojected)


def project_back(work, dprojected, dresid, vector, weights, sums_two, sums_attend, bias_up, devices):
    count, feature = dresid.shape
    tile = 128
    half = feature // 2
    lanes = 16 * feature // devices // 128
    capacity = count // devices

    def kernel(
        work_ref, d_ref, e_ref, dresid_ref, vector_ref, weight_ref, two_ref, left_ref, right_ref, bias_ref,
        out_ref, sums,
    ):
        sums[...] = jnp.zeros_like(sums)

        def rows_of(index, carry):
            rows = pl.ds(pl.multiple_of(index * tile, tile), tile)
            da = jnp.zeros((tile, feature), jnp.float32)
            for part in range(3):
                middle = part * feature + half
                da += by_rows(d_ref[part, rows, :], weight_ref[:, middle - half : middle])
                da += by_rows(e_ref[part, rows, :], weight_ref[:, middle : middle + half])
            unit, scale = normed(work_ref[rows, :].astype(jnp.float32))
            out_ref[rows, :feature] = (
                dresid_ref[rows, :] + norm_back(da, vector_ref[0:1, :], unit, scale)
            ).astype(jnp.bfloat16)
            sums[0:1, :] += jnp.sum(da * unit, 0, keepdims=True)
            sums[1:2, :] += jnp.sum(da, 0, keepdims=True)
            return carry

        lax.fori_loop(0, count // tile, rows_of, 0)
        sums[2:4, :] = two_ref[0:2, :]
        sums[4:6, :half] = left_ref[0:2, :]
        sums[4:6, half:] = right_ref[0:2, :]
        sums[6:8, :] = two_ref[2:4, :]
        for row in range(FF // feature):
            sums[8 + row : 9 + row, :] = bias_ref[0:1, row * feature : (row + 1) * feature]
        place_in = iota((capacity, 128), 0)
        for device in range(devices):
            block = jnp.zeros((capacity, 128), jnp.float32)
            for lane in range(lanes):
                first = device * lanes + lane
                row, column = divmod(first * 128, feature)
                value = sums[row : row + 1, column : column + 128]
                high = value.astype(jnp.bfloat16).astype(jnp.float32)
                block = jnp.where(place_in == lane, high, block)
                block = jnp.where(place_in == lanes + lane, value - high, block)
            out_ref[device * capacity : (device + 1) * capacity, feature:] = block.astype(
                jnp.bfloat16
            )

    return pl.pallas_call(
        kernel,
        grid=(1,),
        out_shape=shaped((count, feature + 128), jnp.bfloat16),
        in_specs=[
            whole(count, feature),
            whole(3, count, half),
            whole(3, count, half),
            whole(count, feature),
            whole(*vector.shape),
            whole(feature, 3 * feature),
            whole(8, feature),
            whole(8, half),
            whole(8, half),
            whole(1, FF),
        ],
        out_specs=whole(count, feature + 128),
        scratch_shapes=[pltpu.VMEM((16, feature), jnp.float32)],
        compiler_params=settings(LIMIT),
        cost_estimate=cost(6 * count * feature * feature, 6 * feature * feature),
    )(work, *dprojected, dresid, vector, weights, sums_two, *sums_attend, bias_up)


def settle(own, got, back, squares, devices, feature):
    rows, columns = own.shape
    lanes = 16 * feature // devices // 128
    capacity = back.shape[1]

    def kernel(squares_ref, own_ref, *refs):
        got_refs, (back_ref, grad_ref, packet_ref) = refs[: len(got)], refs[len(got) :]
        grad = own_ref[...]
        for ref in got_refs:
            grad += ref[...].astype(jnp.float32)
        grad_ref[...] = grad
        total = squares_ref[0, 0] + jnp.sum(grad * grad)
        sums = jnp.sum(back_ref[...].astype(jnp.float32), 0)
        packet_ref[:, :lanes, :] = jnp.broadcast_to(
            (sums[:lanes] + sums[lanes : 2 * lanes])[None], (devices, lanes, 128)
        )
        packet_ref[:, lanes:, :] = jnp.full((devices, 1, 128), total, jnp.float32)

    return pl.pallas_call(
        kernel,
        grid=(1,),
        out_shape=[
            shaped((rows, columns), jnp.float32),
            shaped((devices, lanes + 1, 128), jnp.float32),
        ],
        in_specs=[SCALARS, whole(rows, columns)]
        + [whole(rows, columns)] * len(got)
        + [pl.BlockSpec((devices, capacity, 128), lambda step: (0, 0, feature // 128))],
        out_specs=[whole(rows, columns), whole(devices, lanes + 1, 128)],
        compiler_params=settings(60),
        cost_estimate=cost(8 * rows * columns, 16 * rows * columns),
    )(squares.reshape(1, 1), own, *got, back)


def finish(packets, first_grad, up_grad, down_grad, wide, down, vector):
    devices, lanes, _ = packets.shape
    lanes -= 1
    rows, columns = wide[0].shape
    down_rows, feature = down[0].shape
    vector_rows = vector[0].shape[0]
    steps = 2
    tile, down_tile = columns // steps, down_rows // steps
    first_columns = first_grad.shape[1]

    def kernel(packets_ref, first_ref, up_ref, down_grad_ref, *refs):
        wide_refs, down_refs, vector_refs = refs[:3], refs[3:6], refs[6:9]
        norm_ref, wide_new, down_new, vector_new = refs[9], refs[10:13], refs[13:16], refs[16:19]
        sums, factor_ref = refs[19:]
        step = pl.program_id(0)

        def put(new, old, gradient, decay):
            for ref, value in zip(
                new, advance(*(ref[...] for ref in old), gradient, factor_ref[0], decay), strict=True
            ):
                ref[...] = value

        @pl.when(step == 0)
        def _():
            for place_of in range(vector_rows * feature // 128):
                device, lane = divmod(place_of, lanes)
                row, column = divmod(place_of * 128, feature)
                sums[row : row + 1, column : column + 128] = packets_ref[device, lane : lane + 1]
            gradient = sums[...]
            shares = packets_ref[:, lanes, :1]
            total = jnp.sum(shares) + jnp.sum(gradient * gradient)
            norm = jnp.sqrt(jnp.full((1, 1), total))
            norm_ref[...] = norm
            factor_ref[0] = jnp.sum(clip_norm / jnp.maximum(norm, clip_norm))
            put(vector_new, vector_refs, gradient, 0.0)

        for index in range(steps):

            @pl.when(step == index)
            def _():
                first = index * tile
                parts = []
                if first < first_columns:
                    parts.append(first_ref[:, first : min(first + tile, first_columns)])
                if first + tile > first_columns:
                    low = max(first - first_columns, 0)
                    high = first + tile - first_columns
                    if low < feature:
                        parts.append(up_ref[:, FF + low : FF + min(high, feature)])
                    if high > feature:
                        parts.append(up_ref[:, max(low - feature, 0) : high - feature])
                gradient = parts[0] if len(parts) == 1 else jnp.concatenate(parts, 1)
                put(wide_new, wide_refs, gradient, decay_rate)

        put(down_new, down_refs, down_grad_ref[...], decay_rate)

    def tiles(shape):
        return pl.BlockSpec(shape, lambda step: (0, step))

    wide_specs = [tiles((rows, tile))] * 3
    down_specs = [pl.BlockSpec((down_tile, feature), lambda step: (step, 0))] * 3
    vector_specs = [whole(vector_rows, feature)] * 3
    return pl.pallas_call(
        kernel,
        grid=(steps,),
        out_shape=[shaped((1, 1), jnp.float32)]
        + [shaped(part.shape, jnp.float32) for part in (*wide, *down, *vector)],
        in_specs=[
            whole(*packets.shape),
            whole(*first_grad.shape),
            whole(*up_grad.shape),
            down_specs[0],
        ]
        + wide_specs
        + down_specs
        + vector_specs,
        out_specs=[whole(1, 1)] + wide_specs + down_specs + vector_specs,
        scratch_shapes=[
            pltpu.VMEM((vector_rows, feature), jnp.float32),
            pltpu.SMEM((1,), jnp.float32),
        ],
        compiler_params=settings(60),
        cost_estimate=cost(20 * rows * columns, 40 * rows * columns),
    )(packets, first_grad, up_grad, down_grad, *wide, *down, *vector)


def structured(devices, feature):
    rows = feature // devices
    return devices % PLANE == 0 and feature % devices == 0 and (2 * rows) % 16 == 0


def body(
    tokens,
    cotangent,
    segment_ids,
    wide_weight,
    wide_moment,
    wide_average,
    down_weight,
    down_moment,
    down_average,
    vector_weight,
    vector_moment,
    vector_average,
):
    devices = lax.axis_size("dev")
    count, feature = tokens.shape
    if not structured(devices, feature):
        return plain_body(
            tokens,
            cotangent,
            segment_ids,
            wide_weight,
            wide_moment,
            wide_average,
            down_weight,
            down_moment,
            down_average,
            vector_weight,
            vector_moment,
            vector_average,
        )
    depth = devices // PLANE
    capacity = count // devices
    where = place()
    core = where[3]

    wide_low, down_low = wide_weight.astype(jnp.bfloat16), down_weight.astype(jnp.bfloat16)
    rows, columns = wide_low.shape
    parts = wide_low.reshape(rows, 2, 2, columns // 4)
    keep, give = core_order(core, parts[:, :, 0], parts[:, :, 1])
    got = lax.ppermute(give, "dev", flips(devices, 1))
    pair = jnp.concatenate(core_order(core, keep, got), 0)

    send_rows, send_grads, slot = route(segment_ids.reshape(1, count), tokens, cotangent, devices)
    first_own = along_z(pair[:, 0])
    send_rows, first_own[1] = pin(send_rows, first_own[1])
    first_own = stacked(first_own, 2)

    work = exchange(send_rows.reshape(devices, capacity, -1)).reshape(count, -1)
    first_near = pin(*to_neighbours(*first_own))

    first_far = to_diagonal(*first_near)
    first_got = to_partner(*first_own, *first_near)
    first_far, first_got = pin(first_far, first_got)
    first_got = first_got + to_partner(*first_far)
    first_got, work, up_block = pin(first_got, work, pair[:, 1])

    up_own = stacked(along_z(up_block), 1)
    flipped_one, projected, first_weights, out_weights = project(
        where, work, vector_weight, (*first_own, *first_near, *first_far, *first_got)
    )
    projected, up_own, down_block, send_grads = pin(projected, up_own, down_low, send_grads)

    up_near = to_neighbours(*up_own)
    down_own = stacked(along_z(down_block), 2)
    pairs = feature // 256
    attended_a, stats_a, carried = attend(projected, work, vector_weight, out_weights, 0, pairs)
    carried, up_near, down_own, send_grads = pin(carried, up_near, down_own, send_grads)

    up_far = to_diagonal(*up_near)
    up_got = to_partner(*up_own, *up_near)
    grads = exchange(send_grads.reshape(devices, capacity, feature)).reshape(count, feature)
    attended_b, stats_b, resid, low_two = attend(
        projected, work, vector_weight, out_weights, pairs, pairs, carried
    )
    low_two, up_far, up_got = pin(low_two, up_far, up_got)
    up_got = up_got + to_partner(*up_far)
    low_two, up_got, down_own = pin(low_two, up_got, down_own)

    down_near = to_neighbours(*down_own)
    hidden, slope, up_weights = widen(
        where, low_two, vector_weight[8:].reshape(1, FF), (*up_own, *up_near, *up_far, *up_got)
    )
    hidden, down_near = pin(hidden, down_near)

    down_far = to_diagonal(*down_near)
    down_got = to_partner(*down_own, *down_near)
    down_mine, down_theirs = down_gradient(where, hidden, grads, depth)
    down_far, down_got, down_mine, down_theirs = pin(down_far, down_got, down_mine, down_theirs)

    got = send(down_theirs, 1)
    down_got = down_got + to_partner(*down_far)
    down_got, got = pin(down_got, got)
    down_fold = Fold(down_mine, got)
    down_to, down_got = pin(down_fold.diagonal(), down_got)

    got = over_diagonal(*down_to)
    output, down_weights = narrow(
        where, hidden, resid, vector_weight, (*down_own, *down_near, *down_far, *down_got)
    )
    output, down_weights, got = pin(output, down_weights, got)
    down_to, output = pin(down_fold.neighbours(*got), output)

    back_out = exchange(output.reshape(devices, capacity, feature)).reshape(count, feature)
    got = over_plane(*down_to)
    dresid, dlow, sums_two, bias_up_grad, up_mine, up_theirs = feed_back(
        where, slope, low_two, grads, resid, vector_weight, up_weights, down_weights,
        (attended_a, attended_b), depth,
    )
    dlow, got, up_mine, up_theirs, back_out = pin(dlow, got, up_mine, up_theirs, back_out)
    down_sums, dlow, up_theirs = pin(down_fold.column(*got), dlow, up_theirs)

    down_got = over_column(down_sums)
    up_got = send(up_theirs, 1)
    dleft, sums_left = attend_back(projected, work, stats_a, dlow, out_weights, 0, pairs)
    up_got, dleft, dlow = pin(up_got, dleft, dlow)
    up_fold = Fold(up_mine, up_got)
    up_to, dlow = pin(up_fold.diagonal(), dlow)

    up_got = over_diagonal(*up_to)
    dright, sums_right = attend_back(projected, work, stats_b, dlow, out_weights, pairs, pairs)
    up_got, dright, down_got = pin(up_got, dright, down_got)
    up_to, dright = pin(up_fold.neighbours(*up_got), dright)

    up_got = over_plane(*up_to)
    both = project_back(
        work, (dleft, dright), dresid, vector_weight, first_weights,
        sums_two, (sums_left, sums_right), bias_up_grad, devices,
    )
    both, dright = pin(both, dright)

    back = exchange(both.reshape(devices, capacity, -1))
    first_mine, first_theirs = first_gradient(where, flipped_one, (dleft, dright), depth)
    first_mine, first_theirs, up_got = pin(first_mine, first_theirs, up_got)

    first_got = send(first_theirs, 1)
    up_sums = up_fold.column(*up_got)
    first_got, up_sums = pin(first_got, up_sums)
    first_fold = Fold(first_mine, first_got)
    first_to, up_sums = pin(first_fold.diagonal(), up_sums)

    got = pin(*over_diagonal(*first_to))
    first_to, back, up_sums = pin(first_fold.neighbours(*got), back, up_sums)
    up_got = over_column(up_sums)

    got = over_plane(*first_to)
    got, up_first = pin(got, up_got[0])
    down_grad = total_of(down_sums[0], *down_got)
    first_sums, back_out = pin(first_fold.column(*got), back_out)

    first_got = over_column(first_sums)
    up_grad = total_of(up_sums[0], up_first, *up_got[1:])
    squares = jnp.sum(up_grad * up_grad) + jnp.sum(down_grad * down_grad)
    block_output = give_back(slot, back_out)
    first_got, up_grad, block_output, down_grad, squares = pin(
        first_got, up_grad, block_output, down_grad, squares
    )
    first_grad, packet = settle(first_sums[0], first_got, back, squares, devices, feature)
    packets = exchange(packet)
    input_grad = give_back(slot, back.reshape(count, -1))
    grad_norm, *new = finish(
        packets, first_grad, up_grad, down_grad,
        (wide_weight, wide_moment, wide_average),
        (down_weight, down_moment, down_average),
        (vector_weight, vector_moment, vector_average),
    )
    return (block_output, input_grad, grad_norm.reshape(()), *new)


def solution(mesh):
    placed = (
        P("dev", None),
        P("dev", None),
        P("dev"),
        P("dev", None),
        P("dev", None),
        P("dev", None),
        P("dev", None),
        P("dev", None),
        P("dev", None),
        P(),
        P(),
        P(),
    )
    return jax.shard_map(
        body,
        mesh=mesh,
        in_specs=placed,
        out_specs=(
            P("dev", None),
            P("dev", None),
            P(),
            P("dev", None),
            P("dev", None),
            P("dev", None),
            P("dev", None),
            P("dev", None),
            P("dev", None),
            P(),
            P(),
            P(),
        ),
        check_vma=False,
    )
```

```python
import math

import jax
import jax.numpy as jnp
from jax import lax
from jax.experimental import pallas as pl
from jax.experimental.pallas import tpu as pltpu
from jax.sharding import PartitionSpec as P

HEADS = 12
HEAD = 64
FF = 3072
DOCS_DEV = 4
PLANE = 8
MIB = 1 << 20


epsilon = 1e-05
masked_value = -1e30
momentum = 0.9
learn_rate = 0.01
decay_rate = 0.0001
average_rate = 0.8
clip_norm = 2048.0


def norm_rows(values, gain_row, shift_row):
    center = values - jnp.mean(values, -1, keepdims=True)
    spread = jnp.mean(center * center, -1, keepdims=True)
    return center * lax.rsqrt(spread + epsilon) * gain_row + shift_row


def gelu_exact(values):
    return jax.nn.gelu(values, approximate=False)


def product(matrix, other):
    return jnp.dot(matrix, other, preferred_element_type=jnp.float32)


def against(matrix, other):
    return lax.dot_general(
        matrix, other, (((1,), (1,)), ((), ())), preferred_element_type=jnp.float32
    )


def inner_rows(matrix, other):
    return lax.dot_general(
        matrix, other, (((0,), (0,)), ((), ())), preferred_element_type=jnp.float32
    )


def advance(weight, moment, average, gradient, factor, decay_term):
    update = factor * gradient + decay_term * weight
    new_moment = momentum * moment + update
    new_weight = weight - learn_rate * (update + momentum * new_moment)
    new_average = average_rate * average + (1.0 - average_rate) * new_weight
    return (new_weight, new_moment, new_average)


def routing(segment_ids, devices, capacity):
    row_count = segment_ids.shape[0]
    is_live = segment_ids >= 0
    target = jnp.where(is_live, segment_ids // DOCS_DEV, devices)
    onehot = (target[:, None] == jnp.arange(devices, dtype=jnp.int32)[None, :]).astype(jnp.int32)
    earlier = jnp.cumsum(onehot, axis=0) - onehot
    within = jnp.sum(earlier * onehot, axis=1)
    slot_of = jnp.where(is_live, target * capacity + within, row_count)
    anchor = (
        jnp.full((row_count,), row_count, jnp.int32)
        .at[slot_of]
        .set(jnp.arange(row_count, dtype=jnp.int32), mode="drop")
    )
    return (is_live, jnp.minimum(slot_of, row_count - 1), anchor)


def plain_body(
    tokens,
    cotangent,
    segment_ids,
    wide_weight,
    wide_moment,
    wide_average,
    down_weight,
    down_moment,
    down_average,
    vector_weight,
    vector_moment,
    vector_average,
):
    wide_full, down_full = (
        lax.all_gather(wide_weight.astype(jnp.bfloat16), "dev", axis=0, tiled=True),
        lax.all_gather(down_weight.astype(jnp.bfloat16), "dev", axis=0, tiled=True),
    )
    devices = lax.axis_size("dev")
    row_count, feature = tokens.shape
    capacity = row_count // devices
    is_live, slot_of, anchor = routing(segment_ids, devices, capacity)
    blank_row = jnp.zeros((1, feature), jnp.bfloat16)
    send_rows = jnp.concatenate([tokens, blank_row], 0)[anchor].reshape(devices, capacity, feature)
    send_grads = jnp.concatenate([cotangent, blank_row], 0)[anchor].reshape(
        devices, capacity, feature
    )
    send_ids = jnp.concatenate([segment_ids, jnp.full((1,), -1, jnp.int32)], 0)[anchor].reshape(
        devices, capacity
    )
    work_rows, work_grads, work_ids = (
        lax.all_to_all(send_rows, "dev", split_axis=0, concat_axis=0, tiled=True),
        lax.all_to_all(send_grads, "dev", split_axis=0, concat_axis=0, tiled=True),
        lax.all_to_all(send_ids, "dev", split_axis=0, concat_axis=0, tiled=True),
    )
    work_rows = work_rows.reshape(row_count, feature)
    work_grads = work_grads.reshape(row_count, feature)
    work_ids = work_ids.reshape(row_count)
    gain_one, shift_one, gain_two, shift_two, bias_query, bias_value, bias_out, bias_down = [
        vector_weight[row_index] for row_index in range(8)
    ]
    bias_up = vector_weight[8:].reshape(FF)
    w_qkv = wide_full[:, : 3 * feature]
    w_out = wide_full[:, 3 * feature : 4 * feature]
    w_up = wide_full[:, 4 * feature :]
    work_float = work_rows.astype(jnp.float32)
    low_one = norm_rows(work_float, gain_one, shift_one).astype(jnp.bfloat16)
    bias_all = jnp.concatenate([bias_query, jnp.zeros_like(bias_query), bias_value])
    projected = (product(low_one, w_qkv) + bias_all).astype(jnp.bfloat16)
    queries = projected[:, :feature].reshape(row_count, HEADS, HEAD)
    key_rows = projected[:, feature : 2 * feature].reshape(row_count, HEADS, HEAD)
    value_rows = projected[:, 2 * feature :].reshape(row_count, HEADS, HEAD)
    same_seg = work_ids[:, None] == work_ids[None, :]
    block_rows = min(512, row_count)
    group_size = math.gcd(HEADS, 4)
    group_count = HEADS // group_size

    def scores_of(offset, first_head):
        query_part = queries[offset : offset + block_rows, first_head : first_head + group_size]
        raw_scores = (
            jnp.einsum(
                "qhd,khd->hqk",
                query_part,
                key_rows[:, first_head : first_head + group_size],
                preferred_element_type=jnp.float32,
            )
            * 0.125
        )
        return jnp.where(same_seg[None], raw_scores, masked_value)

    stored = []
    offset = 0
    head_outs = []
    for group in range(group_count):
        first_head = group * group_size
        scores = scores_of(offset, first_head)
        row_max = jnp.max(scores, -1, keepdims=True)
        powers = jnp.exp(scores - row_max)
        row_sums = jnp.sum(powers, -1, keepdims=True)
        prob_low = (powers / row_sums).astype(jnp.bfloat16)
        head_outs.append(
            jnp.einsum(
                "hqk,khd->qhd",
                prob_low,
                value_rows[:, first_head : first_head + group_size],
                preferred_element_type=jnp.float32,
            )
        )
        stored.append((row_max, row_sums))
    out_blocks = jnp.concatenate(head_outs, 1)
    attended = out_blocks.reshape(row_count, feature).astype(jnp.bfloat16)
    resid = work_float + product(attended, w_out) + bias_out
    low_two = norm_rows(resid, gain_two, shift_two).astype(jnp.bfloat16)
    up_float = product(low_two, w_up) + bias_up
    hidden = gelu_exact(up_float).astype(jnp.bfloat16)
    output_low = (resid + product(hidden, down_full) + bias_down).astype(jnp.bfloat16)
    dy_float = work_grads.astype(jnp.float32)
    dhidden = against(work_grads, down_full)
    gelu_pull = jax.vjp(gelu_exact, up_float)[1]
    dup_low = gelu_pull(dhidden)[0].astype(jnp.bfloat16)
    da_two = against(dup_low, w_up)
    norm_two_pull = jax.vjp(norm_rows, resid, gain_two, shift_two)[1]
    dres_norm, dgain_two, dshift_two = norm_two_pull(da_two)
    dresid = dy_float + dres_norm
    dres_low = dresid.astype(jnp.bfloat16)
    dattended = against(dres_low, w_out).astype(jnp.bfloat16).reshape(row_count, HEADS, HEAD)
    dkey_parts = [
        jnp.zeros((row_count, group_size, HEAD), jnp.float32) for group in range(group_count)
    ]
    dvalue_parts = [
        jnp.zeros((row_count, group_size, HEAD), jnp.float32) for group in range(group_count)
    ]
    position = 0
    offset = 0
    pieces = []
    for group in range(group_count):
        first_head = group * group_size
        scores = scores_of(offset, first_head)
        row_max, row_sums = stored[position]
        position += 1
        prob_float = jnp.exp(scores - row_max) / row_sums
        prob_low = prob_float.astype(jnp.bfloat16)
        dout_part = dattended[offset : offset + block_rows, first_head : first_head + group_size]
        value_part = value_rows[:, first_head : first_head + group_size]
        dvalue_parts[group] = jnp.einsum(
            "hqk,qhd->khd", prob_low, dout_part, preferred_element_type=jnp.float32
        )
        dprob = jnp.einsum(
            "qhd,khd->hqk", dout_part, value_part, preferred_element_type=jnp.float32
        )
        dscore = (prob_float * (dprob - jnp.sum(prob_float * dprob, -1, keepdims=True))).astype(
            jnp.bfloat16
        )
        pieces.append(
            jnp.einsum(
                "hqk,khd->qhd",
                dscore,
                key_rows[:, first_head : first_head + group_size],
                preferred_element_type=jnp.float32,
            )
            * 0.125
        )
        query_part = queries[offset : offset + block_rows, first_head : first_head + group_size]
        dkey_parts[group] = (
            jnp.einsum("hqk,qhd->khd", dscore, query_part, preferred_element_type=jnp.float32)
            * 0.125
        )
    dquery_blocks = jnp.concatenate(pieces, 1)
    dquery_low = dquery_blocks.reshape(row_count, feature).astype(jnp.bfloat16)
    dkey_low = jnp.concatenate(dkey_parts, 1).reshape(row_count, feature).astype(jnp.bfloat16)
    dvalue_low = jnp.concatenate(dvalue_parts, 1).reshape(row_count, feature).astype(jnp.bfloat16)
    dqkv_low = jnp.concatenate([dquery_low, dkey_low, dvalue_low], 1)
    da_one = against(dqkv_low, w_qkv)
    norm_one_pull = jax.vjp(norm_rows, work_float, gain_one, shift_one)[1]
    dinput_norm, dgain_one, dshift_one = norm_one_pull(da_one)
    dinput_low = (dresid + dinput_norm).astype(jnp.bfloat16)
    back_out, back_grad = (
        lax.all_to_all(
            output_low.reshape(devices, capacity, feature),
            "dev",
            split_axis=0,
            concat_axis=0,
            tiled=True,
        ),
        lax.all_to_all(
            dinput_low.reshape(devices, capacity, feature),
            "dev",
            split_axis=0,
            concat_axis=0,
            tiled=True,
        ),
    )
    block_output = jnp.where(
        is_live[:, None], back_out.reshape(row_count, feature)[slot_of], jnp.zeros_like(tokens)
    )
    input_grad = jnp.where(
        is_live[:, None], back_grad.reshape(row_count, feature)[slot_of], jnp.zeros_like(tokens)
    )
    vector_rows = jnp.stack(
        [
            dgain_one,
            dshift_one,
            dgain_two,
            dshift_two,
            jnp.sum(dquery_low.astype(jnp.float32), 0),
            jnp.sum(dvalue_low.astype(jnp.float32), 0),
            jnp.sum(dres_low.astype(jnp.float32), 0),
            jnp.sum(dy_float, 0),
        ],
        0,
    )
    bias_up_grad = jnp.sum(dup_low.astype(jnp.float32), 0).reshape(FF // feature, feature)
    vector_partial = jnp.concatenate([vector_rows, bias_up_grad], 0)
    down_grad = lax.psum_scatter(
        inner_rows(hidden, work_grads), "dev", scatter_dimension=0, tiled=True
    )
    wide_grad = lax.psum_scatter(
        jnp.concatenate(
            [
                inner_rows(low_one, dqkv_low),
                jnp.concatenate([inner_rows(attended, dres_low), inner_rows(low_two, dup_low)], 1),
            ],
            1,
        ),
        "dev",
        scatter_dimension=0,
        tiled=True,
    )
    shard_squares = jnp.sum(wide_grad * wide_grad) + jnp.sum(down_grad * down_grad)
    vector_grad = lax.psum(vector_partial, "dev")
    total = lax.psum(shard_squares, "dev") + jnp.sum(vector_grad * vector_grad)
    grad_norm = jnp.sqrt(total)
    factor = clip_norm / jnp.maximum(grad_norm, clip_norm)
    wide_new, wide_moment_new, wide_average_new = advance(
        wide_weight, wide_moment, wide_average, wide_grad, factor, decay_rate
    )
    down_new, down_moment_new, down_average_new = advance(
        down_weight, down_moment, down_average, down_grad, factor, decay_rate
    )
    vector_new, vector_moment_new, vector_average_new = advance(
        vector_weight, vector_moment, vector_average, vector_grad, factor, 0.0
    )
    return (
        block_output,
        input_grad,
        grad_norm,
        wide_new,
        wide_moment_new,
        wide_average_new,
        down_new,
        down_moment_new,
        down_average_new,
        vector_new,
        vector_moment_new,
        vector_average_new,
    )


def flips(devices, mask):
    return [(i, i ^ mask) for i in range(devices)]


def shifts(devices, step):
    return [(i, (i + PLANE * step) % devices) for i in range(devices)]


def place():
    me = lax.axis_index("dev")
    return jnp.stack([me // PLANE, (me // 4) % 2, (me // 2) % 2, me % 2]).astype(jnp.int32)


def core_order(core, mine, theirs):
    first = jnp.where(core == 0, mine, theirs)
    second = jnp.where(core == 0, theirs, mine)
    return first, second


def pin(*values):
    return lax.optimization_barrier(values)


def send(value, mask):
    return lax.ppermute(value, "dev", flips(lax.axis_size("dev"), mask))


def along_z(block):
    devices = lax.axis_size("dev")
    return [block] + [
        lax.ppermute(block, "dev", shifts(devices, k)) for k in range(1, devices // PLANE)
    ]


def stacked(blocks, stacks):
    depth = len(blocks)
    each = depth // stacks
    return tuple(jnp.stack(blocks[k : k + each], 0) for k in range(0, depth, each))


def to_neighbours(*own):
    return tuple(send(stack, 2) for stack in own) + tuple(send(stack, 4) for stack in own)


def to_diagonal(*near):
    if len(near) == 4:
        return send(near[0], 4), send(near[3], 2)
    half = near[0].shape[0] // 2
    return send(near[0][:half], 4), send(near[1][half:], 2)


def to_partner(*pieces):
    return tuple(send(piece, 1) for piece in pieces)


def total_of(*terms):
    return sum(term.astype(jnp.float32) for term in terms)


def low_sum(*terms):
    return total_of(*terms).astype(jnp.bfloat16)


class Fold:
    def __init__(self, mine, got):
        self.mine, self.got = mine, got
        self.half = mine.shape[1] // 2

    def pair(self, spot, steps):
        return self.mine[spot, steps], self.got[spot, steps]

    def diagonal(self):
        first, last = slice(None, self.half), slice(self.half, None)
        return low_sum(*self.pair(3, first)), low_sum(*self.pair(3, last))

    def neighbours(self, got_a, got_b):
        first, last = slice(None, self.half), slice(self.half, None)
        to_x = (low_sum(*self.pair(1, first), got_a), low_sum(*self.pair(1, last)))
        to_y = (low_sum(*self.pair(2, first)), low_sum(*self.pair(2, last), got_b))
        return jnp.concatenate(to_x, 0), jnp.concatenate(to_y, 0)

    def column(self, got_x, got_y):
        total = total_of(*self.pair(0, slice(None)), got_x, got_y)
        return (total[0],) + tuple(
            total[k].astype(jnp.bfloat16) for k in range(1, total.shape[0])
        )


def over_diagonal(to_a, to_b):
    return send(to_a, 4), send(to_b, 2)


def over_plane(to_x, to_y):
    return send(to_x, 2), send(to_y, 4)


def over_column(sums):
    devices = lax.axis_size("dev")
    return tuple(lax.ppermute(sums[k], "dev", shifts(devices, k)) for k in range(1, len(sums)))


def exchange(rows):
    return lax.all_to_all(rows, "dev", split_axis=0, concat_axis=0, tiled=True)


FAR = pl.BlockSpec(memory_space=pltpu.HBM)
SCALARS = pl.BlockSpec(memory_space=pltpu.SMEM)


def whole(*shape):
    return pl.BlockSpec(shape, lambda *_: (0,) * len(shape))


LIMIT = 48


def settings(limit):
    return pltpu.CompilerParams(vmem_limit_bytes=limit * MIB)


def cost(flops, moved, exps=0):
    return pl.CostEstimate(flops=int(flops), bytes_accessed=int(moved), transcendentals=int(exps))


def shaped(shape, dtype):
    return jax.ShapeDtypeStruct(shape, dtype)


def by_rows(matrix, other):
    return lax.dot_general(
        matrix, other, (((1,), (1,)), ((), ())), preferred_element_type=jnp.float32
    )


def by_columns(matrix, other):
    return lax.dot_general(
        matrix, other, (((0,), (0,)), ((), ())), preferred_element_type=jnp.float32
    )


def normed(values):
    center = values - jnp.mean(values, -1, keepdims=True)
    scale = lax.rsqrt(jnp.mean(center * center, -1, keepdims=True) + epsilon)
    return center * scale, scale


def norm_back(grad, gain, unit, scale):
    inner = grad * gain
    return scale * (
        inner
        - jnp.mean(inner, -1, keepdims=True)
        - unit * jnp.mean(inner * unit, -1, keepdims=True)
    )


def iota(shape, axis):
    return lax.broadcasted_iota(jnp.int32, shape, axis)


def slots_of(ids_row, capacity, groups):
    count = ids_row.shape[1]
    square = (count, count)
    ids = jnp.sum(
        jnp.where(iota(square, 0) == iota(square, 1), ids_row, 0), axis=1, keepdims=True
    )
    group = jnp.right_shift(ids, DOCS_DEV.bit_length() - 1)
    lanes = max(128, groups)
    onehot = jnp.where(group == iota((count, lanes), 1), 1.0, 0.0)
    lower = jnp.where(iota(square, 0) > iota(square, 1), 1.0, 0.0).astype(jnp.bfloat16)
    earlier = product(lower, onehot.astype(jnp.bfloat16))
    within = jnp.sum(earlier * onehot, axis=1, keepdims=True).astype(jnp.int32)
    return ids, jnp.where(ids >= 0, group * capacity + within, -1)


def route(ids_row, tokens, cotangent, devices):
    count, feature = tokens.shape

    def kernel(ids_ref, tokens_ref, cotangent_ref, rows_ref, grads_ref, slot_ref):
        ids, slot = slots_of(ids_ref[...], count // devices, devices)
        slot_ref[...] = slot
        move = jnp.where(slot == iota((count, count), 1), 1.0, 0.0).astype(jnp.bfloat16)
        code = jnp.where(ids >= 0, jnp.bitwise_and(ids, DOCS_DEV - 1) + 1, 0)
        code = jnp.broadcast_to(code.astype(jnp.float32), (count, 128)).astype(jnp.bfloat16)
        rows_ref[:, :feature] = by_columns(move, tokens_ref[...]).astype(jnp.bfloat16)
        rows_ref[:, feature:] = by_columns(move, code).astype(jnp.bfloat16)
        grads_ref[...] = by_columns(move, cotangent_ref[...]).astype(jnp.bfloat16)

    return pl.pallas_call(
        kernel,
        out_shape=[
            shaped((count, feature + 128), jnp.bfloat16),
            shaped((count, feature), jnp.bfloat16),
            shaped((count, 1), jnp.int32),
        ],
        compiler_params=settings(LIMIT),
        cost_estimate=cost(4 * count * count * feature, 8 * count * feature),
    )(ids_row, tokens, cotangent)


def give_back(slot, rows):
    count, feature = rows.shape[0], rows.shape[1] // 256 * 256

    def kernel(slot_ref, rows_ref, out_ref):
        move = jnp.where(slot_ref[...] == iota((count, count), 1), 1.0, 0.0).astype(jnp.bfloat16)
        out_ref[...] = product(move, rows_ref[...]).astype(jnp.bfloat16)

    return pl.pallas_call(
        kernel,
        grid=(1,),
        out_shape=shaped((count, feature), jnp.bfloat16),
        in_specs=[whole(count, 1), whole(count, feature)],
        out_specs=whole(count, feature),
        compiler_params=settings(LIMIT),
        cost_estimate=cost(2 * count * count * feature, 4 * count * feature),
    )(slot, rows)


def pieces_of(where_ref, pieces):
    z, y, x, core = where_ref[0], where_ref[1], where_ref[2], where_ref[3]
    count = len(pieces) // 2
    depth = 2 * pieces[count - 1].shape[0]
    columns = ((y, x), (y, 1 - x), (1 - y, x), (1 - y, 1 - x))
    for part, group in ((core, pieces[:count]), (1 - core, pieces[count:])):
        reached = 0
        for piece in group:
            for index in range(piece.shape[0]):
                yy, xx = columns[reached // depth]
                step = reached % depth
                zz = lax.rem(z - step + depth, depth)
                yield piece.at[index], step, (zz * 2 + yy) * 2 + xx, part
                reached += 1


def wide_copies(where_ref, pieces, buffer, sems):
    copies = []
    for source, _, chip, part in pieces_of(where_ref, pieces):
        rows, columns = source.shape
        target = buffer.at[
            pl.ds(pl.multiple_of(chip * rows, 16), rows),
            pl.ds(pl.multiple_of(part * columns, 128), columns),
        ]
        copies.append(pltpu.make_async_copy(source, target, sems.at[len(copies)]))
    return copies


def down_copies(where_ref, pieces, buffer, sems):
    copies = []
    for source, _, chip, part in pieces_of(where_ref, pieces):
        rows = source.shape[0]
        row = pl.multiple_of((chip * 2 + part) * rows, 16)
        copies.append(
            pltpu.make_async_copy(source, buffer.at[pl.ds(row, rows)], sems.at[len(copies)])
        )
    return copies


def project(where, work, vector, pieces):
    count, feature = work.shape[0], vector.shape[1]
    copies_count = sum(piece.shape[0] for piece in pieces)
    tile = 256

    def kernel(where_ref, work_ref, vector_ref, *refs):
        (
            flipped_ref, out_ref, weights_ref, output_ref, low, buffer, sems, store_sems
        ) = refs[len(pieces):]
        copies = wide_copies(where_ref, refs[:len(pieces)], buffer, sems)
        for copy in copies:
            copy.start()

        def rows_of(index, carry):
            rows = pl.ds(pl.multiple_of(index * 64, 64), 64)
            unit, _ = normed(work_ref[rows, :].astype(jnp.float32))
            low[rows, :] = (unit * vector_ref[0:1, :] + vector_ref[1:2, :]).astype(jnp.bfloat16)
            return carry

        lax.fori_loop(0, count // 64, rows_of, 0)
        flipped_ref[...] = low[...].astype(jnp.float32).T.astype(jnp.bfloat16)
        for copy in copies:
            copy.wait()
        stores = [
            pltpu.make_async_copy(
                buffer.at[:, pl.ds(0, 3 * feature)], weights_ref, store_sems.at[0]
            ),
            pltpu.make_async_copy(
                buffer.at[:, pl.ds(3 * feature, feature)], output_ref, store_sems.at[1]
            ),
        ]
        for store in stores:
            store.start()
        for part, bias in ((0, 4), (1, None), (2, 5)):

            def columns_of(index, carry):
                inner = pl.ds(pl.multiple_of(index * tile, tile), tile)
                columns = pl.ds(pl.multiple_of(part * feature + index * tile, tile), tile)
                value = product(low[...], buffer[:, columns])
                if bias is not None:
                    value = value + vector_ref[bias : bias + 1, inner]
                out_ref[:, columns] = value.astype(jnp.bfloat16)
                return carry

            lax.fori_loop(0, feature // tile, columns_of, 0)
        for store in stores:
            store.wait()

    return pl.pallas_call(
        kernel,
        grid=(1,),
        out_shape=[
            shaped((feature, count), jnp.bfloat16),
            shaped((count, 3 * feature), jnp.bfloat16),
            shaped((feature, 3 * feature), jnp.bfloat16),
            shaped((feature, feature), jnp.bfloat16),
        ],
        in_specs=[SCALARS, whole(count, feature), whole(*vector.shape)] + [FAR] * len(pieces),
        out_specs=[whole(feature, count), whole(count, 3 * feature), FAR, FAR],
        scratch_shapes=[
            pltpu.VMEM((count, feature), jnp.bfloat16),
            pltpu.VMEM((feature, 4 * feature), jnp.bfloat16),
            pltpu.SemaphoreType.DMA((copies_count,)),
            pltpu.SemaphoreType.DMA((2,)),
        ],
        compiler_params=settings(60),
        cost_estimate=cost(6 * count * feature * feature, 12 * feature * feature),
    )(where, work, vector, *pieces)


def fill_cap(code_ref, cap):
    code = code_ref[...].astype(jnp.float32)
    cap[...] = jnp.where(code[:, :1] == code.T[:1], -masked_value, masked_value)


def one_head(values, head):
    lanes = iota(values.shape, 1)
    inside = (lanes >= head * HEAD) & (lanes < (head + 1) * HEAD)
    return jnp.where(inside, values, 0.0).astype(jnp.bfloat16)


def attend(projected, work, vector, weights, first, pairs, left=None):
    count, feature = work.shape[0], vector.shape[1]
    all_pairs = feature // 128
    tile = 512
    ends = left is not None

    def kernel(q_ref, k_ref, v_ref, code_ref, *refs):
        if ends:
            (
                weight_ref, work_ref, vector_ref, left_ref, flipped_ref, stat_ref, resid_ref, low_ref,
                cap, right, total,
            ) = refs
        else:
            flipped_ref, stat_ref, attended_ref, cap = refs
        pair = pl.program_id(0)

        @pl.when(pair == 0)
        def _():
            fill_cap(code_ref, cap)

        keys = k_ref[...]
        values = v_ref[...].astype(jnp.float32).T.astype(jnp.bfloat16)
        scaled = q_ref[...].astype(jnp.float32) * 0.125
        heads = []
        for head in range(2):
            query = one_head(scaled, head)
            parts = []
            for start in range(0, count, tile):
                span = slice(start, start + tile)
                scores = jnp.minimum(by_rows(keys, query[span]), cap[:, span])
                most = jnp.max(scores, 0, keepdims=True)
                powers = jnp.exp(scores - most)
                sums = jnp.sum(powers, 0, keepdims=True)
                stat_ref[0, head : head + 1, span] = most + jnp.log(sums)
                mixed = product(
                    values[head * HEAD : (head + 1) * HEAD], powers.astype(jnp.bfloat16)
                )
                parts.append(mixed * (1.0 / sums))
            heads.append(jnp.concatenate(parts, 1))
        both = jnp.concatenate(heads, 0)
        flipped_ref[...] = both.astype(jnp.bfloat16)
        attended = both.T.astype(jnp.bfloat16)
        if ends:
            right[pair] = attended
        else:
            attended_ref[...] = attended

        if ends:

            @pl.when(pair == pairs - 1)
            def _():
                middle = feature - pairs * 128
                for start in range(0, feature, 256):
                    span = slice(start, start + 256)
                    value = product(left_ref[...], weight_ref[:middle, span])
                    for index in range(pairs):
                        rows = slice(middle + index * 128, middle + (index + 1) * 128)
                        value = value + product(right[index], weight_ref[rows, span])
                    total[:, span] = value

                def rows_of(index, carry):
                    rows = pl.ds(pl.multiple_of(index * 64, 64), 64)
                    resid = (
                        work_ref[rows, :].astype(jnp.float32) + total[rows, :] + vector_ref[6:7, :]
                    )
                    resid_ref[rows, :] = resid
                    unit, _ = normed(resid)
                    low_ref[rows, :] = (unit * vector_ref[2:3, :] + vector_ref[3:4, :]).astype(
                        jnp.bfloat16
                    )
                    return carry

                lax.fori_loop(0, count // 64, rows_of, 0)

    def columns_at(offset):
        return pl.BlockSpec((count, 128), lambda pair: (0, offset + pair))

    wide = whole(count, feature)
    return pl.pallas_call(
        kernel,
        grid=(pairs,),
        out_shape=[
            shaped((pairs * 128, count), jnp.bfloat16),
            shaped((pairs, 8, count), jnp.float32),
        ]
        + (
            [shaped((count, feature), jnp.float32), shaped((count, feature), jnp.bfloat16)]
            if ends
            else [shaped((count, pairs * 128), jnp.bfloat16)]
        ),
        in_specs=[
            columns_at(first),
            columns_at(all_pairs + first),
            columns_at(2 * all_pairs + first),
            pl.BlockSpec((count, 128), lambda pair: (0, all_pairs)),
        ]
        + (
            [whole(feature, feature), wide, whole(*vector.shape), whole(*left.shape)]
            if ends
            else []
        ),
        out_specs=[
            pl.BlockSpec((128, count), lambda pair: (pair, 0)),
            pl.BlockSpec((1, 8, count), lambda pair: (pair, 0, 0)),
        ]
        + ([wide, wide] if ends else [columns_at(0)]),
        scratch_shapes=[pltpu.VMEM((count, count), jnp.float32)]
        + (
            [
                pltpu.VMEM((pairs, count, 128), jnp.bfloat16),
                pltpu.VMEM((count, feature), jnp.float32),
            ]
            if ends
            else []
        ),
        compiler_params=settings(60),
        cost_estimate=cost(
            8 * count * count * pairs * 128, 14 * count * feature, 2 * pairs * count * count
        ),
    )(
        projected, projected, projected, work,
        *([weights, work, vector, left] if ends else []),
    )


def widen(where, low, bias_row, pieces):
    count, feature = low.shape
    wide = bias_row.shape[1]
    tile = feature
    steps = wide // tile

    def kernel(where_ref, low_ref, bias_ref, *refs):
        hidden_ref, slope_ref, weights_ref, buffer, sems, store_sem = refs[len(pieces):]
        step = pl.program_id(0)
        store = pltpu.make_async_copy(buffer, weights_ref, store_sem)

        @pl.when(step == 0)
        def _():
            copies = wide_copies(where_ref, refs[:len(pieces)], buffer, sems)
            for copy in copies:
                copy.start()
            for copy in copies:
                copy.wait()
            store.start()

        columns = pl.ds(pl.multiple_of(step * tile, tile), tile)
        up = product(low_ref[...], buffer[:, columns]) + bias_ref[...]
        below = 0.5 * (1.0 + lax.erf(up * (0.5**0.5)))
        hidden_ref[...] = (up * below).astype(jnp.bfloat16)
        slope_ref[...] = below + up * (jnp.exp(-0.5 * up * up) * ((2.0 * math.pi) ** -0.5))

        @pl.when(step == steps - 1)
        def _():
            store.wait()

    block = pl.BlockSpec((count, tile), lambda step: (0, step))
    return pl.pallas_call(
        kernel,
        grid=(steps,),
        out_shape=[
            shaped((count, wide), jnp.bfloat16),
            shaped((count, wide), jnp.float32),
            shaped((feature, wide), jnp.bfloat16),
        ],
        in_specs=[
            SCALARS,
            whole(count, feature),
            pl.BlockSpec((1, tile), lambda step: (0, step)),
        ]
        + [FAR] * len(pieces),
        out_specs=[block, block, FAR],
        scratch_shapes=[
            pltpu.VMEM((feature, wide), jnp.bfloat16),
            pltpu.SemaphoreType.DMA((sum(piece.shape[0] for piece in pieces),)),
            pltpu.SemaphoreType.DMA,
        ],
        compiler_params=settings(60),
        cost_estimate=cost(
            2 * count * feature * wide, 2 * feature * wide + 6 * count * wide, count * wide
        ),
    )(where, low, bias_row, *pieces)


def down_gradient(where, hidden, grads, depth):
    count, wide = hidden.shape
    feature = grads.shape[1]
    rows = wide // (depth * PLANE)
    part = wide // depth

    def kernel(where_ref, hidden_ref, grads_ref, mine_ref, theirs_ref, result):
        y, x, core = where_ref[1], where_ref[2], where_ref[3]
        result[...] = by_columns(hidden_ref[...], grads_ref[...])
        for yy in range(2):
            for xx in range(2):
                spot = jnp.bitwise_xor(y, yy) * 2 + jnp.bitwise_xor(x, xx)
                first = (yy * 2 + xx) * 2
                for target, side in ((mine_ref, core), (theirs_ref, 1 - core)):
                    row = pl.multiple_of((first + side) * rows, 16)
                    target[spot, 0] = result[pl.ds(row, rows), :].astype(jnp.bfloat16)

    shape = shaped((4, depth, rows, feature), jnp.bfloat16)
    block = pl.BlockSpec((4, 1, rows, feature), lambda step, where_ref: (0, step, 0, 0))
    return pl.pallas_call(
        kernel,
        out_shape=[shape, shape],
        grid_spec=pltpu.PrefetchScalarGridSpec(
            num_scalar_prefetch=1,
            grid=(depth,),
            in_specs=[
                pl.BlockSpec(
                    (count, part),
                    lambda step, where_ref: (0, lax.rem(where_ref[0] + step, depth)),
                ),
                whole(count, feature),
            ],
            out_specs=[block, block],
            scratch_shapes=[pltpu.VMEM((part, feature), jnp.float32)],
        ),
        compiler_params=settings(LIMIT),
        cost_estimate=cost(2 * count * wide * feature, 2 * wide * (count + feature)),
    )(where, hidden, grads)


def put_wide(where_ref, result, mine_ref, theirs_ref):
    z, y, x, core = where_ref[0], where_ref[1], where_ref[2], where_ref[3]
    _, depth, rows, _ = mine_ref.shape
    for chip in range(4 * depth):
        zz, yy, xx = chip // 4, (chip // 2) % 2, chip % 2
        step = lax.rem(zz - z + depth, depth)
        spot = jnp.bitwise_xor(y, yy) * 2 + jnp.bitwise_xor(x, xx)
        for target, side in ((mine_ref, core), (theirs_ref, 1 - core)):
            row = pl.multiple_of((chip * 2 + side) * rows, 8)
            target[spot, step] = result[pl.ds(row, rows), :].astype(jnp.bfloat16)


def narrow(where, hidden, resid, vector, pieces):
    count, wide = hidden.shape
    feature = resid.shape[1]
    tile = 256

    def kernel(where_ref, hidden_ref, resid_ref, vector_ref, *refs):
        out_ref, weights_ref, buffer, sems, store_sem = refs[len(pieces):]
        copies = down_copies(where_ref, refs[:len(pieces)], buffer, sems)
        for copy in copies:
            copy.start()
        for copy in copies:
            copy.wait()
        store = pltpu.make_async_copy(buffer, weights_ref, store_sem)
        store.start()

        def columns_of(index, carry):
            columns = pl.ds(pl.multiple_of(index * tile, tile), tile)
            value = product(hidden_ref[...], buffer[:, columns])
            out_ref[:, columns] = (
                resid_ref[:, columns] + (value + vector_ref[7:8, columns])
            ).astype(jnp.bfloat16)
            return carry

        lax.fori_loop(0, feature // tile, columns_of, 0)
        store.wait()

    return pl.pallas_call(
        kernel,
        grid=(1,),
        out_shape=[
            shaped((count, feature), jnp.bfloat16),
            shaped((wide, feature), jnp.bfloat16),
        ],
        in_specs=[SCALARS, whole(count, wide), whole(count, feature), whole(*vector.shape)]
        + [FAR] * len(pieces),
        out_specs=[whole(count, feature), FAR],
        scratch_shapes=[
            pltpu.VMEM((wide, feature), jnp.bfloat16),
            pltpu.SemaphoreType.DMA((sum(piece.shape[0] for piece in pieces),)),
            pltpu.SemaphoreType.DMA,
        ],
        compiler_params=settings(LIMIT),
        cost_estimate=cost(2 * count * wide * feature, 6 * wide * feature),
    )(where, hidden, resid, vector, *pieces)


def feed_back(where, slope, low, grads, resid, vector, up_weights, down_weights, attended, depth):
    count, wide = slope.shape
    feature = resid.shape[1]
    tile = feature
    steps = wide // tile
    half = feature // 2
    chip_rows = feature // (PLANE * depth)

    def kernel(
        where_ref, slope_ref, low_ref, grads_ref, resid_ref, vector_ref, up_ref, down_ref, left_ref, right_ref,
        dresid_ref, dlow_ref, sums_ref, bias_ref, mine_ref, theirs_ref, back, flipped, result,
    ):
        step = pl.program_id(0)

        @pl.when(step == 0)
        def _():
            flipped[...] = low_ref[...].astype(jnp.float32).T.astype(jnp.bfloat16)
            back[...] = jnp.zeros_like(back)

        @pl.when(step < steps)
        def _():
            dup = (slope_ref[...] * by_rows(grads_ref[...], down_ref[...])).astype(jnp.bfloat16)
            bias_ref[...] = jnp.sum(dup.astype(jnp.float32), 0, keepdims=True)
            back[...] += by_rows(dup, up_ref[...])
            result[...] = product(flipped[...], dup)

        @pl.when(step == steps)
        def _():
            sums_ref[...] = jnp.zeros_like(sums_ref)

            def rows_of(index, carry):
                rows = pl.ds(pl.multiple_of(index * 64, 64), 64)
                unit, scale = normed(resid_ref[rows, :])
                da = back[rows, :]
                dy = grads_ref[rows, :].astype(jnp.float32)
                dresid = dy + norm_back(da, vector_ref[2:3, :], unit, scale)
                dresid_ref[rows, :] = dresid
                dlow = dresid.astype(jnp.bfloat16)
                dlow_ref[rows, :] = dlow
                for row, value in enumerate((da * unit, da, dlow.astype(jnp.float32), dy)):
                    sums_ref[row : row + 1, :] += jnp.sum(value, 0, keepdims=True)
                return carry

            lax.fori_loop(0, count // 64, rows_of, 0)
            result[:half, :] = product(left_ref[...], dlow_ref[...])
            result[half:, :] = product(right_ref[...], dlow_ref[...])

        put_wide(where_ref, result, mine_ref, theirs_ref)

    def at(step):
        return jnp.minimum(step, steps - 1)

    def columns_at(rows):
        return pl.BlockSpec((rows, tile), lambda step: (0, at(step)))

    all_rows = whole(count, feature)
    split = shaped((4, depth, chip_rows, (steps + 1) * feature), jnp.bfloat16)
    block = pl.BlockSpec((4, depth, chip_rows, feature), lambda step: (0, 0, 0, step))
    return pl.pallas_call(
        kernel,
        grid=(steps + 1,),
        out_shape=[
            shaped((count, feature), jnp.float32),
            shaped((count, feature), jnp.bfloat16),
            shaped((8, feature), jnp.float32),
            shaped((1, wide), jnp.float32),
            split,
            split,
        ],
        in_specs=[
            SCALARS,
            columns_at(count),
            all_rows,
            all_rows,
            all_rows,
            whole(*vector.shape),
            columns_at(feature),
            pl.BlockSpec((tile, feature), lambda step: (at(step), 0)),
            whole(half, count),
            whole(half, count),
        ],
        out_specs=[all_rows, all_rows, whole(8, feature), columns_at(1), block, block],
        scratch_shapes=[
            pltpu.VMEM((count, feature), jnp.float32),
            pltpu.VMEM((feature, count), jnp.bfloat16),
            pltpu.VMEM((feature, feature), jnp.float32),
        ],
        compiler_params=settings(60),
        cost_estimate=cost(6 * count * wide * feature, 8 * wide * feature + 10 * count * wide),
    )(where, slope, low, grads, resid, vector, up_weights, down_weights, *attended)


def attend_back(projected, work, stats, dlow, weights, first, pairs):
    count, feature = dlow.shape
    all_pairs = feature // 128
    tile = 512
    wide = pairs * 128

    def kernel(
        q_ref, k_ref, v_ref, code_ref, stat_ref, dlow_ref, weight_ref, out_ref, sums_ref, douts, cap
    ):
        pair = pl.program_id(0)

        @pl.when(pair == 0)
        def _():
            fill_cap(code_ref, cap)
            for start in range(0, wide, 128):
                span = slice(start, start + 128)
                douts[start // 128] = by_rows(dlow_ref[...], weight_ref[span, :]).astype(
                    jnp.bfloat16
                )

        keys, values = k_ref[...], v_ref[...]
        wide_keys = keys.astype(jnp.float32)
        dquery = jnp.zeros((count, 128), jnp.float32)
        scaled = q_ref[...].astype(jnp.float32) * 0.125
        dout = douts[pair].astype(jnp.float32)
        dkey = jnp.zeros((count, 128), jnp.float32)
        dvalue = jnp.zeros((count, 128), jnp.float32)
        for head in range(2):
            query = one_head(scaled, head)
            dhead = one_head(dout, head)
            for start in range(0, count, tile):
                span = slice(start, start + tile)
                scores = jnp.minimum(by_rows(keys, query[span]), cap[:, span])
                probs = jnp.exp(scores - stat_ref[0, head : head + 1, span])
                dprob = by_rows(values, dhead[span])
                inner = jnp.sum(probs * dprob, 0, keepdims=True)
                dscore = (probs * (dprob - inner)).astype(jnp.bfloat16)
                dvalue = dvalue + product(probs.astype(jnp.bfloat16), dhead[span])
                dkey = dkey + product(dscore, query[span])
                dquery = dquery + by_columns(dscore, one_head(wide_keys, head))
        dquery = (dquery * 0.125).astype(jnp.bfloat16)
        dvalue = dvalue.astype(jnp.bfloat16)
        out_ref[0] = dquery
        out_ref[1] = dkey.astype(jnp.bfloat16)
        out_ref[2] = dvalue
        sums_ref[0:1, :] = jnp.sum(dquery.astype(jnp.float32), 0, keepdims=True)
        sums_ref[1:2, :] = jnp.sum(dvalue.astype(jnp.float32), 0, keepdims=True)

    def columns_at(offset):
        return pl.BlockSpec((count, 128), lambda pair: (0, offset + pair))

    return pl.pallas_call(
        kernel,
        grid=(pairs,),
        out_shape=[
            shaped((3, count, wide), jnp.bfloat16),
            shaped((8, wide), jnp.float32),
        ],
        in_specs=[
            columns_at(first),
            columns_at(all_pairs + first),
            columns_at(2 * all_pairs + first),
            pl.BlockSpec((count, 128), lambda pair: (0, all_pairs)),
            pl.BlockSpec((1, 8, count), lambda pair: (pair, 0, 0)),
            whole(count, feature),
            pl.BlockSpec((wide, feature), lambda pair: (first // pairs, 0)),
        ],
        out_specs=[
            pl.BlockSpec((3, count, 128), lambda pair: (0, 0, pair)),
            pl.BlockSpec((8, 128), lambda pair: (0, pair)),
        ],
        scratch_shapes=[
            pltpu.VMEM((pairs, count, 128), jnp.bfloat16),
            pltpu.VMEM((count, count), jnp.float32),
        ],
        compiler_params=settings(LIMIT),
        cost_estimate=cost(
            14 * count * count * wide, 16 * count * feature, 2 * pairs * count * count
        ),
    )(projected, projected, projected, work, stats, dlow, weights)


def first_gradient(where, flipped, dprojected, depth):
    feature, count = flipped.shape
    half = feature // 2
    rows = feature // (PLANE * depth)

    def kernel(where_ref, flipped_ref, d_ref, e_ref, mine_ref, theirs_ref, result):
        result[:, :half] = product(flipped_ref[...], d_ref[0])
        result[:, half:] = product(flipped_ref[...], e_ref[0])
        put_wide(where_ref, result, mine_ref, theirs_ref)

    shape = shaped((4, depth, rows, 3 * feature), jnp.bfloat16)
    block = pl.BlockSpec((4, depth, rows, feature), lambda step: (0, 0, 0, step))
    part = pl.BlockSpec((1, count, half), lambda step: (step, 0, 0))
    return pl.pallas_call(
        kernel,
        grid=(3,),
        out_shape=[shape, shape],
        in_specs=[SCALARS, whole(feature, count), part, part],
        out_specs=[block, block],
        scratch_shapes=[pltpu.VMEM((feature, feature), jnp.float32)],
        compiler_params=settings(60),
        cost_estimate=cost(6 * count * feature * feature, 16 * feature * feature),
    )(where, flipped, *dprojected)


def project_back(work, dprojected, dresid, vector, weights, sums_two, sums_attend, bias_up, devices):
    count, feature = dresid.shape
    tile = 128
    half = feature // 2
    lanes = 16 * feature // devices // 128
    capacity = count // devices

    def kernel(
        work_ref, d_ref, e_ref, dresid_ref, vector_ref, weight_ref, two_ref, left_ref, right_ref, bias_ref,
        out_ref, sums,
    ):
        sums[...] = jnp.zeros_like(sums)

        def rows_of(index, carry):
            rows = pl.ds(pl.multiple_of(index * tile, tile), tile)
            da = jnp.zeros((tile, feature), jnp.float32)
            for part in range(3):
                middle = part * feature + half
                da += by_rows(d_ref[part, rows, :], weight_ref[:, middle - half : middle])
                da += by_rows(e_ref[part, rows, :], weight_ref[:, middle : middle + half])
            unit, scale = normed(work_ref[rows, :].astype(jnp.float32))
            out_ref[rows, :feature] = (
                dresid_ref[rows, :] + norm_back(da, vector_ref[0:1, :], unit, scale)
            ).astype(jnp.bfloat16)
            sums[0:1, :] += jnp.sum(da * unit, 0, keepdims=True)
            sums[1:2, :] += jnp.sum(da, 0, keepdims=True)
            return carry

        lax.fori_loop(0, count // tile, rows_of, 0)
        sums[2:4, :] = two_ref[0:2, :]
        sums[4:6, :half] = left_ref[0:2, :]
        sums[4:6, half:] = right_ref[0:2, :]
        sums[6:8, :] = two_ref[2:4, :]
        for row in range(FF // feature):
            sums[8 + row : 9 + row, :] = bias_ref[0:1, row * feature : (row + 1) * feature]
        place_in = iota((capacity, 128), 0)
        for device in range(devices):
            block = jnp.zeros((capacity, 128), jnp.float32)
            for lane in range(lanes):
                first = device * lanes + lane
                row, column = divmod(first * 128, feature)
                value = sums[row : row + 1, column : column + 128]
                high = value.astype(jnp.bfloat16).astype(jnp.float32)
                block = jnp.where(place_in == lane, high, block)
                block = jnp.where(place_in == lanes + lane, value - high, block)
            out_ref[device * capacity : (device + 1) * capacity, feature:] = block.astype(
                jnp.bfloat16
            )

    return pl.pallas_call(
        kernel,
        grid=(1,),
        out_shape=shaped((count, feature + 128), jnp.bfloat16),
        in_specs=[
            whole(count, feature),
            whole(3, count, half),
            whole(3, count, half),
            whole(count, feature),
            whole(*vector.shape),
            whole(feature, 3 * feature),
            whole(8, feature),
            whole(8, half),
            whole(8, half),
            whole(1, FF),
        ],
        out_specs=whole(count, feature + 128),
        scratch_shapes=[pltpu.VMEM((16, feature), jnp.float32)],
        compiler_params=settings(LIMIT),
        cost_estimate=cost(6 * count * feature * feature, 6 * feature * feature),
    )(work, *dprojected, dresid, vector, weights, sums_two, *sums_attend, bias_up)


def settle(own, got, back, squares, devices, feature):
    rows, columns = own.shape
    lanes = 16 * feature // devices // 128
    capacity = back.shape[1]

    def kernel(squares_ref, own_ref, *refs):
        got_refs, (back_ref, grad_ref, packet_ref) = refs[: len(got)], refs[len(got) :]
        grad = own_ref[...]
        for ref in got_refs:
            grad += ref[...].astype(jnp.float32)
        grad_ref[...] = grad
        total = squares_ref[0, 0] + jnp.sum(grad * grad)
        sums = jnp.sum(back_ref[...].astype(jnp.float32), 0)
        packet_ref[:, :lanes, :] = jnp.broadcast_to(
            (sums[:lanes] + sums[lanes : 2 * lanes])[None], (devices, lanes, 128)
        )
        packet_ref[:, lanes:, :] = jnp.full((devices, 1, 128), total, jnp.float32)

    return pl.pallas_call(
        kernel,
        grid=(1,),
        out_shape=[
            shaped((rows, columns), jnp.float32),
            shaped((devices, lanes + 1, 128), jnp.float32),
        ],
        in_specs=[SCALARS, whole(rows, columns)]
        + [whole(rows, columns)] * len(got)
        + [pl.BlockSpec((devices, capacity, 128), lambda step: (0, 0, feature // 128))],
        out_specs=[whole(rows, columns), whole(devices, lanes + 1, 128)],
        compiler_params=settings(60),
        cost_estimate=cost(8 * rows * columns, 16 * rows * columns),
    )(squares.reshape(1, 1), own, *got, back)


def finish(packets, first_grad, up_grad, down_grad, wide, down, vector):
    devices, lanes, _ = packets.shape
    lanes -= 1
    rows, columns = wide[0].shape
    down_rows, feature = down[0].shape
    vector_rows = vector[0].shape[0]
    steps = 2
    tile, down_tile = columns // steps, down_rows // steps
    first_columns = first_grad.shape[1]

    def kernel(packets_ref, first_ref, up_ref, down_grad_ref, *refs):
        wide_refs, down_refs, vector_refs = refs[:3], refs[3:6], refs[6:9]
        norm_ref, wide_new, down_new, vector_new = refs[9], refs[10:13], refs[13:16], refs[16:19]
        sums, factor_ref = refs[19:]
        step = pl.program_id(0)

        def put(new, old, gradient, decay):
            for ref, value in zip(
                new, advance(*(ref[...] for ref in old), gradient, factor_ref[0], decay), strict=True
            ):
                ref[...] = value

        @pl.when(step == 0)
        def _():
            for place_of in range(vector_rows * feature // 128):
                device, lane = divmod(place_of, lanes)
                row, column = divmod(place_of * 128, feature)
                sums[row : row + 1, column : column + 128] = packets_ref[device, lane : lane + 1]
            gradient = sums[...]
            shares = packets_ref[:, lanes, :1]
            total = jnp.sum(shares) + jnp.sum(gradient * gradient)
            norm = jnp.sqrt(jnp.full((1, 1), total))
            norm_ref[...] = norm
            factor_ref[0] = jnp.sum(clip_norm / jnp.maximum(norm, clip_norm))
            put(vector_new, vector_refs, gradient, 0.0)

        for index in range(steps):

            @pl.when(step == index)
            def _():
                first = index * tile
                parts = []
                if first < first_columns:
                    parts.append(first_ref[:, first : min(first + tile, first_columns)])
                if first + tile > first_columns:
                    low = max(first - first_columns, 0)
                    high = first + tile - first_columns
                    if low < feature:
                        parts.append(up_ref[:, FF + low : FF + min(high, feature)])
                    if high > feature:
                        parts.append(up_ref[:, max(low - feature, 0) : high - feature])
                gradient = parts[0] if len(parts) == 1 else jnp.concatenate(parts, 1)
                put(wide_new, wide_refs, gradient, decay_rate)

        put(down_new, down_refs, down_grad_ref[...], decay_rate)

    def tiles(shape):
        return pl.BlockSpec(shape, lambda step: (0, step))

    wide_specs = [tiles((rows, tile))] * 3
    down_specs = [pl.BlockSpec((down_tile, feature), lambda step: (step, 0))] * 3
    vector_specs = [whole(vector_rows, feature)] * 3
    return pl.pallas_call(
        kernel,
        grid=(steps,),
        out_shape=[shaped((1, 1), jnp.float32)]
        + [shaped(part.shape, jnp.float32) for part in (*wide, *down, *vector)],
        in_specs=[
            whole(*packets.shape),
            whole(*first_grad.shape),
            whole(*up_grad.shape),
            down_specs[0],
        ]
        + wide_specs
        + down_specs
        + vector_specs,
        out_specs=[whole(1, 1)] + wide_specs + down_specs + vector_specs,
        scratch_shapes=[
            pltpu.VMEM((vector_rows, feature), jnp.float32),
            pltpu.SMEM((1,), jnp.float32),
        ],
        compiler_params=settings(60),
        cost_estimate=cost(20 * rows * columns, 40 * rows * columns),
    )(packets, first_grad, up_grad, down_grad, *wide, *down, *vector)


def structured(devices, feature):
    rows = feature // devices
    return devices % PLANE == 0 and feature % devices == 0 and (2 * rows) % 16 == 0


def body(
    tokens,
    cotangent,
    segment_ids,
    wide_weight,
    wide_moment,
    wide_average,
    down_weight,
    down_moment,
    down_average,
    vector_weight,
    vector_moment,
    vector_average,
):
    devices = lax.axis_size("dev")
    count, feature = tokens.shape
    if not structured(devices, feature):
        return plain_body(
            tokens,
            cotangent,
            segment_ids,
            wide_weight,
            wide_moment,
            wide_average,
            down_weight,
            down_moment,
            down_average,
            vector_weight,
            vector_moment,
            vector_average,
        )
    depth = devices // PLANE
    capacity = count // devices
    where = place()
    core = where[3]

    wide_low, down_low = wide_weight.astype(jnp.bfloat16), down_weight.astype(jnp.bfloat16)
    rows, columns = wide_low.shape
    parts = wide_low.reshape(rows, 2, 2, columns // 4)
    keep, give = core_order(core, parts[:, :, 0], parts[:, :, 1])
    got = lax.ppermute(give, "dev", flips(devices, 1))
    pair = jnp.concatenate(core_order(core, keep, got), 0)

    send_rows, send_grads, slot = route(segment_ids.reshape(1, count), tokens, cotangent, devices)
    first_own = along_z(pair[:, 0])
    send_rows, first_own[1] = pin(send_rows, first_own[1])
    first_own = stacked(first_own, 2)

    work = exchange(send_rows.reshape(devices, capacity, -1)).reshape(count, -1)
    first_near = pin(*to_neighbours(*first_own))

    first_far = to_diagonal(*first_near)
    first_got = to_partner(*first_own, *first_near)
    first_far, first_got = pin(first_far, first_got)
    first_got = first_got + to_partner(*first_far)
    first_got, work, up_block = pin(first_got, work, pair[:, 1])

    up_own = stacked(along_z(up_block), 1)
    flipped_one, projected, first_weights, out_weights = project(
        where, work, vector_weight, (*first_own, *first_near, *first_far, *first_got)
    )
    projected, up_own, down_block, send_grads = pin(projected, up_own, down_low, send_grads)

    up_near = to_neighbours(*up_own)
    down_own = stacked(along_z(down_block), 2)
    pairs = feature // 256
    attended_a, stats_a, carried = attend(projected, work, vector_weight, out_weights, 0, pairs)
    carried, up_near, down_own, send_grads = pin(carried, up_near, down_own, send_grads)

    up_far = to_diagonal(*up_near)
    up_got = to_partner(*up_own, *up_near)
    grads = exchange(send_grads.reshape(devices, capacity, feature)).reshape(count, feature)
    attended_b, stats_b, resid, low_two = attend(
        projected, work, vector_weight, out_weights, pairs, pairs, carried
    )
    low_two, up_far, up_got = pin(low_two, up_far, up_got)
    up_got = up_got + to_partner(*up_far)
    low_two, up_got, down_own = pin(low_two, up_got, down_own)

    down_near = to_neighbours(*down_own)
    hidden, slope, up_weights = widen(
        where, low_two, vector_weight[8:].reshape(1, FF), (*up_own, *up_near, *up_far, *up_got)
    )
    hidden, down_near = pin(hidden, down_near)

    down_far = to_diagonal(*down_near)
    down_got = to_partner(*down_own, *down_near)
    down_mine, down_theirs = down_gradient(where, hidden, grads, depth)
    down_far, down_got, down_mine, down_theirs = pin(down_far, down_got, down_mine, down_theirs)

    got = send(down_theirs, 1)
    down_got = down_got + to_partner(*down_far)
    down_got, got = pin(down_got, got)
    down_fold = Fold(down_mine, got)
    down_to, down_got = pin(down_fold.diagonal(), down_got)

    got = over_diagonal(*down_to)
    output, down_weights = narrow(
        where, hidden, resid, vector_weight, (*down_own, *down_near, *down_far, *down_got)
    )
    output, down_weights, got = pin(output, down_weights, got)
    down_to, output = pin(down_fold.neighbours(*got), output)

    back_out = exchange(output.reshape(devices, capacity, feature)).reshape(count, feature)
    got = over_plane(*down_to)
    dresid, dlow, sums_two, bias_up_grad, up_mine, up_theirs = feed_back(
        where, slope, low_two, grads, resid, vector_weight, up_weights, down_weights,
        (attended_a, attended_b), depth,
    )
    dlow, got, up_mine, up_theirs, back_out = pin(dlow, got, up_mine, up_theirs, back_out)
    down_sums, dlow, up_theirs = pin(down_fold.column(*got), dlow, up_theirs)

    down_got = over_column(down_sums)
    up_got = send(up_theirs, 1)
    dleft, sums_left = attend_back(projected, work, stats_a, dlow, out_weights, 0, pairs)
    up_got, dleft, dlow = pin(up_got, dleft, dlow)
    up_fold = Fold(up_mine, up_got)
    up_to, dlow = pin(up_fold.diagonal(), dlow)

    up_got = over_diagonal(*up_to)
    dright, sums_right = attend_back(projected, work, stats_b, dlow, out_weights, pairs, pairs)
    up_got, dright, down_got = pin(up_got, dright, down_got)
    up_to, dright = pin(up_fold.neighbours(*up_got), dright)

    up_got = over_plane(*up_to)
    both = project_back(
        work, (dleft, dright), dresid, vector_weight, first_weights,
        sums_two, (sums_left, sums_right), bias_up_grad, devices,
    )
    both, dright = pin(both, dright)

    back = exchange(both.reshape(devices, capacity, -1))
    first_mine, first_theirs = first_gradient(where, flipped_one, (dleft, dright), depth)
    first_mine, first_theirs, up_got = pin(first_mine, first_theirs, up_got)

    first_got = send(first_theirs, 1)
    up_sums = up_fold.column(*up_got)
    first_got, up_sums = pin(first_got, up_sums)
    first_fold = Fold(first_mine, first_got)
    first_to, up_sums = pin(first_fold.diagonal(), up_sums)

    got = pin(*over_diagonal(*first_to))
    first_to, back, up_sums = pin(first_fold.neighbours(*got), back, up_sums)
    up_got = over_column(up_sums)

    got = over_plane(*first_to)
    got, up_first = pin(got, up_got[0])
    first_sums, back_out, down_got = pin(first_fold.column(*got), back_out, down_got)
    down_grad = total_of(down_sums[0], *down_got)

    first_got = over_column(first_sums)
    up_grad = total_of(up_sums[0], up_first, *up_got[1:])
    squares = jnp.sum(up_grad * up_grad) + jnp.sum(down_grad * down_grad)
    block_output = give_back(slot, back_out)
    first_got, up_grad, block_output, down_grad, squares = pin(
        first_got, up_grad, block_output, down_grad, squares
    )
    first_grad, packet = settle(first_sums[0], first_got, back, squares, devices, feature)
    packets = exchange(packet)
    input_grad = give_back(slot, back.reshape(count, -1))
    grad_norm, *new = finish(
        packets, first_grad, up_grad, down_grad,
        (wide_weight, wide_moment, wide_average),
        (down_weight, down_moment, down_average),
        (vector_weight, vector_moment, vector_average),
    )
    return (block_output, input_grad, grad_norm.reshape(()), *new)


def solution(mesh):
    placed = (
        P("dev", None),
        P("dev", None),
        P("dev"),
        P("dev", None),
        P("dev", None),
        P("dev", None),
        P("dev", None),
        P("dev", None),
        P("dev", None),
        P(),
        P(),
        P(),
    )
    return jax.shard_map(
        body,
        mesh=mesh,
        in_specs=placed,
        out_specs=(
            P("dev", None),
            P("dev", None),
            P(),
            P("dev", None),
            P("dev", None),
            P("dev", None),
            P("dev", None),
            P("dev", None),
            P("dev", None),
            P(),
            P(),
            P(),
        ),
        check_vma=False,
    )
```
